32 devices in a mesh: expert: 4 (over y, x), shard: 8 (over z, core).
Axes of the slice: x: 2, y: 2, z: 4, core: 2. Of those that a mesh axis runs over, the one named last changes fastest.
Arguments:
- inputs: bfloat16 [16384, 1536], P(('expert', 'shard')), may hold values from -6 to 6
- attn_gain: bfloat16 [1536], P('shard'), may hold values from 0.5 to 1.5
- qkv_weight: bfloat16 [1536, 2560], P('shard'), may hold values from -0.21875 to 0.21875
- out_weight: bfloat16 [1536, 1536], P('shard'), may hold values from -0.4375 to 0.4375
- ffn_gain: bfloat16 [1536], P('shard'), may hold values from 0.5 to 1.5
- router_weight: bfloat16 [1536, 20], P('shard'), may hold values from -0.078125 to 0.078125
- expand_weight: bfloat16 [20, 1536, 1024], P('expert', 'shard'), may hold values from -0.15625 to 0.15625
- project_weight: bfloat16 [20, 512, 1536], P('expert', 'shard'), may hold values from -1.5 to 1.5
- segment_ids: int32 [32, 512], P(('expert', 'shard')), may hold values from 0 to 3, never falling along the last dimension, each value on 1 to 256 neighbouring positions
- routes: int32 [16384, 8], P(('expert', 'shard')), may hold values from 0 to 19, all different within a row; in each aligned block of 512 rows (0 to 511, 512 to 1023, ...) at most 256 rows name the same one
- out_grad: bfloat16 [16384, 1536], P(('expert', 'shard')), may hold values from -6 to 6
Outputs:
- output: bfloat16 [16384, 1536], P(('expert', 'shard'))
- input_grad: float32 [16384, 1536], P(('expert', 'shard'))
- attn_gain_grad: float32 [1536], P('shard')
- qkv_grad: float32 [1536, 2560], P('shard')
- out_weight_grad: float32 [1536, 1536], P('shard')
- ffn_gain_grad: float32 [1536], P('shard')
- router_grad: float32 [1536, 20], P('shard')
- expand_grad: float32 [20, 1536, 1024], P('expert', 'shard')
- project_grad: float32 [20, 512, 1536], P('expert', 'shard')
The draws below stay inside these ranges and needn't reach their ends.
Inputs may be any that keep to these rules, and one draw needn't show every extreme that they name: `routes`: each row names 8 different experts. Within the 512 rows of one device no expert is named by more than 256 rows, and in every draw some expert is named by exactly 256 rows of some device. `segment_ids`: along each sequence the numbers never fall; each document holds 1 to 256 places and one holds exactly 256.
All inputs are finite; a program needn't handle non-finite values.
Results may differ from the reference program's by a relative error of at most 0.023.
Values may be sent and summed in bfloat16 or wider, within the bound.
A program may use at most 320 MiB of HBM per device.

```python
import math
import jax
import jax.numpy as jnp
import numpy as np
from jax import lax

D = 1536
HEADS = 24
KV_HEADS = 8
HEAD = 64
FF = 512
TOP = 8
SEQ_LEN = 512
EXPERTS = 20
TOK_DEV = 512
TOKENS = 16384
SEQS = 32
CAP = 256
N_EXPERT = 4
N_SHARD = 8


def with_spikes(drawn, rng, source, target, parts, factor):
    def block_of(position):
        return (jnp.arange(drawn.shape[position]) // (drawn.shape[position] // parts)).reshape((-1,) + (1,) * (drawn.ndim - 1 - position))

    near = jax.random.permutation(rng, parts)[block_of(target)]
    second = (block_of(target) + parts // 2) % parts
    return jnp.where((block_of(source) == near) | (block_of(source) == second), factor * drawn, drawn)


def levels(rng, extent, cuts, least, top_value):
    factor_of, own = 1.0, jax.random.fold_in(rng, 6)
    for axis_at, shards_of in cuts:
        draws = jnp.exp(jax.random.uniform(jax.random.fold_in(own, axis_at), (shards_of,), jnp.float32, least / len(cuts), top_value / len(cuts)))
        factor_of = factor_of * jnp.repeat(draws, extent[axis_at] // shards_of).reshape([-1 if axis == axis_at else 1 for axis in range(len(extent))])
    return factor_of


def profile(amount, total, reach, slope):
    weights = [(1 << 20) // math.isqrt(standing ** slope) + 1 for standing in range(2, amount + 1)]
    surplus, given = total - reach - (amount - 1), [1] * (amount - 1)
    while surplus > 0:
        candidates = [i for i in range(amount - 1) if given[i] < reach]
        whole, remaining = sum([weights[i] for i in candidates]), surplus
        for i in candidates:
            extra = min(reach - given[i], max(1, remaining * weights[i] // whole), surplus)
            given[i] = given[i] + extra
            surplus = surplus - extra
    return np.array([reach] + given)


def uneven_parts(rng, amount, total, limit, slope):
    if amount == 2:
        one = jax.random.randint(rng, (), max(1, total - limit), min(limit, total - 1) + 1)
        return jnp.stack([one, total - one])
    tallies = jnp.asarray(profile(amount, total, limit, slope), jnp.int32)
    pairs = (amount - 1) // 2
    donor, sink = tallies[1:1 + 2 * pairs:2], tallies[2:2 + 2 * pairs:2]
    margin = jnp.minimum(donor - 1, limit - sink)
    shifted = jax.random.randint(jax.random.fold_in(rng, 1), (pairs,), 0, 1 << 20) % (margin + 1)
    tallies = tallies.at[1:1 + 2 * pairs:2].set(donor - shifted).at[2:2 + 2 * pairs:2].set(sink + shifted)
    return tallies[jax.random.permutation(jax.random.fold_in(rng, 2), amount)]


def deal_out(stream_key, own, number, rows, count, top, reach, skew):
    sequence = jax.random.permutation(stream_key, count)
    heavy_load, common = portions_of(count, rows * top, reach, skew, True), portions_of(count, rows * top, reach, skew, False)
    places = jnp.arange(count)

    def named(sizes, rotation):
        used = int((sizes > 0).sum())
        fixed = max(1, used // 4)
        passed = fixed + (places - fixed + rotation * (used - fixed)) % max(1, count - fixed)
        return jnp.zeros((count,), jnp.int32).at[sequence[jnp.where(places < fixed, places, passed)]].set(jnp.asarray(sizes, jnp.int32))

    sizes = jnp.where(number % 4 == 0, named(heavy_load, number // 4), named(common, number - number // 4 - 1))
    mixed = jax.random.permutation(jax.random.fold_in(own, 3), count)
    donor, taker = mixed[0:count // 2 * 2:2], mixed[1:count // 2 * 2:2]
    slack = jnp.minimum(sizes[donor] - 1, reach - sizes[taker]) // 2
    slack = jnp.where((donor == sequence[0]) | (taker == sequence[0]) | (sizes[taker] == 0), 0, jnp.maximum(slack, 0))
    passed = jax.random.randint(jax.random.fold_in(own, 4), (count // 2,), 0, 1 << 20) % (slack + 1)
    sizes = sizes.at[donor].add(-passed).at[taker].add(passed)
    items = jnp.searchsorted(jnp.cumsum(sizes), jnp.arange(rows * top), side="right").astype(jnp.int32)
    table = items.reshape(top, rows).T
    table = table[jax.random.permutation(jax.random.fold_in(own, 1), rows)]
    rotation = jax.random.randint(jax.random.fold_in(own, 2), (rows, 1), 0, top)
    return jnp.take_along_axis(table, (jnp.arange(top)[None, :] + rotation) % top, axis=1)


def portions_of(count, total, most, skew, full):
    loads = [(1 << 20) // math.isqrt(grade ** skew) + 1 for grade in range(1, count + 1)]
    largest = most if full else min(most, max(-(-total // count), total * loads[0] // sum(loads)))
    least = 1 if total - largest >= count - 1 else 0
    given, rest = [largest] + [least] * (count - 1), total - largest - least * (count - 1)
    while rest > 0:
        free = [i for i in range(1, count) if given[i] < largest] or [i for i in range(1, count) if given[i] < most]
        mass, budget = sum([loads[i] for i in free]), rest
        for i in free:
            more = min(most - given[i], max(1, budget * loads[i] // mass), rest)
            given[i] = given[i] + more
            rest = rest - more
    return np.array(given)


def centred(stream_key, extent, spread, most, split=(), held_as=jnp.bfloat16):
    gain = levels(stream_key, extent, split, -0.22, 0.18) if split else 1.0
    values = jax.random.normal(stream_key, extent, jnp.float32) * spread * gain
    return jnp.minimum(jnp.maximum(values, -most), most).astype(held_as)


def noise_with(key, extent, scale, bound, pieces, heavy, held_as=jnp.bfloat16):
    entries = scale * jax.random.normal(key, extent, jnp.float32)
    if pieces:
        entries = entries * levels(key, extent, pieces, -0.22, 0.18)
    return jnp.clip(with_spikes(entries, jax.random.fold_in(key, 3), *heavy), -bound, bound).astype(held_as)


def setup_inputs(seed: int = 0) -> dict:
    splits = jax.random.split(jax.random.key(seed), 12)
    inputs = noise_with(splits[0], (TOKENS, D), 1.0, 6.0, ((0, 32),), (0, 1, 32, 2.75))
    attn_gain = jnp.clip(1.0 + 0.1 * jax.random.normal(splits[1], (D,), jnp.float32), 0.5, 1.5).astype(jnp.bfloat16)
    qkv_weight = centred(splits[2], (D, (HEADS + 2 * KV_HEADS) * HEAD), (D // 2) ** -0.5, 0.21875, ((0, 8),))
    out_weight = centred(splits[3], (HEADS * HEAD, D), (HEADS * HEAD // 8) ** -0.5, 0.4375, ((0, 8),))
    ffn_gain = jnp.clip(1.0 + 0.1 * jax.random.normal(splits[4], (D,), jnp.float32), 0.5, 1.5).astype(jnp.bfloat16)
    router_weight = centred(splits[5], (D, EXPERTS), (4 * D) ** -0.5, 0.078125, ((0, 8),))
    expand_weight = centred(splits[6], (EXPERTS, D, 2 * FF), D ** -0.5, 0.15625, ((0, 4), (1, 8)))
    project_weight = centred(splits[7], (EXPERTS, FF, D), (FF // 32) ** -0.5, 1.5, ((0, 4), (1, 8)))
    segment_ids = jax.vmap(lambda own: jnp.searchsorted(jnp.cumsum(uneven_parts(own, 4, SEQ_LEN, SEQ_LEN // 2, 1)), jnp.arange(SEQ_LEN), side="right"))(jax.random.split(splits[8], SEQS)).reshape((SEQS, SEQ_LEN)).astype(jnp.int32)
    routes_keys = jax.random.split(jax.random.fold_in(splits[9], 1), TOKENS // TOK_DEV)
    routes_turns = jax.random.permutation(jax.random.fold_in(splits[9], 3), TOKENS // TOK_DEV)
    routes = jax.vmap(lambda own, number: deal_out(jax.random.fold_in(splits[9], 2), own, number, TOK_DEV, EXPERTS, TOP, CAP, 1))(routes_keys, routes_turns).reshape((TOKENS, TOP))
    out_grad = noise_with(splits[10], (TOKENS, D), 1.0, 6.0, ((0, 32),), (0, 1, 32, 2.75))
    return dict(inputs=inputs, attn_gain=attn_gain, qkv_weight=qkv_weight, out_weight=out_weight, ffn_gain=ffn_gain, router_weight=router_weight, expand_weight=expand_weight, project_weight=project_weight, segment_ids=segment_ids, routes=routes, out_grad=out_grad)


EPSILON = 1e-06
ROPE_THETA = 10000.0
MASKED = -1e+30
HIGHEST = lax.Precision.HIGHEST

@jax.custom_vjp
def low(v):
    return lax.optimization_barrier(v.astype(jnp.bfloat16)).astype(jnp.float32)

@jax.custom_vjp
def low_back(v):
    return v

def low_keep(v):
    return (low(v), None)

def low_pass(kept, grad):
    return (grad,)

def back_keep(v):
    return (v, None)

def back_low(kept, grad):
    return (low(grad),)
low.defvjp(low_keep, low_pass)
low_back.defvjp(back_keep, back_low)

def rms_scale(values):
    return lax.rsqrt(lax.optimization_barrier(jnp.mean(values * values, axis=-1, keepdims=True)) + EPSILON)

def angles():
    frequency = ROPE_THETA ** (-2.0 * jnp.arange(HEAD // 2, dtype=jnp.float32) / HEAD)
    positions = jnp.arange(SEQ_LEN, dtype=jnp.float32)
    angle_table = positions[:, None] * frequency[None, :]
    return (jnp.cos(angle_table)[:, None, :], jnp.sin(angle_table)[:, None, :])

def rotary(values, cosine, sine_table):
    half_width = values.shape[-1] // 2
    first_half = values[..., :half_width]
    second_half = values[..., half_width:]
    return jnp.concatenate([first_half * cosine - second_half * sine_table, second_half * cosine + first_half * sine_table], axis=-1)

def sequence_attention(packed):
    queries, key_rows, value_rows, segments = packed
    group_size = HEADS // KV_HEADS
    grouped = queries.reshape(SEQ_LEN, KV_HEADS, group_size, HEAD)
    raw_scores = jnp.einsum('qcgd,kcd->cgqk', grouped, key_rows, precision=HIGHEST)
    scores = low_back(raw_scores * HEAD ** (-0.5))
    places = jnp.arange(SEQ_LEN, dtype=jnp.int32)
    allowed = (places[:, None] >= places[None, :]) & (segments[:, None] == segments[None, :])
    prob_rows = low(jax.nn.softmax(jnp.where(allowed, scores, MASKED), axis=-1))
    mixed_rows = jnp.einsum('cgqk,kcd->qcgd', prob_rows, value_rows, precision=HIGHEST)
    return mixed_rows.reshape(SEQ_LEN, HEADS * HEAD)

def mixture(ffn_in, gate_probs, routes, expand_weight, project_weight):
    window = N_EXPERT * N_SHARD * CAP
    flat_routes = routes.reshape(-1)
    expert_ids = jnp.arange(EXPERTS, dtype=jnp.int32)
    counts = lax.optimization_barrier(jnp.sum((flat_routes[:, None] == expert_ids[None, :]).astype(jnp.int32), axis=0)).astype(jnp.int32)
    starts = (jnp.cumsum(counts) - counts).astype(jnp.int32)
    sorted_index = jnp.argsort(flat_routes, stable=True).astype(jnp.int32)
    padded = jnp.concatenate([sorted_index, jnp.zeros((window,), jnp.int32)])
    offsets = jnp.arange(window, dtype=jnp.int32)
    entry_table = padded[starts[:, None] + offsets[None, :]]
    live_table = offsets[None, :] < counts[:, None]
    token_table = (entry_table // TOP).astype(jnp.int32)
    gate_table = jnp.where(live_table, gate_probs.reshape(-1)[entry_table], 0.0)

    def one_expert(packed):
        token_rows, gate_weights, expand_one, project_one = packed
        rows_in = low_back(ffn_in[token_rows])
        both_parts = low_back(jnp.dot(rows_in, expand_one, precision=HIGHEST))
        inner_rows = low(jax.nn.silu(both_parts[:, :FF]) * both_parts[:, FF:])
        result = low(low_back(jnp.dot(inner_rows, project_one, precision=HIGHEST)))
        return gate_weights[:, None] * result
    weighted = lax.map(jax.checkpoint(one_expert), (token_table, gate_table, expand_weight, project_weight))
    return jnp.zeros((TOKENS, D), jnp.float32).at[token_table.reshape(-1)].add(weighted.reshape(-1, D))

def forward(inputs, attn_gain, qkv_weight, out_weight, ffn_gain, router_weight, expand_weight, project_weight, segment_ids, routes):
    query_width = HEADS * HEAD
    key_width = KV_HEADS * HEAD
    normed = low(inputs * rms_scale(inputs) * attn_gain)
    projected = low_back(jnp.dot(normed, qkv_weight, precision=HIGHEST))
    cosine, sine_table = angles()
    queries = low(rotary(projected[:, :query_width].reshape(SEQS, SEQ_LEN, HEADS, HEAD), cosine, sine_table))
    key_rows = low(rotary(projected[:, query_width:query_width + key_width].reshape(SEQS, SEQ_LEN, KV_HEADS, HEAD), cosine, sine_table))
    value_rows = low(projected[:, query_width + key_width:].reshape(SEQS, SEQ_LEN, KV_HEADS, HEAD))
    mixed_rows = lax.map(jax.checkpoint(sequence_attention), (queries, key_rows, value_rows, segment_ids))
    mixed_rows = low(low_back(mixed_rows.reshape(SEQS * SEQ_LEN, query_width)))
    attended = low_back(jnp.dot(mixed_rows, out_weight, precision=HIGHEST))
    hidden = inputs + attended
    ffn_in = low(hidden * rms_scale(hidden) * ffn_gain)
    logits = low_back(jnp.dot(ffn_in, router_weight, precision=HIGHEST))
    gate_probs = jax.nn.softmax(jnp.take_along_axis(logits, routes, axis=1), axis=-1)
    return hidden + mixture(ffn_in, gate_probs, routes, expand_weight, project_weight)

def reference(inputs, attn_gain, qkv_weight, out_weight, ffn_gain, router_weight, expand_weight, project_weight, segment_ids, routes, out_grad):
    floats = tuple((member.astype(jnp.float32) for member in (inputs, attn_gain, qkv_weight, out_weight, ffn_gain, router_weight, expand_weight, project_weight)))

    def whole_layer(*weights):
        return forward(*weights, segment_ids, routes)
    output, pullback = jax.vjp(whole_layer, *floats)
    gradients = pullback(out_grad.astype(jnp.float32))
    return (output.astype(jnp.bfloat16), gradients[0], gradients[1], gradients[2], gradients[3], gradients[4], gradients[5], gradients[6], gradients[7])
```

```python
import functools

import jax
import jax.numpy as jnp
import numpy as np
from jax import lax
from jax.experimental import pallas as pl
from jax.experimental.pallas import tpu as pltpu
from jax.sharding import PartitionSpec as P

HEADS = 24
KV_HEADS = 8
HEAD = 64
FF = 512
TOP = 8
SEQ_LEN = 512
GROUP = HEADS // KV_HEADS
PAIRS = KV_HEADS // 2
QW = 2 * GROUP * HEAD
KW = 2 * HEAD
BLOCK = QW + 2 * KW
MISC = 128
QB = 128

EPSILON = 1e-06
ROPE_THETA = 10000.0
MASKED = -1e30
F32 = jnp.float32
BF16 = jnp.bfloat16


def dot_nn(a, b):
    return lax.dot_general(a, b, (((1,), (0,)), ((), ())), preferred_element_type=F32)


def dot_nt(a, b):
    return lax.dot_general(a, b, (((1,), (1,)), ((), ())), preferred_element_type=F32)


def dot_tn(a, b):
    return lax.dot_general(a, b, (((0,), (0,)), ((), ())), preferred_element_type=F32)


def rope_tables():
    frequency = (np.float32(ROPE_THETA) ** (-2.0 * np.arange(HEAD // 2) / HEAD)).astype(np.float32)
    angle = np.arange(SEQ_LEN, dtype=np.float32)[:, None] * frequency[None, :]
    cosine, sine = np.cos(angle).astype(np.float32), np.sin(angle).astype(np.float32)
    zero = np.zeros_like(sine)
    cos_table = np.concatenate([cosine] * 4, axis=1)
    left_table = np.concatenate([-sine, zero] * 2, axis=1)
    right_table = np.concatenate([zero, sine] * 2, axis=1)
    return cos_table, left_table, right_table


def turn(values, cos_table, left_table, right_table, sign):
    parts = []
    for c in range(values.shape[1] // 128):
        piece = values[:, 128 * c : 128 * (c + 1)]
        ahead = pltpu.roll(piece, 96, 1) * left_table
        behind = pltpu.roll(piece, 32, 1) * right_table
        parts.append(piece * cos_table + sign * (ahead + behind))
    return parts[0] if len(parts) == 1 else jnp.concatenate(parts, axis=1)


def key_range(block):
    return max(0, block - 2) * QB, (block + 1) * QB


def block_mask(seg_col, seg_row, block):
    low, high = key_range(block)
    rows = lax.broadcasted_iota(jnp.int32, (QB, high - low), 0) + block * QB
    cols = lax.broadcasted_iota(jnp.int32, (QB, high - low), 1) + low
    same = seg_col[block * QB : (block + 1) * QB, :] == seg_row[:, low:high]
    return jnp.concatenate([(rows >= cols) & same] * GROUP, axis=0)


def heads_of(values, pair, block):
    rows = values[block * QB : (block + 1) * QB, :]
    first = pair * GROUP
    return jnp.concatenate(
        [rows[:, HEAD * h : HEAD * (h + 1)] for h in range(first, first + GROUP)], axis=0
    )


def attention_forward_kernel(
    x_ref, gain_ref, w_ref, cos_ref, left_ref, right_ref, seg_col_ref, seg_row_ref,
    normed_ref, proj_ref, mixed_ref, lse_ref,
):
    @pl.when(pl.program_id(0) == 0)
    def _():
        x = x_ref[...].astype(F32)
        scale = lax.rsqrt(jnp.mean(x * x, axis=-1, keepdims=True) + EPSILON)
        normed_ref[...] = (x * scale * gain_ref[...].astype(F32)).astype(BF16)

    projected = dot_nn(normed_ref[...], w_ref[...])
    turned = turn(
        projected[:, : QW + KW], cos_ref[...], left_ref[...], right_ref[...], 1.0
    ).astype(BF16)
    queries, keys = turned[:, :QW], turned[:, QW:]
    values = projected[:, QW + KW :].astype(BF16)
    proj_ref[...] = jnp.concatenate([turned, values], axis=1)
    seg_col, seg_row = seg_col_ref[...], seg_row_ref[...]
    for block in range(SEQ_LEN // QB):
        low, high = key_range(block)
        allowed = block_mask(seg_col, seg_row, block)
        outs = []
        for pair in range(2):
            q3 = heads_of(queries, pair, block)
            k1 = keys[low:high, HEAD * pair : HEAD * (pair + 1)]
            v1 = values[low:high, HEAD * pair : HEAD * (pair + 1)]
            scores = jnp.where(allowed, dot_nt(q3, k1) * HEAD**-0.5, MASKED)
            top = jnp.max(scores, axis=-1, keepdims=True)
            weights = jnp.exp(scores - top)
            total = jnp.sum(weights, axis=-1, keepdims=True)
            mixed = dot_nn(weights.astype(BF16), v1) * (1.0 / total)
            logsum = top + jnp.log(total)
            for h in range(GROUP):
                outs.append(mixed[h * QB : (h + 1) * QB, :])
                lse_ref[0, block * QB : (block + 1) * QB, pair * GROUP + h : pair * GROUP + h + 1] = (
                    logsum[h * QB : (h + 1) * QB, :]
                )
        mixed_ref[block * QB : (block + 1) * QB, :] = jnp.concatenate(outs, axis=1).astype(BF16)


def whole_spec(shape):
    return pl.BlockSpec(shape, lambda *_: (0,) * len(shape))


def attention_forward(x, gain_row, w_full, tables, seg_col, seg_row):
    tokens, width = x.shape
    table = whole_spec((SEQ_LEN, 128))
    return pl.pallas_call(
        attention_forward_kernel,
        grid=(PAIRS,),
        in_specs=[
            whole_spec((tokens, width)),
            whole_spec((1, width)),
            pl.BlockSpec((width, BLOCK), lambda j: (0, j)),
            table, table, table,
            whole_spec((SEQ_LEN, 1)),
            whole_spec((1, SEQ_LEN)),
        ],
        out_specs=[
            whole_spec((tokens, width)),
            pl.BlockSpec((tokens, BLOCK), lambda j: (0, j)),
            pl.BlockSpec((tokens, QW), lambda j: (0, j)),
            pl.BlockSpec((1, tokens, 8), lambda j: (j, 0, 0)),
        ],
        out_shape=[
            jax.ShapeDtypeStruct((tokens, width), BF16),
            jax.ShapeDtypeStruct((tokens, PAIRS * BLOCK), BF16),
            jax.ShapeDtypeStruct((tokens, HEADS * HEAD), BF16),
            jax.ShapeDtypeStruct((PAIRS, tokens, 8), F32),
        ],
        compiler_params=pltpu.CompilerParams(vmem_limit_bytes=48 << 20),
        cost_estimate=pl.CostEstimate(flops=10 * 10**9, bytes_accessed=20 << 20, transcendentals=4 << 20),
        name="attention_forward",
    )(x, gain_row, w_full, *tables, seg_col, seg_row)


def attention_backward_kernel(
    ag_ref, out_ref, proj_ref, mixed_ref, lse_ref, cos_ref, left_ref, right_ref,
    seg_col_ref, seg_row_ref, dproj_ref,
):
    grads = dot_nt(ag_ref[...], out_ref[...]).astype(BF16)
    product = grads.astype(F32) * mixed_ref[...].astype(F32)
    queries, keys, values = (
        proj_ref[:, :QW], proj_ref[:, QW : QW + KW], proj_ref[:, QW + KW :],
    )
    seg_col, seg_row = seg_col_ref[...], seg_row_ref[...]
    blocks = SEQ_LEN // QB
    dk = [[jnp.zeros((QB, HEAD), F32) for _ in range(blocks)] for _ in range(2)]
    dv = [[jnp.zeros((QB, HEAD), F32) for _ in range(blocks)] for _ in range(2)]
    dq_rows = []
    for block in range(blocks):
        low, high = key_range(block)
        allowed = block_mask(seg_col, seg_row, block)
        dqs = []
        for pair in range(2):
            q3, g3, o3 = (heads_of(v, pair, block) for v in (queries, grads, product))
            k1 = keys[low:high, HEAD * pair : HEAD * (pair + 1)]
            v1 = values[low:high, HEAD * pair : HEAD * (pair + 1)]
            logsum = jnp.concatenate(
                [
                    lse_ref[0, block * QB : (block + 1) * QB, pair * GROUP + h : pair * GROUP + h + 1]
                    for h in range(GROUP)
                ],
                axis=0,
            )
            scores = jnp.where(allowed, dot_nt(q3, k1) * HEAD**-0.5, MASKED)
            probs = jnp.exp(scores - logsum)
            inner = jnp.sum(o3, axis=-1, keepdims=True)
            score_grads = (probs * (dot_nt(g3, v1) - inner)).astype(BF16)
            dq = dot_nn(score_grads, k1)
            dk_part = dot_tn(score_grads, q3)
            dv_part = dot_tn(probs.astype(BF16), g3)
            for at in range(low // QB, high // QB):
                rows = slice(at * QB - low, (at + 1) * QB - low)
                dk[pair][at] += dk_part[rows]
                dv[pair][at] += dv_part[rows]
            dqs += [dq[h * QB : (h + 1) * QB, :] for h in range(GROUP)]
        dq_rows.append(jnp.concatenate(dqs, axis=1))
    dq_all = jnp.concatenate(dq_rows, axis=0)
    dk_all = jnp.concatenate([jnp.concatenate(d, axis=0) for d in dk], axis=1)
    dv_all = jnp.concatenate([jnp.concatenate(d, axis=0) for d in dv], axis=1)
    turned = jnp.concatenate([dq_all, dk_all], axis=1) * HEAD**-0.5
    back = turn(turned, cos_ref[...], left_ref[...], right_ref[...], -1.0)
    dproj_ref[...] = jnp.concatenate([back, dv_all], axis=1).astype(BF16)


def attention_backward(ag, out_full, proj, mixed, lse, tables, seg_col, seg_row):
    tokens, width = ag.shape
    table = whole_spec((SEQ_LEN, 128))
    return pl.pallas_call(
        attention_backward_kernel,
        grid=(PAIRS,),
        in_specs=[
            whole_spec((tokens, width)),
            pl.BlockSpec((QW, width), lambda j: (j, 0)),
            pl.BlockSpec((tokens, BLOCK), lambda j: (0, j)),
            pl.BlockSpec((tokens, QW), lambda j: (0, j)),
            pl.BlockSpec((1, tokens, 8), lambda j: (j, 0, 0)),
            table, table, table,
            whole_spec((SEQ_LEN, 1)),
            whole_spec((1, SEQ_LEN)),
        ],
        out_specs=pl.BlockSpec((tokens, BLOCK), lambda j: (0, j)),
        out_shape=jax.ShapeDtypeStruct((tokens, PAIRS * BLOCK), BF16),
        compiler_params=pltpu.CompilerParams(vmem_limit_bytes=48 << 20),
        cost_estimate=pl.CostEstimate(flops=10 * 10**9, bytes_accessed=20 << 20, transcendentals=4 << 20),
        name="attention_backward",
    )(ag, out_full, proj, mixed, lse, *tables, seg_col, seg_row)


def middle_kernel(
    mixed_ref, out_ref, x_ref, gain_ref, router_ref, routes_ref,
    hidden_ref, ffn_ref, gates_ref, slots_ref,
):
    hidden = x_ref[...].astype(F32) + dot_nn(mixed_ref[...], out_ref[...])
    scale = lax.rsqrt(jnp.mean(hidden * hidden, axis=-1, keepdims=True) + EPSILON)
    hidden_ref[...] = hidden
    ffn_in = (hidden * scale * gain_ref[...].astype(F32)).astype(BF16)
    ffn_ref[...] = ffn_in
    logits = dot_nt(router_ref[...], ffn_in)
    experts, tokens = logits.shape
    index = lax.broadcasted_iota(jnp.int32, (experts, tokens), 0)
    flags = index == routes_ref[0:1, :]
    for k in range(1, TOP):
        flags = flags | (index == routes_ref[k : k + 1, :])
    chosen = jnp.where(flags, logits, MASKED)
    weights = jnp.where(flags, jnp.exp(chosen - jnp.max(chosen, axis=0, keepdims=True)), 0.0)
    gates_ref[...] = weights / jnp.sum(weights, axis=0, keepdims=True)
    earlier = lax.broadcasted_iota(jnp.int32, (tokens, tokens), 0)
    later = lax.broadcasted_iota(jnp.int32, (tokens, tokens), 1)
    before = jnp.where(earlier < later, 1.0, 0.0).astype(BF16)
    ranks = dot_nn(jnp.where(flags, 1.0, 0.0).astype(BF16), before)
    slots_ref[...] = jnp.where(flags, ranks, -1.0)


def middle(mixed, out_full, x, gain_row, router_rows, routes_rows):
    tokens, width = x.shape
    experts = router_rows.shape[0]
    return pl.pallas_call(
        middle_kernel,
        out_shape=[
            jax.ShapeDtypeStruct((tokens, width), F32),
            jax.ShapeDtypeStruct((tokens, width), BF16),
            jax.ShapeDtypeStruct((experts, tokens), F32),
            jax.ShapeDtypeStruct((experts, tokens), F32),
        ],
        compiler_params=pltpu.CompilerParams(vmem_limit_bytes=48 << 20),
        cost_estimate=pl.CostEstimate(flops=3 * 10**9, bytes_accessed=16 << 20, transcendentals=1 << 14),
        name="middle",
    )(mixed, out_full, x, gain_row, router_rows, routes_rows)


def expert_kernel(capacity, expert, first, *refs):
    x_ref, u_ref, meta_ref, we_ref, wp_ref = refs[:5]
    refs = refs[5:]
    if not first:
        out_in_ref, dx_in_ref = refs[:2]
        refs = refs[2:]
    out_ref, dx_ref, gg_ref, dwe_ref, dwp_ref, xs_ref, us_ref, bs_ref, is_ref = refs
    g = pl.program_id(0)
    tokens = x_ref.shape[1]
    slot_row = meta_ref[0, expert : expert + 1, :]
    gate_row = meta_ref[0, 8 + expert : 9 + expert, :]
    index = lax.broadcasted_iota(jnp.int32, (capacity, tokens), 0).astype(F32)
    pick = jnp.where(index == slot_row, 1.0, 0.0)
    gate_col = jnp.sum(pick * gate_row, axis=1, keepdims=True)
    place = pick.astype(BF16)
    rows = pl.ds(pl.multiple_of(g * capacity, capacity), capacity)
    x = dot_nn(place, x_ref[0]).astype(BF16)
    xs_ref[rows, :] = x
    u_rows = dot_nn(place, u_ref[0]).astype(BF16)
    us_ref[rows, :] = u_rows
    gate = dot_nn(x, we_ref[:, :FF])
    up = dot_nn(x, we_ref[:, FF:])
    back = dot_nt(u_rows, wp_ref[...])
    sig = 1.0 / (1.0 + jnp.exp(-gate))
    act = gate * sig
    inner = act * up
    inner_low = inner.astype(BF16)
    gate_grad = jnp.sum(inner * back, axis=1, keepdims=True)
    gg_ref[0] = jnp.broadcast_to(jnp.sum(pick * gate_grad, axis=0, keepdims=True), (8, tokens))
    is_ref[rows, :] = (inner * gate_col).astype(BF16)
    inner_grads = back * gate_col
    gate_back = inner_grads * up * sig * (1.0 + gate * (1.0 - sig))
    both = jnp.concatenate([gate_back, inner_grads * act], axis=1).astype(BF16)
    bs_ref[rows, :] = both
    result = dot_nn(inner_low, wp_ref[...]).astype(BF16)
    weighted = (pick * gate_row).astype(BF16)
    out_part = dot_tn(weighted, result)
    row_grads = dot_nt(both, we_ref[...]).astype(BF16)
    dx_part = dot_tn(place, row_grads)
    if not first:
        out_part = out_part + out_in_ref[0].astype(F32)
        dx_part = dx_part + dx_in_ref[0].astype(F32)
    out_ref[0] = out_part.astype(BF16)
    dx_ref[0] = dx_part.astype(BF16)

    @pl.when(g == pl.num_programs(0) - 1)
    def _():
        step = 256

        @pl.loop(0, xs_ref.shape[1] // step)
        def _(c):
            at = pl.ds(pl.multiple_of(c * step, step), step)
            dwe_ref[at, :] = dot_tn(xs_ref[:, at], bs_ref[...]).astype(BF16)

        @pl.loop(0, FF // step)
        def _(c):
            at = pl.ds(pl.multiple_of(c * step, step), step)
            dwp_ref[at, :] = dot_tn(is_ref[:, at], us_ref[...]).astype(BF16)


def expert_call(capacity, expert, x_all, u_all, meta, we, wp, carried):
    groups, tokens, width = x_all.shape
    first = carried is None
    rows = groups * capacity
    block = pl.BlockSpec((1, tokens, width), lambda g: (g, 0, 0))
    single = pl.Buffered(buffer_count=1)
    held = jax.ShapeDtypeStruct((groups, tokens, width), BF16)
    flops = 2 * rows * width * (4 * tokens + 9 * FF)
    return pl.pallas_call(
        functools.partial(expert_kernel, capacity, expert, first),
        grid=(groups,),
        in_specs=[
            block,
            block,
            pl.BlockSpec((1,) + meta.shape[1:], lambda g: (g, 0, 0)),
            pl.BlockSpec(we.shape, lambda g: (0, 0), pipeline_mode=single),
            pl.BlockSpec(wp.shape, lambda g: (0, 0), pipeline_mode=single),
        ]
        + ([] if first else [block, block]),
        out_specs=[
            block,
            block,
            pl.BlockSpec((1, 8, tokens), lambda g: (g, 0, 0)),
            pl.BlockSpec(we.shape, lambda g: (0, 0)),
            pl.BlockSpec(wp.shape, lambda g: (0, 0)),
        ],
        out_shape=[
            held,
            held,
            jax.ShapeDtypeStruct((groups, 8, tokens), F32),
            jax.ShapeDtypeStruct(we.shape, BF16),
            jax.ShapeDtypeStruct(wp.shape, BF16),
        ],
        scratch_shapes=[
            pltpu.VMEM((rows, width), BF16),
            pltpu.VMEM((rows, width), BF16),
            pltpu.VMEM((rows, 2 * FF), BF16),
            pltpu.VMEM((rows, FF), BF16),
        ],
        compiler_params=pltpu.CompilerParams(vmem_limit_bytes=60 << 20),
        cost_estimate=pl.CostEstimate(
            flops=flops, bytes_accessed=6 * groups * tokens * width * 2, transcendentals=rows * FF
        ),
        name="expert",
    )(x_all, u_all, meta, we, wp, *(() if first else carried))


def norm_back(values, gain_row, grad_rows):
    scale_rows = lax.rsqrt(jnp.mean(values * values, axis=-1, keepdims=True) + EPSILON)
    weighted = gain_row * grad_rows
    inner_mean = jnp.mean(weighted * values, axis=-1, keepdims=True)
    input_part = (
        scale_rows * weighted - values * (scale_rows * scale_rows * scale_rows) * inner_mean
    )
    gain_part = jnp.sum(grad_rows * values * scale_rows, axis=0)
    return (input_part, gain_part)


def to_blocks(weight):
    rows = weight.shape[0]
    qs = weight[:, : HEADS * HEAD].reshape(rows, PAIRS, QW)
    ks = weight[:, HEADS * HEAD : (HEADS + KV_HEADS) * HEAD].reshape(rows, PAIRS, KW)
    vs = weight[:, (HEADS + KV_HEADS) * HEAD :].reshape(rows, PAIRS, KW)
    return jnp.concatenate([qs, ks, vs], axis=2).reshape(rows, PAIRS * BLOCK)


def from_blocks(weight):
    rows = weight.shape[0]
    parts = weight.reshape(rows, PAIRS, BLOCK)
    return jnp.concatenate(
        [
            parts[:, :, :QW].reshape(rows, PAIRS * QW),
            parts[:, :, QW : QW + KW].reshape(rows, PAIRS * KW),
            parts[:, :, QW + KW :].reshape(rows, PAIRS * KW),
        ],
        axis=1,
    )


def shifted(value, distance, groups):
    if distance % groups == 0:
        return value
    return lax.ppermute(value, "expert", [(i, (i + distance) % groups) for i in range(groups)])


def local(
    inputs, attn_gain, qkv_weight, out_weight, ffn_gain, router_weight,
    expand_weight, project_weight, segment_ids, routes, out_grad,
):
    groups = lax.axis_size("expert")
    me = lax.axis_index("expert")
    tokens, width = inputs.shape
    experts = router_weight.shape[1]
    local_count = expand_weight.shape[0]
    capacity = 8 * ((5 * tokens * TOP + 32 * experts - 1) // (32 * experts))

    misc = jnp.concatenate(
        [
            attn_gain[:, None],
            ffn_gain[:, None],
            router_weight,
            jnp.zeros((attn_gain.shape[0], MISC - 2 - experts), BF16),
        ],
        axis=1,
    )
    packed = jnp.concatenate([to_blocks(qkv_weight), misc], axis=1)
    qkv_full = lax.all_gather(packed, "shard", axis=0, tiled=True)
    out_full = lax.all_gather(out_weight, "shard", axis=0, tiled=True)
    expand_full = [
        lax.all_gather(expand_weight[e], "shard", axis=0, tiled=True) for e in range(local_count)
    ]
    project_full = [
        lax.all_gather(project_weight[e], "shard", axis=0, tiled=True) for e in range(local_count)
    ]
    u_all = jnp.stack([shifted(out_grad, d, groups) for d in range(groups)])

    misc_rows = qkv_full[:, PAIRS * BLOCK :].T
    gain_one, gain_two = misc_rows[0:1], misc_rows[1:2]
    router_rows = misc_rows[2 : 2 + experts]
    tables = tuple(jnp.asarray(t) for t in rope_tables())
    seg_row = segment_ids.reshape(1, tokens)
    seg_col = segment_ids.reshape(tokens, 1)
    normed, proj, mixed, lse = attention_forward(
        inputs, gain_one, qkv_full, tables, seg_col, seg_row
    )
    hidden, ffn_in, gates, slots = middle(
        mixed, out_full, inputs, gain_two, router_rows, routes.T
    )

    def by_group(rows):
        return jnp.pad(
            rows.reshape(groups, local_count, tokens), ((0, 0), (0, 8 - local_count), (0, 0))
        )

    meta_out = jnp.concatenate([by_group(slots), by_group(gates)], axis=1)
    x_all = jnp.stack([shifted(ffn_in, d, groups) for d in range(groups)])
    meta = jnp.stack(
        [
            shifted(
                lax.dynamic_index_in_dim(meta_out, (me + d) % groups, 0, keepdims=False), d, groups
            )
            for d in range(groups)
        ]
    )

    carried, gate_grads, expand_grads, project_grads = None, [], [], []
    for e in range(local_count):
        out_acc, dx_acc, gg, dwe, dwp = expert_call(
            capacity, e, x_all, u_all, meta, expand_full[e], project_full[e], carried
        )
        carried = (out_acc, dx_acc)
        gate_grads.append(gg[:, 0])
        expand_grads.append(lax.psum_scatter(dwe, "shard", scatter_dimension=0, tiled=True))
        project_grads.append(lax.psum_scatter(dwp, "shard", scatter_dimension=0, tiled=True))
    expand_grad = jnp.stack(expand_grads).astype(F32)
    project_grad = jnp.stack(project_grads).astype(F32)

    gg_sent = jnp.stack(gate_grads, axis=1)
    gg_home = jnp.stack([shifted(gg_sent[d], -d, groups) for d in range(groups)])
    gg_dense = jnp.roll(gg_home, me, axis=0).reshape(experts, tokens)
    dx_home = [shifted(dx_acc[d], -d, groups) for d in range(groups)]
    out_home = [shifted(out_acc[d], -d, groups) for d in range(groups)]
    output = (hidden + sum(o.astype(F32) for o in out_home)).astype(BF16)

    logit_grads = (
        gates * (gg_dense - jnp.sum(gates * gg_dense, axis=0, keepdims=True))
    ).astype(BF16)
    router_part = dot_nn(logit_grads, ffn_in)
    ffn_grads = dot_tn(logit_grads, router_rows) + sum(d.astype(F32) for d in dx_home)
    upstream = out_grad.astype(F32)
    hidden_part, gain_two_grad = norm_back(hidden, gain_two.astype(F32), ffn_grads)
    hidden_grads = upstream + hidden_part
    attended_grads = hidden_grads.astype(BF16)
    dproj = attention_backward(
        attended_grads, out_full, proj, mixed, lse, tables, seg_col, seg_row
    )
    out_part = dot_tn(mixed, attended_grads).astype(BF16)
    qkv_part = dot_tn(normed, dproj).astype(BF16)
    normed_grads = dot_nt(dproj, qkv_full[:, : PAIRS * BLOCK])
    input_part, gain_one_grad = norm_back(
        inputs.astype(F32), gain_one.astype(F32), normed_grads
    )
    input_grad = hidden_grads + input_part

    misc_part = jnp.concatenate(
        [
            gain_one_grad[None],
            gain_two_grad[None],
            router_part,
            jnp.zeros((MISC - 2 - experts, width), F32),
        ],
        axis=0,
    ).astype(BF16)
    out_share = lax.psum_scatter(out_part, "shard", scatter_dimension=0, tiled=True)
    qkv_share = lax.psum_scatter(
        jnp.concatenate([qkv_part, misc_part.T], axis=1), "shard", scatter_dimension=0, tiled=True
    )
    out_total = lax.psum(out_share, "expert").astype(F32)
    qkv_total = lax.psum(qkv_share, "expert").astype(F32)
    misc_total = qkv_total[:, PAIRS * BLOCK :]
    return (
        output,
        input_grad,
        misc_total[:, 0],
        from_blocks(qkv_total[:, : PAIRS * BLOCK]),
        out_total,
        misc_total[:, 1],
        misc_total[:, 2 : 2 + experts],
        expand_grad,
        project_grad,
    )


def solution(mesh):
    rows = P(("expert", "shard"), None)
    return jax.shard_map(
        local,
        mesh=mesh,
        in_specs=(
            rows, P("shard"), P("shard", None), P("shard", None), P("shard"), P("shard", None),
            P("expert", "shard", None), P("expert", "shard", None), rows, rows, rows,
        ),
        out_specs=(
            rows, rows, P("shard"), P("shard", None), P("shard", None), P("shard"),
            P("shard", None), P("expert", "shard", None), P("expert", "shard", None),
        ),
        check_vma=False,
    )
```

```python
import functools

import jax
import jax.numpy as jnp
import numpy as np
from jax import lax
from jax.experimental import pallas as pl
from jax.experimental.pallas import tpu as pltpu
from jax.sharding import PartitionSpec as P

HEADS = 24
KV_HEADS = 8
HEAD = 64
FF = 512
TOP = 8
SEQ_LEN = 512
GROUP = HEADS // KV_HEADS
PAIRS = KV_HEADS // 2
QW = 2 * GROUP * HEAD
KW = 2 * HEAD
BLOCK = QW + 2 * KW
MISC = 128
QB = 128

EPSILON = 1e-06
ROPE_THETA = 10000.0
MASKED = -1e30
F32 = jnp.float32
BF16 = jnp.bfloat16


def dot_nn(a, b):
    return lax.dot_general(a, b, (((1,), (0,)), ((), ())), preferred_element_type=F32)


def dot_nt(a, b):
    return lax.dot_general(a, b, (((1,), (1,)), ((), ())), preferred_element_type=F32)


def dot_tn(a, b):
    return lax.dot_general(a, b, (((0,), (0,)), ((), ())), preferred_element_type=F32)


def rope_tables():
    frequency = (np.float32(ROPE_THETA) ** (-2.0 * np.arange(HEAD // 2) / HEAD)).astype(np.float32)
    angle = np.arange(SEQ_LEN, dtype=np.float32)[:, None] * frequency[None, :]
    cosine, sine = np.cos(angle).astype(np.float32), np.sin(angle).astype(np.float32)
    zero = np.zeros_like(sine)
    cos_table = np.concatenate([cosine] * 4, axis=1)
    left_table = np.concatenate([-sine, zero] * 2, axis=1)
    right_table = np.concatenate([zero, sine] * 2, axis=1)
    return cos_table, left_table, right_table


def turn(values, cos_table, left_table, right_table, sign):
    parts = []
    for c in range(values.shape[1] // 128):
        piece = values[:, 128 * c : 128 * (c + 1)]
        ahead = pltpu.roll(piece, 96, 1) * left_table
        behind = pltpu.roll(piece, 32, 1) * right_table
        parts.append(piece * cos_table + sign * (ahead + behind))
    return parts[0] if len(parts) == 1 else jnp.concatenate(parts, axis=1)


def key_range(block):
    return max(0, block - 2) * QB, (block + 1) * QB


def block_mask(seg_col, seg_row, block):
    low, high = key_range(block)
    rows = lax.broadcasted_iota(jnp.int32, (QB, high - low), 0) + block * QB
    cols = lax.broadcasted_iota(jnp.int32, (QB, high - low), 1) + low
    same = seg_col[block * QB : (block + 1) * QB, :] == seg_row[:, low:high]
    return jnp.concatenate([(rows >= cols) & same] * GROUP, axis=0)


def heads_of(values, pair, block):
    rows = values[block * QB : (block + 1) * QB, :]
    first = pair * GROUP
    return jnp.concatenate(
        [rows[:, HEAD * h : HEAD * (h + 1)] for h in range(first, first + GROUP)], axis=0
    )


def attention_forward_kernel(
    x_ref, gain_ref, w_ref, cos_ref, left_ref, right_ref, seg_col_ref, seg_row_ref,
    normed_ref, proj_ref, mixed_ref, lse_ref,
):
    @pl.when(pl.program_id(0) == 0)
    def _():
        x = x_ref[...].astype(F32)
        scale = lax.rsqrt(jnp.mean(x * x, axis=-1, keepdims=True) + EPSILON)
        normed_ref[...] = (x * scale * gain_ref[...].astype(F32)).astype(BF16)

    projected = dot_nn(normed_ref[...], w_ref[...])
    turned = turn(
        projected[:, : QW + KW], cos_ref[...], left_ref[...], right_ref[...], 1.0
    ).astype(BF16)
    queries, keys = turned[:, :QW], turned[:, QW:]
    values = projected[:, QW + KW :].astype(BF16)
    proj_ref[...] = jnp.concatenate([turned, values], axis=1)
    seg_col, seg_row = seg_col_ref[...], seg_row_ref[...]
    for block in range(SEQ_LEN // QB):
        low, high = key_range(block)
        allowed = block_mask(seg_col, seg_row, block)
        outs = []
        for pair in range(2):
            q3 = heads_of(queries, pair, block)
            k1 = keys[low:high, HEAD * pair : HEAD * (pair + 1)]
            v1 = values[low:high, HEAD * pair : HEAD * (pair + 1)]
            scores = jnp.where(allowed, dot_nt(q3, k1) * HEAD**-0.5, MASKED)
            top = jnp.max(scores, axis=-1, keepdims=True)
            weights = jnp.exp(scores - top)
            total = jnp.sum(weights, axis=-1, keepdims=True)
            mixed = dot_nn(weights.astype(BF16), v1) * (1.0 / total)
            logsum = top + jnp.log(total)
            for h in range(GROUP):
                outs.append(mixed[h * QB : (h + 1) * QB, :])
                lse_ref[0, block * QB : (block + 1) * QB, pair * GROUP + h : pair * GROUP + h + 1] = (
                    logsum[h * QB : (h + 1) * QB, :]
                )
        mixed_ref[block * QB : (block + 1) * QB, :] = jnp.concatenate(outs, axis=1).astype(BF16)


def whole_spec(shape):
    return pl.BlockSpec(shape, lambda *_: (0,) * len(shape))


def attention_forward(x, gain_row, w_full, tables, seg_col, seg_row):
    tokens, width = x.shape
    table = whole_spec((SEQ_LEN, 128))
    return pl.pallas_call(
        attention_forward_kernel,
        grid=(PAIRS,),
        in_specs=[
            whole_spec((tokens, width)),
            whole_spec((1, width)),
            pl.BlockSpec((width, BLOCK), lambda j: (0, j)),
            table, table, table,
            whole_spec((SEQ_LEN, 1)),
            whole_spec((1, SEQ_LEN)),
        ],
        out_specs=[
            whole_spec((tokens, width)),
            pl.BlockSpec((tokens, BLOCK), lambda j: (0, j)),
            pl.BlockSpec((tokens, QW), lambda j: (0, j)),
            pl.BlockSpec((1, tokens, 8), lambda j: (j, 0, 0)),
        ],
        out_shape=[
            jax.ShapeDtypeStruct((tokens, width), BF16),
            jax.ShapeDtypeStruct((tokens, PAIRS * BLOCK), BF16),
            jax.ShapeDtypeStruct((tokens, HEADS * HEAD), BF16),
            jax.ShapeDtypeStruct((PAIRS, tokens, 8), F32),
        ],
        compiler_params=pltpu.CompilerParams(vmem_limit_bytes=48 << 20),
        cost_estimate=pl.CostEstimate(flops=10 * 10**9, bytes_accessed=20 << 20, transcendentals=4 << 20),
        name="attention_forward",
    )(x, gain_row, w_full, *tables, seg_col, seg_row)


def attention_backward_kernel(
    ag_ref, out_ref, proj_ref, mixed_ref, lse_ref, cos_ref, left_ref, right_ref,
    seg_col_ref, seg_row_ref, dproj_ref,
):
    grads = dot_nt(ag_ref[...], out_ref[...]).astype(BF16)
    product = grads.astype(F32) * mixed_ref[...].astype(F32)
    queries, keys, values = (
        proj_ref[:, :QW], proj_ref[:, QW : QW + KW], proj_ref[:, QW + KW :],
    )
    seg_col, seg_row = seg_col_ref[...], seg_row_ref[...]
    blocks = SEQ_LEN // QB
    dk = [[jnp.zeros((QB, HEAD), F32) for _ in range(blocks)] for _ in range(2)]
    dv = [[jnp.zeros((QB, HEAD), F32) for _ in range(blocks)] for _ in range(2)]
    dq_rows = []
    for block in range(blocks):
        low, high = key_range(block)
        allowed = block_mask(seg_col, seg_row, block)
        dqs = []
        for pair in range(2):
            q3, g3, o3 = (heads_of(v, pair, block) for v in (queries, grads, product))
            k1 = keys[low:high, HEAD * pair : HEAD * (pair + 1)]
            v1 = values[low:high, HEAD * pair : HEAD * (pair + 1)]
            logsum = jnp.concatenate(
                [
                    lse_ref[0, block * QB : (block + 1) * QB, pair * GROUP + h : pair * GROUP + h + 1]
                    for h in range(GROUP)
                ],
                axis=0,
            )
            scores = jnp.where(allowed, dot_nt(q3, k1) * HEAD**-0.5, MASKED)
            probs = jnp.exp(scores - logsum)
            inner = jnp.sum(o3, axis=-1, keepdims=True)
            score_grads = (probs * (dot_nt(g3, v1) - inner)).astype(BF16)
            dq = dot_nn(score_grads, k1)
            dk_part = dot_tn(score_grads, q3)
            dv_part = dot_tn(probs.astype(BF16), g3)
            for at in range(low // QB, high // QB):
                rows = slice(at * QB - low, (at + 1) * QB - low)
                dk[pair][at] += dk_part[rows]
                dv[pair][at] += dv_part[rows]
            dqs += [dq[h * QB : (h + 1) * QB, :] for h in range(GROUP)]
        dq_rows.append(jnp.concatenate(dqs, axis=1))
    dq_all = jnp.concatenate(dq_rows, axis=0)
    dk_all = jnp.concatenate([jnp.concatenate(d, axis=0) for d in dk], axis=1)
    dv_all = jnp.concatenate([jnp.concatenate(d, axis=0) for d in dv], axis=1)
    turned = jnp.concatenate([dq_all, dk_all], axis=1) * HEAD**-0.5
    back = turn(turned, cos_ref[...], left_ref[...], right_ref[...], -1.0)
    dproj_ref[...] = jnp.concatenate([back, dv_all], axis=1).astype(BF16)


def attention_backward(ag, out_full, proj, mixed, lse, tables, seg_col, seg_row):
    tokens, width = ag.shape
    table = whole_spec((SEQ_LEN, 128))
    return pl.pallas_call(
        attention_backward_kernel,
        grid=(PAIRS,),
        in_specs=[
            whole_spec((tokens, width)),
            pl.BlockSpec((QW, width), lambda j: (j, 0)),
            pl.BlockSpec((tokens, BLOCK), lambda j: (0, j)),
            pl.BlockSpec((tokens, QW), lambda j: (0, j)),
            pl.BlockSpec((1, tokens, 8), lambda j: (j, 0, 0)),
            table, table, table,
            whole_spec((SEQ_LEN, 1)),
            whole_spec((1, SEQ_LEN)),
        ],
        out_specs=pl.BlockSpec((tokens, BLOCK), lambda j: (0, j)),
        out_shape=jax.ShapeDtypeStruct((tokens, PAIRS * BLOCK), BF16),
        compiler_params=pltpu.CompilerParams(vmem_limit_bytes=48 << 20),
        cost_estimate=pl.CostEstimate(flops=10 * 10**9, bytes_accessed=20 << 20, transcendentals=4 << 20),
        name="attention_backward",
    )(ag, out_full, proj, mixed, lse, *tables, seg_col, seg_row)


def middle_kernel(
    mixed_ref, out_ref, x_ref, gain_ref, router_ref, routes_ref,
    hidden_ref, ffn_ref, gates_ref, slots_ref,
):
    hidden = x_ref[...].astype(F32) + dot_nn(mixed_ref[...], out_ref[...])
    scale = lax.rsqrt(jnp.mean(hidden * hidden, axis=-1, keepdims=True) + EPSILON)
    hidden_ref[...] = hidden
    ffn_in = (hidden * scale * gain_ref[...].astype(F32)).astype(BF16)
    ffn_ref[...] = ffn_in
    logits = dot_nt(router_ref[...], ffn_in)
    experts, tokens = logits.shape
    index = lax.broadcasted_iota(jnp.int32, (experts, tokens), 0)
    flags = index == routes_ref[0:1, :]
    for k in range(1, TOP):
        flags = flags | (index == routes_ref[k : k + 1, :])
    chosen = jnp.where(flags, logits, MASKED)
    weights = jnp.where(flags, jnp.exp(chosen - jnp.max(chosen, axis=0, keepdims=True)), 0.0)
    gates_ref[...] = weights / jnp.sum(weights, axis=0, keepdims=True)
    earlier = lax.broadcasted_iota(jnp.int32, (tokens, tokens), 0)
    later = lax.broadcasted_iota(jnp.int32, (tokens, tokens), 1)
    before = jnp.where(earlier < later, 1.0, 0.0).astype(BF16)
    ranks = dot_nn(jnp.where(flags, 1.0, 0.0).astype(BF16), before)
    slots_ref[...] = jnp.where(flags, ranks, -1.0)


def middle(mixed, out_full, x, gain_row, router_rows, routes_rows):
    tokens, width = x.shape
    experts = router_rows.shape[0]
    return pl.pallas_call(
        middle_kernel,
        out_shape=[
            jax.ShapeDtypeStruct((tokens, width), F32),
            jax.ShapeDtypeStruct((tokens, width), BF16),
            jax.ShapeDtypeStruct((experts, tokens), F32),
            jax.ShapeDtypeStruct((experts, tokens), F32),
        ],
        compiler_params=pltpu.CompilerParams(vmem_limit_bytes=48 << 20),
        cost_estimate=pl.CostEstimate(flops=3 * 10**9, bytes_accessed=16 << 20, transcendentals=1 << 14),
        name="middle",
    )(mixed, out_full, x, gain_row, router_rows, routes_rows)


def expert_kernel(capacity, shards, expert, first, *refs):
    x_ref, u_ref, meta_ref, we_ref, wp_ref = refs[:5]
    refs = refs[5:]
    if not first:
        out_in_ref, dx_in_ref = refs[:2]
        refs = refs[2:]
    out_ref, dx_ref, gg_ref, dw_ref, xs_ref, us_ref, bs_ref, is_ref = refs
    g = pl.program_id(0)
    tokens = x_ref.shape[1]
    slot_row = meta_ref[0, expert : expert + 1, :]
    gate_row = meta_ref[0, 8 + expert : 9 + expert, :]
    index = lax.broadcasted_iota(jnp.int32, (capacity, tokens), 0).astype(F32)
    pick = jnp.where(index == slot_row, 1.0, 0.0)
    gate_col = jnp.sum(pick * gate_row, axis=1, keepdims=True)
    place = pick.astype(BF16)
    rows = pl.ds(pl.multiple_of(g * capacity, capacity), capacity)
    x = dot_nn(place, x_ref[0]).astype(BF16)
    xs_ref[rows, :] = x
    u_rows = dot_nn(place, u_ref[0]).astype(BF16)
    us_ref[rows, :] = u_rows
    gate = dot_nn(x, we_ref[0, :, :FF])
    up = dot_nn(x, we_ref[0, :, FF:])
    back = dot_nt(u_rows, wp_ref[0])
    sig = 1.0 / (1.0 + jnp.exp(-gate))
    act = gate * sig
    inner = act * up
    inner_low = inner.astype(BF16)
    gate_grad = jnp.sum(inner * back, axis=1, keepdims=True)
    gg_ref[0] = jnp.broadcast_to(jnp.sum(pick * gate_grad, axis=0, keepdims=True), (8, tokens))
    is_ref[rows, :] = (inner * gate_col).astype(BF16)
    inner_grads = back * gate_col
    gate_back = inner_grads * up * sig * (1.0 + gate * (1.0 - sig))
    both = jnp.concatenate([gate_back, inner_grads * act], axis=1).astype(BF16)
    bs_ref[rows, :] = both
    result = dot_nn(inner_low, wp_ref[0]).astype(BF16)
    weighted = (pick * gate_row).astype(BF16)
    out_part = dot_tn(weighted, result)
    row_grads = dot_nt(both, we_ref[0]).astype(BF16)
    dx_part = dot_tn(place, row_grads)
    if not first:
        out_part = out_part + out_in_ref[0].astype(F32)
        dx_part = dx_part + dx_in_ref[0].astype(F32)
    out_ref[0] = out_part.astype(BF16)
    dx_ref[0] = dx_part.astype(BF16)

    @pl.when(g == pl.num_programs(0) - 1)
    def _():
        step, half = 384, FF // 2
        tall, short = xs_ref.shape[1] // shards, FF // shards
        side = xs_ref.shape[1] - 2 * FF

        @pl.loop(0, xs_ref.shape[1] // step)
        def _(c):
            at = pl.ds(pl.multiple_of(c * step, step), step)
            value = dot_tn(xs_ref[:, at], bs_ref[...]).astype(BF16)
            for i in range(step // tall):
                dw_ref[c * (step // tall) + i, :tall, :] = value[i * tall : (i + 1) * tall]

        @pl.loop(0, FF // half)
        def _(c):
            at = pl.ds(pl.multiple_of(c * half, half), half)
            value = dot_tn(is_ref[:, at], us_ref[...]).astype(BF16)
            for i in range(half // short):
                s, low = c * (half // short) + i, i * short
                middle_row, high = low + short // 2, low + short
                dw_ref[s, tall : tall + short, :] = value[low:high, : 2 * FF]
                dw_ref[s, tall + short :, :side] = value[low:middle_row, 2 * FF :]
                dw_ref[s, tall + short :, side:] = value[middle_row:high, 2 * FF :]


def expert_call(capacity, shards, expert, x_all, u_all, meta, we, wp, at, carried):
    groups, tokens, width = x_all.shape
    first = carried is None
    rows = groups * capacity
    packed = (shards, (width + FF + FF // 2) // shards, 2 * FF)
    block = pl.BlockSpec((1, tokens, width), lambda g: (g, 0, 0))
    single = pl.Buffered(buffer_count=1)
    held = jax.ShapeDtypeStruct((groups, tokens, width), BF16)
    flops = 2 * rows * width * (4 * tokens + 9 * FF)
    return pl.pallas_call(
        functools.partial(expert_kernel, capacity, shards, expert, first),
        grid=(groups,),
        in_specs=[
            block,
            block,
            pl.BlockSpec((1,) + meta.shape[1:], lambda g: (g, 0, 0)),
            pl.BlockSpec((1,) + we.shape[1:], lambda g: (at, 0, 0), pipeline_mode=single),
            pl.BlockSpec((1,) + wp.shape[1:], lambda g: (at, 0, 0), pipeline_mode=single),
        ]
        + ([] if first else [block, block]),
        out_specs=[
            block,
            block,
            pl.BlockSpec((1, 8, tokens), lambda g: (g, 0, 0)),
            whole_spec(packed),
        ],
        out_shape=[
            held,
            held,
            jax.ShapeDtypeStruct((groups, 8, tokens), F32),
            jax.ShapeDtypeStruct(packed, BF16),
        ],
        scratch_shapes=[
            pltpu.VMEM((rows, width), BF16),
            pltpu.VMEM((rows, width), BF16),
            pltpu.VMEM((rows, 2 * FF), BF16),
            pltpu.VMEM((rows, FF), BF16),
        ],
        compiler_params=pltpu.CompilerParams(vmem_limit_bytes=60 << 20),
        cost_estimate=pl.CostEstimate(
            flops=flops, bytes_accessed=6 * groups * tokens * width * 2, transcendentals=rows * FF
        ),
        name="expert",
    )(x_all, u_all, meta, we, wp, *(() if first else carried))


def flipped(index, mask):
    out, bit = index, 1
    while bit <= mask:
        if mask & bit:
            out = out + bit - 2 * bit * ((index // bit) % 2)
        bit *= 2
    return out


def send(source, target, send_sem, recv_sem, device):
    return pltpu.make_async_remote_copy(
        src_ref=source, dst_ref=target, send_sem=send_sem, recv_sem=recv_sem,
        device_id=device, device_id_type=pl.DeviceIdType.MESH,
    )


def greet(devices):
    barrier = pltpu.get_barrier_semaphore()
    for device in devices:
        pl.semaphore_signal(barrier, inc=1, device_id=device, device_id_type=pl.DeviceIdType.MESH)
    pl.semaphore_wait(barrier, len(devices))


def gather_kernel(parts, levels, count, *refs):
    ins, outs = refs[:count], refs[count : 2 * count]
    local_sem, near_send, near_recv, team_send, team_recv, core_send, core_recv = refs[2 * count :]
    group, shard = lax.axis_index("expert"), lax.axis_index("shard")
    level, core = shard // 2, shard % 2
    part = group % parts
    other = shard + 1 - 2 * core
    far = [flipped(level, k) * 2 + core for k in range(levels)]
    far_other = [flipped(level, k) * 2 + 1 - core for k in range(levels)]
    team_part = [flipped(part, k) for k in range(parts)]
    team = [group - part + t for t in team_part]
    greet(
        [(group, other)]
        + [(group, far[k]) for k in range(1, levels)]
        + [(team[t], shard) for t in range(1, parts)]
    )
    sends = []

    def push(*args):
        copy = send(*args)
        copy.start()
        sends.append(copy)

    own = pl.ds(shard * parts, parts)
    locals_ = []
    for i in range(count):
        for k in range(1, levels):
            push(
                ins[i].at[part], outs[i].at[shard * parts + part],
                near_send.at[i, k], near_recv.at[i, k], (group, far[k]),
            )
    for i in range(count):
        push(ins[i], outs[i].at[own], core_send.at[i, 0, 0], core_recv.at[i, 0, 0], (group, other))
        copy = pltpu.make_async_copy(ins[i], outs[i].at[own], local_sem.at[i])
        copy.start()
        locals_.append(copy)
    for i in range(count):
        for k in range(1, levels):
            piece = outs[i].at[far[k] * parts + part]
            send(piece, piece, near_send.at[i, k], near_recv.at[i, k], (group, other)).wait_recv()
            for t in range(1, parts):
                push(piece, piece, team_send.at[i, k, t], team_recv.at[i, k, t], (team[t], shard))
            push(piece, piece, core_send.at[i, k, 0], core_recv.at[i, k, 0], (group, other))
        for k in range(1, levels):
            for t in range(1, parts):
                piece = outs[i].at[far[k] * parts + team_part[t]]
                send(
                    piece, piece, team_send.at[i, k, t], team_recv.at[i, k, t], (group, other)
                ).wait_recv()
                push(piece, piece, core_send.at[i, k, t], core_recv.at[i, k, t], (group, other))
    for i in range(count):
        piece = outs[i].at[pl.ds(other * parts, parts)]
        send(piece, piece, core_send.at[i, 0, 0], core_recv.at[i, 0, 0], (group, other)).wait_recv()
        for k in range(1, levels):
            for t in range(parts):
                piece = outs[i].at[far_other[k] * parts + team_part[t]]
                send(
                    piece, piece, core_send.at[i, k, t], core_recv.at[i, k, t], (group, other)
                ).wait_recv()
    for copy in sends:
        copy.wait_send()
    for copy in locals_:
        copy.wait()


def gather_weights(blocks, groups, shards):
    rows = blocks[0].shape[0]
    parts = next(p for p in (4, 2, 1) if groups % p == 0 and rows % (16 * p) == 0)
    levels, count = shards // 2, len(blocks)
    blocks = [b.reshape(parts, rows // parts, b.shape[1]) for b in blocks]
    dma = pltpu.SemaphoreType.DMA
    outs = pl.pallas_call(
        functools.partial(gather_kernel, parts, levels, count),
        in_specs=[pl.BlockSpec(memory_space=pl.ANY)] * count,
        out_specs=[pl.BlockSpec(memory_space=pl.ANY)] * count,
        out_shape=[
            jax.ShapeDtypeStruct((shards * parts,) + b.shape[1:], b.dtype) for b in blocks
        ],
        scratch_shapes=[
            dma((count,)),
            dma((count, levels)), dma((count, levels)),
            dma((count, levels, parts)), dma((count, levels, parts)),
            dma((count, levels, parts)), dma((count, levels, parts)),
        ],
        compiler_params=pltpu.CompilerParams(collective_id=0, has_side_effects=True),
        name="gather_weights",
    )(*blocks)
    return [o.reshape(shards * rows, o.shape[2]) for o in outs]


def reduce_kernel(groups, levels, rows, chunk, *refs):
    (mixed_ref, ag_ref, normed_ref, dproj_ref, misc_ref, out_ref,
     mixed_t, normed_t, held, from_core, from_group, summed, from_level, home) = refs[:14]
    core_send, core_recv, group_send, group_recv, level_send, level_recv, home_send, home_recv = refs[14:]
    group, shard = lax.axis_index("expert"), lax.axis_index("shard")
    level, core = shard // 2, shard % 2
    other = shard + 1 - 2 * core
    team = [flipped(group, t) for t in range(groups)]
    far = [flipped(level, k) for k in range(levels)]
    greet(
        [(group, other)]
        + [(group, far[k] * 2 + core) for k in range(1, levels)]
        + [(team[t], shard) for t in range(1, groups)]
    )
    sends = []

    def push(*args):
        copy = send(*args)
        copy.start()
        sends.append(copy)

    def arrived(piece, send_sem, recv_sem):
        send(piece, piece, send_sem, recv_sem, (group, other)).wait_recv()

    mixed_t[...] = mixed_ref[...].T
    normed_t[...] = normed_ref[...].T
    out_cols, qkv_cols = ag_ref.shape[1], dproj_ref.shape[1]
    sources = [
        (0, out_cols, mixed_t, ag_ref),
        (out_cols, out_cols + qkv_cols, normed_t, dproj_ref),
        (out_cols + qkv_cols, out_cols + qkv_cols + MISC, None, misc_ref),
    ]
    for k in range(groups):
        low, high = k * chunk, (k + 1) * chunk
        for start, stop, left, right in sources:
            a, b = max(low, start), min(high, stop)
            if a >= b:
                continue

            @pl.loop(0, 2 * levels)
            def _(s):
                at = pl.ds(pl.multiple_of(s * rows, rows), rows)
                if left is None:
                    value = right[at, a - start : b - start]
                else:
                    value = dot_nn(left[at, :], right[:, a - start : b - start]).astype(BF16)
                held[k, s % 2, s // 2, :, a - low : b - low] = value

        push(held.at[k, 1 - core], from_core.at[k], core_send.at[k], core_recv.at[k], (group, other))
    for k in range(groups):
        arrived(from_core.at[k], core_send.at[k], core_recv.at[k])

        @pl.loop(0, levels)
        def _(z):
            held[k, core, z] = (held[k, core, z].astype(F32) + from_core[k, z].astype(F32)).astype(BF16)

    order = list(range(1, levels)) + [0]
    for k in order:
        for t in range(1, groups):
            push(
                held.at[team[t], core, far[k]], from_group.at[t, k],
                group_send.at[t, k], group_recv.at[t, k], (team[t], shard),
            )
    for k in order:
        total = held[group, core, far[k]].astype(F32)
        for t in range(1, groups):
            arrived(from_group.at[t, k], group_send.at[t, k], group_recv.at[t, k])
            total = total + from_group[t, k].astype(F32)
        summed[k] = total.astype(BF16)
        if k:
            push(
                summed.at[k], from_level.at[k], level_send.at[k], level_recv.at[k],
                (group, far[k] * 2 + core),
            )
    total = summed[0].astype(F32)
    for k in range(1, levels):
        arrived(from_level.at[k], level_send.at[k], level_recv.at[k])
        total = total + from_level[k].astype(F32)
    home[0] = total.astype(BF16)
    for t in range(1, groups):
        push(home.at[0], home.at[t], home_send.at[t], home_recv.at[t], (team[t], shard))
    out_ref[group] = home[0]
    for t in range(1, groups):
        arrived(home.at[t], home_send.at[t], home_recv.at[t])
        out_ref[team[t]] = home[t]
    for copy in sends:
        copy.wait_send()


def reduce_weights(mixed, ag, normed, dproj, misc_cols, groups, shards):
    tokens, width = normed.shape
    levels, rows = shards // 2, width // shards
    total = ag.shape[1] + dproj.shape[1] + MISC
    chunk = 128 * (-(-total // (128 * groups)))
    dma = pltpu.SemaphoreType.DMA
    vmem = pl.BlockSpec(memory_space=pltpu.VMEM)
    piece = (rows, chunk)
    return pl.pallas_call(
        functools.partial(reduce_kernel, groups, levels, rows, chunk),
        in_specs=[vmem] * 5,
        out_specs=vmem,
        out_shape=jax.ShapeDtypeStruct((groups,) + piece, BF16),
        scratch_shapes=[
            pltpu.VMEM((mixed.shape[1], tokens), BF16),
            pltpu.VMEM((width, tokens), BF16),
            pltpu.VMEM((groups, 2, levels) + piece, BF16),
            pltpu.VMEM((groups, levels) + piece, BF16),
            pltpu.VMEM((groups, levels) + piece, BF16),
            pltpu.VMEM((levels,) + piece, BF16),
            pltpu.VMEM((levels,) + piece, BF16),
            pltpu.VMEM((groups,) + piece, BF16),
            dma((groups,)), dma((groups,)),
            dma((groups, levels)), dma((groups, levels)),
            dma((levels,)), dma((levels,)),
            dma((groups,)), dma((groups,)),
        ],
        compiler_params=pltpu.CompilerParams(
            collective_id=1, has_side_effects=True, vmem_limit_bytes=56 << 20
        ),
        cost_estimate=pl.CostEstimate(
            flops=2 * tokens * width * total, bytes_accessed=8 << 20, transcendentals=0
        ),
        name="reduce_weights",
    )(mixed, ag, normed, dproj, misc_cols)


def norm_back(values, gain_row, grad_rows):
    scale_rows = lax.rsqrt(jnp.mean(values * values, axis=-1, keepdims=True) + EPSILON)
    weighted = gain_row * grad_rows
    inner_mean = jnp.mean(weighted * values, axis=-1, keepdims=True)
    input_part = (
        scale_rows * weighted - values * (scale_rows * scale_rows * scale_rows) * inner_mean
    )
    gain_part = jnp.sum(grad_rows * values * scale_rows, axis=0)
    return (input_part, gain_part)


def to_blocks(weight):
    rows = weight.shape[0]
    qs = weight[:, : HEADS * HEAD].reshape(rows, PAIRS, QW)
    ks = weight[:, HEADS * HEAD : (HEADS + KV_HEADS) * HEAD].reshape(rows, PAIRS, KW)
    vs = weight[:, (HEADS + KV_HEADS) * HEAD :].reshape(rows, PAIRS, KW)
    return jnp.concatenate([qs, ks, vs], axis=2).reshape(rows, PAIRS * BLOCK)


def from_blocks(weight):
    rows = weight.shape[0]
    parts = weight.reshape(rows, PAIRS, BLOCK)
    return jnp.concatenate(
        [
            parts[:, :, :QW].reshape(rows, PAIRS * QW),
            parts[:, :, QW : QW + KW].reshape(rows, PAIRS * KW),
            parts[:, :, QW + KW :].reshape(rows, PAIRS * KW),
        ],
        axis=1,
    )


def shifted(value, distance, groups):
    if distance % groups == 0:
        return value
    return lax.ppermute(value, "expert", [(i, (i + distance) % groups) for i in range(groups)])


def bands(count):
    return [(0, 1)] + [(low, min(low + 2, count)) for low in range(1, count, 2)]


def local(
    inputs, attn_gain, qkv_weight, out_weight, ffn_gain, router_weight,
    expand_weight, project_weight, segment_ids, routes, out_grad,
):
    groups, shards = lax.axis_size("expert"), lax.axis_size("shard")
    me = lax.axis_index("expert")
    tokens, width = inputs.shape
    experts = router_weight.shape[1]
    local_count = expand_weight.shape[0]
    capacity = 8 * ((5 * tokens * TOP + 32 * experts - 1) // (32 * experts))

    misc = jnp.concatenate(
        [
            attn_gain[:, None],
            ffn_gain[:, None],
            router_weight,
            jnp.zeros((attn_gain.shape[0], MISC - 2 - experts), BF16),
        ],
        axis=1,
    )
    packed = jnp.concatenate([to_blocks(qkv_weight), misc], axis=1)
    expand_full, project_full, places = [], [], []
    for low, high in bands(local_count):
        expand_full.append(lax.all_gather(expand_weight[low:high], "shard", axis=1, tiled=True))
        project_full.append(lax.all_gather(project_weight[low:high], "shard", axis=1, tiled=True))
        places += [(len(expand_full) - 1, at) for at in range(high - low)]
    qkv_full, out_full = gather_weights([packed, out_weight], groups, shards)
    u_all = jnp.stack([shifted(out_grad, d, groups) for d in range(groups)])

    misc_rows = qkv_full[:, PAIRS * BLOCK :].T
    gain_one, gain_two = misc_rows[0:1], misc_rows[1:2]
    router_rows = misc_rows[2 : 2 + experts]
    tables = tuple(jnp.asarray(t) for t in rope_tables())
    seg_row = segment_ids.reshape(1, tokens)
    seg_col = segment_ids.reshape(tokens, 1)
    normed, proj, mixed, lse = attention_forward(
        inputs, gain_one, qkv_full, tables, seg_col, seg_row
    )
    hidden, ffn_in, gates, slots = middle(
        mixed, out_full, inputs, gain_two, router_rows, routes.T
    )

    def by_group(rows):
        return jnp.pad(
            rows.reshape(groups, local_count, tokens), ((0, 0), (0, 8 - local_count), (0, 0))
        )

    meta_out = jnp.concatenate([by_group(slots), by_group(gates)], axis=1)
    x_all = jnp.stack([shifted(ffn_in, d, groups) for d in range(groups)])
    meta = jnp.stack(
        [
            shifted(
                lax.dynamic_index_in_dim(meta_out, (me + d) % groups, 0, keepdims=False), d, groups
            )
            for d in range(groups)
        ]
    )

    carried, gate_grads, expand_grads, project_grads = None, [], [], []
    tall, short = expand_weight.shape[1], project_weight.shape[1]
    for e in range(local_count):
        band, at = places[e]
        out_acc, dx_acc, gg, dw = expert_call(
            capacity, shards, e, x_all, u_all, meta, expand_full[band], project_full[band], at, carried
        )
        carried = (out_acc, dx_acc)
        gate_grads.append(gg[:, 0])
        share = lax.psum_scatter(dw, "shard", scatter_dimension=0, tiled=True)[0].astype(F32)
        expand_grads.append(share[:tall])
        rest = share[tall + short :]
        side = jnp.concatenate([rest[:, : width - 2 * FF], rest[:, width - 2 * FF :]], axis=0)
        project_grads.append(jnp.concatenate([share[tall : tall + short], side], axis=1))
    expand_grad = jnp.stack(expand_grads)
    project_grad = jnp.stack(project_grads)

    gg_sent = jnp.stack(gate_grads, axis=1)
    gg_home = jnp.stack([shifted(gg_sent[d], -d, groups) for d in range(groups)])
    gg_dense = jnp.roll(gg_home, me, axis=0).reshape(experts, tokens)
    dx_home = [shifted(dx_acc[d], -d, groups) for d in range(groups)]
    out_home = [shifted(out_acc[d], -d, groups) for d in range(groups)]
    output = (hidden + sum(o.astype(F32) for o in out_home)).astype(BF16)

    logit_grads = (
        gates * (gg_dense - jnp.sum(gates * gg_dense, axis=0, keepdims=True))
    ).astype(BF16)
    router_part = dot_nn(logit_grads, ffn_in)
    ffn_grads = dot_tn(logit_grads, router_rows) + sum(d.astype(F32) for d in dx_home)
    upstream = out_grad.astype(F32)
    hidden_part, gain_two_grad = norm_back(hidden, gain_two.astype(F32), ffn_grads)
    hidden_grads = upstream + hidden_part
    attended_grads = hidden_grads.astype(BF16)
    dproj = attention_backward(
        attended_grads, out_full, proj, mixed, lse, tables, seg_col, seg_row
    )
    normed_grads = dot_nt(dproj, qkv_full[:, : PAIRS * BLOCK])
    input_part, gain_one_grad = norm_back(
        inputs.astype(F32), gain_one.astype(F32), normed_grads
    )
    input_grad = hidden_grads + input_part

    misc_part = jnp.concatenate(
        [
            gain_one_grad[None],
            gain_two_grad[None],
            router_part,
            jnp.zeros((MISC - 2 - experts, width), F32),
        ],
        axis=0,
    ).astype(BF16)
    shares = reduce_weights(
        mixed, attended_grads, normed, dproj, misc_part.T, groups, shards
    )
    totals = shares.transpose(1, 0, 2).reshape(tall, -1)
    out_cols, all_cols = out_weight.shape[1], out_weight.shape[1] + PAIRS * BLOCK
    misc_total = totals[:, all_cols : all_cols + MISC].astype(F32)
    return (
        output,
        input_grad,
        misc_total[:, 0],
        from_blocks(totals[:, out_cols:all_cols]).astype(F32),
        totals[:, :out_cols].astype(F32),
        misc_total[:, 1],
        misc_total[:, 2 : 2 + experts],
        expand_grad,
        project_grad,
    )


def solution(mesh):
    rows = P(("expert", "shard"), None)
    return jax.shard_map(
        local,
        mesh=mesh,
        in_specs=(
            rows, P("shard"), P("shard", None), P("shard", None), P("shard"), P("shard", None),
            P("expert", "shard", None), P("expert", "shard", None), rows, rows, rows,
        ),
        out_specs=(
            rows, rows, P("shard"), P("shard", None), P("shard", None), P("shard"),
            P("shard", None), P("expert", "shard", None), P("expert", "shard", None),
        ),
        check_vma=False,
    )
```

```python
import functools

import jax
import jax.numpy as jnp
import numpy as np
from jax import lax
from jax.experimental import pallas as pl
from jax.experimental.pallas import tpu as pltpu
from jax.sharding import PartitionSpec as P

HEADS = 24
KV_HEADS = 8
HEAD = 64
FF = 512
TOP = 8
SEQ_LEN = 512
GROUP = HEADS // KV_HEADS
PAIRS = KV_HEADS // 2
QW = 2 * GROUP * HEAD
KW = 2 * HEAD
BLOCK = QW + 2 * KW
MISC = 128
QB = 128

EPSILON = 1e-06
ROPE_THETA = 10000.0
MASKED = -1e30
F32 = jnp.float32
BF16 = jnp.bfloat16


def dot_nn(a, b):
    return lax.dot_general(a, b, (((1,), (0,)), ((), ())), preferred_element_type=F32)


def dot_nt(a, b):
    return lax.dot_general(a, b, (((1,), (1,)), ((), ())), preferred_element_type=F32)


def dot_tn(a, b):
    return lax.dot_general(a, b, (((0,), (0,)), ((), ())), preferred_element_type=F32)


def rope_tables():
    frequency = (np.float32(ROPE_THETA) ** (-2.0 * np.arange(HEAD // 2) / HEAD)).astype(np.float32)
    angle = np.arange(SEQ_LEN, dtype=np.float32)[:, None] * frequency[None, :]
    cosine, sine = np.cos(angle).astype(np.float32), np.sin(angle).astype(np.float32)
    zero = np.zeros_like(sine)
    cos_table = np.concatenate([cosine] * 4, axis=1)
    left_table = np.concatenate([-sine, zero] * 2, axis=1)
    right_table = np.concatenate([zero, sine] * 2, axis=1)
    return cos_table, left_table, right_table


def turn(values, cos_table, left_table, right_table, sign):
    parts = []
    for c in range(values.shape[1] // 128):
        piece = values[:, 128 * c : 128 * (c + 1)]
        ahead = pltpu.roll(piece, 96, 1) * left_table
        behind = pltpu.roll(piece, 32, 1) * right_table
        parts.append(piece * cos_table + sign * (ahead + behind))
    return parts[0] if len(parts) == 1 else jnp.concatenate(parts, axis=1)


def key_range(block):
    return max(0, block - 2) * QB, (block + 1) * QB


def block_mask(seg_col, seg_row, block):
    low, high = key_range(block)
    rows = lax.broadcasted_iota(jnp.int32, (QB, high - low), 0) + block * QB
    cols = lax.broadcasted_iota(jnp.int32, (QB, high - low), 1) + low
    same = seg_col[block * QB : (block + 1) * QB, :] == seg_row[:, low:high]
    return jnp.concatenate([(rows >= cols) & same] * GROUP, axis=0)


def heads_of(values, pair, block):
    rows = values[block * QB : (block + 1) * QB, :]
    first = pair * GROUP
    return jnp.concatenate(
        [rows[:, HEAD * h : HEAD * (h + 1)] for h in range(first, first + GROUP)], axis=0
    )


def attention_forward_kernel(
    x_ref, gain_ref, w_ref, cos_ref, left_ref, right_ref, seg_col_ref, seg_row_ref,
    normed_ref, proj_ref, mixed_ref, lse_ref,
):
    @pl.when(pl.program_id(0) == 0)
    def _():
        x = x_ref[...].astype(F32)
        scale = lax.rsqrt(jnp.mean(x * x, axis=-1, keepdims=True) + EPSILON)
        normed_ref[...] = (x * scale * gain_ref[...].astype(F32)).astype(BF16)

    projected = dot_nn(normed_ref[...], w_ref[...])
    turned = turn(
        projected[:, : QW + KW], cos_ref[...], left_ref[...], right_ref[...], 1.0
    ).astype(BF16)
    queries, keys = turned[:, :QW], turned[:, QW:]
    values = projected[:, QW + KW :].astype(BF16)
    proj_ref[...] = jnp.concatenate([turned, values], axis=1)
    seg_col, seg_row = seg_col_ref[...], seg_row_ref[...]
    for block in range(SEQ_LEN // QB):
        low, high = key_range(block)
        allowed = block_mask(seg_col, seg_row, block)
        outs = []
        for pair in range(2):
            q3 = heads_of(queries, pair, block)
            k1 = keys[low:high, HEAD * pair : HEAD * (pair + 1)]
            v1 = values[low:high, HEAD * pair : HEAD * (pair + 1)]
            scores = jnp.where(allowed, dot_nt(q3, k1) * HEAD**-0.5, MASKED)
            top = jnp.max(scores, axis=-1, keepdims=True)
            weights = jnp.exp(scores - top)
            total = jnp.sum(weights, axis=-1, keepdims=True)
            mixed = dot_nn(weights.astype(BF16), v1) * (1.0 / total)
            logsum = top + jnp.log(total)
            for h in range(GROUP):
                outs.append(mixed[h * QB : (h + 1) * QB, :])
                lse_ref[0, block * QB : (block + 1) * QB, pair * GROUP + h : pair * GROUP + h + 1] = (
                    logsum[h * QB : (h + 1) * QB, :]
                )
        mixed_ref[block * QB : (block + 1) * QB, :] = jnp.concatenate(outs, axis=1).astype(BF16)


def whole_spec(shape):
    return pl.BlockSpec(shape, lambda *_: (0,) * len(shape))


def attention_forward(x, gain_row, w_full, tables, seg_col, seg_row):
    tokens, width = x.shape
    table = whole_spec((SEQ_LEN, 128))
    return pl.pallas_call(
        attention_forward_kernel,
        grid=(PAIRS,),
        in_specs=[
            whole_spec((tokens, width)),
            whole_spec((1, width)),
            pl.BlockSpec((width, BLOCK), lambda j: (0, j)),
            table, table, table,
            whole_spec((SEQ_LEN, 1)),
            whole_spec((1, SEQ_LEN)),
        ],
        out_specs=[
            whole_spec((tokens, width)),
            pl.BlockSpec((tokens, BLOCK), lambda j: (0, j)),
            pl.BlockSpec((tokens, QW), lambda j: (0, j)),
            pl.BlockSpec((1, tokens, 8), lambda j: (j, 0, 0)),
        ],
        out_shape=[
            jax.ShapeDtypeStruct((tokens, width), BF16),
            jax.ShapeDtypeStruct((tokens, PAIRS * BLOCK), BF16),
            jax.ShapeDtypeStruct((tokens, HEADS * HEAD), BF16),
            jax.ShapeDtypeStruct((PAIRS, tokens, 8), F32),
        ],
        compiler_params=pltpu.CompilerParams(vmem_limit_bytes=48 << 20),
        cost_estimate=pl.CostEstimate(flops=10 * 10**9, bytes_accessed=20 << 20, transcendentals=4 << 20),
        name="attention_forward",
    )(x, gain_row, w_full, *tables, seg_col, seg_row)


def attention_backward_kernel(
    ag_ref, out_ref, proj_ref, mixed_ref, lse_ref, cos_ref, left_ref, right_ref,
    seg_col_ref, seg_row_ref, dproj_ref,
):
    grads = dot_nt(ag_ref[...], out_ref[...]).astype(BF16)
    product = grads.astype(F32) * mixed_ref[...].astype(F32)
    queries, keys, values = (
        proj_ref[:, :QW], proj_ref[:, QW : QW + KW], proj_ref[:, QW + KW :],
    )
    seg_col, seg_row = seg_col_ref[...], seg_row_ref[...]
    blocks = SEQ_LEN // QB
    dk = [[jnp.zeros((QB, HEAD), F32) for _ in range(blocks)] for _ in range(2)]
    dv = [[jnp.zeros((QB, HEAD), F32) for _ in range(blocks)] for _ in range(2)]
    dq_rows = []
    for block in range(blocks):
        low, high = key_range(block)
        allowed = block_mask(seg_col, seg_row, block)
        dqs = []
        for pair in range(2):
            q3, g3, o3 = (heads_of(v, pair, block) for v in (queries, grads, product))
            k1 = keys[low:high, HEAD * pair : HEAD * (pair + 1)]
            v1 = values[low:high, HEAD * pair : HEAD * (pair + 1)]
            logsum = jnp.concatenate(
                [
                    lse_ref[0, block * QB : (block + 1) * QB, pair * GROUP + h : pair * GROUP + h + 1]
                    for h in range(GROUP)
                ],
                axis=0,
            )
            scores = jnp.where(allowed, dot_nt(q3, k1) * HEAD**-0.5, MASKED)
            probs = jnp.exp(scores - logsum)
            inner = jnp.sum(o3, axis=-1, keepdims=True)
            score_grads = (probs * (dot_nt(g3, v1) - inner)).astype(BF16)
            dq = dot_nn(score_grads, k1)
            dk_part = dot_tn(score_grads, q3)
            dv_part = dot_tn(probs.astype(BF16), g3)
            for at in range(low // QB, high // QB):
                rows = slice(at * QB - low, (at + 1) * QB - low)
                dk[pair][at] += dk_part[rows]
                dv[pair][at] += dv_part[rows]
            dqs += [dq[h * QB : (h + 1) * QB, :] for h in range(GROUP)]
        dq_rows.append(jnp.concatenate(dqs, axis=1))
    dq_all = jnp.concatenate(dq_rows, axis=0)
    dk_all = jnp.concatenate([jnp.concatenate(d, axis=0) for d in dk], axis=1)
    dv_all = jnp.concatenate([jnp.concatenate(d, axis=0) for d in dv], axis=1)
    turned = jnp.concatenate([dq_all, dk_all], axis=1) * HEAD**-0.5
    back = turn(turned, cos_ref[...], left_ref[...], right_ref[...], -1.0)
    dproj_ref[...] = jnp.concatenate([back, dv_all], axis=1).astype(BF16)


def attention_backward(ag, out_full, proj, mixed, lse, tables, seg_col, seg_row):
    tokens, width = ag.shape
    table = whole_spec((SEQ_LEN, 128))
    return pl.pallas_call(
        attention_backward_kernel,
        grid=(PAIRS,),
        in_specs=[
            whole_spec((tokens, width)),
            pl.BlockSpec((QW, width), lambda j: (j, 0)),
            pl.BlockSpec((tokens, BLOCK), lambda j: (0, j)),
            pl.BlockSpec((tokens, QW), lambda j: (0, j)),
            pl.BlockSpec((1, tokens, 8), lambda j: (j, 0, 0)),
            table, table, table,
            whole_spec((SEQ_LEN, 1)),
            whole_spec((1, SEQ_LEN)),
        ],
        out_specs=pl.BlockSpec((tokens, BLOCK), lambda j: (0, j)),
        out_shape=jax.ShapeDtypeStruct((tokens, PAIRS * BLOCK), BF16),
        compiler_params=pltpu.CompilerParams(vmem_limit_bytes=48 << 20),
        cost_estimate=pl.CostEstimate(flops=10 * 10**9, bytes_accessed=20 << 20, transcendentals=4 << 20),
        name="attention_backward",
    )(ag, out_full, proj, mixed, lse, *tables, seg_col, seg_row)


def middle_kernel(
    mixed_ref, out_ref, x_ref, gain_ref, router_ref, routes_ref,
    hidden_ref, ffn_ref, gates_ref, meta_ref,
):
    hidden = x_ref[...].astype(F32) + dot_nn(mixed_ref[...], out_ref[...])
    scale = lax.rsqrt(jnp.mean(hidden * hidden, axis=-1, keepdims=True) + EPSILON)
    hidden_ref[...] = hidden
    ffn_in = (hidden * scale * gain_ref[...].astype(F32)).astype(BF16)
    ffn_ref[...] = ffn_in
    logits = dot_nt(router_ref[...], ffn_in)
    experts, tokens = logits.shape
    index = lax.broadcasted_iota(jnp.int32, (experts, tokens), 0)
    flags = index == routes_ref[0:1, :]
    for k in range(1, TOP):
        flags = flags | (index == routes_ref[k : k + 1, :])
    chosen = jnp.where(flags, logits, MASKED)
    weights = jnp.where(flags, jnp.exp(chosen - jnp.max(chosen, axis=0, keepdims=True)), 0.0)
    gates = weights / jnp.sum(weights, axis=0, keepdims=True)
    gates_ref[...] = gates
    earlier = lax.broadcasted_iota(jnp.int32, (tokens, tokens), 0)
    later = lax.broadcasted_iota(jnp.int32, (tokens, tokens), 1)
    before = jnp.where(earlier < later, 1.0, 0.0).astype(BF16)
    ranks = dot_nn(jnp.where(flags, 1.0, 0.0).astype(BF16), before)
    slots = jnp.where(flags, ranks, -1.0)
    groups = meta_ref.shape[0]
    count = experts // groups
    meta_ref[...] = jnp.zeros(meta_ref.shape, F32)
    for e in range(experts):
        meta_ref[e // count, e % count : e % count + 1, :] = slots[e : e + 1]
        meta_ref[e // count, 8 + e % count : 9 + e % count, :] = gates[e : e + 1]


def middle(mixed, out_full, x, gain_row, router_rows, routes_rows, groups):
    tokens, width = x.shape
    experts = router_rows.shape[0]
    return pl.pallas_call(
        middle_kernel,
        out_shape=[
            jax.ShapeDtypeStruct((tokens, width), F32),
            jax.ShapeDtypeStruct((tokens, width), BF16),
            jax.ShapeDtypeStruct((experts, tokens), F32),
            jax.ShapeDtypeStruct((groups, 16, tokens), F32),
        ],
        compiler_params=pltpu.CompilerParams(vmem_limit_bytes=48 << 20),
        cost_estimate=pl.CostEstimate(flops=3 * 10**9, bytes_accessed=16 << 20, transcendentals=1 << 14),
        name="middle",
    )(mixed, out_full, x, gain_row, router_rows, routes_rows)


def flipped(index, mask):
    out, bit = index, 1
    while bit <= mask:
        if mask & bit:
            out = out + bit - 2 * bit * ((index // bit) % 2)
        bit *= 2
    return out


def send(source, target, send_sem, recv_sem, device):
    return pltpu.make_async_remote_copy(
        src_ref=source, dst_ref=target, send_sem=send_sem, recv_sem=recv_sem,
        device_id=device, device_id_type=pl.DeviceIdType.MESH,
    )


def greet(devices):
    barrier = pltpu.get_barrier_semaphore()
    for device in devices:
        pl.semaphore_signal(barrier, inc=1, device_id=device, device_id_type=pl.DeviceIdType.MESH)
    pl.semaphore_wait(barrier, len(devices))


def gather_kernel(parts, levels, count, *refs):
    ins, outs = refs[:count], refs[count : 2 * count]
    bounce = refs[2 * count : 3 * count]
    local_sem, near_send, near_recv, team_send, team_recv, core_send, core_recv = refs[3 * count :]
    group, shard = lax.axis_index("expert"), lax.axis_index("shard")
    level, core = shard // 2, shard % 2
    part = group % parts
    other = shard + 1 - 2 * core
    far = [flipped(level, k) * 2 + core for k in range(levels)]
    far_other = [flipped(level, k) * 2 + 1 - core for k in range(levels)]
    team_part = [flipped(part, k) for k in range(parts)]
    team = [group - part + t for t in team_part]
    greet(
        [(group, other)]
        + [(group, far[k]) for k in range(1, levels)]
        + [(team[t], shard) for t in range(1, parts)]
    )
    sends = []

    def push(*args):
        copy = send(*args)
        copy.start()
        sends.append(copy)

    own = pl.ds(shard * parts, parts)
    loads = [pltpu.make_async_copy(ins[i], bounce[i], local_sem.at[0, i]) for i in range(count)]
    stores = [pltpu.make_async_copy(bounce[i], outs[i].at[own], local_sem.at[1, i]) for i in range(count)]
    for copy in loads:
        copy.start()
    for i in range(count):
        for k in range(1, levels):
            push(
                ins[i].at[part], outs[i].at[shard * parts + part],
                near_send.at[i, k], near_recv.at[i, k], (group, far[k]),
            )
    for i in range(count):
        push(ins[i], outs[i].at[own], core_send.at[i, 0, 0], core_recv.at[i, 0, 0], (group, other))
    for load, store in zip(loads, stores):
        load.wait()
        store.start()
    for i in range(count):
        for k in range(1, levels):
            piece = outs[i].at[far[k] * parts + part]
            send(piece, piece, near_send.at[i, k], near_recv.at[i, k], (group, other)).wait_recv()
            for t in range(1, parts):
                push(piece, piece, team_send.at[i, k, t], team_recv.at[i, k, t], (team[t], shard))
            push(piece, piece, core_send.at[i, k, 0], core_recv.at[i, k, 0], (group, other))
        for k in range(1, levels):
            for t in range(1, parts):
                piece = outs[i].at[far[k] * parts + team_part[t]]
                send(
                    piece, piece, team_send.at[i, k, t], team_recv.at[i, k, t], (group, other)
                ).wait_recv()
                push(piece, piece, core_send.at[i, k, t], core_recv.at[i, k, t], (group, other))
    for i in range(count):
        piece = outs[i].at[pl.ds(other * parts, parts)]
        send(piece, piece, core_send.at[i, 0, 0], core_recv.at[i, 0, 0], (group, other)).wait_recv()
        for k in range(1, levels):
            for t in range(parts):
                piece = outs[i].at[far_other[k] * parts + team_part[t]]
                send(
                    piece, piece, core_send.at[i, k, t], core_recv.at[i, k, t], (group, other)
                ).wait_recv()
    for copy in sends:
        copy.wait_send()
    for copy in stores:
        copy.wait()


def gather_weights(blocks, groups, shards):
    rows = blocks[0].shape[0]
    parts = next(p for p in (4, 2, 1) if groups % p == 0 and rows % (16 * p) == 0)
    levels, count = shards // 2, len(blocks)
    blocks = [b.reshape(parts, rows // parts, b.shape[1]) for b in blocks]
    dma = pltpu.SemaphoreType.DMA
    outs = pl.pallas_call(
        functools.partial(gather_kernel, parts, levels, count),
        in_specs=[pl.BlockSpec(memory_space=pl.ANY)] * count,
        out_specs=[pl.BlockSpec(memory_space=pl.ANY)] * count,
        out_shape=[
            jax.ShapeDtypeStruct((shards * parts,) + b.shape[1:], b.dtype) for b in blocks
        ],
        scratch_shapes=[pltpu.VMEM(b.shape, b.dtype) for b in blocks]
        + [
            dma((2, count)),
            dma((count, levels)), dma((count, levels)),
            dma((count, levels, parts)), dma((count, levels, parts)),
            dma((count, levels, parts)), dma((count, levels, parts)),
        ],
        compiler_params=pltpu.CompilerParams(collective_id=0, has_side_effects=True),
        name="gather_weights",
    )(*blocks)
    return [o.reshape(shards * rows, o.shape[2]) for o in outs]


def reduce_kernel(groups, levels, rows, chunk, *refs):
    (mixed_ref, ag_ref, normed_ref, dproj_ref, misc_ref, out_grad_ref, qkv_grad_ref, misc_grad_ref,
     mixed_t, normed_t, held, from_core, from_group, summed, from_level, home) = refs[:16]
    core_send, core_recv, group_send, group_recv, level_send, level_recv, home_send, home_recv = refs[16:]
    group, shard = lax.axis_index("expert"), lax.axis_index("shard")
    level, core = shard // 2, shard % 2
    other = shard + 1 - 2 * core
    team = [flipped(group, t) for t in range(groups)]
    far = [flipped(level, k) for k in range(levels)]
    greet(
        [(group, other)]
        + [(group, far[k] * 2 + core) for k in range(1, levels)]
        + [(team[t], shard) for t in range(1, groups)]
    )
    sends = []

    def push(*args):
        copy = send(*args)
        copy.start()
        sends.append(copy)

    def arrived(piece, send_sem, recv_sem):
        send(piece, piece, send_sem, recv_sem, (group, other)).wait_recv()

    mixed_t[...] = mixed_ref[...].T
    normed_t[...] = normed_ref[...].T
    out_cols, qkv_cols = ag_ref.shape[1], dproj_ref.shape[1]
    sources = [
        (0, out_cols, mixed_t, ag_ref),
        (out_cols, out_cols + qkv_cols, normed_t, dproj_ref),
        (out_cols + qkv_cols, out_cols + qkv_cols + MISC, None, misc_ref),
    ]
    for k in range(groups):
        low, high = k * chunk, (k + 1) * chunk
        for start, stop, left, right in sources:
            a, b = max(low, start), min(high, stop)
            if a >= b:
                continue

            @pl.loop(0, 2 * levels)
            def _(s):
                at = pl.ds(pl.multiple_of(s * rows, rows), rows)
                if left is None:
                    value = right[at, a - start : b - start]
                else:
                    value = dot_nn(left[at, :], right[:, a - start : b - start]).astype(BF16)
                held[k, s % 2, s // 2, :, a - low : b - low] = value

        push(held.at[k, 1 - core], from_core.at[k], core_send.at[k], core_recv.at[k], (group, other))
    for k in range(groups):
        arrived(from_core.at[k], core_send.at[k], core_recv.at[k])

        @pl.loop(0, levels)
        def _(z):
            held[k, core, z] = (held[k, core, z].astype(F32) + from_core[k, z].astype(F32)).astype(BF16)

    order = list(range(1, levels)) + [0]
    for k in order:
        for t in range(1, groups):
            push(
                held.at[team[t], core, far[k]], from_group.at[t, k],
                group_send.at[t, k], group_recv.at[t, k], (team[t], shard),
            )
    for k in order:
        total = held[group, core, far[k]].astype(F32)
        for t in range(1, groups):
            arrived(from_group.at[t, k], group_send.at[t, k], group_recv.at[t, k])
            total = total + from_group[t, k].astype(F32)
        summed[k] = total.astype(BF16)
        if k:
            push(
                summed.at[k], from_level.at[k], level_send.at[k], level_recv.at[k],
                (group, far[k] * 2 + core),
            )
    total = summed[0].astype(F32)
    for k in range(1, levels):
        arrived(from_level.at[k], level_send.at[k], level_recv.at[k])
        total = total + from_level[k].astype(F32)
    home[group] = total.astype(BF16)
    for t in range(1, groups):
        push(home.at[group], home.at[group], home_send.at[t], home_recv.at[t], (team[t], shard))
    for t in range(1, groups):
        arrived(home.at[team[t]], home_send.at[t], home_recv.at[t])
    tile = 128
    for at in range(0, out_cols + qkv_cols + MISC, tile):
        value = home[at // chunk, :, at % chunk : at % chunk + tile].astype(F32)
        if at < out_cols:
            out_grad_ref[:, at : at + tile] = value
        elif at < out_cols + qkv_cols:
            j, inside = divmod(at - out_cols, BLOCK)
            if inside < QW:
                to = j * QW + inside
            elif inside < QW + KW:
                to = PAIRS * QW + j * KW + inside - QW
            else:
                to = PAIRS * (QW + KW) + j * KW + inside - QW - KW
            qkv_grad_ref[:, to : to + tile] = value
        else:
            misc_grad_ref[...] = value
    for copy in sends:
        copy.wait_send()


def reduce_weights(mixed, ag, normed, dproj, misc_cols, groups, shards):
    tokens, width = normed.shape
    levels, rows = shards // 2, width // shards
    total = ag.shape[1] + dproj.shape[1] + MISC
    chunk = 128 * (-(-total // (128 * groups)))
    dma = pltpu.SemaphoreType.DMA
    vmem = pl.BlockSpec(memory_space=pltpu.VMEM)
    piece = (rows, chunk)
    return pl.pallas_call(
        functools.partial(reduce_kernel, groups, levels, rows, chunk),
        in_specs=[vmem] * 5,
        out_specs=[vmem] * 3,
        out_shape=[
            jax.ShapeDtypeStruct((rows, cols), F32) for cols in (ag.shape[1], dproj.shape[1], MISC)
        ],
        scratch_shapes=[
            pltpu.VMEM((mixed.shape[1], tokens), BF16),
            pltpu.VMEM((width, tokens), BF16),
            pltpu.VMEM((groups, 2, levels) + piece, BF16),
            pltpu.VMEM((groups, levels) + piece, BF16),
            pltpu.VMEM((groups, levels) + piece, BF16),
            pltpu.VMEM((levels,) + piece, BF16),
            pltpu.VMEM((levels,) + piece, BF16),
            pltpu.VMEM((groups,) + piece, BF16),
            dma((groups,)), dma((groups,)),
            dma((groups, levels)), dma((groups, levels)),
            dma((levels,)), dma((levels,)),
            dma((groups,)), dma((groups,)),
        ],
        compiler_params=pltpu.CompilerParams(
            collective_id=1, has_side_effects=True, vmem_limit_bytes=56 << 20
        ),
        cost_estimate=pl.CostEstimate(
            flops=2 * tokens * width * total, bytes_accessed=8 << 20, transcendentals=0
        ),
        name="reduce_weights",
    )(mixed, ag, normed, dproj, misc_cols)


def expert_kernel(capacity, shards, groups, count, base, stage, *refs):
    refs = list(refs)
    take = lambda n: [refs.pop(0) for _ in range(n)]
    if stage == "first":
        x_own, meta_own = take(2)
        u_ins = take(3 if groups == 4 else groups)
    else:
        x_ref, u_ref, meta_ref, out_in, dx_in, gg_in = take(6)
    we_ref, wp_ref = take(2)
    if stage == "first":
        x_all, u_all, meta_all, out_ref, dx_ref, gg_ref, dw_out = take(7)
    elif stage == "last":
        out_ref, dx_home, gg_home, dw_out = take(4)
    else:
        out_ref, dx_ref, gg_ref, dw_out = take(4)
    xs, us, bs, inn, dw, dw_sem = take(6)
    if stage == "first":
        x_buf, u_buf, meta_buf = take(3)
        x_send, x_recv, meta_send, meta_recv, load_sem, u_sem, meta_sem, keep_sem, pass_sem = take(9)
    elif stage == "last":
        dx_buf, gg_buf, dx_send, dx_recv, gg_send, gg_recv, keep_sem = take(7)
    turn_at, expert = pl.program_id(0), pl.program_id(1)
    last_turn, last = groups - 1, count - 1
    group, shard = lax.axis_index("expert"), lax.axis_index("shard")
    team = [flipped(group, t) for t in range(groups)]
    tokens = xs.shape[2] and (u_buf.shape[1] if stage == "first" else x_ref.shape[1])
    width = xs.shape[2]

    if stage == "first":

        relay = groups == 4
        near = [1, 2] if relay else list(range(1, groups))
        half = tokens // 2

        def x_copy(t):
            return send(x_own, x_all.at[t], x_send.at[t], x_recv.at[t], (team[t], shard))

        def passed(source, target, part, sems):
            at = pl.ds(part * half, half)
            return send(
                source.at[at], target.at[3, at], sems.at[0, part], sems.at[1, part],
                (team[2 - part], shard),
            )

        def x_pass(part):
            return passed(x_all.at[1 + part], x_all, part, pass_sem.at[0])

        def u_pass(part):
            return passed(u_ins[1 + part], u_all, part, pass_sem.at[1])

        def meta_copy(t):
            return send(
                meta_own.at[team[t]], meta_all.at[t], meta_send.at[t], meta_recv.at[t], (team[t], shard)
            )

        def u_load(t):
            source = u_all.at[t] if relay and t == 3 else u_ins[t]
            return pltpu.make_async_copy(source, u_buf.at[t % 2], u_sem.at[t % 2])

        def x_keep():
            return pltpu.make_async_copy(x_buf, x_all.at[0], keep_sem.at[0])

        def meta_keep():
            return pltpu.make_async_copy(meta_buf, meta_all.at[0], keep_sem.at[1])

        def u_keep(t):
            return pltpu.make_async_copy(u_buf.at[t % 2], u_all.at[t], keep_sem.at[2 + t])

        for t in range(groups):

            @pl.when((turn_at == t) & (expert == 0))
            def _():
                if t == 0:
                    u_load(0).start()
                    greet([(team[k], shard) for k in range(1, groups)])
                    for k in range(1, groups):
                        meta_copy(k).start()
                    for k in near:
                        x_copy(k).start()
                    if relay:
                        u_pass(0).start()
                        u_pass(1).start()
                    fetch_x, fetch_meta = x_own, meta_own.at[group]
                else:
                    if not relay:
                        x_copy(t).wait_recv()
                    elif t == 1:
                        for k in near:
                            x_copy(k).wait_recv()
                        x_pass(0).start()
                        x_pass(1).start()
                    elif t == 3:
                        for part in range(2):
                            x_pass(part).wait_recv()
                            u_pass(part).wait_recv()
                        u_load(3).start()
                    meta_copy(t).wait_recv()
                    u_keep(t - 1).wait()
                    if t == 1:
                        x_keep().wait()
                        meta_keep().wait()
                    fetch_x, fetch_meta = x_all.at[t], meta_all.at[t]
                load = pltpu.make_async_copy(fetch_x, x_buf, load_sem)
                load_meta = pltpu.make_async_copy(fetch_meta, meta_buf, meta_sem)
                load.start()
                load_meta.start()
                if t + 1 < groups and not (relay and t == 2):
                    u_load(t + 1).start()
                u_load(t).wait()
                load_meta.wait()
                load.wait()
                if not (relay and t == 3):
                    u_keep(t).start()
                if t == 0:
                    x_keep().start()
                    meta_keep().start()

        x_now, u_now, meta_now = x_buf, u_buf.at[turn_at % 2], meta_buf
    else:
        x_now, u_now, meta_now = x_ref.at[0], u_ref.at[0], meta_ref.at[0]

    if stage == "last":
        slot = turn_at % 3

        def dx_copy(i):
            t = (i + 1) % groups
            return send(dx_buf.at[i % 3], dx_home.at[t], dx_send.at[t], dx_recv.at[t], (team[t], shard))

        def gg_copy(i):
            t = (i + 1) % groups
            return send(gg_buf.at[i], gg_home.at[group], gg_send.at[t], gg_recv.at[t], (team[t], shard))

        @pl.when((turn_at == 0) & (expert == 0))
        def _():
            greet([(team[k], shard) for k in range(1, groups)])

        for i in range(3, groups):

            @pl.when((turn_at == i) & (expert == 0))
            def _():
                dx_copy(i - 3).wait_send()

        dx_now, gg_now = dx_buf.at[slot], gg_buf.at[turn_at]
    else:
        dx_now, gg_now = dx_ref.at[0], gg_ref.at[0]

    @pl.when(expert == 0)
    def _():
        if stage == "first":
            out_ref[0] = jnp.zeros((tokens, width), BF16)
            dx_now[...] = jnp.zeros((tokens, width), BF16)
            gg_now[...] = jnp.zeros((8, tokens), F32)
        else:
            out_ref[0] = out_in[0]
            dx_now[...] = dx_in[0]
            gg_now[...] = gg_in[0]

    slot_row = meta_now[pl.ds(base + expert, 1), :]
    gate_row = meta_now[pl.ds(8 + base + expert, 1), :]
    index = lax.broadcasted_iota(jnp.int32, (capacity, tokens), 0).astype(F32)
    pick = jnp.where(index == slot_row, 1.0, 0.0)
    gate_col = jnp.sum(pick * gate_row, axis=1, keepdims=True)
    place = pick.astype(BF16)
    rows = pl.ds(pl.multiple_of(turn_at * capacity, capacity), capacity)
    step = 512
    for c in range(0, width, step):
        xs[expert, rows, c : c + step] = dot_nn(place, x_now[:, c : c + step]).astype(BF16)
        us[expert, rows, c : c + step] = dot_nn(place, u_now[:, c : c + step]).astype(BF16)
    x = xs[expert, rows, :]
    gate = dot_nn(x, we_ref[0, :, :FF])
    up = dot_nn(x, we_ref[0, :, FF:])
    back = dot_nt(us[expert, rows, :], wp_ref[0])
    sig = 1.0 / (1.0 + jnp.exp(-gate))
    act = gate * sig
    inner = act * up
    inner_low = inner.astype(BF16)
    gate_grad = jnp.sum(inner * back, axis=1, keepdims=True)
    here = lax.broadcasted_iota(jnp.int32, (8, tokens), 0) == base + expert
    gg_now[...] = jnp.where(here, jnp.sum(pick * gate_grad, axis=0, keepdims=True), gg_now[...])
    inn[expert, rows, :] = (inner * gate_col).astype(BF16)
    inner_grads = back * gate_col
    bs[expert, rows, :FF] = (inner_grads * up * sig * (1.0 + gate * (1.0 - sig))).astype(BF16)
    bs[expert, rows, FF:] = (inner_grads * act).astype(BF16)
    both = bs[expert, rows, :]
    weighted_t = (pick * gate_row).astype(BF16).T
    place_t = place.T
    for c in range(0, width, step):
        result = dot_nn(inner_low, wp_ref[0, :, c : c + step]).astype(BF16)
        out_ref[0, :, c : c + step] = (
            out_ref[0, :, c : c + step].astype(F32) + dot_nn(weighted_t, result)
        ).astype(BF16)
        row_grads = dot_nt(both, we_ref[0, c : c + step, :]).astype(BF16)
        dx_now[:, c : c + step] = (
            dx_now[:, c : c + step].astype(F32) + dot_nn(place_t, row_grads)
        ).astype(BF16)

    if stage == "last":
        for i in range(groups):

            @pl.when((turn_at == i) & (expert == last))
            def _():
                if i < last_turn:
                    gg_copy(i).start()
                    dx_copy(i).start()
                else:
                    pltpu.make_async_copy(dx_buf.at[i % 3], dx_home.at[0], keep_sem.at[0]).start()
                    pltpu.make_async_copy(gg_buf.at[i], gg_home.at[group], keep_sem.at[1]).start()

    def store_weights(e):
        return pltpu.make_async_copy(dw, dw_out.at[:, e], dw_sem)

    @pl.when(turn_at == last_turn)
    def _():
        @pl.when(expert > 0)
        def _():
            store_weights(0).wait()

        wide, half = 384, FF // 2
        tall, short = width // shards, FF // shards
        side = width - 2 * FF

        @pl.loop(0, width // wide)
        def _(c):
            at = pl.ds(pl.multiple_of(c * wide, wide), wide)
            value = dot_tn(xs[expert, :, at], bs[expert]).astype(BF16)
            for i in range(wide // tall):
                dw[c * (wide // tall) + i, :tall, :] = value[i * tall : (i + 1) * tall]

        @pl.loop(0, FF // half)
        def _(c):
            at = pl.ds(pl.multiple_of(c * half, half), half)
            value = dot_tn(inn[expert, :, at], us[expert]).astype(BF16)
            for i in range(half // short):
                s, low = c * (half // short) + i, i * short
                mid, high = low + short // 2, low + short
                dw[s, tall : tall + short, :] = value[low:high, : 2 * FF]
                dw[s, tall + short :, :side] = value[low:mid, 2 * FF :]
                dw[s, tall + short :, side:] = value[mid:high, 2 * FF :]

        store_weights(expert).start()

    @pl.when((turn_at == last_turn) & (expert == last))
    def _():
        store_weights(0).wait()
        if stage == "first":
            if not relay:
                u_keep(last_turn).wait()
            for t in range(1, groups):
                meta_copy(t).wait_send()
            for t in near:
                x_copy(t).wait_send()
            if relay:
                for part in range(2):
                    x_pass(part).wait_send()
                    u_pass(part).wait_send()
        if stage == "last":
            for i in range(groups - 1):
                if i + 3 >= groups:
                    dx_copy(i).wait_send()
                gg_copy(i).wait_send()
            for i in range(groups - 1):
                dx_copy(i).wait_recv()
                t = (i + 1) % groups
                send(
                    gg_buf.at[i], gg_home.at[team[t]], gg_send.at[t], gg_recv.at[t], (team[t], shard)
                ).wait_recv()
            pltpu.make_async_copy(dx_buf.at[last_turn % 3], dx_home.at[0], keep_sem.at[0]).wait()
            pltpu.make_async_copy(gg_buf.at[last_turn], gg_home.at[group], keep_sem.at[1]).wait()


def expert_call(capacity, shards, groups, base, stage, data, we, wp):
    count = we.shape[0]
    tokens, width = data[0].shape[-2:]
    total = groups * capacity
    anywhere = pl.BlockSpec(memory_space=pl.ANY)
    turned = (lambda i: i) if stage == "first" else (lambda i: lax.rem(i + 1, groups))
    block = pl.BlockSpec((1, tokens, width), lambda i, e: (turned(i), 0, 0))
    small = pl.BlockSpec((1, 8, tokens), lambda i, e: (turned(i), 0, 0))
    dma = pltpu.SemaphoreType.DMA
    many = jax.ShapeDtypeStruct((groups, tokens, width), BF16)
    grads = jax.ShapeDtypeStruct((groups, 8, tokens), F32)
    packed = (shards, (width + FF + FF // 2) // shards, 2 * FF)
    weights = jax.ShapeDtypeStruct((shards, count) + packed[1:], BF16)
    meta = jax.ShapeDtypeStruct((groups, 16, tokens), F32)
    scratch = [
        pltpu.VMEM((count, total, width), BF16),
        pltpu.VMEM((count, total, width), BF16),
        pltpu.VMEM((count, total, 2 * FF), BF16),
        pltpu.VMEM((count, total, FF), BF16),
        pltpu.VMEM(packed, BF16),
        dma,
    ]
    if stage == "first":
        in_specs = [anywhere] * len(data)
        out_specs = [anywhere] * 3 + [block, block, small, anywhere]
        out_shape = [many, many, meta, many, many, grads, weights]
        scratch += [
            pltpu.VMEM((tokens, width), BF16),
            pltpu.VMEM((2, tokens, width), BF16),
            pltpu.VMEM((16, tokens), F32),
            dma((groups,)), dma((groups,)), dma((groups,)), dma((groups,)),
            dma, dma((2,)), dma, dma((2 + groups,)), dma((2, 2, 2)),
        ]
    else:
        meta_block = pl.BlockSpec((1, 16, tokens), lambda i, e: (turned(i), 0, 0))
        in_specs = [block, block, meta_block, block, block, small]
        if stage == "last":
            out_specs = [block, anywhere, anywhere, anywhere]
            scratch += [
                pltpu.VMEM((3, tokens, width), BF16),
                pltpu.VMEM((groups, 8, tokens), F32),
                dma((groups,)), dma((groups,)), dma((groups,)), dma((groups,)), dma((2,)),
            ]
        else:
            out_specs = [block, block, small, anywhere]
        out_shape = [many, many, grads, weights]
    weight_specs = [
        pl.BlockSpec((1,) + w.shape[1:], lambda i, e: (e, 0, 0)) for w in (we, wp)
    ]
    remote = {"first": 2, "last": 3}
    return pl.pallas_call(
        functools.partial(expert_kernel, capacity, shards, groups, count, base, stage),
        grid=(groups, count),
        in_specs=in_specs + weight_specs,
        out_specs=out_specs,
        out_shape=out_shape,
        scratch_shapes=scratch,
        compiler_params=pltpu.CompilerParams(
            vmem_limit_bytes=62 << 20,
            **({"collective_id": remote[stage], "has_side_effects": True} if stage in remote else {}),
        ),
        cost_estimate=pl.CostEstimate(
            flops=2 * count * total * width * (4 * tokens + 9 * FF),
            bytes_accessed=6 * groups * tokens * width * 2,
            transcendentals=count * total * FF,
        ),
        name="experts_" + stage,
    )(*data, we, wp)


def norm_back(values, gain_row, grad_rows):
    scale_rows = lax.rsqrt(jnp.mean(values * values, axis=-1, keepdims=True) + EPSILON)
    weighted = gain_row * grad_rows
    inner_mean = jnp.mean(weighted * values, axis=-1, keepdims=True)
    input_part = (
        scale_rows * weighted - values * (scale_rows * scale_rows * scale_rows) * inner_mean
    )
    gain_part = jnp.sum(grad_rows * values * scale_rows, axis=0)
    return (input_part, gain_part)


def to_blocks(weight):
    rows = weight.shape[0]
    qs = weight[:, : HEADS * HEAD].reshape(rows, PAIRS, QW)
    ks = weight[:, HEADS * HEAD : (HEADS + KV_HEADS) * HEAD].reshape(rows, PAIRS, KW)
    vs = weight[:, (HEADS + KV_HEADS) * HEAD :].reshape(rows, PAIRS, KW)
    return jnp.concatenate([qs, ks, vs], axis=2).reshape(rows, PAIRS * BLOCK)


def unpack_kernel(tall, short, *refs):
    *ins, expand_ref, project_ref = refs
    at = 0
    for ref in ins:
        for i in range(ref.shape[0]):
            value = ref[i].astype(F32)
            expand_ref[at] = value[:tall]
            side = project_ref.shape[2] - 2 * FF
            project_ref[at, :, : 2 * FF] = value[tall : tall + short]
            project_ref[at, : short // 2, 2 * FF :] = value[tall + short :, :side]
            project_ref[at, short // 2 :, 2 * FF :] = value[tall + short :, side:]
            at += 1


def unpack_weights(shares, tall, short, width):
    count = sum(s.shape[0] for s in shares)
    return pl.pallas_call(
        functools.partial(unpack_kernel, tall, short),
        out_shape=[
            jax.ShapeDtypeStruct((count, tall, 2 * FF), F32),
            jax.ShapeDtypeStruct((count, short, width), F32),
        ],
        compiler_params=pltpu.CompilerParams(vmem_limit_bytes=32 << 20),
        name="unpack_weights",
    )(*shares)


def exchanged(value, flip, groups):
    if flip == 0:
        return value
    return lax.ppermute(value, "expert", [(i, i ^ flip) for i in range(groups)])


def bands(count):
    return [(0, 2), (2, count - 2), (count - 2, count)]


def local(
    inputs, attn_gain, qkv_weight, out_weight, ffn_gain, router_weight,
    expand_weight, project_weight, segment_ids, routes, out_grad,
):
    groups, shards = lax.axis_size("expert"), lax.axis_size("shard")
    tokens, width = inputs.shape
    experts = router_weight.shape[1]
    local_count = expand_weight.shape[0]
    capacity = 8 * ((5 * tokens * TOP + 32 * experts - 1) // (32 * experts))

    misc = jnp.concatenate(
        [
            attn_gain[:, None],
            ffn_gain[:, None],
            router_weight,
            jnp.zeros((attn_gain.shape[0], MISC - 2 - experts), BF16),
        ],
        axis=1,
    )
    packed = jnp.concatenate([to_blocks(qkv_weight), misc], axis=1)
    expand_full, project_full = [], []
    for low, high in bands(local_count):
        expand_full.append(lax.all_gather(expand_weight[low:high], "shard", axis=1, tiled=True))
        project_full.append(lax.all_gather(project_weight[low:high], "shard", axis=1, tiled=True))
    qkv_full, out_full = gather_weights([packed, out_weight], groups, shards)
    misc_rows = qkv_full[:, PAIRS * BLOCK :].T
    out_grad_late, misc_rows = lax.optimization_barrier((out_grad, misc_rows))
    u_parts = [
        exchanged(out_grad_late, t, groups) for t in range(3 if groups == 4 else groups)
    ]
    gain_one, gain_two = misc_rows[0:1], misc_rows[1:2]
    router_rows = misc_rows[2 : 2 + experts]
    tables = tuple(jnp.asarray(t) for t in rope_tables())
    seg_row = segment_ids.reshape(1, tokens)
    seg_col = segment_ids.reshape(tokens, 1)
    normed, proj, mixed, lse = attention_forward(
        inputs, gain_one, qkv_full, tables, seg_col, seg_row
    )
    hidden, ffn_in, gates, meta_own = middle(
        mixed, out_full, inputs, gain_two, router_rows, routes.T, groups
    )
    tall, short = expand_weight.shape[1], project_weight.shape[1]
    call = functools.partial(expert_call, capacity, shards, groups)

    def share_out(dw):
        return lax.psum_scatter(dw, "shard", scatter_dimension=0, tiled=True)[0]

    x_all, u_all, meta, out_acc, dx_acc, gg, dw = call(
        0, "first", (ffn_in, meta_own, *u_parts), expand_full[0], project_full[0]
    )
    shares = [share_out(dw)]
    out_acc, dx_acc, gg, dw = call(
        2, "between", (x_all, u_all, meta, out_acc, dx_acc, gg), expand_full[1], project_full[1]
    )
    shares.append(share_out(dw))
    out_acc, dx_home, gg_home, dw = call(
        local_count - 2, "last", (x_all, u_all, meta, out_acc, dx_acc, gg),
        expand_full[2], project_full[2],
    )
    shares.append(share_out(dw))
    dx_home, shares[0] = lax.optimization_barrier((dx_home, shares[0]))

    gg_dense = gg_home[:, :local_count].reshape(experts, tokens)
    out_home = [exchanged(out_acc[t], t, groups) for t in range(groups)]
    logit_grads = (
        gates * (gg_dense - jnp.sum(gates * gg_dense, axis=0, keepdims=True))
    ).astype(BF16)
    router_part = dot_nn(logit_grads, ffn_in)
    ffn_grads = dot_tn(logit_grads, router_rows) + jnp.sum(dx_home.astype(F32), axis=0)
    upstream = out_grad.astype(F32)
    hidden_part, gain_two_grad = norm_back(hidden, gain_two.astype(F32), ffn_grads)
    hidden_grads = upstream + hidden_part
    attended_grads = hidden_grads.astype(BF16)
    dproj = attention_backward(
        attended_grads, out_full, proj, mixed, lse, tables, seg_col, seg_row
    )
    normed_grads = dot_nt(dproj, qkv_full[:, : PAIRS * BLOCK])
    input_part, gain_one_grad = norm_back(
        inputs.astype(F32), gain_one.astype(F32), normed_grads
    )
    input_grad = hidden_grads + input_part

    dproj, shares[1] = lax.optimization_barrier((dproj, shares[1]))
    misc_part = jnp.concatenate(
        [
            gain_one_grad[None],
            gain_two_grad[None],
            router_part,
            jnp.zeros((MISC - 2 - experts, width), F32),
        ],
        axis=0,
    ).astype(BF16)
    out_weight_grad, qkv_grad, misc_total = reduce_weights(
        mixed, attended_grads, normed, dproj, misc_part.T, groups, shards
    )
    out_weight_grad, *out_home = lax.optimization_barrier((out_weight_grad, *out_home))
    output = (hidden + sum(o.astype(F32) for o in out_home)).astype(BF16)
    expand_grad, project_grad = unpack_weights(shares, tall, short, width)
    return (
        output,
        input_grad,
        misc_total[:, 0],
        qkv_grad,
        out_weight_grad,
        misc_total[:, 1],
        misc_total[:, 2 : 2 + experts],
        expand_grad,
        project_grad,
    )


def solution(mesh):
    rows = P(("expert", "shard"), None)
    return jax.shard_map(
        local,
        mesh=mesh,
        in_specs=(
            rows, P("shard"), P("shard", None), P("shard", None), P("shard"), P("shard", None),
            P("expert", "shard", None), P("expert", "shard", None), rows, rows, rows,
        ),
        out_specs=(
            rows, rows, P("shard"), P("shard", None), P("shard", None), P("shard"),
            P("shard", None), P("expert", "shard", None), P("expert", "shard", None),
        ),
        check_vma=False,
    )
```

```python
import functools

import jax
import jax.numpy as jnp
import numpy as np
from jax import lax
from jax.experimental import pallas as pl
from jax.experimental.pallas import tpu as pltpu
from jax.sharding import PartitionSpec as P

HEADS = 24
KV_HEADS = 8
HEAD = 64
FF = 512
TOP = 8
SEQ_LEN = 512
GROUP = HEADS // KV_HEADS
PAIRS = KV_HEADS // 2
QW = 2 * GROUP * HEAD
KW = 2 * HEAD
BLOCK = QW + 2 * KW
MISC = 128
QB = 128

EPSILON = 1e-06
ROPE_THETA = 10000.0
MASKED = -1e30
F32 = jnp.float32
BF16 = jnp.bfloat16


def dot_nn(a, b):
    return lax.dot_general(a, b, (((1,), (0,)), ((), ())), preferred_element_type=F32)


def dot_nt(a, b):
    return lax.dot_general(a, b, (((1,), (1,)), ((), ())), preferred_element_type=F32)


def dot_tn(a, b):
    return lax.dot_general(a, b, (((0,), (0,)), ((), ())), preferred_element_type=F32)


def rope_tables():
    frequency = (np.float32(ROPE_THETA) ** (-2.0 * np.arange(HEAD // 2) / HEAD)).astype(np.float32)
    angle = np.arange(SEQ_LEN, dtype=np.float32)[:, None] * frequency[None, :]
    cosine, sine = np.cos(angle).astype(np.float32), np.sin(angle).astype(np.float32)
    zero = np.zeros_like(sine)
    cos_table = np.concatenate([cosine] * 4, axis=1)
    left_table = np.concatenate([-sine, zero] * 2, axis=1)
    right_table = np.concatenate([zero, sine] * 2, axis=1)
    return cos_table, left_table, right_table


def turn(values, cos_table, left_table, right_table, sign):
    parts = []
    for c in range(values.shape[1] // 128):
        piece = values[:, 128 * c : 128 * (c + 1)]
        ahead = pltpu.roll(piece, 96, 1) * left_table
        behind = pltpu.roll(piece, 32, 1) * right_table
        parts.append(piece * cos_table + sign * (ahead + behind))
    return parts[0] if len(parts) == 1 else jnp.concatenate(parts, axis=1)


def key_range(block):
    return max(0, block - 2) * QB, (block + 1) * QB


def block_mask(seg_col, seg_row, block):
    low, high = key_range(block)
    rows = lax.broadcasted_iota(jnp.int32, (QB, high - low), 0) + block * QB
    cols = lax.broadcasted_iota(jnp.int32, (QB, high - low), 1) + low
    same = seg_col[block * QB : (block + 1) * QB, :] == seg_row[:, low:high]
    return jnp.concatenate([(rows >= cols) & same] * GROUP, axis=0)


def heads_of(values, pair, block):
    rows = values[block * QB : (block + 1) * QB, :]
    first = pair * GROUP
    return jnp.concatenate(
        [rows[:, HEAD * h : HEAD * (h + 1)] for h in range(first, first + GROUP)], axis=0
    )


def attention_forward_kernel(
    parts, levels, x_ref, gain_ref, w_ref, cos_ref, left_ref, right_ref, seg_col_ref, seg_row_ref,
    part_ref, normed_ref, proj_ref, mixed_ref, lse_ref, full_ref, *sems,
):
    step = pl.program_id(0)
    plan = Gather(parts, levels, [full_ref], sems)

    @pl.when(step == 0)
    def _():
        plan.greet(near=False)
        plan.own_to_mate(lambda: full_ref.at[pl.ds(plan.shard * parts, parts)], 0)
        for k in range(1, levels):
            plan.spread(0, k)

    @pl.when(step == PAIRS - 1)
    def _():
        plan.team_to_mate(0)

    @pl.when(step == 0)
    def _():
        x = x_ref[...].astype(F32)
        scale = lax.rsqrt(jnp.mean(x * x, axis=-1, keepdims=True) + EPSILON)
        normed_ref[...] = (x * scale * gain_ref[...].astype(F32)).astype(BF16)

    projected = dot_nn(normed_ref[...], w_ref[...])
    turned = turn(
        projected[:, : QW + KW], cos_ref[...], left_ref[...], right_ref[...], 1.0
    ).astype(BF16)
    queries, keys = turned[:, :QW], turned[:, QW:]
    values = projected[:, QW + KW :].astype(BF16)
    proj_ref[...] = jnp.concatenate([turned, values], axis=1)
    seg_col, seg_row = seg_col_ref[...], seg_row_ref[...]
    for block in range(SEQ_LEN // QB):
        low, high = key_range(block)
        allowed = block_mask(seg_col, seg_row, block)
        outs = []
        for pair in range(2):
            q3 = heads_of(queries, pair, block)
            k1 = keys[low:high, HEAD * pair : HEAD * (pair + 1)]
            v1 = values[low:high, HEAD * pair : HEAD * (pair + 1)]
            scores = jnp.where(allowed, dot_nt(q3, k1) * HEAD**-0.5, MASKED)
            top = jnp.max(scores, axis=-1, keepdims=True)
            weights = jnp.exp(scores - top)
            total = jnp.sum(weights, axis=-1, keepdims=True)
            mixed = dot_nn(weights.astype(BF16), v1) * (1.0 / total)
            logsum = top + jnp.log(total)
            for h in range(GROUP):
                outs.append(mixed[h * QB : (h + 1) * QB, :])
                lse_ref[0, block * QB : (block + 1) * QB, pair * GROUP + h : pair * GROUP + h + 1] = (
                    logsum[h * QB : (h + 1) * QB, :]
                )
        mixed_ref[block * QB : (block + 1) * QB, :] = jnp.concatenate(outs, axis=1).astype(BF16)

    @pl.when(step == PAIRS - 1)
    def _():
        plan.mate_arrived(0)
        plan.finish()


def whole_spec(shape):
    return pl.BlockSpec(shape, lambda *_: (0,) * len(shape))


def attention_forward(x, gain_row, w_full, tables, seg_col, seg_row, out_part, groups, shards):
    tokens, width = x.shape
    parts, levels = gather_parts(groups, width // shards), shards // 2
    table = whole_spec((SEQ_LEN, 128))
    *kept, out_full = pl.pallas_call(
        functools.partial(attention_forward_kernel, parts, levels),
        grid=(PAIRS,),
        in_specs=[
            whole_spec((tokens, width)),
            whole_spec((1, width)),
            pl.BlockSpec((width, BLOCK), lambda j: (0, j)),
            table, table, table,
            whole_spec((SEQ_LEN, 1)),
            whole_spec((1, SEQ_LEN)),
            pl.BlockSpec(memory_space=pl.ANY),
        ],
        out_specs=[
            whole_spec((tokens, width)),
            pl.BlockSpec((tokens, BLOCK), lambda j: (0, j)),
            pl.BlockSpec((tokens, QW), lambda j: (0, j)),
            pl.BlockSpec((1, tokens, 8), lambda j: (j, 0, 0)),
            pl.BlockSpec(memory_space=pl.ANY),
        ],
        out_shape=[
            jax.ShapeDtypeStruct((tokens, width), BF16),
            jax.ShapeDtypeStruct((tokens, PAIRS * BLOCK), BF16),
            jax.ShapeDtypeStruct((tokens, HEADS * HEAD), BF16),
            jax.ShapeDtypeStruct((PAIRS, tokens, 8), F32),
            jax.ShapeDtypeStruct(out_part.shape, BF16),
        ],
        scratch_shapes=gather_sems(levels, parts, 1),
        input_output_aliases={8: 4},
        compiler_params=pltpu.CompilerParams(
            vmem_limit_bytes=48 << 20, collective_id=4, has_side_effects=True
        ),
        cost_estimate=pl.CostEstimate(flops=10 * 10**9, bytes_accessed=20 << 20, transcendentals=4 << 20),
        name="attention_forward",
    )(x, gain_row, w_full, *tables, seg_col, seg_row, out_part)
    return *kept, out_full.reshape(width, -1)


def attention_backward_kernel(
    ag_ref, out_ref, proj_ref, mixed_ref, lse_ref, cos_ref, left_ref, right_ref,
    seg_col_ref, seg_row_ref, dproj_ref,
):
    grads = dot_nt(ag_ref[...], out_ref[...]).astype(BF16)
    product = grads.astype(F32) * mixed_ref[...].astype(F32)
    queries, keys, values = (
        proj_ref[:, :QW], proj_ref[:, QW : QW + KW], proj_ref[:, QW + KW :],
    )
    seg_col, seg_row = seg_col_ref[...], seg_row_ref[...]
    blocks = SEQ_LEN // QB
    dk = [[jnp.zeros((QB, HEAD), F32) for _ in range(blocks)] for _ in range(2)]
    dv = [[jnp.zeros((QB, HEAD), F32) for _ in range(blocks)] for _ in range(2)]
    dq_rows = []
    for block in range(blocks):
        low, high = key_range(block)
        allowed = block_mask(seg_col, seg_row, block)
        dqs = []
        for pair in range(2):
            q3, g3, o3 = (heads_of(v, pair, block) for v in (queries, grads, product))
            k1 = keys[low:high, HEAD * pair : HEAD * (pair + 1)]
            v1 = values[low:high, HEAD * pair : HEAD * (pair + 1)]
            logsum = jnp.concatenate(
                [
                    lse_ref[0, block * QB : (block + 1) * QB, pair * GROUP + h : pair * GROUP + h + 1]
                    for h in range(GROUP)
                ],
                axis=0,
            )
            scores = jnp.where(allowed, dot_nt(q3, k1) * HEAD**-0.5, MASKED)
            probs = jnp.exp(scores - logsum)
            inner = jnp.sum(o3, axis=-1, keepdims=True)
            score_grads = (probs * (dot_nt(g3, v1) - inner)).astype(BF16)
            dq = dot_nn(score_grads, k1)
            dk_part = dot_tn(score_grads, q3)
            dv_part = dot_tn(probs.astype(BF16), g3)
            for at in range(low // QB, high // QB):
                rows = slice(at * QB - low, (at + 1) * QB - low)
                dk[pair][at] += dk_part[rows]
                dv[pair][at] += dv_part[rows]
            dqs += [dq[h * QB : (h + 1) * QB, :] for h in range(GROUP)]
        dq_rows.append(jnp.concatenate(dqs, axis=1))
    dq_all = jnp.concatenate(dq_rows, axis=0)
    dk_all = jnp.concatenate([jnp.concatenate(d, axis=0) for d in dk], axis=1)
    dv_all = jnp.concatenate([jnp.concatenate(d, axis=0) for d in dv], axis=1)
    turned = jnp.concatenate([dq_all, dk_all], axis=1) * HEAD**-0.5
    back = turn(turned, cos_ref[...], left_ref[...], right_ref[...], -1.0)
    dproj_ref[...] = jnp.concatenate([back, dv_all], axis=1).astype(BF16)


def attention_backward(ag, out_full, proj, mixed, lse, tables, seg_col, seg_row):
    tokens, width = ag.shape
    table = whole_spec((SEQ_LEN, 128))
    return pl.pallas_call(
        attention_backward_kernel,
        grid=(PAIRS,),
        in_specs=[
            whole_spec((tokens, width)),
            pl.BlockSpec((QW, width), lambda j: (j, 0)),
            pl.BlockSpec((tokens, BLOCK), lambda j: (0, j)),
            pl.BlockSpec((tokens, QW), lambda j: (0, j)),
            pl.BlockSpec((1, tokens, 8), lambda j: (j, 0, 0)),
            table, table, table,
            whole_spec((SEQ_LEN, 1)),
            whole_spec((1, SEQ_LEN)),
        ],
        out_specs=pl.BlockSpec((tokens, BLOCK), lambda j: (0, j)),
        out_shape=jax.ShapeDtypeStruct((tokens, PAIRS * BLOCK), BF16),
        compiler_params=pltpu.CompilerParams(vmem_limit_bytes=48 << 20),
        cost_estimate=pl.CostEstimate(flops=10 * 10**9, bytes_accessed=20 << 20, transcendentals=4 << 20),
        name="attention_backward",
    )(ag, out_full, proj, mixed, lse, *tables, seg_col, seg_row)


def middle_kernel(
    mixed_ref, out_ref, x_ref, gain_ref, router_ref, routes_ref,
    hidden_ref, ffn_ref, gates_ref, meta_ref,
):
    hidden = x_ref[...].astype(F32) + dot_nn(mixed_ref[...], out_ref[...])
    scale = lax.rsqrt(jnp.mean(hidden * hidden, axis=-1, keepdims=True) + EPSILON)
    hidden_ref[...] = hidden
    ffn_in = (hidden * scale * gain_ref[...].astype(F32)).astype(BF16)
    ffn_ref[...] = ffn_in
    logits = dot_nt(router_ref[...], ffn_in)
    experts, tokens = logits.shape
    index = lax.broadcasted_iota(jnp.int32, (experts, tokens), 0)
    flags = index == routes_ref[0:1, :]
    for k in range(1, TOP):
        flags = flags | (index == routes_ref[k : k + 1, :])
    chosen = jnp.where(flags, logits, MASKED)
    weights = jnp.where(flags, jnp.exp(chosen - jnp.max(chosen, axis=0, keepdims=True)), 0.0)
    gates = weights / jnp.sum(weights, axis=0, keepdims=True)
    gates_ref[...] = gates
    earlier = lax.broadcasted_iota(jnp.int32, (tokens, tokens), 0)
    later = lax.broadcasted_iota(jnp.int32, (tokens, tokens), 1)
    before = jnp.where(earlier < later, 1.0, 0.0).astype(BF16)
    ranks = dot_nn(jnp.where(flags, 1.0, 0.0).astype(BF16), before)
    slots = jnp.where(flags, ranks, -1.0)
    groups = meta_ref.shape[0]
    count = experts // groups
    meta_ref[...] = jnp.zeros(meta_ref.shape, F32)
    for e in range(experts):
        meta_ref[e // count, e % count : e % count + 1, :] = slots[e : e + 1]
        meta_ref[e // count, 8 + e % count : 9 + e % count, :] = gates[e : e + 1]


def middle(mixed, out_full, x, gain_row, router_rows, routes_rows, groups):
    tokens, width = x.shape
    experts = router_rows.shape[0]
    return pl.pallas_call(
        middle_kernel,
        out_shape=[
            jax.ShapeDtypeStruct((tokens, width), F32),
            jax.ShapeDtypeStruct((tokens, width), BF16),
            jax.ShapeDtypeStruct((experts, tokens), F32),
            jax.ShapeDtypeStruct((groups, 16, tokens), F32),
        ],
        compiler_params=pltpu.CompilerParams(vmem_limit_bytes=48 << 20),
        cost_estimate=pl.CostEstimate(flops=3 * 10**9, bytes_accessed=16 << 20, transcendentals=1 << 14),
        name="middle",
    )(mixed, out_full, x, gain_row, router_rows, routes_rows)


def flipped(index, mask):
    out, bit = index, 1
    while bit <= mask:
        if mask & bit:
            out = out + bit - 2 * bit * ((index // bit) % 2)
        bit *= 2
    return out


def send(source, target, send_sem, recv_sem, device):
    return pltpu.make_async_remote_copy(
        src_ref=source, dst_ref=target, send_sem=send_sem, recv_sem=recv_sem,
        device_id=device, device_id_type=pl.DeviceIdType.MESH,
    )


def greet(devices):
    barrier = pltpu.get_barrier_semaphore()
    for device in devices:
        pl.semaphore_signal(barrier, inc=1, device_id=device, device_id_type=pl.DeviceIdType.MESH)
    pl.semaphore_wait(barrier, len(devices))


class Gather:
    def __init__(self, parts, levels, blocks, sems):
        self.parts, self.levels, self.blocks = parts, levels, blocks
        self.near_send, self.near_recv, self.team_send, self.team_recv, self.core_send, self.core_recv = sems
        self.group, self.shard = lax.axis_index("expert"), lax.axis_index("shard")
        level, self.core = self.shard // 2, self.shard % 2
        self.part = self.group % parts
        self.other = self.shard + 1 - 2 * self.core
        self.far = [flipped(level, k) * 2 + self.core for k in range(levels)]
        self.far_other = [flipped(level, k) * 2 + 1 - self.core for k in range(levels)]
        self.team_part = [flipped(self.part, k) for k in range(parts)]
        self.team = [self.group - self.part + t for t in self.team_part]
        self.mate = (self.group, self.other)
        self.sends = []

    def greet(self, near=True):
        greet(
            [self.mate]
            + [(self.group, self.far[k]) for k in range(1, self.levels) if near]
            + [(self.team[t], self.shard) for t in range(1, self.parts)]
        )

    def push(self, make):
        make().start()
        self.sends.append(make)

    def arrived(self, piece, send_sem, recv_sem):
        send(piece, piece, send_sem, recv_sem, self.mate).wait_recv()

    def near(self, own, i):
        for k in range(1, self.levels):
            self.push(
                lambda k=k: send(
                    own.at[self.part], self.blocks[i].at[self.shard * self.parts + self.part],
                    self.near_send.at[i, k], self.near_recv.at[i, k], (self.group, self.far[k]),
                )
            )

    def near_arrived(self, i, k):
        piece = self.blocks[i].at[self.far[k] * self.parts + self.part]
        self.arrived(piece, self.near_send.at[i, k], self.near_recv.at[i, k])

    def spread(self, i, k):
        def piece():
            return self.blocks[i].at[self.far[k] * self.parts + self.part]

        for t in range(1, self.parts):
            self.push(
                lambda t=t: send(
                    piece(), piece(), self.team_send.at[i, k, t], self.team_recv.at[i, k, t],
                    (self.team[t], self.shard),
                )
            )
        self.push(
            lambda: send(
                piece(), piece(), self.core_send.at[i, k, 0], self.core_recv.at[i, k, 0], self.mate
            )
        )

    def own_to_mate(self, own, i):
        self.push(
            lambda: send(
                own(), self.blocks[i].at[pl.ds(self.shard * self.parts, self.parts)],
                self.core_send.at[i, 0, 0], self.core_recv.at[i, 0, 0], self.mate,
            )
        )

    def team_to_mate(self, i):
        for k in range(1, self.levels):
            for t in range(1, self.parts):

                def piece(k=k, t=t):
                    return self.blocks[i].at[self.far[k] * self.parts + self.team_part[t]]

                self.arrived(piece(), self.team_send.at[i, k, t], self.team_recv.at[i, k, t])
                self.push(
                    lambda piece=piece, k=k, t=t: send(
                        piece(), piece(), self.core_send.at[i, k, t], self.core_recv.at[i, k, t],
                        self.mate,
                    )
                )

    def mate_arrived(self, i):
        piece = self.blocks[i].at[pl.ds(self.other * self.parts, self.parts)]
        self.arrived(piece, self.core_send.at[i, 0, 0], self.core_recv.at[i, 0, 0])
        for k in range(1, self.levels):
            for t in range(self.parts):
                piece = self.blocks[i].at[self.far_other[k] * self.parts + self.team_part[t]]
                self.arrived(piece, self.core_send.at[i, k, t], self.core_recv.at[i, k, t])

    def finish(self):
        for make in self.sends:
            make().wait_send()


def gather_sems(levels, parts, count):
    dma = pltpu.SemaphoreType.DMA
    return [dma((count, levels))] * 2 + [dma((count, levels, parts))] * 4


def gather_parts(groups, rows):
    return next(p for p in (4, 2, 1) if groups % p == 0 and rows % (16 * p) == 0)


def gather_kernel(parts, levels, count, *refs):
    ins, outs = refs[:count], refs[count : 2 * count]
    bounce = refs[2 * count : 3 * count]
    local_sem = refs[3 * count]
    plan = Gather(parts, levels, outs, refs[3 * count + 1 :])
    plan.greet()
    own = pl.ds(plan.shard * parts, parts)
    loads = [pltpu.make_async_copy(ins[i], bounce[i], local_sem.at[0, i]) for i in range(count)]
    stores = [pltpu.make_async_copy(bounce[i], outs[i].at[own], local_sem.at[1, i]) for i in range(count)]
    for copy in loads:
        copy.start()
    for i in range(count):
        plan.near(ins[i], i)
    plan.own_to_mate(lambda: ins[0], 0)
    for load, store in zip(loads, stores):
        load.wait()
        store.start()
    for k in range(1, levels):
        plan.near_arrived(0, k)
        plan.spread(0, k)
    plan.team_to_mate(0)
    for k in range(1, levels):
        plan.near_arrived(1, k)
    plan.mate_arrived(0)
    plan.finish()
    for copy in stores:
        copy.wait()


def gather_weights(blocks, groups, shards):
    rows = blocks[0].shape[0]
    parts = gather_parts(groups, rows)
    levels, count = shards // 2, len(blocks)
    blocks = [b.reshape(parts, rows // parts, b.shape[1]) for b in blocks]
    return pl.pallas_call(
        functools.partial(gather_kernel, parts, levels, count),
        in_specs=[pl.BlockSpec(memory_space=pl.ANY)] * count,
        out_specs=[pl.BlockSpec(memory_space=pl.ANY)] * count,
        out_shape=[
            jax.ShapeDtypeStruct((shards * parts,) + b.shape[1:], b.dtype) for b in blocks
        ],
        scratch_shapes=[pltpu.VMEM(b.shape, b.dtype) for b in blocks]
        + [pltpu.SemaphoreType.DMA((2, count))]
        + gather_sems(levels, parts, count),
        compiler_params=pltpu.CompilerParams(collective_id=0, has_side_effects=True),
        name="gather_weights",
    )(*blocks)


def reduce_kernel(groups, levels, rows, chunk, *refs):
    (mixed_ref, ag_ref, normed_ref, dproj_ref, misc_ref, out_grad_ref, qkv_grad_ref, misc_grad_ref,
     mixed_t, normed_t, held, from_core, from_group, summed, from_level, home) = refs[:16]
    core_send, core_recv, group_send, group_recv, level_send, level_recv, home_send, home_recv = refs[16:]
    group, shard = lax.axis_index("expert"), lax.axis_index("shard")
    level, core = shard // 2, shard % 2
    other = shard + 1 - 2 * core
    team = [flipped(group, t) for t in range(groups)]
    far = [flipped(level, k) for k in range(levels)]
    greet(
        [(group, other)]
        + [(group, far[k] * 2 + core) for k in range(1, levels)]
        + [(team[t], shard) for t in range(1, groups)]
    )
    sends = []

    def push(*args):
        copy = send(*args)
        copy.start()
        sends.append(copy)

    def arrived(piece, send_sem, recv_sem):
        send(piece, piece, send_sem, recv_sem, (group, other)).wait_recv()

    mixed_t[...] = mixed_ref[...].T
    normed_t[...] = normed_ref[...].T
    out_cols, qkv_cols = ag_ref.shape[1], dproj_ref.shape[1]
    sources = [
        (0, out_cols, mixed_t, ag_ref),
        (out_cols, out_cols + qkv_cols, normed_t, dproj_ref),
        (out_cols + qkv_cols, out_cols + qkv_cols + MISC, None, misc_ref),
    ]
    for k in range(groups):
        low, high = k * chunk, (k + 1) * chunk
        for start, stop, left, right in sources:
            a, b = max(low, start), min(high, stop)
            if a >= b:
                continue

            @pl.loop(0, 2 * levels)
            def _(s):
                at = pl.ds(pl.multiple_of(s * rows, rows), rows)
                if left is None:
                    value = right[at, a - start : b - start]
                else:
                    value = dot_nn(left[at, :], right[:, a - start : b - start]).astype(BF16)
                held[k, s % 2, s // 2, :, a - low : b - low] = value

        push(held.at[k, 1 - core], from_core.at[k], core_send.at[k], core_recv.at[k], (group, other))
    for k in range(groups):
        arrived(from_core.at[k], core_send.at[k], core_recv.at[k])

        @pl.loop(0, levels)
        def _(z):
            held[k, core, z] = (held[k, core, z].astype(F32) + from_core[k, z].astype(F32)).astype(BF16)

    order = list(range(1, levels)) + [0]
    for k in order:
        for t in range(1, groups):
            push(
                held.at[team[t], core, far[k]], from_group.at[t, k],
                group_send.at[t, k], group_recv.at[t, k], (team[t], shard),
            )
    for k in order:
        total = held[group, core, far[k]].astype(F32)
        for t in range(1, groups):
            arrived(from_group.at[t, k], group_send.at[t, k], group_recv.at[t, k])
            total = total + from_group[t, k].astype(F32)
        summed[k] = total.astype(BF16)
        if k:
            push(
                summed.at[k], from_level.at[k], level_send.at[k], level_recv.at[k],
                (group, far[k] * 2 + core),
            )
    total = summed[0].astype(F32)
    for k in range(1, levels):
        arrived(from_level.at[k], level_send.at[k], level_recv.at[k])
        total = total + from_level[k].astype(F32)
    home[group] = total.astype(BF16)
    for t in range(1, groups):
        push(home.at[group], home.at[group], home_send.at[t], home_recv.at[t], (team[t], shard))
    for t in range(1, groups):
        arrived(home.at[team[t]], home_send.at[t], home_recv.at[t])
    tile = 128
    for at in range(0, out_cols + qkv_cols + MISC, tile):
        value = home[at // chunk, :, at % chunk : at % chunk + tile].astype(F32)
        if at < out_cols:
            out_grad_ref[:, at : at + tile] = value
        elif at < out_cols + qkv_cols:
            j, inside = divmod(at - out_cols, BLOCK)
            if inside < QW:
                to = j * QW + inside
            elif inside < QW + KW:
                to = PAIRS * QW + j * KW + inside - QW
            else:
                to = PAIRS * (QW + KW) + j * KW + inside - QW - KW
            qkv_grad_ref[:, to : to + tile] = value
        else:
            misc_grad_ref[...] = value
    for copy in sends:
        copy.wait_send()


def reduce_weights(mixed, ag, normed, dproj, misc_cols, groups, shards):
    tokens, width = normed.shape
    levels, rows = shards // 2, width // shards
    total = ag.shape[1] + dproj.shape[1] + MISC
    chunk = 128 * (-(-total // (128 * groups)))
    dma = pltpu.SemaphoreType.DMA
    vmem = pl.BlockSpec(memory_space=pltpu.VMEM)
    piece = (rows, chunk)
    return pl.pallas_call(
        functools.partial(reduce_kernel, groups, levels, rows, chunk),
        in_specs=[vmem] * 5,
        out_specs=[vmem] * 3,
        out_shape=[
            jax.ShapeDtypeStruct((rows, cols), F32) for cols in (ag.shape[1], dproj.shape[1], MISC)
        ],
        scratch_shapes=[
            pltpu.VMEM((mixed.shape[1], tokens), BF16),
            pltpu.VMEM((width, tokens), BF16),
            pltpu.VMEM((groups, 2, levels) + piece, BF16),
            pltpu.VMEM((groups, levels) + piece, BF16),
            pltpu.VMEM((groups, levels) + piece, BF16),
            pltpu.VMEM((levels,) + piece, BF16),
            pltpu.VMEM((levels,) + piece, BF16),
            pltpu.VMEM((groups,) + piece, BF16),
            dma((groups,)), dma((groups,)),
            dma((groups, levels)), dma((groups, levels)),
            dma((levels,)), dma((levels,)),
            dma((groups,)), dma((groups,)),
        ],
        compiler_params=pltpu.CompilerParams(
            collective_id=1, has_side_effects=True, vmem_limit_bytes=56 << 20
        ),
        cost_estimate=pl.CostEstimate(
            flops=2 * tokens * width * total, bytes_accessed=8 << 20, transcendentals=0
        ),
        name="reduce_weights",
    )(mixed, ag, normed, dproj, misc_cols)


def expert_kernel(capacity, shards, groups, count, base, stage, *refs):
    refs = list(refs)
    take = lambda n: [refs.pop(0) for _ in range(n)]
    if stage == "first":
        x_own, meta_own = take(2)
        u_ins = take(3 if groups == 4 else groups)
    else:
        x_ref, u_ref, meta_ref, out_in, dx_in, gg_in = take(6)
    packed_ref = take(1)[0]
    if stage == "last":
        take(1)
    if stage == "first":
        x_all, u_all, meta_all, out_ref, dx_ref, gg_ref, dw_out = take(7)
    elif stage == "last":
        out_home, dx_home, gg_home, dw_out = take(4)
    else:
        out_ref, dx_ref, gg_ref, dw_out = take(4)
    xs, us, bs, inn, dw, dw_sem, we_all, wp_all, we_sem, wp_sem = take(10)
    if stage == "first":
        x_buf, u_buf, meta_buf = take(3)
        x_send, x_recv, meta_send, meta_recv, load_sem, u_sem, meta_sem, keep_sem, pass_sem = take(9)
    elif stage == "last":
        buf, passing, gg_buf = take(3)
        load_sem, pass_send, pass_recv, dx_send, dx_recv, gg_send, gg_recv, keep_sem = take(8)
    turn_at, expert = pl.program_id(0), pl.program_id(1)
    last_turn, last = groups - 1, count - 1
    group, shard = lax.axis_index("expert"), lax.axis_index("shard")
    team = [flipped(group, t) for t in range(groups)]
    width = xs.shape[2]
    tokens = x_buf.shape[0] if stage == "first" else x_ref.shape[1]
    tall, short = width // shards, FF // shards
    side = width - 2 * FF
    we_ref, wp_ref = we_all.at[expert], wp_all.at[expert]

    @pl.when((turn_at == 0) & (expert == 0))
    def _():
        for e in range(count):

            @pl.loop(0, shards)
            def _(s):
                a = pl.ds(pl.multiple_of(s * tall, 16), tall)
                b = pl.ds(pl.multiple_of(s * short, 16), short)
                low = pl.ds(pl.multiple_of(s * short, 16), short // 2)
                high = pl.ds(pl.multiple_of(s * short + short // 2, 16), short // 2)
                source = packed_ref.at[s, e]
                rest = pl.ds(tall + short, short // 2)
                for piece, target, sem in (
                    (source.at[:tall], we_all.at[e, a], we_sem),
                    (source.at[tall : tall + short], wp_all.at[e, b, : 2 * FF], wp_sem),
                    (source.at[rest, :side], wp_all.at[e, low, 2 * FF :], wp_sem),
                    (source.at[rest, side:], wp_all.at[e, high, 2 * FF :], wp_sem),
                ):
                    pltpu.make_async_copy(piece, target, sem.at[e]).start()

    if stage == "first":

        relay = groups == 4
        near = [1, 2] if relay else list(range(1, groups))
        half = tokens // 2

        def x_copy(t):
            return send(x_own, x_all.at[t], x_send.at[t], x_recv.at[t], (team[t], shard))

        def passed(source, target, part, sems):
            at = pl.ds(part * half, half)
            return send(
                source.at[at], target.at[3, at], sems.at[0, part], sems.at[1, part],
                (team[2 - part], shard),
            )

        def x_pass(part):
            return passed(x_all.at[1 + part], x_all, part, pass_sem.at[0])

        def u_pass(part):
            return passed(u_ins[1 + part], u_all, part, pass_sem.at[1])

        def meta_copy(t):
            return send(
                meta_own.at[team[t]], meta_all.at[t], meta_send.at[t], meta_recv.at[t], (team[t], shard)
            )

        def u_load(t):
            source = u_all.at[t] if relay and t == 3 else u_ins[t]
            return pltpu.make_async_copy(source, u_buf.at[t % 2], u_sem.at[t % 2])

        def x_keep():
            return pltpu.make_async_copy(x_buf, x_all.at[0], keep_sem.at[0])

        def meta_keep():
            return pltpu.make_async_copy(meta_buf, meta_all.at[0], keep_sem.at[1])

        def u_keep(t):
            return pltpu.make_async_copy(u_buf.at[t % 2], u_all.at[t], keep_sem.at[2 + t])

        for t in range(groups):

            @pl.when((turn_at == t) & (expert == 0))
            def _():
                if t == 0:
                    u_load(0).start()
                    greet([(team[k], shard) for k in range(1, groups)])
                    for k in range(1, groups):
                        meta_copy(k).start()
                    for k in near:
                        x_copy(k).start()
                    if relay:
                        u_pass(0).start()
                        u_pass(1).start()
                    fetch_x, fetch_meta = x_own, meta_own.at[group]
                else:
                    if not relay:
                        x_copy(t).wait_recv()
                    elif t == 1:
                        for k in near:
                            x_copy(k).wait_recv()
                        x_pass(0).start()
                        x_pass(1).start()
                    elif t == 3:
                        for part in range(2):
                            x_pass(part).wait_recv()
                            u_pass(part).wait_recv()
                        u_load(3).start()
                    meta_copy(t).wait_recv()
                    u_keep(t - 1).wait()
                    if t == 1:
                        x_keep().wait()
                        meta_keep().wait()
                    fetch_x, fetch_meta = x_all.at[t], meta_all.at[t]
                load = pltpu.make_async_copy(fetch_x, x_buf, load_sem)
                load_meta = pltpu.make_async_copy(fetch_meta, meta_buf, meta_sem)
                load.start()
                load_meta.start()
                if t + 1 < groups and not (relay and t == 2):
                    u_load(t + 1).start()
                u_load(t).wait()
                load_meta.wait()
                load.wait()
                if not (relay and t == 3):
                    u_keep(t).start()
                if t == 0:
                    x_keep().start()
                    meta_keep().start()

        x_now, u_now, meta_now = x_buf, u_buf.at[turn_at % 2], meta_buf
    else:
        x_now, u_now, meta_now = x_ref.at[0], u_ref.at[0], meta_ref.at[0]

    if stage == "last":
        relay = groups == 4
        slots, half = buf.shape[1], tokens // 2
        halves = [pl.ds(0, half), pl.ds(half, half)]

        def kept(kind, i):
            return buf.at[kind, i % slots]

        def load(kind, i):
            source = dx_in if kind else out_in
            return pltpu.make_async_copy(
                source.at[last_turn - i], kept(kind, i), load_sem.at[kind, i % 2]
            )

        def store(i):
            return pltpu.make_async_copy(kept(0, i), out_home.at[last_turn - i], keep_sem.at[2 + i])

        def pass_copy(kind, part):
            return send(
                kept(kind, 0).at[halves[part]], passing.at[kind, part],
                pass_send.at[kind, part], pass_recv.at[kind, part], (team[1 + part], shard),
            )

        def dx_copy(i):
            t = last_turn - i
            return send(kept(1, i), dx_home.at[t], dx_send.at[t], dx_recv.at[t], (team[t], shard))

        def dx_half(part):
            at = halves[part]
            return send(
                kept(1, 1).at[at], dx_home.at[2, at], dx_send.at[2 + part], dx_recv.at[2 + part],
                (team[2], shard),
            )

        def gg_copy(i):
            t = last_turn - i
            return send(gg_buf.at[i], gg_home.at[group], gg_send.at[t], gg_recv.at[t], (team[t], shard))

        def own_copies():
            return [
                pltpu.make_async_copy(kept(1, last_turn), dx_home.at[0], keep_sem.at[0]),
                pltpu.make_async_copy(gg_buf.at[last_turn], gg_home.at[group], keep_sem.at[1]),
            ]

        for i in range(groups):

            @pl.when((turn_at == i) & (expert == 0))
            def _():
                if i == 0:
                    for kind in range(2):
                        load(kind, 0).start()
                    greet([(team[k], shard) for k in range(1, groups)])
                if i + 1 < groups:
                    if i + 1 >= slots:
                        dx_copy(i + 1 - slots).wait_send()
                        store(i + 1 - slots).wait()
                    for kind in range(2):
                        load(kind, i + 1).start()
                for kind in range(2):
                    load(kind, i).wait()

        at_now = turn_at % slots
        out_now, dx_now, gg_now = buf.at[0, at_now], buf.at[1, at_now], gg_buf.at[turn_at]
    else:
        out_now, dx_now, gg_now = out_ref.at[0], dx_ref.at[0], gg_ref.at[0]

    @pl.when(expert == 0)
    def _():
        if stage == "first":
            out_now[...] = jnp.zeros((tokens, width), BF16)
            dx_now[...] = jnp.zeros((tokens, width), BF16)
            gg_now[...] = jnp.zeros((8, tokens), F32)
        else:
            gg_now[...] = gg_in[0]
        if stage == "between":
            out_now[...] = out_in[0]
            dx_now[...] = dx_in[0]

    @pl.when(turn_at == 0)
    def _():
        pltpu.make_async_copy(we_ref, we_ref, we_sem.at[expert]).wait()
        pltpu.make_async_copy(wp_ref, wp_ref, wp_sem.at[expert]).wait()

    slot_row = meta_now[pl.ds(base + expert, 1), :]
    gate_row = meta_now[pl.ds(8 + base + expert, 1), :]
    index = lax.broadcasted_iota(jnp.int32, (capacity, tokens), 0).astype(F32)
    pick = jnp.where(index == slot_row, 1.0, 0.0)
    gate_col = jnp.sum(pick * gate_row, axis=1, keepdims=True)
    place = pick.astype(BF16)
    rows = pl.ds(pl.multiple_of(turn_at * capacity, capacity), capacity)
    step = 512
    for c in range(0, width, step):
        xs[expert, rows, c : c + step] = dot_nn(place, x_now[:, c : c + step]).astype(BF16)
        us[expert, rows, c : c + step] = dot_nn(place, u_now[:, c : c + step]).astype(BF16)
    x = xs[expert, rows, :]
    gate = dot_nn(x, we_ref[:, :FF])
    up = dot_nn(x, we_ref[:, FF:])
    back = dot_nt(us[expert, rows, :], wp_ref[...])
    sig = 1.0 / (1.0 + jnp.exp(-gate))
    act = gate * sig
    inner = act * up
    inner_low = inner.astype(BF16)
    gate_grad = jnp.sum(inner * back, axis=1, keepdims=True)
    here = lax.broadcasted_iota(jnp.int32, (8, tokens), 0) == base + expert
    gg_now[...] = jnp.where(here, jnp.sum(pick * gate_grad, axis=0, keepdims=True), gg_now[...])
    inn[expert, rows, :] = (inner * gate_col).astype(BF16)
    inner_grads = back * gate_col
    bs[expert, rows, :FF] = (inner_grads * up * sig * (1.0 + gate * (1.0 - sig))).astype(BF16)
    bs[expert, rows, FF:] = (inner_grads * act).astype(BF16)
    both = bs[expert, rows, :]
    weighted_t = (pick * gate_row).astype(BF16).T
    place_t = place.T
    for c in range(0, width, step):
        result = dot_nn(inner_low, wp_ref[:, c : c + step]).astype(BF16)
        out_now[:, c : c + step] = (
            out_now[:, c : c + step].astype(F32) + dot_nn(weighted_t, result)
        ).astype(BF16)
        row_grads = dot_nt(both, we_ref[c : c + step, :]).astype(BF16)
        dx_now[:, c : c + step] = (
            dx_now[:, c : c + step].astype(F32) + dot_nn(place_t, row_grads)
        ).astype(BF16)

    if stage == "last":

        def add_passed(kind):
            for part in range(2):
                pass_copy(kind, part).wait_recv()
                target = kept(kind, 1 + part).at[halves[part]]
                target[...] = (target[...].astype(F32) + passing[kind, part].astype(F32)).astype(BF16)

        for i in range(groups):

            @pl.when((turn_at == i) & (expert == last))
            def _():
                if i < last_turn:
                    gg_copy(i).start()
                else:
                    for copy in own_copies():
                        copy.start()
                if not relay:
                    store(i).start()
                    if i < last_turn:
                        dx_copy(i).start()
                elif i == 0:
                    for kind in (1, 0):
                        for part in range(2):
                            pass_copy(kind, part).start()
                elif i == 1:
                    dx_half(1).start()
                elif i == 2:
                    add_passed(1)
                    dx_copy(2).start()
                    dx_half(0).start()
                else:
                    add_passed(0)
                    for k in range(1, groups):
                        store(k).start()

    def store_weights(e):
        return pltpu.make_async_copy(dw, dw_out.at[:, (1 if stage == "last" else 0) + e], dw_sem)

    @pl.when(turn_at == last_turn)
    def _():
        @pl.when(expert > 0)
        def _():
            store_weights(0).wait()

        wide, half = 384, FF // 2

        @pl.loop(0, width // wide)
        def _(c):
            at = pl.ds(pl.multiple_of(c * wide, wide), wide)
            value = dot_tn(xs[expert, :, at], bs[expert]).astype(BF16)
            for i in range(wide // tall):
                dw[c * (wide // tall) + i, :tall, :] = value[i * tall : (i + 1) * tall]

        @pl.loop(0, FF // half)
        def _(c):
            at = pl.ds(pl.multiple_of(c * half, half), half)
            value = dot_tn(inn[expert, :, at], us[expert]).astype(BF16)
            for i in range(half // short):
                s, low = c * (half // short) + i, i * short
                mid, high = low + short // 2, low + short
                dw[s, tall : tall + short, :] = value[low:high, : 2 * FF]
                dw[s, tall + short :, :side] = value[low:mid, 2 * FF :]
                dw[s, tall + short :, side:] = value[mid:high, 2 * FF :]

        store_weights(expert).start()

    @pl.when((turn_at == last_turn) & (expert == last))
    def _():
        store_weights(0).wait()
        if stage == "first":
            if not relay:
                u_keep(last_turn).wait()
            for t in range(1, groups):
                meta_copy(t).wait_send()
            for t in near:
                x_copy(t).wait_send()
            if relay:
                for part in range(2):
                    x_pass(part).wait_send()
                    u_pass(part).wait_send()
        if stage == "last":
            for i in range(groups - 1):
                t = last_turn - i
                gg_copy(i).wait_send()
                send(
                    gg_buf.at[i], gg_home.at[team[t]], gg_send.at[t], gg_recv.at[t], (team[t], shard)
                ).wait_recv()
            if relay:
                for part in range(2):
                    dx_half(part).wait()
                    for kind in range(2):
                        pass_copy(kind, part).wait_send()
                dx_copy(2).wait()
                for k in range(1, groups):
                    store(k).wait()
            else:
                for i in range(groups - 1):
                    if i + slots >= groups:
                        dx_copy(i).wait_send()
                    dx_copy(i).wait_recv()
                for i in range(groups - slots, groups):
                    store(i).wait()
            for copy in own_copies():
                copy.wait()


def expert_call(capacity, shards, groups, base, stage, data, packed_weights, total_count, grads_in=()):
    count = packed_weights.shape[1]
    tokens, width = data[0].shape[-2:]
    total = groups * capacity
    anywhere = pl.BlockSpec(memory_space=pl.ANY)
    turned = (lambda i: i) if stage == "first" else (lambda i: groups - 1 - i)
    block = pl.BlockSpec((1, tokens, width), lambda i, e: (turned(i), 0, 0))
    small = pl.BlockSpec((1, 8, tokens), lambda i, e: (turned(i), 0, 0))
    dma = pltpu.SemaphoreType.DMA
    many = jax.ShapeDtypeStruct((groups, tokens, width), BF16)
    grads = jax.ShapeDtypeStruct((groups, 8, tokens), F32)
    packed = (shards, (width + FF + FF // 2) // shards, 2 * FF)
    weights = jax.ShapeDtypeStruct((shards, total_count) + packed[1:], BF16)
    meta = jax.ShapeDtypeStruct((groups, 16, tokens), F32)
    scratch = [
        pltpu.VMEM((count, total, width), BF16),
        pltpu.VMEM((count, total, width), BF16),
        pltpu.VMEM((count, total, 2 * FF), BF16),
        pltpu.VMEM((count, total, FF), BF16),
        pltpu.VMEM(packed, BF16),
        dma,
        pltpu.VMEM((count, width, 2 * FF), BF16),
        pltpu.VMEM((count, FF, width), BF16),
        dma((count,)), dma((count,)),
    ]
    if stage == "first":
        in_specs = [anywhere] * len(data)
        out_specs = [anywhere] * 3 + [block, block, small, anywhere]
        out_shape = [many, many, meta, many, many, grads, weights]
        scratch += [
            pltpu.VMEM((tokens, width), BF16),
            pltpu.VMEM((2, tokens, width), BF16),
            pltpu.VMEM((16, tokens), F32),
            dma((groups,)), dma((groups,)), dma((groups,)), dma((groups,)),
            dma, dma((2,)), dma, dma((2 + groups,)), dma((2, 2, 2)),
        ]
    else:
        meta_block = pl.BlockSpec((1, 16, tokens), lambda i, e: (turned(i), 0, 0))
        in_specs = [block, block, meta_block, block, block, small]
        out_specs = [block, block, small, anywhere]
        if stage == "last":
            in_specs[3:5] = [anywhere] * 2
            out_specs = [anywhere] * 4
            slots = groups if groups == 4 else 3
            passed = 2 if groups == 4 else 1
            scratch += [
                pltpu.VMEM((2, slots, tokens, width), BF16),
                pltpu.VMEM((passed, passed, tokens // 2, width), BF16),
                pltpu.VMEM((groups, 8, tokens), F32),
                dma((2, 2)), dma((2, 2)), dma((2, 2)),
                dma((groups,)), dma((groups,)), dma((groups,)), dma((groups,)), dma((2 + groups,)),
            ]
        out_shape = [many, many, grads, weights]
    remote = {"first": 2, "last": 3}
    return pl.pallas_call(
        functools.partial(expert_kernel, capacity, shards, groups, count, base, stage),
        grid=(groups, count),
        in_specs=in_specs + [anywhere] * (1 + len(grads_in)),
        out_specs=out_specs,
        out_shape=out_shape,
        scratch_shapes=scratch,
        compiler_params=pltpu.CompilerParams(
            vmem_limit_bytes=62 << 20,
            **({"collective_id": remote[stage], "has_side_effects": True} if stage in remote else {}),
        ),
        cost_estimate=pl.CostEstimate(
            flops=2 * count * total * width * (4 * tokens + 9 * FF),
            bytes_accessed=6 * groups * tokens * width * 2,
            transcendentals=count * total * FF,
        ),
        name="experts_" + stage,
        input_output_aliases={len(data) + 1: 3} if grads_in else {},
    )(*data, packed_weights, *grads_in)


def norm_back(values, gain_row, grad_rows):
    scale_rows = lax.rsqrt(jnp.mean(values * values, axis=-1, keepdims=True) + EPSILON)
    weighted = gain_row * grad_rows
    inner_mean = jnp.mean(weighted * values, axis=-1, keepdims=True)
    input_part = (
        scale_rows * weighted - values * (scale_rows * scale_rows * scale_rows) * inner_mean
    )
    gain_part = jnp.sum(grad_rows * values * scale_rows, axis=0)
    return (input_part, gain_part)


def to_blocks(weight):
    rows = weight.shape[0]
    qs = weight[:, : HEADS * HEAD].reshape(rows, PAIRS, QW)
    ks = weight[:, HEADS * HEAD : (HEADS + KV_HEADS) * HEAD].reshape(rows, PAIRS, KW)
    vs = weight[:, (HEADS + KV_HEADS) * HEAD :].reshape(rows, PAIRS, KW)
    return jnp.concatenate([qs, ks, vs], axis=2).reshape(rows, PAIRS * BLOCK)


def pack_kernel(cuts, expand_ref, project_ref, *outs):
    short = project_ref.shape[1]
    tall = expand_ref.shape[1]
    side = project_ref.shape[2] - 2 * FF
    for (low, high), out in zip(cuts, outs):
        for e in range(low, high):
            out[e - low, :tall] = expand_ref[e]
            out[e - low, tall : tall + short] = project_ref[e, :, : 2 * FF]
            out[e - low, tall + short :, :side] = project_ref[e, : short // 2, 2 * FF :]
            out[e - low, tall + short :, side:] = project_ref[e, short // 2 :, 2 * FF :]


def pack_weights(expand, project):
    cuts = bands(expand.shape[0])
    rows = expand.shape[1] + project.shape[1] + project.shape[1] // 2
    return pl.pallas_call(
        functools.partial(pack_kernel, cuts),
        out_shape=[
            jax.ShapeDtypeStruct((high - low, rows, 2 * FF), BF16) for low, high in cuts
        ],
        compiler_params=pltpu.CompilerParams(vmem_limit_bytes=32 << 20),
        name="pack_weights",
    )(expand, project)


def hidden_back_kernel(
    dx_ref, gg_ref, gates_ref, router_ref, hidden_ref, gain_ref, up_ref, ffn_ref,
    grads_ref, low_ref, router_grad_ref, gain_grad_ref,
):
    gates, groups = gates_ref[...], gg_ref.shape[0]
    count = gates.shape[0] // groups
    gate_grads = jnp.concatenate([gg_ref[g, :count] for g in range(groups)], axis=0)
    mean = jnp.sum(gates * gate_grads, axis=0, keepdims=True)
    logit_grads = (gates * (gate_grads - mean)).astype(BF16)
    ffn_grads = dot_tn(logit_grads, router_ref[...])
    for g in range(dx_ref.shape[0]):
        ffn_grads = ffn_grads + dx_ref[g].astype(F32)
    hidden = hidden_ref[...]
    part, gain_part = norm_back(hidden, gain_ref[...].astype(F32), ffn_grads)
    hidden_grads = up_ref[...].astype(F32) + part
    grads_ref[...] = hidden_grads
    low_ref[...] = hidden_grads.astype(BF16)
    router_part = dot_nn(logit_grads, ffn_ref[...])

    @pl.when(pl.program_id(0) == 0)
    def _():
        router_grad_ref[...] = router_part
        gain_grad_ref[...] = gain_part[None]

    @pl.when(pl.program_id(0) > 0)
    def _():
        router_grad_ref[...] += router_part
        gain_grad_ref[...] += gain_part[None]


def hidden_back(sources, dx_home, gg_home, gates, router_rows, hidden, gain_row, out_grad, ffn_in):
    groups, tokens, width = dx_home.shape
    experts = gates.shape[0]
    step = 128
    rows = pl.BlockSpec((step, width), lambda i: (i, 0))
    return pl.pallas_call(
        hidden_back_kernel,
        grid=(tokens // step,),
        in_specs=[
            pl.BlockSpec((sources, step, width), lambda i: (0, i, 0)),
            pl.BlockSpec((groups, 8, step), lambda i: (0, 0, i)),
            pl.BlockSpec((experts, step), lambda i: (0, i)),
            whole_spec((experts, width)),
            rows,
            whole_spec((1, width)),
            rows,
            rows,
        ],
        out_specs=[rows, rows, whole_spec((experts, width)), whole_spec((1, width))],
        out_shape=[
            jax.ShapeDtypeStruct((tokens, width), F32),
            jax.ShapeDtypeStruct((tokens, width), BF16),
            jax.ShapeDtypeStruct((experts, width), F32),
            jax.ShapeDtypeStruct((1, width), F32),
        ],
        compiler_params=pltpu.CompilerParams(vmem_limit_bytes=48 << 20),
        cost_estimate=pl.CostEstimate(flops=10**8, bytes_accessed=20 << 20, transcendentals=0),
        name="hidden_back",
    )(dx_home, gg_home, gates, router_rows, hidden, gain_row, out_grad, ffn_in)


def unpack_kernel(tall, short, *refs):
    *ins, expand_ref, project_ref = refs
    at = 0
    for ref in ins:
        for i in range(ref.shape[0]):
            value = ref[i].astype(F32)
            expand_ref[at] = value[:tall]
            side = project_ref.shape[2] - 2 * FF
            project_ref[at, :, : 2 * FF] = value[tall : tall + short]
            project_ref[at, : short // 2, 2 * FF :] = value[tall + short :, :side]
            project_ref[at, short // 2 :, 2 * FF :] = value[tall + short :, side:]
            at += 1


def unpack_weights(shares, tall, short, width):
    count = sum(s.shape[0] for s in shares)
    return pl.pallas_call(
        functools.partial(unpack_kernel, tall, short),
        out_shape=[
            jax.ShapeDtypeStruct((count, tall, 2 * FF), F32),
            jax.ShapeDtypeStruct((count, short, width), F32),
        ],
        compiler_params=pltpu.CompilerParams(vmem_limit_bytes=32 << 20),
        name="unpack_weights",
    )(*shares)


def exchanged(value, flip, groups):
    if flip == 0:
        return value
    return lax.ppermute(value, "expert", [(i, i ^ flip) for i in range(groups)])


def bands(count):
    return [(0, 2), (2, count - 2), (count - 2, count)]


def local(
    inputs, attn_gain, qkv_weight, out_weight, ffn_gain, router_weight,
    expand_weight, project_weight, segment_ids, routes, out_grad,
):
    groups, shards = lax.axis_size("expert"), lax.axis_size("shard")
    tokens, width = inputs.shape
    experts = router_weight.shape[1]
    local_count = expand_weight.shape[0]
    capacity = 8 * ((5 * tokens * TOP + 32 * experts - 1) // (32 * experts))

    misc = jnp.concatenate(
        [
            attn_gain[:, None],
            ffn_gain[:, None],
            router_weight,
            jnp.zeros((attn_gain.shape[0], MISC - 2 - experts), BF16),
        ],
        axis=1,
    )
    packed = jnp.concatenate([to_blocks(qkv_weight), misc], axis=1)
    packed_full = [
        lax.all_gather(p, "shard", axis=0) for p in pack_weights(expand_weight, project_weight)
    ]
    qkv_full, out_part = gather_weights([packed, out_weight], groups, shards)
    qkv_full = qkv_full.reshape(width, -1)
    misc_rows = qkv_full[:, PAIRS * BLOCK :].T
    out_grad_late, misc_rows = lax.optimization_barrier((out_grad, misc_rows))
    u_parts = [
        exchanged(out_grad_late, t, groups) for t in range(3 if groups == 4 else groups)
    ]
    gain_one, gain_two = misc_rows[0:1], misc_rows[1:2]
    router_rows = misc_rows[2 : 2 + experts]
    tables = tuple(jnp.asarray(t) for t in rope_tables())
    seg_row = segment_ids.reshape(1, tokens)
    seg_col = segment_ids.reshape(tokens, 1)
    normed, proj, mixed, lse, out_full = attention_forward(
        inputs, gain_one, qkv_full, tables, seg_col, seg_row, out_part, groups, shards
    )
    hidden, ffn_in, gates, meta_own = middle(
        mixed, out_full, inputs, gain_two, router_rows, routes.T, groups
    )
    tall, short = expand_weight.shape[1], project_weight.shape[1]
    call = functools.partial(expert_call, capacity, shards, groups)

    def share_out(dw):
        return lax.psum_scatter(dw, "shard", scatter_dimension=0, tiled=True)[0]

    x_all, u_all, meta, out_acc, dx_acc, gg, dw = call(
        0, "first", (ffn_in, meta_own, *u_parts), packed_full[0], 2
    )
    shares = [share_out(dw)]
    out_acc, dx_acc, gg, dw = call(
        2, "between", (x_all, u_all, meta, out_acc, dx_acc, gg), packed_full[1], local_count - 2
    )
    out_acc, dx_home, gg_home, dw = call(
        local_count - 2, "last", (x_all, u_all, meta, out_acc, dx_acc, gg), packed_full[2],
        local_count - 2, (dw,),
    )
    shares.append(share_out(dw))
    sources = 3 if groups == 4 else groups
    dx_home, shares[0] = lax.optimization_barrier((dx_home, shares[0]))
    out_home = [exchanged(out_acc[t], t, groups) for t in range(sources)]
    hidden_grads, attended_grads, router_part, gain_two_grad = hidden_back(
        sources, dx_home, gg_home, gates, router_rows, hidden, gain_two, out_grad, ffn_in
    )
    dproj = attention_backward(
        attended_grads, out_full, proj, mixed, lse, tables, seg_col, seg_row
    )
    normed_grads = dot_nt(dproj, qkv_full[:, : PAIRS * BLOCK])
    input_part, gain_one_grad = norm_back(
        inputs.astype(F32), gain_one.astype(F32), normed_grads
    )
    input_grad = hidden_grads + input_part

    misc_part = jnp.concatenate(
        [
            gain_one_grad[None],
            gain_two_grad,
            router_part,
            jnp.zeros((MISC - 2 - experts, width), F32),
        ],
        axis=0,
    ).astype(BF16)
    out_weight_grad, qkv_grad, misc_total = reduce_weights(
        mixed, attended_grads, normed, dproj, misc_part.T, groups, shards
    )
    out_weight_grad, *out_home = lax.optimization_barrier((out_weight_grad, *out_home))
    output = (hidden + sum(o.astype(F32) for o in out_home)).astype(BF16)
    expand_grad, project_grad = unpack_weights(shares, tall, short, width)
    return (
        output,
        input_grad,
        misc_total[:, 0],
        qkv_grad,
        out_weight_grad,
        misc_total[:, 1],
        misc_total[:, 2 : 2 + experts],
        expand_grad,
        project_grad,
    )


def solution(mesh):
    rows = P(("expert", "shard"), None)
    return jax.shard_map(
        local,
        mesh=mesh,
        in_specs=(
            rows, P("shard"), P("shard", None), P("shard", None), P("shard"), P("shard", None),
            P("expert", "shard", None), P("expert", "shard", None), rows, rows, rows,
        ),
        out_specs=(
            rows, rows, P("shard"), P("shard", None), P("shard", None), P("shard"),
            P("shard", None), P("expert", "shard", None), P("expert", "shard", None),
        ),
        check_vma=False,
    )
```

```python
import functools

import jax
import jax.numpy as jnp
import numpy as np
from jax import lax
from jax.experimental import pallas as pl
from jax.experimental.pallas import tpu as pltpu
from jax.sharding import PartitionSpec as P

HEADS = 24
KV_HEADS = 8
HEAD = 64
FF = 512
TOP = 8
SEQ_LEN = 512
GROUP = HEADS // KV_HEADS
PAIRS = KV_HEADS // 2
QW = 2 * GROUP * HEAD
KW = 2 * HEAD
BLOCK = QW + 2 * KW
MISC = 128
QB = 128

EPSILON = 1e-06
ROPE_THETA = 10000.0
MASKED = -1e30
F32 = jnp.float32
BF16 = jnp.bfloat16


def dot_nn(a, b):
    return lax.dot_general(a, b, (((1,), (0,)), ((), ())), preferred_element_type=F32)


def dot_nt(a, b):
    return lax.dot_general(a, b, (((1,), (1,)), ((), ())), preferred_element_type=F32)


def dot_tn(a, b):
    return lax.dot_general(a, b, (((0,), (0,)), ((), ())), preferred_element_type=F32)


def rope_tables():
    frequency = (np.float32(ROPE_THETA) ** (-2.0 * np.arange(HEAD // 2) / HEAD)).astype(np.float32)
    angle = np.arange(SEQ_LEN, dtype=np.float32)[:, None] * frequency[None, :]
    cosine, sine = np.cos(angle).astype(np.float32), np.sin(angle).astype(np.float32)
    zero = np.zeros_like(sine)
    cos_table = np.concatenate([cosine] * 4, axis=1)
    left_table = np.concatenate([-sine, zero] * 2, axis=1)
    right_table = np.concatenate([zero, sine] * 2, axis=1)
    return cos_table, left_table, right_table


def turn(values, cos_table, left_table, right_table, sign):
    parts = []
    for c in range(values.shape[1] // 128):
        piece = values[:, 128 * c : 128 * (c + 1)]
        ahead = pltpu.roll(piece, 96, 1) * left_table
        behind = pltpu.roll(piece, 32, 1) * right_table
        parts.append(piece * cos_table + sign * (ahead + behind))
    return parts[0] if len(parts) == 1 else jnp.concatenate(parts, axis=1)


def key_range(block):
    return max(0, block - 2) * QB, (block + 1) * QB


def block_mask(seg_col, seg_row, block):
    low, high = key_range(block)
    rows = lax.broadcasted_iota(jnp.int32, (QB, high - low), 0) + block * QB
    cols = lax.broadcasted_iota(jnp.int32, (QB, high - low), 1) + low
    same = seg_col[block * QB : (block + 1) * QB, :] == seg_row[:, low:high]
    return jnp.concatenate([(rows >= cols) & same] * GROUP, axis=0)


def heads_of(values, pair, block):
    rows = values[block * QB : (block + 1) * QB, :]
    first = pair * GROUP
    return jnp.concatenate(
        [rows[:, HEAD * h : HEAD * (h + 1)] for h in range(first, first + GROUP)], axis=0
    )


def attention_forward_kernel(
    parts, levels, x_ref, gain_ref, w_ref, cos_ref, left_ref, right_ref, seg_col_ref, seg_row_ref,
    part_ref, normed_ref, proj_ref, mixed_ref, lse_ref, full_ref, *sems,
):
    step = pl.program_id(0)
    plan = Gather(parts, levels, [full_ref], sems)

    @pl.when(step == 0)
    def _():
        plan.greet(near=False)
        plan.own_to_mate(lambda: full_ref.at[pl.ds(plan.shard * parts, parts)], 0)
        for k in range(1, levels):
            plan.spread(0, k)

    @pl.when(step == 0)
    def _():
        x = x_ref[...].astype(F32)
        scale = lax.rsqrt(jnp.mean(x * x, axis=-1, keepdims=True) + EPSILON)
        normed_ref[...] = (x * scale * gain_ref[...].astype(F32)).astype(BF16)

    projected = dot_nn(normed_ref[...], w_ref[...])
    turned = turn(
        projected[:, : QW + KW], cos_ref[...], left_ref[...], right_ref[...], 1.0
    ).astype(BF16)
    queries, keys = turned[:, :QW], turned[:, QW:]
    values = projected[:, QW + KW :].astype(BF16)
    proj_ref[...] = jnp.concatenate([turned, values], axis=1)
    seg_col, seg_row = seg_col_ref[...], seg_row_ref[...]
    for block in range(SEQ_LEN // QB):
        low, high = key_range(block)
        allowed = block_mask(seg_col, seg_row, block)
        outs = []
        for pair in range(2):
            q3 = heads_of(queries, pair, block)
            k1 = keys[low:high, HEAD * pair : HEAD * (pair + 1)]
            v1 = values[low:high, HEAD * pair : HEAD * (pair + 1)]
            scores = jnp.where(allowed, dot_nt(q3, k1) * HEAD**-0.5, MASKED)
            top = jnp.max(scores, axis=-1, keepdims=True)
            weights = jnp.exp(scores - top)
            total = jnp.sum(weights, axis=-1, keepdims=True)
            mixed = dot_nn(weights.astype(BF16), v1) * (1.0 / total)
            logsum = top + jnp.log(total)
            for h in range(GROUP):
                outs.append(mixed[h * QB : (h + 1) * QB, :])
                lse_ref[0, block * QB : (block + 1) * QB, pair * GROUP + h : pair * GROUP + h + 1] = (
                    logsum[h * QB : (h + 1) * QB, :]
                )
        mixed_ref[block * QB : (block + 1) * QB, :] = jnp.concatenate(outs, axis=1).astype(BF16)

    @pl.when(step == PAIRS - 1)
    def _():
        plan.team_to_mate(0)
        plan.mate_arrived(0)
        plan.finish()


def whole_spec(shape):
    return pl.BlockSpec(shape, lambda *_: (0,) * len(shape))


def attention_forward(x, gain_row, w_full, tables, seg_col, seg_row, out_part, groups, shards):
    tokens, width = x.shape
    parts, levels = gather_parts(groups, width // shards), shards // 2
    table = whole_spec((SEQ_LEN, 128))
    *kept, out_full = pl.pallas_call(
        functools.partial(attention_forward_kernel, parts, levels),
        grid=(PAIRS,),
        in_specs=[
            whole_spec((tokens, width)),
            whole_spec((1, width)),
            pl.BlockSpec((width, BLOCK), lambda j: (0, j)),
            table, table, table,
            whole_spec((SEQ_LEN, 1)),
            whole_spec((1, SEQ_LEN)),
            pl.BlockSpec(memory_space=pl.ANY),
        ],
        out_specs=[
            whole_spec((tokens, width)),
            pl.BlockSpec((tokens, BLOCK), lambda j: (0, j)),
            pl.BlockSpec((tokens, QW), lambda j: (0, j)),
            pl.BlockSpec((1, tokens, 8), lambda j: (j, 0, 0)),
            pl.BlockSpec(memory_space=pl.ANY),
        ],
        out_shape=[
            jax.ShapeDtypeStruct((tokens, width), BF16),
            jax.ShapeDtypeStruct((tokens, PAIRS * BLOCK), BF16),
            jax.ShapeDtypeStruct((tokens, HEADS * HEAD), BF16),
            jax.ShapeDtypeStruct((PAIRS, tokens, 8), F32),
            jax.ShapeDtypeStruct(out_part.shape, BF16),
        ],
        scratch_shapes=gather_sems(levels, parts, 1),
        input_output_aliases={8: 4},
        compiler_params=pltpu.CompilerParams(
            vmem_limit_bytes=62 << 20, collective_id=4, has_side_effects=True
        ),
        cost_estimate=pl.CostEstimate(flops=10 * 10**9, bytes_accessed=20 << 20, transcendentals=4 << 20),
        name="attention_forward",
    )(x, gain_row, w_full, *tables, seg_col, seg_row, out_part)
    return *kept, out_full.reshape(width, -1)


def attention_backward_kernel(
    groups, levels, ag_ref, out_ref, proj_ref, mixed_ref, lse_ref, cos_ref, left_ref, right_ref,
    seg_col_ref, seg_row_ref, all_ref, dproj_ref, sum_ref, mixed_t, *rest,
):
    step = pl.program_id(0)
    plan = Reduce(groups, levels, rest[:4], rest[4:])

    @pl.when(step == 0)
    def _():
        plan.greet(False)
        mixed_t[...] = all_ref[...].T
        plan.fill([(0, ag_ref.shape[1], mixed_t, ag_ref)])

    @pl.when(step == 1)
    def _():
        plan.merge()

    @pl.when(step == 2)
    def _():
        plan.spread()

    grads = dot_nt(ag_ref[...], out_ref[...]).astype(BF16)
    product = grads.astype(F32) * mixed_ref[...].astype(F32)
    queries, keys, values = (
        proj_ref[:, :QW], proj_ref[:, QW : QW + KW], proj_ref[:, QW + KW :],
    )
    seg_col, seg_row = seg_col_ref[...], seg_row_ref[...]
    blocks = SEQ_LEN // QB
    dk = [[jnp.zeros((QB, HEAD), F32) for _ in range(blocks)] for _ in range(2)]
    dv = [[jnp.zeros((QB, HEAD), F32) for _ in range(blocks)] for _ in range(2)]
    dq_rows = []
    for block in range(blocks):
        low, high = key_range(block)
        allowed = block_mask(seg_col, seg_row, block)
        dqs = []
        for pair in range(2):
            q3, g3, o3 = (heads_of(v, pair, block) for v in (queries, grads, product))
            k1 = keys[low:high, HEAD * pair : HEAD * (pair + 1)]
            v1 = values[low:high, HEAD * pair : HEAD * (pair + 1)]
            logsum = jnp.concatenate(
                [
                    lse_ref[0, block * QB : (block + 1) * QB, pair * GROUP + h : pair * GROUP + h + 1]
                    for h in range(GROUP)
                ],
                axis=0,
            )
            scores = jnp.where(allowed, dot_nt(q3, k1) * HEAD**-0.5, MASKED)
            probs = jnp.exp(scores - logsum)
            inner = jnp.sum(o3, axis=-1, keepdims=True)
            score_grads = (probs * (dot_nt(g3, v1) - inner)).astype(BF16)
            dq = dot_nn(score_grads, k1)
            dk_part = dot_tn(score_grads, q3)
            dv_part = dot_tn(probs.astype(BF16), g3)
            for at in range(low // QB, high // QB):
                rows = slice(at * QB - low, (at + 1) * QB - low)
                dk[pair][at] += dk_part[rows]
                dv[pair][at] += dv_part[rows]
            dqs += [dq[h * QB : (h + 1) * QB, :] for h in range(GROUP)]
        dq_rows.append(jnp.concatenate(dqs, axis=1))
    dq_all = jnp.concatenate(dq_rows, axis=0)
    dk_all = jnp.concatenate([jnp.concatenate(d, axis=0) for d in dk], axis=1)
    dv_all = jnp.concatenate([jnp.concatenate(d, axis=0) for d in dv], axis=1)
    turned = jnp.concatenate([dq_all, dk_all], axis=1) * HEAD**-0.5
    back = turn(turned, cos_ref[...], left_ref[...], right_ref[...], -1.0)
    dproj_ref[...] = jnp.concatenate([back, dv_all], axis=1).astype(BF16)

    @pl.when(step == PAIRS - 1)
    def _():
        for k in range(levels):
            sum_ref[k] = plan.collect(k).astype(BF16)
        plan.finish()


def attention_backward(ag, out_full, proj, mixed, lse, tables, seg_col, seg_row, groups, shards):
    tokens, width = ag.shape
    levels, rows = shards // 2, width // shards
    chunk = chunk_of(width, groups)
    table = whole_spec((SEQ_LEN, 128))
    return pl.pallas_call(
        functools.partial(attention_backward_kernel, groups, levels),
        grid=(PAIRS,),
        in_specs=[
            whole_spec((tokens, width)),
            pl.BlockSpec((QW, width), lambda j: (j, 0)),
            pl.BlockSpec((tokens, BLOCK), lambda j: (0, j)),
            pl.BlockSpec((tokens, QW), lambda j: (0, j)),
            pl.BlockSpec((1, tokens, 8), lambda j: (j, 0, 0)),
            table, table, table,
            whole_spec((SEQ_LEN, 1)),
            whole_spec((1, SEQ_LEN)),
            whole_spec((tokens, mixed.shape[1])),
        ],
        out_specs=[
            pl.BlockSpec((tokens, BLOCK), lambda j: (0, j)),
            whole_spec((levels, rows, chunk)),
        ],
        out_shape=[
            jax.ShapeDtypeStruct((tokens, PAIRS * BLOCK), BF16),
            jax.ShapeDtypeStruct((levels, rows, chunk), BF16),
        ],
        scratch_shapes=[pltpu.VMEM((mixed.shape[1], tokens), BF16)]
        + reduce_buffers(groups, levels, rows, chunk)
        + reduce_sems(groups, levels),
        compiler_params=pltpu.CompilerParams(
            vmem_limit_bytes=62 << 20, collective_id=5, has_side_effects=True
        ),
        cost_estimate=pl.CostEstimate(flops=10 * 10**9, bytes_accessed=20 << 20, transcendentals=4 << 20),
        name="attention_backward",
    )(ag, out_full, proj, mixed, lse, *tables, seg_col, seg_row, mixed)


def middle_kernel(
    mixed_ref, out_ref, x_ref, gain_ref, router_ref, routes_ref,
    hidden_ref, ffn_ref, gates_ref, meta_ref,
):
    hidden = x_ref[...].astype(F32) + dot_nn(mixed_ref[...], out_ref[...])
    scale = lax.rsqrt(jnp.mean(hidden * hidden, axis=-1, keepdims=True) + EPSILON)
    hidden_ref[...] = hidden
    ffn_in = (hidden * scale * gain_ref[...].astype(F32)).astype(BF16)
    ffn_ref[...] = ffn_in
    logits = dot_nt(router_ref[...], ffn_in)
    experts, tokens = logits.shape
    index = lax.broadcasted_iota(jnp.int32, (experts, tokens), 0)
    flags = index == routes_ref[0:1, :]
    for k in range(1, TOP):
        flags = flags | (index == routes_ref[k : k + 1, :])
    chosen = jnp.where(flags, logits, MASKED)
    weights = jnp.where(flags, jnp.exp(chosen - jnp.max(chosen, axis=0, keepdims=True)), 0.0)
    gates = weights / jnp.sum(weights, axis=0, keepdims=True)
    gates_ref[...] = gates
    earlier = lax.broadcasted_iota(jnp.int32, (tokens, tokens), 0)
    later = lax.broadcasted_iota(jnp.int32, (tokens, tokens), 1)
    before = jnp.where(earlier < later, 1.0, 0.0).astype(BF16)
    ranks = dot_nn(jnp.where(flags, 1.0, 0.0).astype(BF16), before)
    slots = jnp.where(flags, ranks, -1.0)
    groups = meta_ref.shape[0]
    count = experts // groups
    meta_ref[...] = jnp.zeros(meta_ref.shape, F32)
    for e in range(experts):
        meta_ref[e // count, e % count : e % count + 1, :] = slots[e : e + 1]
        meta_ref[e // count, 8 + e % count : 9 + e % count, :] = gates[e : e + 1]


def middle(mixed, out_full, x, gain_row, router_rows, routes_rows, groups):
    tokens, width = x.shape
    experts = router_rows.shape[0]
    return pl.pallas_call(
        middle_kernel,
        out_shape=[
            jax.ShapeDtypeStruct((tokens, width), F32),
            jax.ShapeDtypeStruct((tokens, width), BF16),
            jax.ShapeDtypeStruct((experts, tokens), F32),
            jax.ShapeDtypeStruct((groups, 16, tokens), F32),
        ],
        compiler_params=pltpu.CompilerParams(vmem_limit_bytes=48 << 20),
        cost_estimate=pl.CostEstimate(flops=3 * 10**9, bytes_accessed=16 << 20, transcendentals=1 << 14),
        name="middle",
    )(mixed, out_full, x, gain_row, router_rows, routes_rows)


def flipped(index, mask):
    out, bit = index, 1
    while bit <= mask:
        if mask & bit:
            out = out + bit - 2 * bit * ((index // bit) % 2)
        bit *= 2
    return out


def send(source, target, send_sem, recv_sem, device):
    return pltpu.make_async_remote_copy(
        src_ref=source, dst_ref=target, send_sem=send_sem, recv_sem=recv_sem,
        device_id=device, device_id_type=pl.DeviceIdType.MESH,
    )


def greet(devices):
    barrier = pltpu.get_barrier_semaphore()
    for device in devices:
        pl.semaphore_signal(barrier, inc=1, device_id=device, device_id_type=pl.DeviceIdType.MESH)
    pl.semaphore_wait(barrier, len(devices))


class Gather:
    def __init__(self, parts, levels, blocks, sems):
        self.parts, self.levels, self.blocks = parts, levels, blocks
        self.near_send, self.near_recv, self.team_send, self.team_recv, self.core_send, self.core_recv = sems
        self.group, self.shard = lax.axis_index("expert"), lax.axis_index("shard")
        level, self.core = self.shard // 2, self.shard % 2
        self.part = self.group % parts
        self.other = self.shard + 1 - 2 * self.core
        self.far = [flipped(level, k) * 2 + self.core for k in range(levels)]
        self.far_other = [flipped(level, k) * 2 + 1 - self.core for k in range(levels)]
        self.team_part = [flipped(self.part, k) for k in range(parts)]
        self.team = [self.group - self.part + t for t in self.team_part]
        self.mate = (self.group, self.other)
        self.sends = []

    def greet(self, near=True):
        greet(
            [self.mate]
            + [(self.group, self.far[k]) for k in range(1, self.levels) if near]
            + [(self.team[t], self.shard) for t in range(1, self.parts)]
        )

    def push(self, make):
        make().start()
        self.sends.append(make)

    def arrived(self, piece, send_sem, recv_sem):
        send(piece, piece, send_sem, recv_sem, self.mate).wait_recv()

    def near(self, own, i):
        for k in range(1, self.levels):
            self.push(
                lambda k=k: send(
                    own.at[self.part], self.blocks[i].at[self.shard * self.parts + self.part],
                    self.near_send.at[i, k], self.near_recv.at[i, k], (self.group, self.far[k]),
                )
            )

    def near_arrived(self, i, k):
        piece = self.blocks[i].at[self.far[k] * self.parts + self.part]
        self.arrived(piece, self.near_send.at[i, k], self.near_recv.at[i, k])

    def spread(self, i, k):
        def piece():
            return self.blocks[i].at[self.far[k] * self.parts + self.part]

        for t in range(1, self.parts):
            self.push(
                lambda t=t: send(
                    piece(), piece(), self.team_send.at[i, k, t], self.team_recv.at[i, k, t],
                    (self.team[t], self.shard),
                )
            )
        self.push(
            lambda: send(
                piece(), piece(), self.core_send.at[i, k, 0], self.core_recv.at[i, k, 0], self.mate
            )
        )

    def own_to_mate(self, own, i):
        self.push(
            lambda: send(
                own(), self.blocks[i].at[pl.ds(self.shard * self.parts, self.parts)],
                self.core_send.at[i, 0, 0], self.core_recv.at[i, 0, 0], self.mate,
            )
        )

    def team_to_mate(self, i):
        for k in range(1, self.levels):
            for t in range(1, self.parts):

                def piece(k=k, t=t):
                    return self.blocks[i].at[self.far[k] * self.parts + self.team_part[t]]

                self.arrived(piece(), self.team_send.at[i, k, t], self.team_recv.at[i, k, t])
                self.push(
                    lambda piece=piece, k=k, t=t: send(
                        piece(), piece(), self.core_send.at[i, k, t], self.core_recv.at[i, k, t],
                        self.mate,
                    )
                )

    def mate_arrived(self, i):
        piece = self.blocks[i].at[pl.ds(self.other * self.parts, self.parts)]
        self.arrived(piece, self.core_send.at[i, 0, 0], self.core_recv.at[i, 0, 0])
        for k in range(1, self.levels):
            for t in range(self.parts):
                piece = self.blocks[i].at[self.far_other[k] * self.parts + self.team_part[t]]
                self.arrived(piece, self.core_send.at[i, k, t], self.core_recv.at[i, k, t])

    def finish(self):
        for make in self.sends:
            make().wait_send()


def gather_sems(levels, parts, count):
    dma = pltpu.SemaphoreType.DMA
    return [dma((count, levels))] * 2 + [dma((count, levels, parts))] * 4


def gather_parts(groups, rows):
    return next(p for p in (4, 2, 1) if groups % p == 0 and rows % (16 * p) == 0)


class Rows:
    def __init__(self, groups, own, outs, sems):
        self.own, self.outs = own, outs
        self.send_sem, self.recv_sem = sems
        group, self.shard = lax.axis_index("expert"), lax.axis_index("shard")
        self.team = [flipped(group, t) for t in range(groups)]
        self.near = range(1, 1 + len(outs))

    def copy(self, t):
        return send(
            self.own, self.outs[t - 1], self.send_sem.at[t], self.recv_sem.at[t],
            (self.team[t], self.shard),
        )

    def start(self):
        for t in self.near:
            self.copy(t).start()

    def finish(self):
        for t in self.near:
            self.copy(t).wait()


def gather_kernel(groups, parts, levels, *refs):
    ins, own_rows, outs, refs = refs[:2], refs[2], refs[3:5], refs[5:]
    count = 2 if groups == 4 else groups - 1
    others, refs = refs[:count], refs[count:]
    bounce, local_sem = refs[:2], refs[2]
    plan = Gather(parts, levels, outs, refs[3:9])
    rows = Rows(groups, own_rows, others, refs[9:11])
    greet(
        [plan.mate]
        + [(plan.group, plan.far[k]) for k in range(1, levels)]
        + [(rows.team[t], rows.shard) for t in range(1, groups)]
    )
    own = pl.ds(plan.shard * parts, parts)
    loads = [pltpu.make_async_copy(ins[i], bounce[i], local_sem.at[0, i]) for i in range(2)]
    stores = [pltpu.make_async_copy(bounce[i], outs[i].at[own], local_sem.at[1, i]) for i in range(2)]
    for copy in loads:
        copy.start()
    for i in range(2):
        plan.near(ins[i], i)
    rows.start()
    plan.own_to_mate(lambda: ins[0], 0)
    for load, store in zip(loads, stores):
        load.wait()
        store.start()
    for k in range(1, levels):
        plan.near_arrived(0, k)
        plan.spread(0, k)
    plan.team_to_mate(0)
    for k in range(1, levels):
        plan.near_arrived(1, k)
    plan.mate_arrived(0)
    plan.finish()
    rows.finish()
    for copy in stores:
        copy.wait()


def gather_weights(blocks, own_rows, groups, shards):
    rows = blocks[0].shape[0]
    parts = gather_parts(groups, rows)
    levels, count = shards // 2, 2 if groups == 4 else groups - 1
    blocks = [b.reshape(parts, rows // parts, b.shape[1]) for b in blocks]
    dma = pltpu.SemaphoreType.DMA
    return pl.pallas_call(
        functools.partial(gather_kernel, groups, parts, levels),
        in_specs=[pl.BlockSpec(memory_space=pl.ANY)] * 3,
        out_specs=[pl.BlockSpec(memory_space=pl.ANY)] * (2 + count),
        out_shape=[
            jax.ShapeDtypeStruct((shards * parts,) + b.shape[1:], b.dtype) for b in blocks
        ]
        + [jax.ShapeDtypeStruct(own_rows.shape, own_rows.dtype)] * count,
        scratch_shapes=[pltpu.VMEM(b.shape, b.dtype) for b in blocks]
        + [dma((2, 2))]
        + gather_sems(levels, parts, 2)
        + [dma((groups,)), dma((groups,))],
        compiler_params=pltpu.CompilerParams(collective_id=0, has_side_effects=True),
        name="gather_weights",
    )(*blocks, own_rows)


class Reduce:
    def __init__(self, groups, levels, refs, sems):
        self.groups, self.levels, self.relay = groups, levels, groups == 4
        self.held, self.from_core, self.passing, self.from_group = refs
        self.core_send, self.core_recv, self.pass_send, self.pass_recv, self.group_send, self.group_recv = sems
        self.group, self.shard = lax.axis_index("expert"), lax.axis_index("shard")
        level, self.core = self.shard // 2, self.shard % 2
        self.mate = (self.group, self.shard + 1 - 2 * self.core)
        self.team = [flipped(self.group, t) for t in range(groups)]
        self.far = [flipped(level, k) for k in range(levels)]
        self.order = sorted(range(levels), key=lambda k: (k & -k or levels, k))
        self.near = [1, 2] if self.relay else list(range(1, groups))
        self.sends = []

    def greet(self, climbs):
        greet(
            [self.mate]
            + [(self.group, self.far[k] * 2 + self.core) for k in range(1, self.levels) if climbs]
            + [(self.team[t], self.shard) for t in range(1, self.groups)]
        )

    def push(self, make):
        make().start()
        self.sends.append(make)

    def arrived(self, piece, send_sem, recv_sem):
        send(piece, piece, send_sem, recv_sem, self.mate).wait_recv()

    def fill(self, sources):
        rows, chunk = self.held.shape[3:]
        for k in range(self.groups):
            low, high = k * chunk, (k + 1) * chunk
            for start, stop, left, right in sources:
                a, b = max(low, start), min(high, stop)
                if a >= b:
                    continue

                @pl.loop(0, 2 * self.levels)
                def _(s):
                    at = pl.ds(pl.multiple_of(s * rows, rows), rows)
                    if left is None:
                        value = right[at, a - start : b - start]
                    else:
                        value = dot_nn(left[at, :], right[:, a - start : b - start]).astype(BF16)
                    self.held[k, s % 2, s // 2, :, a - low : b - low] = value

            self.push(
                lambda k=k: send(
                    self.held.at[k, 1 - self.core], self.from_core.at[k],
                    self.core_send.at[k], self.core_recv.at[k], self.mate,
                )
            )

    def pass_copy(self, part, k):
        half = self.held.shape[3] // 2
        return send(
            self.held.at[self.team[3], self.core, self.far[k], pl.ds(part * half, half)],
            self.passing.at[part, k], self.pass_send.at[part, k], self.pass_recv.at[part, k],
            (self.team[1 + part], self.shard),
        )

    def group_copy(self, t, k):
        return send(
            self.held.at[self.team[t], self.core, self.far[k]], self.from_group.at[t, k],
            self.group_send.at[t, k], self.group_recv.at[t, k], (self.team[t], self.shard),
        )

    def merge(self):
        for k in range(self.groups):
            self.arrived(self.from_core.at[k], self.core_send.at[k], self.core_recv.at[k])

            @pl.loop(0, self.levels)
            def _(z):
                self.held[k, self.core, z] = (
                    self.held[k, self.core, z].astype(F32) + self.from_core[k, z].astype(F32)
                ).astype(BF16)

        for k in self.order:
            if self.relay:
                for part in range(2):
                    self.push(lambda part=part, k=k: self.pass_copy(part, k))
            else:
                for t in self.near:
                    self.push(lambda t=t, k=k: self.group_copy(t, k))

    def spread(self):
        if not self.relay:
            return
        half = self.held.shape[3] // 2
        for k in self.order:
            for part in range(2):
                self.arrived(
                    self.passing.at[part, k], self.pass_send.at[part, k], self.pass_recv.at[part, k]
                )
                at = pl.ds(part * half, half)
                piece = self.held.at[self.team[2 - part], self.core, self.far[k], at]
                piece[...] = (piece[...].astype(F32) + self.passing[part, k].astype(F32)).astype(BF16)
            for t in self.near:
                self.push(lambda t=t, k=k: self.group_copy(t, k))

    def collect(self, k):
        total = self.held[self.group, self.core, self.far[k]].astype(F32)
        for t in self.near:
            self.arrived(self.from_group.at[t, k], self.group_send.at[t, k], self.group_recv.at[t, k])
            total = total + self.from_group[t, k].astype(F32)
        return total

    def bits(self):
        return [bit for bit in (1, 2, 4, 8, 16) if bit < self.levels]

    def climb(self, summed, from_level, sems, bit, only=None):
        for k in range(self.levels) if only is None else [only]:
            if k & bit and not k & (bit - 1):
                self.push(
                    lambda k=k: send(
                        summed.at[k], from_level.at[k], sems[0].at[k], sems[1].at[k],
                        (self.group, self.far[bit] * 2 + self.core),
                    )
                )

    def climbed(self, summed, from_level, sems, bit):
        for k in range(self.levels):
            if k & bit and not k & (bit - 1):
                self.arrived(from_level.at[k], sems[0].at[k], sems[1].at[k])
                to = k - bit
                summed[to] = (summed[to].astype(F32) + from_level[k].astype(F32)).astype(BF16)

    def settle(self, summed, home, home_sems):
        home[self.group] = summed[0]
        for t in range(1, self.groups):
            self.push(
                lambda t=t: send(
                    home.at[self.group], home.at[self.group],
                    home_sems[0].at[t], home_sems[1].at[t], (self.team[t], self.shard),
                )
            )

    def landed(self, home, home_sems):
        for t in range(1, self.groups):
            self.arrived(home.at[self.team[t]], home_sems[0].at[t], home_sems[1].at[t])

    def finish(self):
        for make in self.sends:
            make().wait_send()


def chunk_of(total, groups):
    return 128 * (-(-total // (128 * groups)))


def reduce_buffers(groups, levels, rows, chunk):
    piece = (rows, chunk)
    passing = (2, levels, rows // 2, chunk) if groups == 4 else (1, 1, 16, 128)
    return [
        pltpu.VMEM((groups, 2, levels) + piece, BF16),
        pltpu.VMEM((groups, levels) + piece, BF16),
        pltpu.VMEM(passing, BF16),
        pltpu.VMEM((groups, levels) + piece, BF16),
    ]


def reduce_sems(groups, levels):
    dma = pltpu.SemaphoreType.DMA
    return [dma((groups,))] * 2 + [dma((2, levels))] * 2 + [dma((groups, levels))] * 2


def reduce_kernel(groups, levels, *refs):
    normed_ref, dproj_ref, gain_one_ref, gain_two_ref, router_ref, out_sum_ref, out_ref, qkv_ref = refs[:8]
    refs = refs[8:]
    misc_rows, misc_ref, *refs = refs
    normed_t, summed, from_level, home, out_summed, out_level, out_home = refs[:7]
    plan = Reduce(groups, levels, refs[7:11], refs[11:17])
    level_sems, home_sems, out_level_sems, out_home_sems = (refs[i : i + 2] for i in range(17, 25, 2))
    first, *others = plan.bits()
    plan.greet(True)
    out_summed[...] = out_sum_ref[...]
    plan.climb(out_summed, out_level, out_level_sems, first)
    normed_t[...] = normed_ref[...].T
    experts = router_ref.shape[0]
    misc_rows[...] = jnp.zeros(misc_rows.shape, F32)
    misc_rows[0:1] = gain_one_ref[...]
    misc_rows[1:2] = gain_two_ref[...]
    misc_rows[8 : 8 + experts] = router_ref[...]
    misc_ref[...] = misc_rows[...].T.astype(BF16)
    qkv_cols = dproj_ref.shape[1]
    plan.fill(
        [(0, qkv_cols, normed_t, dproj_ref), (qkv_cols, qkv_cols + MISC, None, misc_ref)]
    )
    plan.merge()
    plan.climbed(out_summed, out_level, out_level_sems, first)
    for bit in others:
        plan.climb(out_summed, out_level, out_level_sems, bit)
        plan.climbed(out_summed, out_level, out_level_sems, bit)
    plan.settle(out_summed, out_home, out_home_sems)
    plan.spread()
    for k in plan.order:
        summed[k] = plan.collect(k).astype(BF16)
        plan.climb(summed, from_level, level_sems, first, k)
    plan.climbed(summed, from_level, level_sems, first)
    for bit in others:
        plan.climb(summed, from_level, level_sems, bit)
        plan.climbed(summed, from_level, level_sems, bit)
    plan.settle(summed, home, home_sems)
    plan.landed(out_home, out_home_sems)
    out_ref[...] = out_home[...]
    plan.landed(home, home_sems)
    qkv_ref[...] = home[...]
    plan.finish()


def reduce_weights(normed, dproj, gain_one, gain_two, router, out_sum, groups, shards):
    tokens, width = normed.shape
    levels, rows = shards // 2, width // shards
    total = dproj.shape[1] + MISC
    chunk, out_chunk = chunk_of(total, groups), out_sum.shape[2]
    dma = pltpu.SemaphoreType.DMA
    vmem = pl.BlockSpec(memory_space=pltpu.VMEM)
    whole, out_whole = (groups, rows, chunk), (groups, rows, out_chunk)
    return pl.pallas_call(
        functools.partial(reduce_kernel, groups, levels),
        in_specs=[vmem] * 6,
        out_specs=[vmem] * 2,
        out_shape=[jax.ShapeDtypeStruct(s, BF16) for s in (out_whole, whole)],
        scratch_shapes=[
            pltpu.VMEM((MISC, width), F32),
            pltpu.VMEM((width, MISC), BF16),
            pltpu.VMEM((width, tokens), BF16),
            pltpu.VMEM((levels, rows, chunk), BF16),
            pltpu.VMEM((levels, rows, chunk), BF16),
            pltpu.VMEM(whole, BF16),
            pltpu.VMEM((levels, rows, out_chunk), BF16),
            pltpu.VMEM((levels, rows, out_chunk), BF16),
            pltpu.VMEM(out_whole, BF16),
        ]
        + reduce_buffers(groups, levels, rows, chunk)
        + reduce_sems(groups, levels)
        + [dma((levels,))] * 2 + [dma((groups,))] * 2 + [dma((levels,))] * 2 + [dma((groups,))] * 2,
        compiler_params=pltpu.CompilerParams(
            collective_id=1, has_side_effects=True, vmem_limit_bytes=62 << 20
        ),
        cost_estimate=pl.CostEstimate(
            flops=2 * tokens * width * total, bytes_accessed=8 << 20, transcendentals=0
        ),
        name="reduce_weights",
    )(normed, dproj, gain_one, gain_two, router, out_sum)


def expert_kernel(capacity, shards, groups, count, base, stage, *refs):
    refs = list(refs)
    take = lambda n: [refs.pop(0) for _ in range(n)]
    if stage == "first":
        x_own, meta_own = take(2)
        u_ins = take(3 if groups == 4 else groups)
    else:
        x_ref, u_ref, meta_ref, out_in, dx_in, gg_in = take(6)
    packed_ref = take(1)[0]
    if stage == "last":
        take(1)
    if stage == "first":
        x_all, u_all, meta_all, out_ref, dx_ref, gg_ref, dw_out = take(7)
    elif stage == "last":
        out_homes = take(3 if groups == 4 else groups)
        dx_home, gg_home, dw_out = take(3)
    else:
        out_ref, dx_ref, gg_ref, dw_out = take(4)
    xs, us, bs, inn, dw, dw_sem, we_all, wp_all, we_sem, wp_sem = take(10)
    if stage == "first":
        x_buf, u_buf, meta_buf = take(3)
        x_send, x_recv, meta_send, meta_recv, load_sem, u_sem, meta_sem, keep_sem, pass_sem = take(9)
    elif stage == "last":
        buf, passing, gg_buf = take(3)
        load_sem, pass_send, pass_recv, dx_send, dx_recv, gg_send, gg_recv, keep_sem = take(8)
    turn_at, expert = pl.program_id(0), pl.program_id(1)
    last_turn, last = groups - 1, count - 1
    group, shard = lax.axis_index("expert"), lax.axis_index("shard")
    team = [flipped(group, t) for t in range(groups)]
    width = xs.shape[2]
    tokens = x_buf.shape[0] if stage == "first" else x_ref.shape[1]
    tall, short = width // shards, FF // shards
    side = width - 2 * FF
    we_ref, wp_ref = we_all.at[expert], wp_all.at[expert]

    @pl.when((turn_at == 0) & (expert == 0))
    def _():
        for e in range(count):

            @pl.loop(0, shards)
            def _(s):
                a = pl.ds(pl.multiple_of(s * tall, 16), tall)
                b = pl.ds(pl.multiple_of(s * short, 16), short)
                low = pl.ds(pl.multiple_of(s * short, 16), short // 2)
                high = pl.ds(pl.multiple_of(s * short + short // 2, 16), short // 2)
                source = packed_ref.at[s, e]
                rest = pl.ds(tall + short, short // 2)
                for piece, target, sem in (
                    (source.at[:tall], we_all.at[e, a], we_sem),
                    (source.at[tall : tall + short], wp_all.at[e, b, : 2 * FF], wp_sem),
                    (source.at[rest, :side], wp_all.at[e, low, 2 * FF :], wp_sem),
                    (source.at[rest, side:], wp_all.at[e, high, 2 * FF :], wp_sem),
                ):
                    pltpu.make_async_copy(piece, target, sem.at[e]).start()

    if stage == "first":

        relay = groups == 4
        near = [1, 2] if relay else list(range(1, groups))
        half = tokens // 2

        def x_copy(t):
            return send(x_own, x_all.at[t], x_send.at[t], x_recv.at[t], (team[t], shard))

        def passed(source, target, part, sems):
            at = pl.ds(part * half, half)
            return send(
                source.at[at], target.at[3, at], sems.at[0, part], sems.at[1, part],
                (team[2 - part], shard),
            )

        def x_pass(part):
            return passed(x_all.at[1 + part], x_all, part, pass_sem.at[0])

        def u_pass(part):
            return passed(u_ins[1 + part], u_all, part, pass_sem.at[1])

        def meta_copy(t):
            return send(
                meta_own.at[team[t]], meta_all.at[t], meta_send.at[t], meta_recv.at[t], (team[t], shard)
            )

        def u_load(t):
            source = u_all.at[t] if relay and t == 3 else u_ins[t]
            return pltpu.make_async_copy(source, u_buf.at[t % 2], u_sem.at[t % 2])

        def x_keep():
            return pltpu.make_async_copy(x_buf, x_all.at[0], keep_sem.at[0])

        def meta_keep():
            return pltpu.make_async_copy(meta_buf, meta_all.at[0], keep_sem.at[1])

        def u_keep(t):
            return pltpu.make_async_copy(u_buf.at[t % 2], u_all.at[t], keep_sem.at[2 + t])

        for t in range(groups):

            @pl.when((turn_at == t) & (expert == 0))
            def _():
                if t == 0:
                    u_load(0).start()
                    greet([(team[k], shard) for k in range(1, groups)])
                    for k in range(1, groups):
                        meta_copy(k).start()
                    for k in near:
                        x_copy(k).start()
                    fetch_x, fetch_meta = x_own, meta_own.at[group]
                else:
                    if not relay:
                        x_copy(t).wait_recv()
                    elif t == 1:
                        for k in near:
                            x_copy(k).wait_recv()
                        for part in range(2):
                            x_pass(part).start()
                        for part in range(2):
                            u_pass(part).start()
                    elif t == 3:
                        for part in range(2):
                            x_pass(part).wait_recv()
                            u_pass(part).wait_recv()
                        u_load(3).start()
                    meta_copy(t).wait_recv()
                    u_keep(t - 1).wait()
                    if t == 1:
                        x_keep().wait()
                        meta_keep().wait()
                    fetch_x, fetch_meta = x_all.at[t], meta_all.at[t]
                load = pltpu.make_async_copy(fetch_x, x_buf, load_sem)
                load_meta = pltpu.make_async_copy(fetch_meta, meta_buf, meta_sem)
                load.start()
                load_meta.start()
                if t + 1 < groups and not (relay and t == 2):
                    u_load(t + 1).start()
                u_load(t).wait()
                load_meta.wait()
                load.wait()
                if not (relay and t == 3):
                    u_keep(t).start()
                if t == 0:
                    x_keep().start()
                    meta_keep().start()

        x_now, u_now, meta_now = x_buf, u_buf.at[turn_at % 2], meta_buf
    else:
        x_now, u_now, meta_now = x_ref.at[0], u_ref.at[0], meta_ref.at[0]

    if stage == "last":
        relay = groups == 4
        slots, half = buf.shape[1], tokens // 2
        halves = [pl.ds(0, half), pl.ds(half, half)]

        def kept(kind, i):
            return buf.at[kind, i % slots]

        def load(kind, i):
            source = dx_in if kind else out_in
            return pltpu.make_async_copy(
                source.at[last_turn - i], kept(kind, i), load_sem.at[kind, i % 2]
            )

        def store(i):
            return pltpu.make_async_copy(kept(0, i), out_homes[last_turn - i], keep_sem.at[2 + i])

        def pass_copy(kind, part):
            return send(
                kept(kind, 0).at[halves[part]], passing.at[kind, part],
                pass_send.at[kind, part], pass_recv.at[kind, part], (team[1 + part], shard),
            )

        def dx_copy(i):
            t = last_turn - i
            return send(kept(1, i), dx_home.at[t], dx_send.at[t], dx_recv.at[t], (team[t], shard))

        def dx_half(part):
            at = halves[part]
            return send(
                kept(1, 1).at[at], dx_home.at[2, at], dx_send.at[2 + part], dx_recv.at[2 + part],
                (team[2], shard),
            )

        def gg_copy(i):
            t = last_turn - i
            return send(gg_buf.at[i], gg_home.at[group], gg_send.at[t], gg_recv.at[t], (team[t], shard))

        def own_copies():
            return [
                pltpu.make_async_copy(kept(1, last_turn), dx_home.at[0], keep_sem.at[0]),
                pltpu.make_async_copy(gg_buf.at[last_turn], gg_home.at[group], keep_sem.at[1]),
            ]

        for i in range(groups):

            @pl.when((turn_at == i) & (expert == 0))
            def _():
                if i == 0:
                    for kind in range(2):
                        load(kind, 0).start()
                    greet([(team[k], shard) for k in range(1, groups)])
                if i + 1 < groups:
                    if i + 1 >= slots:
                        dx_copy(i + 1 - slots).wait_send()
                        store(i + 1 - slots).wait()
                    for kind in range(2):
                        load(kind, i + 1).start()
                for kind in range(2):
                    load(kind, i).wait()

        at_now = turn_at % slots
        out_now, dx_now, gg_now = buf.at[0, at_now], buf.at[1, at_now], gg_buf.at[turn_at]
    else:
        out_now, dx_now, gg_now = out_ref.at[0], dx_ref.at[0], gg_ref.at[0]

    @pl.when(expert == 0)
    def _():
        if stage == "first":
            out_now[...] = jnp.zeros((tokens, width), BF16)
            dx_now[...] = jnp.zeros((tokens, width), BF16)
            gg_now[...] = jnp.zeros((8, tokens), F32)
        else:
            gg_now[...] = gg_in[0]
        if stage == "between":
            out_now[...] = out_in[0]
            dx_now[...] = dx_in[0]

    @pl.when(turn_at == 0)
    def _():
        pltpu.make_async_copy(we_ref, we_ref, we_sem.at[expert]).wait()
        pltpu.make_async_copy(wp_ref, wp_ref, wp_sem.at[expert]).wait()

    slot_row = meta_now[pl.ds(base + expert, 1), :]
    gate_row = meta_now[pl.ds(8 + base + expert, 1), :]
    index = lax.broadcasted_iota(jnp.int32, (capacity, tokens), 0).astype(F32)
    pick = jnp.where(index == slot_row, 1.0, 0.0)
    gate_col = jnp.sum(pick * gate_row, axis=1, keepdims=True)
    place = pick.astype(BF16)
    rows = pl.ds(pl.multiple_of(turn_at * capacity, capacity), capacity)
    step = 512
    for c in range(0, width, step):
        xs[expert, rows, c : c + step] = dot_nn(place, x_now[:, c : c + step]).astype(BF16)
        us[expert, rows, c : c + step] = dot_nn(place, u_now[:, c : c + step]).astype(BF16)
    x = xs[expert, rows, :]
    gate = dot_nn(x, we_ref[:, :FF])
    up = dot_nn(x, we_ref[:, FF:])
    back = dot_nt(us[expert, rows, :], wp_ref[...])
    sig = 1.0 / (1.0 + jnp.exp(-gate))
    act = gate * sig
    inner = act * up
    inner_low = inner.astype(BF16)
    gate_grad = jnp.sum(inner * back, axis=1, keepdims=True)
    here = lax.broadcasted_iota(jnp.int32, (8, tokens), 0) == base + expert
    gg_now[...] = jnp.where(here, jnp.sum(pick * gate_grad, axis=0, keepdims=True), gg_now[...])
    inn[expert, rows, :] = (inner * gate_col).astype(BF16)
    inner_grads = back * gate_col
    bs[expert, rows, :FF] = (inner_grads * up * sig * (1.0 + gate * (1.0 - sig))).astype(BF16)
    bs[expert, rows, FF:] = (inner_grads * act).astype(BF16)
    both = bs[expert, rows, :]
    weighted_t = (pick * gate_row).astype(BF16).T
    place_t = place.T
    for c in range(0, width, step):
        result = dot_nn(inner_low, wp_ref[:, c : c + step]).astype(BF16)
        out_now[:, c : c + step] = (
            out_now[:, c : c + step].astype(F32) + dot_nn(weighted_t, result)
        ).astype(BF16)
        row_grads = dot_nt(both, we_ref[c : c + step, :]).astype(BF16)
        dx_now[:, c : c + step] = (
            dx_now[:, c : c + step].astype(F32) + dot_nn(place_t, row_grads)
        ).astype(BF16)

    if stage == "last":

        def add_passed(kind):
            for part in range(2):
                pass_copy(kind, part).wait_recv()
                target = kept(kind, 1 + part).at[halves[part]]
                target[...] = (target[...].astype(F32) + passing[kind, part].astype(F32)).astype(BF16)

        for i in range(groups):

            @pl.when((turn_at == i) & (expert == last))
            def _():
                if i < last_turn:
                    gg_copy(i).start()
                else:
                    for copy in own_copies():
                        copy.start()
                if not relay:
                    store(i).start()
                    if i < last_turn:
                        dx_copy(i).start()
                elif i == 0:
                    for kind in (1, 0):
                        for part in range(2):
                            pass_copy(kind, part).start()
                elif i == 1:
                    dx_half(1).start()
                elif i == 2:
                    add_passed(1)
                    dx_copy(2).start()
                    dx_half(0).start()
                else:
                    add_passed(0)
                    for k in range(1, groups):
                        store(k).start()

    def store_weights(e):
        return pltpu.make_async_copy(dw, dw_out.at[:, (1 if stage == "last" else 0) + e], dw_sem)

    @pl.when(turn_at == last_turn)
    def _():
        if count > 1:

            @pl.when(expert > 0)
            def _():
                store_weights(0).wait()

        wide, half = 384, FF // 2

        @pl.loop(0, width // wide)
        def _(c):
            at = pl.ds(pl.multiple_of(c * wide, wide), wide)
            value = dot_tn(xs[expert, :, at], bs[expert]).astype(BF16)
            for i in range(wide // tall):
                dw[c * (wide // tall) + i, :tall, :] = value[i * tall : (i + 1) * tall]

        @pl.loop(0, FF // half)
        def _(c):
            at = pl.ds(pl.multiple_of(c * half, half), half)
            value = dot_tn(inn[expert, :, at], us[expert]).astype(BF16)
            for i in range(half // short):
                s, low = c * (half // short) + i, i * short
                mid, high = low + short // 2, low + short
                dw[s, tall : tall + short, :] = value[low:high, : 2 * FF]
                dw[s, tall + short :, :side] = value[low:mid, 2 * FF :]
                dw[s, tall + short :, side:] = value[mid:high, 2 * FF :]

        store_weights(expert).start()

    @pl.when((turn_at == last_turn) & (expert == last))
    def _():
        store_weights(0).wait()
        if stage == "first":
            if not relay:
                u_keep(last_turn).wait()
            for t in range(1, groups):
                meta_copy(t).wait_send()
            for t in near:
                x_copy(t).wait_send()
            if relay:
                for part in range(2):
                    x_pass(part).wait_send()
                    u_pass(part).wait_send()
        if stage == "last":
            for i in range(groups - 1):
                t = last_turn - i
                gg_copy(i).wait_send()
                send(
                    gg_buf.at[i], gg_home.at[team[t]], gg_send.at[t], gg_recv.at[t], (team[t], shard)
                ).wait_recv()
            if relay:
                for part in range(2):
                    dx_half(part).wait()
                    for kind in range(2):
                        pass_copy(kind, part).wait_send()
                dx_copy(2).wait()
                for k in range(1, groups):
                    store(k).wait()
            else:
                for i in range(groups - 1):
                    if i + slots >= groups:
                        dx_copy(i).wait_send()
                    dx_copy(i).wait_recv()
                for i in range(groups - slots, groups):
                    store(i).wait()
            for copy in own_copies():
                copy.wait()


def expert_call(capacity, shards, groups, base, stage, data, packed_weights, total_count, *kept):
    count = packed_weights.shape[1]
    tokens, width = data[0].shape[-2:]
    total = groups * capacity
    anywhere = pl.BlockSpec(memory_space=pl.ANY)
    turned = (lambda i: i) if stage == "first" else (lambda i: groups - 1 - i)
    block = pl.BlockSpec((1, tokens, width), lambda i, e: (turned(i), 0, 0))
    small = pl.BlockSpec((1, 8, tokens), lambda i, e: (turned(i), 0, 0))
    dma = pltpu.SemaphoreType.DMA
    many = jax.ShapeDtypeStruct((groups, tokens, width), BF16)
    grads = jax.ShapeDtypeStruct((groups, 8, tokens), F32)
    packed = (shards, (width + FF + FF // 2) // shards, 2 * FF)
    weights = jax.ShapeDtypeStruct((shards, total_count) + packed[1:], BF16)
    meta = jax.ShapeDtypeStruct((groups, 16, tokens), F32)
    scratch = [
        pltpu.VMEM((count, total, width), BF16),
        pltpu.VMEM((count, total, width), BF16),
        pltpu.VMEM((count, total, 2 * FF), BF16),
        pltpu.VMEM((count, total, FF), BF16),
        pltpu.VMEM(packed, BF16),
        dma,
        pltpu.VMEM((count, width, 2 * FF), BF16),
        pltpu.VMEM((count, FF, width), BF16),
        dma((count,)), dma((count,)),
    ]
    if stage == "first":
        in_specs = [anywhere] * len(data)
        out_specs = [anywhere] * 3 + [block, block, small, anywhere]
        out_shape = [many, many, meta, many, many, grads, weights]
        scratch += [
            pltpu.VMEM((tokens, width), BF16),
            pltpu.VMEM((2, tokens, width), BF16),
            pltpu.VMEM((16, tokens), F32),
            dma((groups,)), dma((groups,)), dma((groups,)), dma((groups,)),
            dma, dma((2,)), dma, dma((2 + groups,)), dma((2, 2, 2)),
        ]
    else:
        meta_block = pl.BlockSpec((1, 16, tokens), lambda i, e: (turned(i), 0, 0))
        in_specs = [block, block, meta_block, block, block, small]
        out_specs = [block, block, small, anywhere]
        if stage == "last":
            in_specs[3:5] = [anywhere] * 2
            sources = 3 if groups == 4 else groups
            out_specs = [anywhere] * (3 + sources)
            slots = groups if groups == 4 else 3
            passed = 2 if groups == 4 else 1
            scratch += [
                pltpu.VMEM((2, slots, tokens, width), BF16),
                pltpu.VMEM((passed, passed, tokens // 2, width), BF16),
                pltpu.VMEM((groups, 8, tokens), F32),
                dma((2, 2)), dma((2, 2)), dma((2, 2)),
                dma((groups,)), dma((groups,)), dma((groups,)), dma((groups,)), dma((2 + groups,)),
            ]
        out_shape = [many, many, grads, weights]
        if stage == "last":
            out_shape[:1] = [jax.ShapeDtypeStruct((tokens, width), BF16)] * sources
    remote = {"first": 2, "last": 3}
    return pl.pallas_call(
        functools.partial(expert_kernel, capacity, shards, groups, count, base, stage),
        grid=(groups, count),
        in_specs=in_specs + [anywhere] * (1 + len(kept)),
        out_specs=out_specs,
        out_shape=out_shape,
        scratch_shapes=scratch,
        compiler_params=pltpu.CompilerParams(
            vmem_limit_bytes=62 << 20,
            **({"collective_id": remote[stage], "has_side_effects": True} if stage in remote else {}),
        ),
        cost_estimate=pl.CostEstimate(
            flops=2 * count * total * width * (4 * tokens + 9 * FF),
            bytes_accessed=6 * groups * tokens * width * 2,
            transcendentals=count * total * FF,
        ),
        name="experts_" + stage,
        input_output_aliases={len(data) + 1: len(out_shape) - 1} if kept else {},
    )(*data, packed_weights, *kept)


def norm_back(values, gain_row, grad_rows):
    scale_rows = lax.rsqrt(jnp.mean(values * values, axis=-1, keepdims=True) + EPSILON)
    weighted = gain_row * grad_rows
    inner_mean = jnp.mean(weighted * values, axis=-1, keepdims=True)
    input_part = (
        scale_rows * weighted - values * (scale_rows * scale_rows * scale_rows) * inner_mean
    )
    gain_part = jnp.sum(grad_rows * values * scale_rows, axis=0)
    return (input_part, gain_part)


def pack_kernel(
    cuts, expand_ref, project_ref, qkv_ref, gain_one_ref, gain_two_ref, router_ref, packed_ref, *refs
):
    *outs, misc = refs
    short = project_ref.shape[1]
    tall = expand_ref.shape[1]
    side = project_ref.shape[2] - 2 * FF
    for (low, high), out in zip(cuts, outs):
        for e in range(low, high):
            out[e - low, :tall] = expand_ref[e]
            out[e - low, tall : tall + short] = project_ref[e, :, : 2 * FF]
            out[e - low, tall + short :, :side] = project_ref[e, : short // 2, 2 * FF :]
            out[e - low, tall + short :, side:] = project_ref[e, short // 2 :, 2 * FF :]
    for j in range(PAIRS):
        at, to = HEADS * HEAD + j * KW, j * BLOCK + QW
        packed_ref[:, j * BLOCK : to] = qkv_ref[:, j * QW : (j + 1) * QW]
        packed_ref[:, to : to + KW] = qkv_ref[:, at : at + KW]
        at += KV_HEADS * HEAD
        packed_ref[:, to + KW : to + 2 * KW] = qkv_ref[:, at : at + KW]
    misc[...] = jnp.zeros(misc.shape, F32)
    misc[0:1] = gain_one_ref[...].astype(F32)
    misc[1:2] = gain_two_ref[...].astype(F32)
    misc[8 : 8 + router_ref.shape[0]] = router_ref[...].astype(F32)
    packed_ref[:, PAIRS * BLOCK :] = misc[...].T.astype(BF16)


def pack_weights(expand, project, qkv, gain_one, gain_two, router):
    cuts = bands(expand.shape[0])
    rows = expand.shape[1] + project.shape[1] + project.shape[1] // 2
    return pl.pallas_call(
        functools.partial(pack_kernel, cuts),
        out_shape=[jax.ShapeDtypeStruct((qkv.shape[0], PAIRS * BLOCK + MISC), BF16)]
        + [jax.ShapeDtypeStruct((high - low, rows, 2 * FF), BF16) for low, high in cuts],
        scratch_shapes=[pltpu.VMEM((MISC, qkv.shape[0]), F32)],
        compiler_params=pltpu.CompilerParams(vmem_limit_bytes=62 << 20),
        name="pack_weights",
    )(expand, project, qkv, gain_one[None], gain_two[None], router.T)


def hidden_back_kernel(
    dx_ref, gg_ref, gates_ref, router_ref, hidden_ref, gain_ref, up_ref, ffn_ref,
    grads_ref, low_ref, router_grad_ref, gain_grad_ref,
):
    gates, groups = gates_ref[...], gg_ref.shape[0]
    count = gates.shape[0] // groups
    gate_grads = jnp.concatenate([gg_ref[g, :count] for g in range(groups)], axis=0)
    mean = jnp.sum(gates * gate_grads, axis=0, keepdims=True)
    logit_grads = (gates * (gate_grads - mean)).astype(BF16)
    ffn_grads = dot_tn(logit_grads, router_ref[...])
    for g in range(dx_ref.shape[0]):
        ffn_grads = ffn_grads + dx_ref[g].astype(F32)
    hidden = hidden_ref[...]
    part, gain_part = norm_back(hidden, gain_ref[...].astype(F32), ffn_grads)
    hidden_grads = up_ref[...].astype(F32) + part
    grads_ref[...] = hidden_grads
    low_ref[...] = hidden_grads.astype(BF16)
    router_part = dot_nn(logit_grads, ffn_ref[...])

    @pl.when(pl.program_id(0) == 0)
    def _():
        router_grad_ref[...] = router_part
        gain_grad_ref[...] = gain_part[None]

    @pl.when(pl.program_id(0) > 0)
    def _():
        router_grad_ref[...] += router_part
        gain_grad_ref[...] += gain_part[None]


def hidden_back(sources, dx_home, gg_home, gates, router_rows, hidden, gain_row, out_grad, ffn_in):
    groups, tokens, width = dx_home.shape
    experts = gates.shape[0]
    step = 128
    rows = pl.BlockSpec((step, width), lambda i: (i, 0))
    return pl.pallas_call(
        hidden_back_kernel,
        grid=(tokens // step,),
        in_specs=[
            pl.BlockSpec((sources, step, width), lambda i: (0, i, 0)),
            pl.BlockSpec((groups, 8, step), lambda i: (0, 0, i)),
            pl.BlockSpec((experts, step), lambda i: (0, i)),
            whole_spec((experts, width)),
            rows,
            whole_spec((1, width)),
            rows,
            rows,
        ],
        out_specs=[rows, rows, whole_spec((experts, width)), whole_spec((1, width))],
        out_shape=[
            jax.ShapeDtypeStruct((tokens, width), F32),
            jax.ShapeDtypeStruct((tokens, width), BF16),
            jax.ShapeDtypeStruct((experts, width), F32),
            jax.ShapeDtypeStruct((1, width), F32),
        ],
        compiler_params=pltpu.CompilerParams(vmem_limit_bytes=62 << 20),
        cost_estimate=pl.CostEstimate(flops=10**8, bytes_accessed=20 << 20, transcendentals=0),
        name="hidden_back",
    )(dx_home, gg_home, gates, router_rows, hidden, gain_row, out_grad, ffn_in)


def input_back_kernel(
    dproj_ref, w_ref, x_ref, gain_ref, hidden_grads_ref, grad_ref, gain_grad_ref, held, inner, scale
):
    c, step = pl.program_id(0), w_ref.shape[0]
    width = x_ref.shape[1]
    at = pl.ds(pl.multiple_of(c * step, step), step)

    @pl.when(c == 0)
    def _():
        x = x_ref[...].astype(F32)
        scale[...] = lax.rsqrt(jnp.mean(x * x, axis=-1, keepdims=True) + EPSILON)
        inner[...] = jnp.zeros(inner.shape, F32)

    normed_grads = dot_nt(dproj_ref[...], w_ref[...])
    x = x_ref[:, at].astype(F32)
    weighted = normed_grads * gain_ref[:, at].astype(F32)
    product = weighted * x
    inner[...] += jnp.sum(product, axis=-1, keepdims=True)
    gain_grad_ref[:, at] = jnp.sum(normed_grads * x * scale[...], axis=0, keepdims=True)
    held[:, at] = weighted

    @pl.when(c == pl.num_programs(0) - 1)
    def _():
        r = scale[...]
        factor = r * r * r * (inner[...] * (1.0 / width))
        for low in range(0, width, step):
            cols = slice(low, low + step)
            grad_ref[:, cols] = (
                hidden_grads_ref[:, cols] + r * held[:, cols] - x_ref[:, cols].astype(F32) * factor
            )


def input_back(dproj, w_full, x, gain_row, hidden_grads):
    tokens, width = x.shape
    step = 256
    return pl.pallas_call(
        input_back_kernel,
        grid=(width // step,),
        in_specs=[
            whole_spec((tokens, dproj.shape[1])),
            pl.BlockSpec((step, dproj.shape[1]), lambda i: (i, 0)),
            whole_spec((tokens, width)),
            whole_spec((1, width)),
            whole_spec((tokens, width)),
        ],
        out_specs=[whole_spec((tokens, width)), whole_spec((1, width))],
        out_shape=[
            jax.ShapeDtypeStruct((tokens, width), F32),
            jax.ShapeDtypeStruct((1, width), F32),
        ],
        scratch_shapes=[
            pltpu.VMEM((tokens, width), F32), pltpu.VMEM((tokens, 1), F32), pltpu.VMEM((tokens, 1), F32),
        ],
        compiler_params=pltpu.CompilerParams(vmem_limit_bytes=62 << 20),
        cost_estimate=pl.CostEstimate(
            flops=2 * tokens * width * dproj.shape[1], bytes_accessed=20 << 20, transcendentals=0
        ),
        name="input_back",
    )(dproj, w_full, x, gain_row, hidden_grads)


def fetched(sources, held, sems):
    for i, source in enumerate(sources):
        pltpu.make_async_copy(source, held[i], sems.at[i]).start()
    for i, source in enumerate(sources):
        pltpu.make_async_copy(source, held[i], sems.at[i]).wait()


def unpack_experts(tall, short, held, expand_ref, project_ref):
    side = project_ref.shape[2] - 2 * FF
    for i in range(held.shape[0]):
        value = held[i].astype(F32)
        expand_ref[i] = value[:tall]
        project_ref[i, :, : 2 * FF] = value[tall : tall + short]
        project_ref[i, : short // 2, 2 * FF :] = value[tall + short :, :side]
        project_ref[i, short // 2 :, 2 * FF :] = value[tall + short :, side:]


def unpack_first_kernel(tall, short, count, *refs):
    sources, refs = refs[:count], refs[count:]
    output_ref, expand_ref, project_ref, out_grad_ref, qkv_grad_ref, misc_ref, *held, sems = refs
    fetched(sources, held, sems)
    share_ref, out_ref, qkv_ref, hidden_ref, *others = held
    total = hidden_ref[...]
    for other in others:
        total = total + other[...].astype(F32)
    output_ref[...] = total.astype(BF16)
    unpack_experts(tall, short, share_ref, expand_ref, project_ref)
    tile = 128
    chunk = out_ref.shape[2]
    for at in range(0, out_grad_ref.shape[1], tile):
        out_grad_ref[:, at : at + tile] = out_ref[
            at // chunk, :, at % chunk : at % chunk + tile
        ].astype(F32)
    chunk, qkv_cols = qkv_ref.shape[2], qkv_grad_ref.shape[1]
    for at in range(0, qkv_cols + MISC, tile):
        value = qkv_ref[at // chunk, :, at % chunk : at % chunk + tile].astype(F32)
        if at < qkv_cols:
            j, inside = divmod(at, BLOCK)
            if inside < QW:
                to = j * QW + inside
            elif inside < QW + KW:
                to = PAIRS * QW + j * KW + inside - QW
            else:
                to = PAIRS * (QW + KW) + j * KW + inside - QW - KW
            qkv_grad_ref[:, to : to + tile] = value
        else:
            misc_ref[...] = value.T


def unpack_first(share, out_total, qkv_total, hidden, out_home, tall, short, total_count):
    width, rows = hidden.shape[1], out_total.shape[1]
    given = (share, out_total, qkv_total, hidden, *out_home)
    count = share.shape[0]
    anywhere = pl.BlockSpec(memory_space=pl.ANY)
    return pl.pallas_call(
        functools.partial(unpack_first_kernel, tall, short, len(given)),
        in_specs=[anywhere] * len(given),
        out_specs=[
            whole_spec(hidden.shape),
            whole_spec((count, tall, 2 * FF)),
            whole_spec((count, short, width)),
            whole_spec((rows, HEADS * HEAD)),
            whole_spec((rows, PAIRS * BLOCK)),
            whole_spec((MISC, rows)),
        ],
        grid=(1,),
        out_shape=[jax.ShapeDtypeStruct(hidden.shape, BF16)]
        + [
            jax.ShapeDtypeStruct(s, F32)
            for s in (
                (total_count, tall, 2 * FF), (total_count, short, width), (rows, HEADS * HEAD),
                (rows, PAIRS * BLOCK), (MISC, rows),
            )
        ],
        scratch_shapes=[pltpu.VMEM(s.shape, s.dtype) for s in given]
        + [pltpu.SemaphoreType.DMA((len(given),))],
        compiler_params=pltpu.CompilerParams(vmem_limit_bytes=62 << 20),
        name="unpack_first",
    )(*given)


def unpack_last_kernel(tall, short, share_ref, expand_in, project_in, expand_ref, project_ref):
    unpack_experts(tall, short, share_ref, expand_ref, project_ref)


def unpack_last(share, expand_grad, project_grad, tall, short):
    start = expand_grad.shape[0] - share.shape[0]
    anywhere = pl.BlockSpec(memory_space=pl.ANY)
    return pl.pallas_call(
        functools.partial(unpack_last_kernel, tall, short),
        grid=(share.shape[0],),
        in_specs=[
            pl.BlockSpec((1,) + share.shape[1:], lambda i: (i, 0, 0)), anywhere, anywhere,
        ],
        out_specs=[
            pl.BlockSpec((1,) + expand_grad.shape[1:], lambda i: (i + start, 0, 0)),
            pl.BlockSpec((1,) + project_grad.shape[1:], lambda i: (i + start, 0, 0)),
        ],
        out_shape=[
            jax.ShapeDtypeStruct(expand_grad.shape, F32), jax.ShapeDtypeStruct(project_grad.shape, F32),
        ],
        input_output_aliases={1: 0, 2: 1},
        compiler_params=pltpu.CompilerParams(vmem_limit_bytes=62 << 20),
        name="unpack_last",
    )(share, expand_grad, project_grad)


def exchanged(value, flip, groups):
    if flip == 0:
        return value
    return lax.ppermute(value, "expert", [(i, i ^ flip) for i in range(groups)])


def bands(count):
    return [(0, 2), (2, 3), (3, count)]


def local(
    inputs, attn_gain, qkv_weight, out_weight, ffn_gain, router_weight,
    expand_weight, project_weight, segment_ids, routes, out_grad,
):
    groups, shards = lax.axis_size("expert"), lax.axis_size("shard")
    tokens, width = inputs.shape
    experts = router_weight.shape[1]
    local_count = expand_weight.shape[0]
    capacity = 8 * ((5 * tokens * TOP + 32 * experts - 1) // (32 * experts))

    packed, *bands_packed = pack_weights(
        expand_weight, project_weight, qkv_weight, attn_gain, ffn_gain, router_weight
    )
    packed_full = [lax.all_gather(p, "shard", axis=0) for p in bands_packed]
    qkv_full, out_part, *u_others = gather_weights(
        [packed, out_weight], out_grad, groups, shards
    )
    qkv_full = qkv_full.reshape(width, -1)
    misc_rows = qkv_full[:, PAIRS * BLOCK :].T
    gain_one, gain_two = misc_rows[0:1], misc_rows[1:2]
    router_rows = misc_rows[8 : 8 + experts]
    tables = tuple(jnp.asarray(t) for t in rope_tables())
    seg_row = segment_ids.reshape(1, tokens)
    seg_col = segment_ids.reshape(tokens, 1)
    normed, proj, mixed, lse, out_full = attention_forward(
        inputs, gain_one, qkv_full, tables, seg_col, seg_row, out_part, groups, shards
    )
    hidden, ffn_in, gates, meta_own = middle(
        mixed, out_full, inputs, gain_two, router_rows, routes.T, groups
    )
    tall, short = expand_weight.shape[1], project_weight.shape[1]
    call = functools.partial(expert_call, capacity, shards, groups)

    def share_out(dw):
        return lax.psum_scatter(dw, "shard", scatter_dimension=0, tiled=True)[0]

    x_all, u_all, meta, out_acc, dx_acc, gg, dw = call(
        0, "first", (ffn_in, meta_own, out_grad, *u_others), packed_full[0], 2
    )
    shares = [share_out(dw)]
    out_acc, dx_acc, gg, dw = call(
        2, "between", (x_all, u_all, meta, out_acc, dx_acc, gg), packed_full[1], local_count - 2
    )
    *out_sent, dx_home, gg_home, dw = call(
        3, "last", (x_all, u_all, meta, out_acc, dx_acc, gg), packed_full[2], local_count - 2, dw
    )
    shares.append(share_out(dw))
    sources = 3 if groups == 4 else groups
    hidden_grads, attended_grads, router_part, gain_two_grad = hidden_back(
        sources, dx_home, gg_home, gates, router_rows, hidden, gain_two, out_grad, ffn_in
    )
    dproj, out_sum = attention_backward(
        attended_grads, out_full, proj, mixed, lse, tables, seg_col, seg_row, groups, shards
    )
    input_grad, gain_one_grad = input_back(dproj, qkv_full, inputs, gain_one, hidden_grads)

    dproj, shares[0], *out_sent = lax.optimization_barrier((dproj, shares[0], *out_sent))
    out_home = [exchanged(o, t, groups) for t, o in enumerate(out_sent)]
    out_total, qkv_total = reduce_weights(
        normed, dproj, gain_one_grad, gain_two_grad, router_part, out_sum, groups, shards
    )
    out_total, *out_home = lax.optimization_barrier((out_total, *out_home))
    output, expand_grad, project_grad, out_weight_grad, qkv_grad, misc_total = unpack_first(
        shares[0], out_total, qkv_total, hidden, out_home, tall, short, local_count
    )
    expand_grad, project_grad = unpack_last(shares[1], expand_grad, project_grad, tall, short)
    return (
        output,
        input_grad,
        misc_total[0],
        qkv_grad,
        out_weight_grad,
        misc_total[1],
        misc_total[8 : 8 + experts].T,
        expand_grad,
        project_grad,
    )


def solution(mesh):
    rows = P(("expert", "shard"), None)
    return jax.shard_map(
        local,
        mesh=mesh,
        in_specs=(
            rows, P("shard"), P("shard", None), P("shard", None), P("shard"), P("shard", None),
            P("expert", "shard", None), P("expert", "shard", None), rows, rows, rows,
        ),
        out_specs=(
            rows, rows, P("shard"), P("shard", None), P("shard", None), P("shard"),
            P("shard", None), P("expert", "shard", None), P("expert", "shard", None),
        ),
        check_vma=False,
    )
```

```python
import functools

import jax
import jax.numpy as jnp
import numpy as np
from jax import lax
from jax.experimental import pallas as pl
from jax.experimental.pallas import tpu as pltpu
from jax.sharding import PartitionSpec as P

HEADS = 24
KV_HEADS = 8
HEAD = 64
FF = 512
TOP = 8
SEQ_LEN = 512
GROUP = HEADS // KV_HEADS
PAIRS = KV_HEADS // 2
QW = 2 * GROUP * HEAD
KW = 2 * HEAD
BLOCK = QW + 2 * KW
MISC = 128
QB = 128

EPSILON = 1e-06
ROPE_THETA = 10000.0
MASKED = -1e30
F32 = jnp.float32
BF16 = jnp.bfloat16


def dot_nn(a, b):
    return lax.dot_general(a, b, (((1,), (0,)), ((), ())), preferred_element_type=F32)


def dot_nt(a, b):
    return lax.dot_general(a, b, (((1,), (1,)), ((), ())), preferred_element_type=F32)


def dot_tn(a, b):
    return lax.dot_general(a, b, (((0,), (0,)), ((), ())), preferred_element_type=F32)


def rope_tables():
    frequency = (np.float32(ROPE_THETA) ** (-2.0 * np.arange(HEAD // 2) / HEAD)).astype(np.float32)
    angle = np.arange(SEQ_LEN, dtype=np.float32)[:, None] * frequency[None, :]
    cosine, sine = np.cos(angle).astype(np.float32), np.sin(angle).astype(np.float32)
    zero = np.zeros_like(sine)
    cos_table = np.concatenate([cosine] * 4, axis=1)
    left_table = np.concatenate([-sine, zero] * 2, axis=1)
    right_table = np.concatenate([zero, sine] * 2, axis=1)
    return cos_table, left_table, right_table


def turn(values, cos_table, left_table, right_table, sign):
    parts = []
    for c in range(values.shape[1] // 128):
        piece = values[:, 128 * c : 128 * (c + 1)]
        ahead = pltpu.roll(piece, 96, 1) * left_table
        behind = pltpu.roll(piece, 32, 1) * right_table
        parts.append(piece * cos_table + sign * (ahead + behind))
    return parts[0] if len(parts) == 1 else jnp.concatenate(parts, axis=1)


def key_range(block):
    return max(0, block - 2) * QB, (block + 1) * QB


def block_mask(seg_col, seg_row, block):
    low, high = key_range(block)
    rows = lax.broadcasted_iota(jnp.int32, (QB, high - low), 0) + block * QB
    cols = lax.broadcasted_iota(jnp.int32, (QB, high - low), 1) + low
    same = seg_col[block * QB : (block + 1) * QB, :] == seg_row[:, low:high]
    return jnp.concatenate([(rows >= cols) & same] * GROUP, axis=0)


def heads_of(values, pair, block):
    rows = values[block * QB : (block + 1) * QB, :]
    first = pair * GROUP
    return jnp.concatenate(
        [rows[:, HEAD * h : HEAD * (h + 1)] for h in range(first, first + GROUP)], axis=0
    )


def attention_forward_kernel(
    parts, levels, x_ref, gain_ref, w_ref, cos_ref, left_ref, right_ref, seg_col_ref, seg_row_ref,
    part_ref, normed_ref, proj_ref, mixed_ref, lse_ref, full_ref, *sems,
):
    step = pl.program_id(0)
    plan = Gather(parts, levels, [full_ref], sems)

    @pl.when(step == 0)
    def _():
        plan.greet(near=False)
        plan.own_to_mate(lambda: full_ref.at[pl.ds(plan.shard * parts, parts)], 0)
        for k in range(1, levels):
            plan.spread(0, k)

    @pl.when(step == 0)
    def _():
        x = x_ref[...].astype(F32)
        scale = lax.rsqrt(jnp.mean(x * x, axis=-1, keepdims=True) + EPSILON)
        normed_ref[...] = (x * scale * gain_ref[...].astype(F32)).astype(BF16)

    projected = dot_nn(normed_ref[...], w_ref[...])
    turned = turn(
        projected[:, : QW + KW], cos_ref[...], left_ref[...], right_ref[...], 1.0
    ).astype(BF16)
    queries, keys = turned[:, :QW], turned[:, QW:]
    values = projected[:, QW + KW :].astype(BF16)
    proj_ref[...] = jnp.concatenate([turned, values], axis=1)
    seg_col, seg_row = seg_col_ref[...], seg_row_ref[...]
    for block in range(SEQ_LEN // QB):
        low, high = key_range(block)
        allowed = block_mask(seg_col, seg_row, block)
        outs = []
        for pair in range(2):
            q3 = heads_of(queries, pair, block)
            k1 = keys[low:high, HEAD * pair : HEAD * (pair + 1)]
            v1 = values[low:high, HEAD * pair : HEAD * (pair + 1)]
            scores = jnp.where(allowed, dot_nt(q3, k1) * HEAD**-0.5, MASKED)
            top = jnp.max(scores, axis=-1, keepdims=True)
            weights = jnp.exp(scores - top)
            total = jnp.sum(weights, axis=-1, keepdims=True)
            mixed = dot_nn(weights.astype(BF16), v1) * (1.0 / total)
            logsum = top + jnp.log(total)
            for h in range(GROUP):
                outs.append(mixed[h * QB : (h + 1) * QB, :])
                lse_ref[0, block * QB : (block + 1) * QB, pair * GROUP + h : pair * GROUP + h + 1] = (
                    logsum[h * QB : (h + 1) * QB, :]
                )
        mixed_ref[block * QB : (block + 1) * QB, :] = jnp.concatenate(outs, axis=1).astype(BF16)

    @pl.when(step == PAIRS - 1)
    def _():
        plan.team_to_mate(0)
        plan.mate_arrived(0)
        plan.finish()


def whole_spec(shape):
    return pl.BlockSpec(shape, lambda *_: (0,) * len(shape))


def attention_forward(x, gain_row, w_full, tables, seg_col, seg_row, out_part, groups, shards):
    tokens, width = x.shape
    parts, levels = gather_parts(groups, width // shards), shards // 2
    table = whole_spec((SEQ_LEN, 128))
    *kept, out_full = pl.pallas_call(
        functools.partial(attention_forward_kernel, parts, levels),
        grid=(PAIRS,),
        in_specs=[
            whole_spec((tokens, width)),
            whole_spec((1, width)),
            pl.BlockSpec((width, BLOCK), lambda j: (0, j)),
            table, table, table,
            whole_spec((SEQ_LEN, 1)),
            whole_spec((1, SEQ_LEN)),
            pl.BlockSpec(memory_space=pl.ANY),
        ],
        out_specs=[
            whole_spec((tokens, width)),
            pl.BlockSpec((tokens, BLOCK), lambda j: (0, j)),
            pl.BlockSpec((tokens, QW), lambda j: (0, j)),
            pl.BlockSpec((1, tokens, 8), lambda j: (j, 0, 0)),
            pl.BlockSpec(memory_space=pl.ANY),
        ],
        out_shape=[
            jax.ShapeDtypeStruct((tokens, width), BF16),
            jax.ShapeDtypeStruct((tokens, PAIRS * BLOCK), BF16),
            jax.ShapeDtypeStruct((tokens, HEADS * HEAD), BF16),
            jax.ShapeDtypeStruct((PAIRS, tokens, 8), F32),
            jax.ShapeDtypeStruct(out_part.shape, BF16),
        ],
        scratch_shapes=gather_sems(levels, parts, 1),
        input_output_aliases={8: 4},
        compiler_params=pltpu.CompilerParams(
            vmem_limit_bytes=62 << 20, collective_id=4, has_side_effects=True
        ),
        cost_estimate=pl.CostEstimate(flops=10 * 10**9, bytes_accessed=20 << 20, transcendentals=4 << 20),
        name="attention_forward",
    )(x, gain_row, w_full, *tables, seg_col, seg_row, out_part)
    return *kept, out_full.reshape(width, -1)


def attention_backward_kernel(
    groups, levels, ag_ref, out_ref, proj_ref, mixed_ref, lse_ref, cos_ref, left_ref, right_ref,
    seg_col_ref, seg_row_ref, all_ref, dproj_ref, sum_ref, mixed_t, *rest,
):
    step = pl.program_id(0)
    plan = Reduce(groups, levels, ag_ref.shape[1], rest[:4], rest[4:])

    @pl.when(step == 0)
    def _():
        plan.greet(False)
        mixed_t[...] = all_ref[...].T
        plan.fill(mixed_t, ag_ref)

    @pl.when(step == 1)
    def _():
        plan.merge()

    @pl.when(step == 2)
    def _():
        plan.spread()

    grads = dot_nt(ag_ref[...], out_ref[...]).astype(BF16)
    product = grads.astype(F32) * mixed_ref[...].astype(F32)
    queries, keys, values = (
        proj_ref[:, :QW], proj_ref[:, QW : QW + KW], proj_ref[:, QW + KW :],
    )
    seg_col, seg_row = seg_col_ref[...], seg_row_ref[...]
    blocks = SEQ_LEN // QB
    dk = [[jnp.zeros((QB, HEAD), F32) for _ in range(blocks)] for _ in range(2)]
    dv = [[jnp.zeros((QB, HEAD), F32) for _ in range(blocks)] for _ in range(2)]
    dq_rows = []
    for block in range(blocks):
        low, high = key_range(block)
        allowed = block_mask(seg_col, seg_row, block)
        dqs = []
        for pair in range(2):
            q3, g3, o3 = (heads_of(v, pair, block) for v in (queries, grads, product))
            k1 = keys[low:high, HEAD * pair : HEAD * (pair + 1)]
            v1 = values[low:high, HEAD * pair : HEAD * (pair + 1)]
            logsum = jnp.concatenate(
                [
                    lse_ref[0, block * QB : (block + 1) * QB, pair * GROUP + h : pair * GROUP + h + 1]
                    for h in range(GROUP)
                ],
                axis=0,
            )
            scores = jnp.where(allowed, dot_nt(q3, k1) * HEAD**-0.5, MASKED)
            probs = jnp.exp(scores - logsum)
            inner = jnp.sum(o3, axis=-1, keepdims=True)
            score_grads = (probs * (dot_nt(g3, v1) - inner)).astype(BF16)
            dq = dot_nn(score_grads, k1)
            dk_part = dot_tn(score_grads, q3)
            dv_part = dot_tn(probs.astype(BF16), g3)
            for at in range(low // QB, high // QB):
                rows = slice(at * QB - low, (at + 1) * QB - low)
                dk[pair][at] += dk_part[rows]
                dv[pair][at] += dv_part[rows]
            dqs += [dq[h * QB : (h + 1) * QB, :] for h in range(GROUP)]
        dq_rows.append(jnp.concatenate(dqs, axis=1))
    dq_all = jnp.concatenate(dq_rows, axis=0)
    dk_all = jnp.concatenate([jnp.concatenate(d, axis=0) for d in dk], axis=1)
    dv_all = jnp.concatenate([jnp.concatenate(d, axis=0) for d in dv], axis=1)
    turned = jnp.concatenate([dq_all, dk_all], axis=1) * HEAD**-0.5
    back = turn(turned, cos_ref[...], left_ref[...], right_ref[...], -1.0)
    dproj_ref[...] = jnp.concatenate([back, dv_all], axis=1).astype(BF16)

    @pl.when(step == PAIRS - 1)
    def _():
        for k in range(levels):
            sum_ref[k] = plan.collect(k).astype(BF16)
        plan.finish()


def attention_backward(ag, out_full, proj, mixed, lse, tables, seg_col, seg_row, groups, shards):
    tokens, width = ag.shape
    levels, rows = shards // 2, width // shards
    chunk = chunk_of(width, groups)
    table = whole_spec((SEQ_LEN, 128))
    return pl.pallas_call(
        functools.partial(attention_backward_kernel, groups, levels),
        grid=(PAIRS,),
        in_specs=[
            whole_spec((tokens, width)),
            pl.BlockSpec((QW, width), lambda j: (j, 0)),
            pl.BlockSpec((tokens, BLOCK), lambda j: (0, j)),
            pl.BlockSpec((tokens, QW), lambda j: (0, j)),
            pl.BlockSpec((1, tokens, 8), lambda j: (j, 0, 0)),
            table, table, table,
            whole_spec((SEQ_LEN, 1)),
            whole_spec((1, SEQ_LEN)),
            whole_spec((tokens, mixed.shape[1])),
        ],
        out_specs=[
            pl.BlockSpec((tokens, BLOCK), lambda j: (0, j)),
            whole_spec((levels, rows, chunk)),
        ],
        out_shape=[
            jax.ShapeDtypeStruct((tokens, PAIRS * BLOCK), BF16),
            jax.ShapeDtypeStruct((levels, rows, chunk), BF16),
        ],
        scratch_shapes=[pltpu.VMEM((mixed.shape[1], tokens), BF16)]
        + reduce_buffers(groups, levels, rows, chunk)
        + reduce_sems(groups, levels),
        compiler_params=pltpu.CompilerParams(
            vmem_limit_bytes=62 << 20, collective_id=5, has_side_effects=True
        ),
        cost_estimate=pl.CostEstimate(flops=10 * 10**9, bytes_accessed=20 << 20, transcendentals=4 << 20),
        name="attention_backward",
    )(ag, out_full, proj, mixed, lse, *tables, seg_col, seg_row, mixed)


def middle_kernel(
    mixed_ref, out_ref, x_ref, gain_ref, router_ref, routes_ref,
    hidden_ref, ffn_ref, gates_ref, meta_ref,
):
    hidden = x_ref[...].astype(F32) + dot_nn(mixed_ref[...], out_ref[...])
    scale = lax.rsqrt(jnp.mean(hidden * hidden, axis=-1, keepdims=True) + EPSILON)
    hidden_ref[...] = hidden
    ffn_in = (hidden * scale * gain_ref[...].astype(F32)).astype(BF16)
    ffn_ref[...] = ffn_in
    logits = dot_nt(router_ref[...], ffn_in)
    experts, tokens = logits.shape
    index = lax.broadcasted_iota(jnp.int32, (experts, tokens), 0)
    flags = index == routes_ref[0:1, :]
    for k in range(1, TOP):
        flags = flags | (index == routes_ref[k : k + 1, :])
    chosen = jnp.where(flags, logits, MASKED)
    weights = jnp.where(flags, jnp.exp(chosen - jnp.max(chosen, axis=0, keepdims=True)), 0.0)
    gates = weights / jnp.sum(weights, axis=0, keepdims=True)
    gates_ref[...] = gates
    earlier = lax.broadcasted_iota(jnp.int32, (tokens, tokens), 0)
    later = lax.broadcasted_iota(jnp.int32, (tokens, tokens), 1)
    before = jnp.where(earlier < later, 1.0, 0.0).astype(BF16)
    ranks = dot_nn(jnp.where(flags, 1.0, 0.0).astype(BF16), before)
    slots = jnp.where(flags, ranks, -1.0)
    groups = meta_ref.shape[0]
    count = experts // groups
    meta_ref[...] = jnp.zeros(meta_ref.shape, F32)
    for e in range(experts):
        meta_ref[e // count, e % count : e % count + 1, :] = slots[e : e + 1]
        meta_ref[e // count, 8 + e % count : 9 + e % count, :] = gates[e : e + 1]


def middle(mixed, out_full, x, gain_row, router_rows, routes_rows, groups):
    tokens, width = x.shape
    experts = router_rows.shape[0]
    return pl.pallas_call(
        middle_kernel,
        out_shape=[
            jax.ShapeDtypeStruct((tokens, width), F32),
            jax.ShapeDtypeStruct((tokens, width), BF16),
            jax.ShapeDtypeStruct((experts, tokens), F32),
            jax.ShapeDtypeStruct((groups, 16, tokens), F32),
        ],
        compiler_params=pltpu.CompilerParams(vmem_limit_bytes=48 << 20),
        cost_estimate=pl.CostEstimate(flops=3 * 10**9, bytes_accessed=16 << 20, transcendentals=1 << 14),
        name="middle",
    )(mixed, out_full, x, gain_row, router_rows, routes_rows)


def flipped(index, mask):
    out, bit = index, 1
    while bit <= mask:
        if mask & bit:
            out = out + bit - 2 * bit * ((index // bit) % 2)
        bit *= 2
    return out


def send(source, target, send_sem, recv_sem, device):
    return pltpu.make_async_remote_copy(
        src_ref=source, dst_ref=target, send_sem=send_sem, recv_sem=recv_sem,
        device_id=device, device_id_type=pl.DeviceIdType.MESH,
    )


def greet(devices):
    barrier = pltpu.get_barrier_semaphore()
    for device in devices:
        pl.semaphore_signal(barrier, inc=1, device_id=device, device_id_type=pl.DeviceIdType.MESH)
    pl.semaphore_wait(barrier, len(devices))


class Gather:
    def __init__(self, parts, levels, blocks, sems):
        self.parts, self.levels, self.blocks = parts, levels, blocks
        self.near_send, self.near_recv, self.team_send, self.team_recv, self.core_send, self.core_recv = sems
        self.group, self.shard = lax.axis_index("expert"), lax.axis_index("shard")
        level, self.core = self.shard // 2, self.shard % 2
        self.part = self.group % parts
        self.other = self.shard + 1 - 2 * self.core
        self.far = [flipped(level, k) * 2 + self.core for k in range(levels)]
        self.far_other = [flipped(level, k) * 2 + 1 - self.core for k in range(levels)]
        self.team_part = [flipped(self.part, k) for k in range(parts)]
        self.team = [self.group - self.part + t for t in self.team_part]
        self.mate = (self.group, self.other)
        self.sends = []

    def greet(self, near=True):
        greet(
            [self.mate]
            + [(self.group, self.far[k]) for k in range(1, self.levels) if near]
            + [(self.team[t], self.shard) for t in range(1, self.parts)]
        )

    def push(self, make):
        make().start()
        self.sends.append(make)

    def arrived(self, piece, send_sem, recv_sem):
        send(piece, piece, send_sem, recv_sem, self.mate).wait_recv()

    def near(self, own, i):
        for k in range(1, self.levels):
            self.push(
                lambda k=k: send(
                    own.at[self.part], self.blocks[i].at[self.shard * self.parts + self.part],
                    self.near_send.at[i, k], self.near_recv.at[i, k], (self.group, self.far[k]),
                )
            )

    def near_arrived(self, i, k):
        piece = self.blocks[i].at[self.far[k] * self.parts + self.part]
        self.arrived(piece, self.near_send.at[i, k], self.near_recv.at[i, k])

    def spread(self, i, k):
        def piece():
            return self.blocks[i].at[self.far[k] * self.parts + self.part]

        for t in range(1, self.parts):
            self.push(
                lambda t=t: send(
                    piece(), piece(), self.team_send.at[i, k, t], self.team_recv.at[i, k, t],
                    (self.team[t], self.shard),
                )
            )
        self.push(
            lambda: send(
                piece(), piece(), self.core_send.at[i, k, 0], self.core_recv.at[i, k, 0], self.mate
            )
        )

    def own_to_mate(self, own, i):
        self.push(
            lambda: send(
                own(), self.blocks[i].at[pl.ds(self.shard * self.parts, self.parts)],
                self.core_send.at[i, 0, 0], self.core_recv.at[i, 0, 0], self.mate,
            )
        )

    def team_to_mate(self, i):
        for k in range(1, self.levels):
            for t in range(1, self.parts):

                def piece(k=k, t=t):
                    return self.blocks[i].at[self.far[k] * self.parts + self.team_part[t]]

                self.arrived(piece(), self.team_send.at[i, k, t], self.team_recv.at[i, k, t])
                self.push(
                    lambda piece=piece, k=k, t=t: send(
                        piece(), piece(), self.core_send.at[i, k, t], self.core_recv.at[i, k, t],
                        self.mate,
                    )
                )

    def mate_arrived(self, i):
        piece = self.blocks[i].at[pl.ds(self.other * self.parts, self.parts)]
        self.arrived(piece, self.core_send.at[i, 0, 0], self.core_recv.at[i, 0, 0])
        for k in range(1, self.levels):
            for t in range(self.parts):
                piece = self.blocks[i].at[self.far_other[k] * self.parts + self.team_part[t]]
                self.arrived(piece, self.core_send.at[i, k, t], self.core_recv.at[i, k, t])

    def finish(self):
        for make in self.sends:
            make().wait_send()


def gather_sems(levels, parts, count):
    dma = pltpu.SemaphoreType.DMA
    return [dma((count, levels))] * 2 + [dma((count, levels, parts))] * 4


def gather_parts(groups, rows):
    return next(p for p in (4, 2, 1) if groups % p == 0 and rows % (16 * p) == 0)


class Rows:
    def __init__(self, groups, own, outs, sems):
        self.own, self.outs = own, outs
        self.send_sem, self.recv_sem = sems
        group, self.shard = lax.axis_index("expert"), lax.axis_index("shard")
        self.team = [flipped(group, t) for t in range(groups)]
        self.near = range(1, 1 + len(outs))

    def copy(self, t):
        return send(
            self.own, self.outs[t - 1], self.send_sem.at[t], self.recv_sem.at[t],
            (self.team[t], self.shard),
        )

    def start(self):
        for t in self.near:
            self.copy(t).start()

    def finish(self):
        for t in self.near:
            self.copy(t).wait()


def gather_kernel(groups, parts, levels, *refs):
    ins, own_rows, outs, refs = refs[:2], refs[2], refs[3:5], refs[5:]
    count = 2 if groups == 4 else groups - 1
    others, refs = refs[:count], refs[count:]
    bounce, local_sem = refs[:2], refs[2]
    plan = Gather(parts, levels, outs, refs[3:9])
    rows = Rows(groups, own_rows, others, refs[9:11])
    greet(
        [plan.mate]
        + [(plan.group, plan.far[k]) for k in range(1, levels)]
        + [(rows.team[t], rows.shard) for t in range(1, groups)]
    )
    own = pl.ds(plan.shard * parts, parts)
    loads = [pltpu.make_async_copy(ins[i], bounce[i], local_sem.at[0, i]) for i in range(2)]
    stores = [pltpu.make_async_copy(bounce[i], outs[i].at[own], local_sem.at[1, i]) for i in range(2)]
    for copy in loads:
        copy.start()
    for i in range(2):
        plan.near(ins[i], i)
    rows.start()
    plan.own_to_mate(lambda: ins[0], 0)
    for load, store in zip(loads, stores):
        load.wait()
        store.start()
    for k in range(1, levels):
        plan.near_arrived(0, k)
        plan.spread(0, k)
    plan.team_to_mate(0)
    for k in range(1, levels):
        plan.near_arrived(1, k)
    plan.mate_arrived(0)
    plan.finish()
    rows.finish()
    for copy in stores:
        copy.wait()


def gather_weights(blocks, own_rows, groups, shards):
    rows = blocks[0].shape[0]
    parts = gather_parts(groups, rows)
    levels, count = shards // 2, 2 if groups == 4 else groups - 1
    blocks = [b.reshape(parts, rows // parts, b.shape[1]) for b in blocks]
    dma = pltpu.SemaphoreType.DMA
    return pl.pallas_call(
        functools.partial(gather_kernel, groups, parts, levels),
        in_specs=[pl.BlockSpec(memory_space=pl.ANY)] * 3,
        out_specs=[pl.BlockSpec(memory_space=pl.ANY)] * (2 + count),
        out_shape=[
            jax.ShapeDtypeStruct((shards * parts,) + b.shape[1:], b.dtype) for b in blocks
        ]
        + [jax.ShapeDtypeStruct(own_rows.shape, own_rows.dtype)] * count,
        scratch_shapes=[pltpu.VMEM(b.shape, b.dtype) for b in blocks]
        + [dma((2, 2))]
        + gather_sems(levels, parts, 2)
        + [dma((groups,)), dma((groups,))],
        compiler_params=pltpu.CompilerParams(collective_id=0, has_side_effects=True),
        name="gather_weights",
    )(*blocks, own_rows)


class Reduce:
    def __init__(self, groups, levels, cols, refs, sems):
        self.groups, self.levels, self.relay = groups, levels, groups == 4
        self.held, self.from_core, self.passing, self.from_group = refs
        self.core_send, self.core_recv, self.pass_send, self.pass_recv, self.group_send, self.group_recv = sems
        self.group, self.shard = lax.axis_index("expert"), lax.axis_index("shard")
        level, self.core = self.shard // 2, self.shard % 2
        self.mate = (self.group, self.shard + 1 - 2 * self.core)
        self.team = [flipped(self.group, t) for t in range(groups)]
        self.far = [flipped(level, k) for k in range(levels)]
        self.order = sorted(range(levels), key=lambda k: (k & -k or levels, k))
        self.near = [1, 2] if self.relay else list(range(1, groups))
        self.sends = []
        turns = ([3] if self.relay else []) + self.near + [0]
        self.even = self.held.shape[4] * groups == cols
        self.chunks = [self.team[t] if self.even else k for k, t in enumerate(turns)]

    def greet(self, climbs):
        greet(
            [self.mate]
            + [(self.group, self.far[k] * 2 + self.core) for k in range(1, self.levels) if climbs]
            + [(self.team[t], self.shard) for t in range(1, self.groups)]
        )

    def push(self, make):
        make().start()
        self.sends.append(make)

    def arrived(self, piece, send_sem, recv_sem):
        send(piece, piece, send_sem, recv_sem, self.mate).wait_recv()

    def fill(self, left, right):
        rows, chunk = self.held.shape[3:]
        tall = 768
        per = tall // rows
        even = self.even
        for k in self.chunks:
            low = k * chunk
            many = chunk if even else max(0, min(chunk, right.shape[1] - low))
            if many:
                at = pl.ds(pl.multiple_of(low, 128), many) if even else slice(low, low + many)

                @pl.loop(0, left.shape[0] // tall)
                def _(c):
                    part = pl.ds(pl.multiple_of(c * tall, tall), tall)
                    value = dot_nn(left[part, :], right[:, at]).astype(BF16)
                    for i in range(per):
                        s = c * per + i
                        self.held[k, s % 2, s // 2, :, :many] = value[i * rows : (i + 1) * rows]

            self.push(
                lambda k=k: send(
                    self.held.at[k, 1 - self.core], self.from_core.at[k],
                    self.core_send.at[k], self.core_recv.at[k], self.mate,
                )
            )

    def pass_copy(self, part, k):
        half = self.held.shape[3] // 2
        return send(
            self.held.at[self.team[3], self.core, self.far[k], pl.ds(part * half, half)],
            self.passing.at[part, k], self.pass_send.at[part, k], self.pass_recv.at[part, k],
            (self.team[1 + part], self.shard),
        )

    def group_copy(self, t, k):
        return send(
            self.held.at[self.team[t], self.core, self.far[k]], self.from_group.at[t, k],
            self.group_send.at[t, k], self.group_recv.at[t, k], (self.team[t], self.shard),
        )

    def merge(self):
        for n, k in enumerate(self.chunks):
            self.arrived(self.from_core.at[k], self.core_send.at[k], self.core_recv.at[k])

            @pl.loop(0, self.levels)
            def _(z):
                self.held[k, self.core, z] = (
                    self.held[k, self.core, z].astype(F32) + self.from_core[k, z].astype(F32)
                ).astype(BF16)

            if self.relay and n == 0:
                for j in self.order:
                    for part in range(2):
                        self.push(lambda part=part, j=j: self.pass_copy(part, j))
        if not self.relay:
            for j in self.order:
                for t in self.near:
                    self.push(lambda t=t, j=j: self.group_copy(t, j))

    def spread(self):
        if not self.relay:
            return
        half = self.held.shape[3] // 2
        for k in self.order:
            for part in range(2):
                self.arrived(
                    self.passing.at[part, k], self.pass_send.at[part, k], self.pass_recv.at[part, k]
                )
                at = pl.ds(part * half, half)
                piece = self.held.at[self.team[2 - part], self.core, self.far[k], at]
                piece[...] = (piece[...].astype(F32) + self.passing[part, k].astype(F32)).astype(BF16)
            for t in self.near:
                self.push(lambda t=t, k=k: self.group_copy(t, k))

    def collect(self, k):
        total = self.held[self.group, self.core, self.far[k]].astype(F32)
        for t in self.near:
            self.arrived(self.from_group.at[t, k], self.group_send.at[t, k], self.group_recv.at[t, k])
            total = total + self.from_group[t, k].astype(F32)
        return total

    def bits(self):
        return [bit for bit in (1, 2, 4, 8, 16) if bit < self.levels]

    def climb(self, summed, from_level, sems, bit, only=None):
        for k in range(self.levels) if only is None else [only]:
            if k & bit and not k & (bit - 1):
                self.push(
                    lambda k=k: send(
                        summed.at[k], from_level.at[k], sems[0].at[k], sems[1].at[k],
                        (self.group, self.far[bit] * 2 + self.core),
                    )
                )

    def climbed(self, summed, from_level, sems, bit):
        for k in range(self.levels):
            if k & bit and not k & (bit - 1):
                self.arrived(from_level.at[k], sems[0].at[k], sems[1].at[k])
                to = k - bit
                summed[to] = (summed[to].astype(F32) + from_level[k].astype(F32)).astype(BF16)

    def settle(self, summed, home, home_sems):
        home[self.group] = summed[0]
        for t in range(1, self.groups):
            self.push(
                lambda t=t: send(
                    home.at[self.group], home.at[self.group],
                    home_sems[0].at[t], home_sems[1].at[t], (self.team[t], self.shard),
                )
            )

    def landed(self, home, home_sems):
        for t in range(1, self.groups):
            self.arrived(home.at[self.team[t]], home_sems[0].at[t], home_sems[1].at[t])

    def finish(self):
        for make in self.sends:
            make().wait_send()


def chunk_of(total, groups):
    return 128 * (-(-total // (128 * groups)))


def reduce_buffers(groups, levels, rows, chunk):
    piece = (rows, chunk)
    passing = (2, levels, rows // 2, chunk) if groups == 4 else (1, 1, 16, 128)
    return [
        pltpu.VMEM((groups, 2, levels) + piece, BF16),
        pltpu.VMEM((groups, levels) + piece, BF16),
        pltpu.VMEM(passing, BF16),
        pltpu.VMEM((groups, levels) + piece, BF16),
    ]


def reduce_sems(groups, levels):
    dma = pltpu.SemaphoreType.DMA
    return [dma((groups,))] * 2 + [dma((2, levels))] * 2 + [dma((groups, levels))] * 2


class FewRows:
    def __init__(self, plan, refs, sems):
        self.plan = plan
        self.rows, self.from_core, self.from_group, self.pieces, self.from_level = refs
        self.core_send, self.core_recv, self.group_send, self.group_recv, self.level_send, self.level_recv = sems

    def start(self):
        plan = self.plan
        plan.push(
            lambda: send(self.rows, self.from_core, self.core_send, self.core_recv, plan.mate)
        )

    def over_groups(self):
        plan = self.plan
        plan.arrived(self.from_core, self.core_send, self.core_recv)
        total = self.rows[...].astype(F32) + self.from_core[...].astype(F32)
        self.from_group[plan.group] = total.astype(BF16)
        for t in range(1, plan.groups):
            plan.push(
                lambda t=t: send(
                    self.from_group.at[plan.group], self.from_group.at[plan.group],
                    self.group_send.at[t], self.group_recv.at[t], (plan.team[t], plan.shard),
                )
            )

    def over_levels(self):
        plan = self.plan
        for t in range(1, plan.groups):
            plan.arrived(self.from_group.at[plan.team[t]], self.group_send.at[t], self.group_recv.at[t])
        total = self.from_group[0].astype(F32)
        for g in range(1, plan.groups):
            total = total + self.from_group[g].astype(F32)
        wide = self.pieces.shape[2]
        for s in range(2 * plan.levels):
            self.pieces[s] = total[:, s * wide : (s + 1) * wide].astype(BF16)
        for k in range(1, plan.levels):
            plan.push(
                lambda k=k: send(
                    self.pieces.at[plan.far[k] * 2 + plan.core], self.from_level.at[k],
                    self.level_send.at[k], self.level_recv.at[k],
                    (plan.group, plan.far[k] * 2 + plan.core),
                )
            )

    def total(self):
        plan = self.plan
        total = self.pieces[plan.shard].astype(F32)
        for k in range(1, plan.levels):
            plan.arrived(self.from_level.at[k], self.level_send.at[k], self.level_recv.at[k])
            total = total + self.from_level[k].astype(F32)
        return total


def reduce_kernel(groups, levels, *refs):
    normed_ref, dproj_ref, gain_one_ref, gain_two_ref, router_ref, out_sum_ref = refs[:6]
    out_ref, qkv_ref, misc_ref, *refs = refs[6:]
    normed_t, summed, from_level, home, out_summed, out_level, out_home = refs[:7]
    plan = Reduce(groups, levels, dproj_ref.shape[1], refs[7:11], refs[11:17])
    level_sems, home_sems, out_level_sems, out_home_sems = (refs[i : i + 2] for i in range(17, 25, 2))
    misc = FewRows(plan, refs[25:30], refs[30:36])
    first, *others = plan.bits()
    plan.greet(True)
    out_summed[...] = out_sum_ref[...]
    plan.climb(out_summed, out_level, out_level_sems, first)
    experts = router_ref.shape[0]
    gains = jnp.concatenate(
        [gain_one_ref[...], gain_two_ref[...], jnp.zeros((6, gain_one_ref.shape[1]), F32)], axis=0
    )
    misc.rows[...] = jnp.zeros(misc.rows.shape, BF16)
    misc.rows[:8] = gains.astype(BF16)
    misc.rows[8 : 8 + experts] = router_ref[...].astype(BF16)
    misc.start()
    normed_t[...] = normed_ref[...].T
    plan.fill(normed_t, dproj_ref)
    plan.merge()
    misc.over_groups()
    plan.spread()
    plan.climbed(out_summed, out_level, out_level_sems, first)
    for bit in others[:1]:
        plan.climb(out_summed, out_level, out_level_sems, bit)
    misc.over_levels()
    for k in plan.order:
        summed[k] = plan.collect(k).astype(BF16)
        plan.climb(summed, from_level, level_sems, first, k)
    for n, bit in enumerate(others):
        plan.climbed(out_summed, out_level, out_level_sems, bit)
        for bit in others[n + 1 : n + 2]:
            plan.climb(out_summed, out_level, out_level_sems, bit)
    plan.settle(out_summed, out_home, out_home_sems)
    plan.climbed(summed, from_level, level_sems, first)
    for bit in others:
        plan.climb(summed, from_level, level_sems, bit)
        plan.climbed(summed, from_level, level_sems, bit)
    plan.settle(summed, home, home_sems)
    misc_ref[...] = misc.total()
    plan.landed(out_home, out_home_sems)
    out_ref[...] = out_home[...]
    plan.landed(home, home_sems)
    qkv_ref[...] = home[...]
    plan.finish()


def reduce_weights(normed, dproj, gain_one, gain_two, router, out_sum, groups, shards):
    tokens, width = normed.shape
    levels, rows = shards // 2, width // shards
    total = dproj.shape[1]
    chunk, out_chunk = chunk_of(total, groups), out_sum.shape[2]
    dma = pltpu.SemaphoreType.DMA
    vmem = pl.BlockSpec(memory_space=pltpu.VMEM)
    whole, out_whole = (groups, rows, chunk), (groups, rows, out_chunk)
    few = 16 * (-(-(8 + router.shape[0]) // 16))
    return pl.pallas_call(
        functools.partial(reduce_kernel, groups, levels),
        in_specs=[vmem] * 6,
        out_specs=[vmem] * 3,
        out_shape=[jax.ShapeDtypeStruct(s, BF16) for s in (out_whole, whole)]
        + [jax.ShapeDtypeStruct((few, rows), F32)],
        scratch_shapes=[
            pltpu.VMEM((width, tokens), BF16),
            pltpu.VMEM((levels, rows, chunk), BF16),
            pltpu.VMEM((levels, rows, chunk), BF16),
            pltpu.VMEM(whole, BF16),
            pltpu.VMEM((levels, rows, out_chunk), BF16),
            pltpu.VMEM((levels, rows, out_chunk), BF16),
            pltpu.VMEM(out_whole, BF16),
        ]
        + reduce_buffers(groups, levels, rows, chunk)
        + reduce_sems(groups, levels)
        + [dma((levels,))] * 2 + [dma((groups,))] * 2 + [dma((levels,))] * 2 + [dma((groups,))] * 2
        + [
            pltpu.VMEM((few, width), BF16),
            pltpu.VMEM((few, width), BF16),
            pltpu.VMEM((groups, few, width), BF16),
            pltpu.VMEM((shards, few, rows), BF16),
            pltpu.VMEM((levels, few, rows), BF16),
            dma, dma, dma((groups,)), dma((groups,)), dma((levels,)), dma((levels,)),
        ],
        compiler_params=pltpu.CompilerParams(
            collective_id=1, has_side_effects=True, vmem_limit_bytes=62 << 20
        ),
        cost_estimate=pl.CostEstimate(
            flops=2 * tokens * width * total, bytes_accessed=8 << 20, transcendentals=0
        ),
        name="reduce_weights",
    )(normed, dproj, gain_one, gain_two, router, out_sum)


def expert_kernel(capacity, shards, groups, count, base, stage, *refs):
    refs = list(refs)
    take = lambda n: [refs.pop(0) for _ in range(n)]
    if stage == "first":
        x_own, meta_own = take(2)
        u_ins = take(3 if groups == 4 else groups)
    else:
        x_ref, u_ref, meta_ref, out_in, dx_in, gg_in = take(6)
    packed_ref = take(1)[0]
    if stage == "last":
        earlier_ref = take(1)[0]
    if stage == "first":
        x_all, u_all, meta_all, out_ref, dx_ref, gg_ref, dw_out = take(7)
    elif stage == "last":
        out_homes = take(3 if groups == 4 else groups)
        dx_home, gg_home, dw_out = take(3)
    else:
        out_ref, dx_ref, gg_ref, dw_out = take(4)
    xs, us, bs, inn, dw, dw_sem, we_all, wp_all, we_sem, wp_sem = take(10)
    if stage != "between":
        core_buf, core_send, core_recv, credit = take(4)
    if stage == "first":
        x_buf, u_buf, meta_buf = take(3)
        x_send, x_recv, meta_send, meta_recv, load_sem, u_sem, meta_sem, keep_sem, pass_sem = take(9)
    elif stage == "last":
        buf, passing, gg_buf = take(3)
        load_sem, pass_send, pass_recv, dx_send, dx_recv, gg_send, gg_recv, keep_sem = take(8)
    turn_at, expert = pl.program_id(0), pl.program_id(1)
    last_turn, last = groups - 1, count - 1
    group, shard = lax.axis_index("expert"), lax.axis_index("shard")
    team = [flipped(group, t) for t in range(groups)]
    core = shard % 2
    mate = (group, shard + 1 - 2 * core)
    width = xs.shape[2]
    tokens = x_buf.shape[0] if stage == "first" else x_ref.shape[1]
    tall, short = width // shards, FF // shards
    side = width - 2 * FF
    we_ref, wp_ref = we_all.at[expert], wp_all.at[expert]

    @pl.when((turn_at == 0) & (expert == 0))
    def _():
        for e in range(count):

            @pl.loop(0, shards)
            def _(s):
                a = pl.ds(pl.multiple_of(s * tall, 16), tall)
                b = pl.ds(pl.multiple_of(s * short, 16), short)
                low = pl.ds(pl.multiple_of(s * short, 16), short // 2)
                high = pl.ds(pl.multiple_of(s * short + short // 2, 16), short // 2)
                source = packed_ref.at[s, e]
                rest = pl.ds(tall + short, short // 2)
                for piece, target, sem in (
                    (source.at[:tall], we_all.at[e, a], we_sem),
                    (source.at[tall : tall + short], wp_all.at[e, b, : 2 * FF], wp_sem),
                    (source.at[rest, :side], wp_all.at[e, low, 2 * FF :], wp_sem),
                    (source.at[rest, side:], wp_all.at[e, high, 2 * FF :], wp_sem),
                ):
                    pltpu.make_async_copy(piece, target, sem.at[e]).start()

    def core_copy(source):
        return send(source.at[:, 1 - core], core_buf, core_send, core_recv, mate)

    def core_add(source):
        core_copy(source).wait()

        @pl.loop(0, shards // 2)
        def _(z):
            core_buf[z] = (dw[z, core].astype(F32) + core_buf[z].astype(F32)).astype(BF16)

    def store_half(at):
        return pltpu.make_async_copy(core_buf, dw_out.at[:, at], dw_sem)

    def core_free(at):
        store_half(at).wait()
        pl.semaphore_signal(credit, inc=1, device_id=mate, device_id_type=pl.DeviceIdType.MESH)

    def own_half():
        return pltpu.make_async_copy(earlier_ref.at[:, core], dw.at[:, core], keep_sem.at[1])

    before = 1 if stage == "last" else 0

    if stage == "first":
        relay = groups == 4
        near = [1, 2] if relay else list(range(1, groups))
        half = tokens // 2

        def x_copy(t):
            return send(x_own, x_all.at[t], x_send.at[t], x_recv.at[t], (team[t], shard))

        def passed(source, target, part, sems):
            at = pl.ds(part * half, half)
            return send(
                source.at[at], target.at[3, at], sems.at[0, part], sems.at[1, part],
                (team[2 - part], shard),
            )

        def x_pass(part):
            return passed(x_all.at[1 + part], x_all, part, pass_sem.at[0])

        def u_pass(part):
            return passed(u_ins[1 + part], u_all, part, pass_sem.at[1])

        def meta_copy(t):
            return send(
                meta_own.at[team[t]], meta_all.at[t], meta_send.at[t], meta_recv.at[t], (team[t], shard)
            )

        def u_load(t):
            source = u_all.at[t] if relay and t == 3 else u_ins[t]
            return pltpu.make_async_copy(source, u_buf.at[t % 2], u_sem.at[t % 2])

        def x_keep():
            return pltpu.make_async_copy(x_buf, x_all.at[0], keep_sem.at[0])

        def meta_keep():
            return pltpu.make_async_copy(meta_buf, meta_all.at[0], keep_sem.at[1])

        def u_keep(t):
            return pltpu.make_async_copy(u_buf.at[t % 2], u_all.at[t], keep_sem.at[2 + t])

        for t in range(groups):

            @pl.when((turn_at == t) & (expert == 0))
            def _():
                if t == 0:
                    u_load(0).start()
                    greet([mate] + [(team[k], shard) for k in range(1, groups)])
                    for k in range(1, groups):
                        meta_copy(k).start()
                    for k in near:
                        x_copy(k).start()
                    fetch_x, fetch_meta = x_own, meta_own.at[group]
                else:
                    if not relay:
                        x_copy(t).wait_recv()
                    elif t == 1:
                        for k in near:
                            x_copy(k).wait_recv()
                        for part in range(2):
                            x_pass(part).start()
                        for part in range(2):
                            u_pass(part).start()
                    elif t == 3:
                        for part in range(2):
                            x_pass(part).wait_recv()
                            u_pass(part).wait_recv()
                        u_load(3).start()
                    meta_copy(t).wait_recv()
                    u_keep(t - 1).wait()
                    if t == 1:
                        x_keep().wait()
                        meta_keep().wait()
                    fetch_x, fetch_meta = x_all.at[t], meta_all.at[t]
                load = pltpu.make_async_copy(fetch_x, x_buf, load_sem)
                load_meta = pltpu.make_async_copy(fetch_meta, meta_buf, meta_sem)
                load.start()
                load_meta.start()
                if t + 1 < groups and not (relay and t == 2):
                    u_load(t + 1).start()
                u_load(t).wait()
                load_meta.wait()
                load.wait()
                if not (relay and t == 3):
                    u_keep(t).start()
                if t == 0:
                    x_keep().start()
                    meta_keep().start()

        x_now, u_now, meta_now = x_buf, u_buf.at[turn_at % 2], meta_buf
    else:
        x_now, u_now, meta_now = x_ref.at[0], u_ref.at[0], meta_ref.at[0]

    if stage == "last":
        relay = groups == 4
        slots, half = buf.shape[1], tokens // 2
        halves = [pl.ds(0, half), pl.ds(half, half)]

        def kept(kind, i):
            return buf.at[kind, i % slots]

        def load(kind, i):
            source = dx_in if kind else out_in
            return pltpu.make_async_copy(
                source.at[last_turn - i], kept(kind, i), load_sem.at[kind, i % 2]
            )

        def store(i):
            return pltpu.make_async_copy(kept(0, i), out_homes[last_turn - i], keep_sem.at[2 + i])

        def pass_copy(kind, part):
            return send(
                kept(kind, 0).at[halves[part]], passing.at[kind, part],
                pass_send.at[kind, part], pass_recv.at[kind, part], (team[1 + part], shard),
            )

        def dx_copy(i):
            t = last_turn - i
            return send(kept(1, i), dx_home.at[t], dx_send.at[t], dx_recv.at[t], (team[t], shard))

        def dx_half(part):
            at = halves[part]
            return send(
                kept(1, 1).at[at], dx_home.at[2, at], dx_send.at[2 + part], dx_recv.at[2 + part],
                (team[2], shard),
            )

        def gg_copy(i):
            t = last_turn - i
            return send(gg_buf.at[i], gg_home.at[group], gg_send.at[t], gg_recv.at[t], (team[t], shard))

        def own_copies():
            return [
                pltpu.make_async_copy(kept(1, last_turn), dx_home.at[0], keep_sem.at[0]),
                pltpu.make_async_copy(gg_buf.at[last_turn], gg_home.at[group], keep_sem.at[1]),
            ]

        for i in range(groups):

            @pl.when((turn_at == i) & (expert == 0))
            def _():
                if i == 0:
                    for kind in range(2):
                        load(kind, 0).start()
                    greet([mate] + [(team[k], shard) for k in range(1, groups)])
                    core_copy(earlier_ref).start()
                    own_half().start()
                if i == 1:
                    own_half().wait()
                    core_add(earlier_ref)
                    store_half(0).start()
                if i == 2:
                    core_free(0)
                if i + 1 < groups:
                    if i + 1 >= slots:
                        dx_copy(i + 1 - slots).wait_send()
                        store(i + 1 - slots).wait()
                    for kind in range(2):
                        load(kind, i + 1).start()
                for kind in range(2):
                    load(kind, i).wait()

        at_now = turn_at % slots
        out_now, dx_now, gg_now = buf.at[0, at_now], buf.at[1, at_now], gg_buf.at[turn_at]
    else:
        out_now, dx_now, gg_now = out_ref.at[0], dx_ref.at[0], gg_ref.at[0]

    @pl.when(expert == 0)
    def _():
        if stage == "first":
            out_now[...] = jnp.zeros((tokens, width), BF16)
            dx_now[...] = jnp.zeros((tokens, width), BF16)
            gg_now[...] = jnp.zeros((8, tokens), F32)
        else:
            gg_now[...] = gg_in[0]
        if stage == "between":
            out_now[...] = out_in[0]
            dx_now[...] = dx_in[0]

    @pl.when(turn_at == 0)
    def _():
        pltpu.make_async_copy(we_ref, we_ref, we_sem.at[expert]).wait()
        pltpu.make_async_copy(wp_ref, wp_ref, wp_sem.at[expert]).wait()

    slot_row = meta_now[pl.ds(base + expert, 1), :]
    gate_row = meta_now[pl.ds(8 + base + expert, 1), :]
    index = lax.broadcasted_iota(jnp.int32, (capacity, tokens), 0).astype(F32)
    pick = jnp.where(index == slot_row, 1.0, 0.0)
    gate_col = jnp.sum(pick * gate_row, axis=1, keepdims=True)
    place = pick.astype(BF16)
    rows = pl.ds(pl.multiple_of(turn_at * capacity, capacity), capacity)
    x = dot_nn(place, x_now[...]).astype(BF16)
    xs[expert, rows, :] = x
    u_rows = dot_nn(place, u_now[...]).astype(BF16)
    us[expert, rows, :] = u_rows
    both_parts = dot_nn(x, we_ref[...])
    gate, up = both_parts[:, :FF], both_parts[:, FF:]
    back = dot_nt(u_rows, wp_ref[...])
    sig = 1.0 / (1.0 + jnp.exp(-gate))
    act = gate * sig
    inner = act * up
    inner_low = inner.astype(BF16)
    gate_grad = jnp.sum(inner * back, axis=1, keepdims=True)
    here = lax.broadcasted_iota(jnp.int32, (8, tokens), 0) == base + expert
    gg_now[...] = jnp.where(here, jnp.sum(pick * gate_grad, axis=0, keepdims=True), gg_now[...])
    inn[expert, rows, :] = (inner * gate_col).astype(BF16)
    inner_grads = back * gate_col
    bs[expert, rows, :FF] = (inner_grads * up * sig * (1.0 + gate * (1.0 - sig))).astype(BF16)
    bs[expert, rows, FF:] = (inner_grads * act).astype(BF16)
    both = bs[expert, rows, :]
    weighted_t = (pick * gate_row).astype(BF16).T
    place_t = place.T
    result = dot_nn(inner_low, wp_ref[...]).astype(BF16)
    out_now[...] = (out_now[...].astype(F32) + dot_nn(weighted_t, result)).astype(BF16)
    row_grads = dot_nt(both, we_ref[...]).astype(BF16)
    dx_now[...] = (dx_now[...].astype(F32) + dot_nn(place_t, row_grads)).astype(BF16)

    if stage == "last":

        def add_passed(kind):
            for part in range(2):
                pass_copy(kind, part).wait_recv()
                target = kept(kind, 1 + part).at[halves[part]]
                target[...] = (target[...].astype(F32) + passing[kind, part].astype(F32)).astype(BF16)

        for i in range(groups):

            @pl.when((turn_at == i) & (expert == last))
            def _():
                if i < last_turn:
                    gg_copy(i).start()
                else:
                    for copy in own_copies():
                        copy.start()
                if not relay:
                    store(i).start()
                    if i < last_turn:
                        dx_copy(i).start()
                elif i == 0:
                    for kind in (1, 0):
                        for part in range(2):
                            pass_copy(kind, part).start()
                elif i == 1:
                    dx_half(1).start()
                elif i == 2:
                    add_passed(1)
                    dx_copy(2).start()
                    dx_half(0).start()
                else:
                    add_passed(0)
                    for k in range(1, groups):
                        store(k).start()

    @pl.when(turn_at == last_turn)
    def _():
        if stage != "between" and count > 1:

            @pl.when(expert > 0)
            def _():
                core_add(dw)
                store_half(before + expert - 1).start()

        wide, half = 384, FF // 2

        @pl.loop(0, width // wide)
        def _(c):
            at = pl.ds(pl.multiple_of(c * wide, wide), wide)
            value = dot_tn(xs[expert, :, at], bs[expert]).astype(BF16)
            for i in range(wide // tall):
                s = c * (wide // tall) + i
                dw[s // 2, s % 2, :tall, :] = value[i * tall : (i + 1) * tall]

        @pl.loop(0, FF // half)
        def _(c):
            at = pl.ds(pl.multiple_of(c * half, half), half)
            value = dot_tn(inn[expert, :, at], us[expert]).astype(BF16)
            for i in range(half // short):
                s, low = c * (half // short) + i, i * short
                mid, high = low + short // 2, low + short
                dw[s // 2, s % 2, tall : tall + short, :] = value[low:high, : 2 * FF]
                dw[s // 2, s % 2, tall + short :, :side] = value[low:mid, 2 * FF :]
                dw[s // 2, s % 2, tall + short :, side:] = value[mid:high, 2 * FF :]

        if stage == "between":
            pltpu.make_async_copy(dw, dw_out, dw_sem).start()
        else:
            if count > 1:

                @pl.when(expert > 0)
                def _():
                    core_free(before + expert - 1)

            if before:
                pl.semaphore_wait(credit, 1)
            else:

                @pl.when(expert > 0)
                def _():
                    pl.semaphore_wait(credit, 1)

            core_copy(dw).start()

    @pl.when((turn_at == last_turn) & (expert == last))
    def _():
        if stage == "between":
            pltpu.make_async_copy(dw, dw_out, dw_sem).wait()
        else:
            core_add(dw)
            store_half(before + last).start()
            store_half(before + last).wait()
        if stage == "first":
            if not relay:
                u_keep(last_turn).wait()
            for t in range(1, groups):
                meta_copy(t).wait_send()
            for t in near:
                x_copy(t).wait_send()
            if relay:
                for part in range(2):
                    x_pass(part).wait_send()
                    u_pass(part).wait_send()
        if stage == "last":
            for i in range(groups - 1):
                t = last_turn - i
                gg_copy(i).wait_send()
                send(
                    gg_buf.at[i], gg_home.at[team[t]], gg_send.at[t], gg_recv.at[t], (team[t], shard)
                ).wait_recv()
            if relay:
                for part in range(2):
                    dx_half(part).wait()
                    for kind in range(2):
                        pass_copy(kind, part).wait_send()
                dx_copy(2).wait()
                for k in range(1, groups):
                    store(k).wait()
            else:
                for i in range(groups - 1):
                    if i + slots >= groups:
                        dx_copy(i).wait_send()
                    dx_copy(i).wait_recv()
                for i in range(groups - slots, groups):
                    store(i).wait()
            for copy in own_copies():
                copy.wait()


def expert_call(capacity, shards, groups, base, stage, data, packed_weights, *kept):
    count = packed_weights.shape[1]
    tokens, width = data[0].shape[-2:]
    total = groups * capacity
    anywhere = pl.BlockSpec(memory_space=pl.ANY)
    turned = (lambda i: i) if stage == "first" else (lambda i: groups - 1 - i)
    block = pl.BlockSpec((1, tokens, width), lambda i, e: (turned(i), 0, 0))
    small = pl.BlockSpec((1, 8, tokens), lambda i, e: (turned(i), 0, 0))
    dma = pltpu.SemaphoreType.DMA
    many = jax.ShapeDtypeStruct((groups, tokens, width), BF16)
    grads = jax.ShapeDtypeStruct((groups, 8, tokens), F32)
    piece = ((width + FF + FF // 2) // shards, 2 * FF)
    summed = 2 if stage == "between" else count + len(kept)
    weights = jax.ShapeDtypeStruct((shards // 2, summed) + piece, BF16)
    meta = jax.ShapeDtypeStruct((groups, 16, tokens), F32)
    scratch = [
        pltpu.VMEM((count, total, width), BF16),
        pltpu.VMEM((count, total, width), BF16),
        pltpu.VMEM((count, total, 2 * FF), BF16),
        pltpu.VMEM((count, total, FF), BF16),
        pltpu.VMEM((shards // 2, 2) + piece, BF16),
        dma,
        pltpu.VMEM((count, width, 2 * FF), BF16),
        pltpu.VMEM((count, FF, width), BF16),
        dma((count,)), dma((count,)),
    ]
    if stage != "between":
        scratch += [
            pltpu.VMEM((shards // 2,) + piece, BF16), dma, dma, pltpu.SemaphoreType.REGULAR,
        ]
    if stage == "first":
        in_specs = [anywhere] * len(data)
        out_specs = [anywhere] * 3 + [block, block, small, anywhere]
        out_shape = [many, many, meta, many, many, grads, weights]
        scratch += [
            pltpu.VMEM((tokens, width), BF16),
            pltpu.VMEM((2, tokens, width), BF16),
            pltpu.VMEM((16, tokens), F32),
            dma((groups,)), dma((groups,)), dma((groups,)), dma((groups,)),
            dma, dma((2,)), dma, dma((2 + groups,)), dma((2, 2, 2)),
        ]
    else:
        meta_block = pl.BlockSpec((1, 16, tokens), lambda i, e: (turned(i), 0, 0))
        in_specs = [block, block, meta_block, block, block, small]
        out_specs = [block, block, small, anywhere]
        if stage == "last":
            in_specs[3:5] = [anywhere] * 2
            sources = 3 if groups == 4 else groups
            out_specs = [anywhere] * (3 + sources)
            slots = groups if groups == 4 else 3
            passed = 2 if groups == 4 else 1
            scratch += [
                pltpu.VMEM((2, slots, tokens, width), BF16),
                pltpu.VMEM((passed, passed, tokens // 2, width), BF16),
                pltpu.VMEM((groups, 8, tokens), F32),
                dma((2, 2)), dma((2, 2)), dma((2, 2)),
                dma((groups,)), dma((groups,)), dma((groups,)), dma((groups,)), dma((2 + groups,)),
            ]
        out_shape = [many, many, grads, weights]
        if stage == "last":
            out_shape[:1] = [jax.ShapeDtypeStruct((tokens, width), BF16)] * sources
    remote = {"first": 2, "last": 3}
    return pl.pallas_call(
        functools.partial(expert_kernel, capacity, shards, groups, count, base, stage),
        grid=(groups, count),
        in_specs=in_specs + [anywhere] * (1 + len(kept)),
        out_specs=out_specs,
        out_shape=out_shape,
        scratch_shapes=scratch,
        compiler_params=pltpu.CompilerParams(
            vmem_limit_bytes=62 << 20,
            **({"collective_id": remote[stage], "has_side_effects": True} if stage in remote else {}),
        ),
        cost_estimate=pl.CostEstimate(
            flops=2 * count * total * width * (4 * tokens + 9 * FF),
            bytes_accessed=6 * groups * tokens * width * 2,
            transcendentals=count * total * FF,
        ),
        name="experts_" + stage,
    )(*data, packed_weights, *kept)


def norm_back(values, gain_row, grad_rows):
    scale_rows = lax.rsqrt(jnp.mean(values * values, axis=-1, keepdims=True) + EPSILON)
    weighted = gain_row * grad_rows
    inner_mean = jnp.mean(weighted * values, axis=-1, keepdims=True)
    input_part = (
        scale_rows * weighted - values * (scale_rows * scale_rows * scale_rows) * inner_mean
    )
    gain_part = jnp.sum(grad_rows * values * scale_rows, axis=0)
    return (input_part, gain_part)


def pack_kernel(
    cuts, expand_ref, project_ref, qkv_ref, gains_ref, router_ref, packed_ref, *refs
):
    *outs, misc = refs
    short = project_ref.shape[1]
    tall = expand_ref.shape[1]
    side = project_ref.shape[2] - 2 * FF
    for (low, high), out in zip(cuts, outs):
        for e in range(low, high):
            out[e - low, :tall] = expand_ref[e]
            out[e - low, tall : tall + short] = project_ref[e, :, : 2 * FF]
            out[e - low, tall + short :, :side] = project_ref[e, : short // 2, 2 * FF :]
            out[e - low, tall + short :, side:] = project_ref[e, short // 2 :, 2 * FF :]
    for j in range(PAIRS):
        at, to = HEADS * HEAD + j * KW, j * BLOCK + QW
        packed_ref[:, j * BLOCK : to] = qkv_ref[:, j * QW : (j + 1) * QW]
        packed_ref[:, to : to + KW] = qkv_ref[:, at : at + KW]
        at += KV_HEADS * HEAD
        packed_ref[:, to + KW : to + 2 * KW] = qkv_ref[:, at : at + KW]
    misc[...] = jnp.zeros(misc.shape, F32)
    misc[0:2] = gains_ref[...].astype(F32)
    misc[8 : 8 + router_ref.shape[0]] = router_ref[...].astype(F32)
    packed_ref[:, PAIRS * BLOCK :] = misc[...].T.astype(BF16)


def pack_weights(expand, project, qkv, gain_one, gain_two, router):
    cuts = bands(expand.shape[0])
    rows = expand.shape[1] + project.shape[1] + project.shape[1] // 2
    return pl.pallas_call(
        functools.partial(pack_kernel, cuts),
        out_shape=[jax.ShapeDtypeStruct((qkv.shape[0], PAIRS * BLOCK + MISC), BF16)]
        + [jax.ShapeDtypeStruct((high - low, rows, 2 * FF), BF16) for low, high in cuts],
        scratch_shapes=[pltpu.VMEM((MISC, qkv.shape[0]), F32)],
        compiler_params=pltpu.CompilerParams(vmem_limit_bytes=62 << 20),
        name="pack_weights",
    )(expand, project, qkv, jnp.stack([gain_one, gain_two]), router.T)


def hidden_back_kernel(
    dx_ref, gg_ref, gates_ref, router_ref, hidden_ref, gain_ref, up_ref, ffn_ref,
    grads_ref, low_ref, router_grad_ref, gain_grad_ref,
):
    gates, groups = gates_ref[...], gg_ref.shape[0]
    count = gates.shape[0] // groups
    gate_grads = jnp.concatenate([gg_ref[g, :count] for g in range(groups)], axis=0)
    mean = jnp.sum(gates * gate_grads, axis=0, keepdims=True)
    logit_grads = (gates * (gate_grads - mean)).astype(BF16)
    ffn_grads = dot_tn(logit_grads, router_ref[...])
    for g in range(dx_ref.shape[0]):
        ffn_grads = ffn_grads + dx_ref[g].astype(F32)
    hidden = hidden_ref[...]
    part, gain_part = norm_back(hidden, gain_ref[...].astype(F32), ffn_grads)
    hidden_grads = up_ref[...].astype(F32) + part
    grads_ref[...] = hidden_grads
    low_ref[...] = hidden_grads.astype(BF16)
    router_part = dot_nn(logit_grads, ffn_ref[...])

    @pl.when(pl.program_id(0) == 0)
    def _():
        router_grad_ref[...] = router_part
        gain_grad_ref[...] = gain_part[None]

    @pl.when(pl.program_id(0) > 0)
    def _():
        router_grad_ref[...] += router_part
        gain_grad_ref[...] += gain_part[None]


def hidden_back(sources, dx_home, gg_home, gates, router_rows, hidden, gain_row, out_grad, ffn_in):
    groups, tokens, width = dx_home.shape
    experts = gates.shape[0]
    step = 128
    rows = pl.BlockSpec((step, width), lambda i: (i, 0))
    return pl.pallas_call(
        hidden_back_kernel,
        grid=(tokens // step,),
        in_specs=[
            pl.BlockSpec((sources, step, width), lambda i: (0, i, 0)),
            pl.BlockSpec((groups, 8, step), lambda i: (0, 0, i)),
            pl.BlockSpec((experts, step), lambda i: (0, i)),
            whole_spec((experts, width)),
            rows,
            whole_spec((1, width)),
            rows,
            rows,
        ],
        out_specs=[rows, rows, whole_spec((experts, width)), whole_spec((1, width))],
        out_shape=[
            jax.ShapeDtypeStruct((tokens, width), F32),
            jax.ShapeDtypeStruct((tokens, width), BF16),
            jax.ShapeDtypeStruct((experts, width), F32),
            jax.ShapeDtypeStruct((1, width), F32),
        ],
        compiler_params=pltpu.CompilerParams(vmem_limit_bytes=62 << 20),
        cost_estimate=pl.CostEstimate(flops=10**8, bytes_accessed=20 << 20, transcendentals=0),
        name="hidden_back",
    )(dx_home, gg_home, gates, router_rows, hidden, gain_row, out_grad, ffn_in)


def input_back_kernel(
    dproj_ref, w_ref, x_ref, gain_ref, hidden_grads_ref, grad_ref, gain_grad_ref, held, inner, scale
):
    c, step = pl.program_id(0), w_ref.shape[0]
    width = x_ref.shape[1]
    at = pl.ds(pl.multiple_of(c * step, step), step)

    @pl.when(c == 0)
    def _():
        x = x_ref[...].astype(F32)
        scale[...] = lax.rsqrt(jnp.mean(x * x, axis=-1, keepdims=True) + EPSILON)
        inner[...] = jnp.zeros(inner.shape, F32)

    normed_grads = dot_nt(dproj_ref[...], w_ref[...])
    x = x_ref[:, at].astype(F32)
    weighted = normed_grads * gain_ref[:, at].astype(F32)
    product = weighted * x
    inner[...] += jnp.sum(product, axis=-1, keepdims=True)
    gain_grad_ref[:, at] = jnp.sum(normed_grads * x * scale[...], axis=0, keepdims=True)
    held[:, at] = weighted

    @pl.when(c == pl.num_programs(0) - 1)
    def _():
        r = scale[...]
        factor = r * r * r * (inner[...] * (1.0 / width))
        for low in range(0, width, step):
            cols = slice(low, low + step)
            grad_ref[:, cols] = (
                hidden_grads_ref[:, cols] + r * held[:, cols] - x_ref[:, cols].astype(F32) * factor
            )


def input_back(dproj, w_full, x, gain_row, hidden_grads):
    tokens, width = x.shape
    step = 256
    return pl.pallas_call(
        input_back_kernel,
        grid=(width // step,),
        in_specs=[
            whole_spec((tokens, dproj.shape[1])),
            pl.BlockSpec((step, dproj.shape[1]), lambda i: (i, 0)),
            whole_spec((tokens, width)),
            whole_spec((1, width)),
            whole_spec((tokens, width)),
        ],
        out_specs=[whole_spec((tokens, width)), whole_spec((1, width))],
        out_shape=[
            jax.ShapeDtypeStruct((tokens, width), F32),
            jax.ShapeDtypeStruct((1, width), F32),
        ],
        scratch_shapes=[
            pltpu.VMEM((tokens, width), F32), pltpu.VMEM((tokens, 1), F32), pltpu.VMEM((tokens, 1), F32),
        ],
        compiler_params=pltpu.CompilerParams(vmem_limit_bytes=62 << 20),
        cost_estimate=pl.CostEstimate(
            flops=2 * tokens * width * dproj.shape[1], bytes_accessed=20 << 20, transcendentals=0
        ),
        name="input_back",
    )(dproj, w_full, x, gain_row, hidden_grads)


def unpack_experts(tall, short, held, expand_ref, project_ref):
    side = project_ref.shape[2] - 2 * FF
    for i in range(held.shape[0]):
        value = held[i].astype(F32)
        expand_ref[i] = value[:tall]
        project_ref[i, :, : 2 * FF] = value[tall : tall + short]
        project_ref[i, : short // 2, 2 * FF :] = value[tall + short :, :side]
        project_ref[i, short // 2 :, 2 * FF :] = value[tall + short :, side:]


def unpack_kernel(tall, short, counts, *refs):
    first_ref, last_ref, hidden_ref, *refs = refs
    others, refs = refs[: counts[2]], refs[counts[2] :]
    out_ref, qkv_ref, few_ref, output_ref, expand_ref, project_ref = refs[:6]
    out_grad_ref, qkv_grad_ref, gain_one_ref, gain_two_ref, router_ref = refs[6:]
    i = pl.program_id(0)

    @pl.when(i < counts[0])
    def _():
        unpack_experts(tall, short, first_ref, expand_ref, project_ref)

    @pl.when(i >= counts[0])
    def _():
        unpack_experts(tall, short, last_ref, expand_ref, project_ref)

    @pl.when(i < 4)
    def _():
        total = hidden_ref[...]
        for other in others:
            total = total + other[...].astype(F32)
        output_ref[...] = total.astype(BF16)

    @pl.when(i == 4)
    def _():
        tile = 128
        chunk = out_ref.shape[2]
        for at in range(0, out_grad_ref.shape[1], tile):
            out_grad_ref[:, at : at + tile] = out_ref[
                at // chunk, :, at % chunk : at % chunk + tile
            ].astype(F32)
        chunk = qkv_ref.shape[2]
        for at in range(0, qkv_grad_ref.shape[1], tile):
            value = qkv_ref[at // chunk, :, at % chunk : at % chunk + tile].astype(F32)
            j, inside = divmod(at, BLOCK)
            if inside < QW:
                to = j * QW + inside
            elif inside < QW + KW:
                to = PAIRS * QW + j * KW + inside - QW
            else:
                to = PAIRS * (QW + KW) + j * KW + inside - QW - KW
            qkv_grad_ref[:, to : to + tile] = value
        gain_one_ref[...] = few_ref[0:1]
        gain_two_ref[...] = few_ref[1:2]
        router_ref[...] = few_ref[8 : 8 + router_ref.shape[0]]


def unpack_weights(shares, out_total, qkv_total, few, hidden, out_home, tall, short, experts):
    tokens, width = hidden.shape
    rows = out_total.shape[1]
    first, last = shares
    counts = (first.shape[0], last.shape[0], len(out_home))
    count = counts[0] + counts[1]
    step = tokens // 4
    block = pl.BlockSpec((step, width), lambda i: (jnp.minimum(i, 3), 0))
    one = (1,) + first.shape[1:]
    return pl.pallas_call(
        functools.partial(unpack_kernel, tall, short, counts),
        grid=(count,),
        in_specs=[
            pl.BlockSpec(one, lambda i: (jnp.minimum(i, counts[0] - 1), 0, 0)),
            pl.BlockSpec(one, lambda i: (jnp.maximum(i - counts[0], 0), 0, 0)),
        ]
        + [block] * (1 + len(out_home))
        + [whole_spec(out_total.shape), whole_spec(qkv_total.shape), whole_spec(few.shape)],
        out_specs=[
            block,
            pl.BlockSpec((1, tall, 2 * FF), lambda i: (i, 0, 0)),
            pl.BlockSpec((1, short, width), lambda i: (i, 0, 0)),
            whole_spec((rows, HEADS * HEAD)),
            whole_spec((rows, PAIRS * BLOCK)),
            whole_spec((1, rows)),
            whole_spec((1, rows)),
            whole_spec((experts, rows)),
        ],
        out_shape=[
            jax.ShapeDtypeStruct(hidden.shape, BF16),
            jax.ShapeDtypeStruct((count, tall, 2 * FF), F32),
            jax.ShapeDtypeStruct((count, short, width), F32),
            jax.ShapeDtypeStruct((rows, HEADS * HEAD), F32),
            jax.ShapeDtypeStruct((rows, PAIRS * BLOCK), F32),
            jax.ShapeDtypeStruct((1, rows), F32),
            jax.ShapeDtypeStruct((1, rows), F32),
            jax.ShapeDtypeStruct((experts, rows), F32),
        ],
        compiler_params=pltpu.CompilerParams(vmem_limit_bytes=62 << 20),
        cost_estimate=pl.CostEstimate(flops=10**7, bytes_accessed=24 << 20, transcendentals=0),
        name="unpack_weights",
    )(first, last, hidden, *out_home, out_total, qkv_total, few)


def exchanged(value, flip, groups):
    if flip == 0:
        return value
    return lax.ppermute(value, "expert", [(i, i ^ flip) for i in range(groups)])


def bands(count):
    return [(0, 2), (2, 3), (3, count)]


def local(
    inputs, attn_gain, qkv_weight, out_weight, ffn_gain, router_weight,
    expand_weight, project_weight, segment_ids, routes, out_grad,
):
    groups, shards = lax.axis_size("expert"), lax.axis_size("shard")
    tokens, width = inputs.shape
    experts = router_weight.shape[1]
    local_count = expand_weight.shape[0]
    capacity = 8 * ((5 * tokens * TOP + 32 * experts - 1) // (32 * experts))

    packed, *bands_packed = pack_weights(
        expand_weight, project_weight, qkv_weight, attn_gain, ffn_gain, router_weight
    )
    packed_full = [lax.all_gather(p, "shard", axis=0) for p in bands_packed]
    qkv_full, out_part, *u_others = gather_weights(
        [packed, out_weight], out_grad, groups, shards
    )
    qkv_full = qkv_full.reshape(width, -1)
    misc_rows = qkv_full[:, PAIRS * BLOCK :].T
    gain_one, gain_two = misc_rows[0:1], misc_rows[1:2]
    router_rows = misc_rows[8 : 8 + experts]
    tables = tuple(jnp.asarray(t) for t in rope_tables())
    seg_row = segment_ids.reshape(1, tokens)
    seg_col = segment_ids.reshape(tokens, 1)
    normed, proj, mixed, lse, out_full = attention_forward(
        inputs, gain_one, qkv_full, tables, seg_col, seg_row, out_part, groups, shards
    )
    hidden, ffn_in, gates, meta_own = middle(
        mixed, out_full, inputs, gain_two, router_rows, routes.T, groups
    )
    tall, short = expand_weight.shape[1], project_weight.shape[1]
    call = functools.partial(expert_call, capacity, shards, groups)

    cores = [[2 * z + core for z in range(shards // 2)] for core in range(2)]

    def share_out(dw):
        return lax.psum_scatter(
            dw, "shard", scatter_dimension=0, axis_index_groups=cores, tiled=True
        )[0]

    x_all, u_all, meta, out_acc, dx_acc, gg, dw = call(
        0, "first", (ffn_in, meta_own, out_grad, *u_others), packed_full[0]
    )
    shares = [share_out(dw)]
    out_acc, dx_acc, gg, dw = call(
        2, "between", (x_all, u_all, meta, out_acc, dx_acc, gg), packed_full[1]
    )
    *out_sent, dx_home, gg_home, dw = call(
        3, "last", (x_all, u_all, meta, out_acc, dx_acc, gg), packed_full[2], dw
    )
    shares.append(share_out(dw))
    sources = 3 if groups == 4 else groups
    hidden_grads, attended_grads, router_part, gain_two_grad = hidden_back(
        sources, dx_home, gg_home, gates, router_rows, hidden, gain_two, out_grad, ffn_in
    )
    dproj, out_sum = attention_backward(
        attended_grads, out_full, proj, mixed, lse, tables, seg_col, seg_row, groups, shards
    )
    input_grad, gain_one_grad = input_back(dproj, qkv_full, inputs, gain_one, hidden_grads)

    dproj, shares[0], *out_sent = lax.optimization_barrier((dproj, shares[0], *out_sent))
    out_home = [exchanged(o, t, groups) for t, o in enumerate(out_sent)]
    out_total, qkv_total, few = reduce_weights(
        normed, dproj, gain_one_grad, gain_two_grad, router_part, out_sum, groups, shards
    )
    out_total, *out_home = lax.optimization_barrier((out_total, *out_home))
    output, expand_grad, project_grad, out_weight_grad, qkv_grad, *gains = unpack_weights(
        shares, out_total, qkv_total, few, hidden, out_home, tall, short, experts
    )
    return (
        output,
        input_grad,
        gains[0][0],
        qkv_grad,
        out_weight_grad,
        gains[1][0],
        gains[2].T,
        expand_grad,
        project_grad,
    )


def solution(mesh):
    rows = P(("expert", "shard"), None)
    return jax.shard_map(
        local,
        mesh=mesh,
        in_specs=(
            rows, P("shard"), P("shard", None), P("shard", None), P("shard"), P("shard", None),
            P("expert", "shard", None), P("expert", "shard", None), rows, rows, rows,
        ),
        out_specs=(
            rows, rows, P("shard"), P("shard", None), P("shard", None), P("shard"),
            P("shard", None), P("expert", "shard", None), P("expert", "shard", None),
        ),
        check_vma=False,
    )
```

```python
import functools

import jax
import jax.numpy as jnp
import numpy as np
from jax import lax
from jax.experimental import pallas as pl
from jax.experimental.pallas import tpu as pltpu
from jax.sharding import PartitionSpec as P

HEADS = 24
KV_HEADS = 8
HEAD = 64
FF = 512
TOP = 8
SEQ_LEN = 512
GROUP = HEADS // KV_HEADS
PAIRS = KV_HEADS // 2
QW = 2 * GROUP * HEAD
KW = 2 * HEAD
BLOCK = QW + 2 * KW
MISC = 128
QB = 128

EPSILON = 1e-06
ROPE_THETA = 10000.0
MASKED = -1e30
F32 = jnp.float32
BF16 = jnp.bfloat16


def dot_nn(a, b):
    return lax.dot_general(a, b, (((1,), (0,)), ((), ())), preferred_element_type=F32)


def dot_nt(a, b):
    return lax.dot_general(a, b, (((1,), (1,)), ((), ())), preferred_element_type=F32)


def dot_tn(a, b):
    return lax.dot_general(a, b, (((0,), (0,)), ((), ())), preferred_element_type=F32)


def rope_tables():
    frequency = (np.float32(ROPE_THETA) ** (-2.0 * np.arange(HEAD // 2) / HEAD)).astype(np.float32)
    angle = np.arange(SEQ_LEN, dtype=np.float32)[:, None] * frequency[None, :]
    cosine, sine = np.cos(angle).astype(np.float32), np.sin(angle).astype(np.float32)
    zero = np.zeros_like(sine)
    cos_table = np.concatenate([cosine] * 4, axis=1)
    left_table = np.concatenate([-sine, zero] * 2, axis=1)
    right_table = np.concatenate([zero, sine] * 2, axis=1)
    return cos_table, left_table, right_table


def turn(values, cos_table, left_table, right_table, sign):
    parts = []
    for c in range(values.shape[1] // 128):
        piece = values[:, 128 * c : 128 * (c + 1)]
        ahead = pltpu.roll(piece, 96, 1) * left_table
        behind = pltpu.roll(piece, 32, 1) * right_table
        parts.append(piece * cos_table + sign * (ahead + behind))
    return parts[0] if len(parts) == 1 else jnp.concatenate(parts, axis=1)


def key_range(block):
    return max(0, block - 2) * QB, (block + 1) * QB


def block_mask(seg_col, seg_row, block):
    low, high = key_range(block)
    rows = lax.broadcasted_iota(jnp.int32, (QB, high - low), 0) + block * QB
    cols = lax.broadcasted_iota(jnp.int32, (QB, high - low), 1) + low
    same = seg_col[block * QB : (block + 1) * QB, :] == seg_row[:, low:high]
    return jnp.concatenate([(rows >= cols) & same] * GROUP, axis=0)


def heads_of(values, pair, block):
    rows = values[block * QB : (block + 1) * QB, :]
    first = pair * GROUP
    return jnp.concatenate(
        [rows[:, HEAD * h : HEAD * (h + 1)] for h in range(first, first + GROUP)], axis=0
    )


def attention_forward_kernel(
    parts, levels, x_ref, gain_ref, w_ref, cos_ref, left_ref, right_ref, seg_col_ref, seg_row_ref,
    part_ref, normed_t_ref, proj_ref, mixed_ref, lse_ref, full_ref, normed_ref, *sems,
):
    step = pl.program_id(0)
    plan = Gather(parts, levels, [full_ref], sems)

    @pl.when(step == 0)
    def _():
        plan.greet(near=False)
        plan.own_to_mate(lambda: full_ref.at[pl.ds(plan.shard * parts, parts)], 0)
        for k in range(1, levels):
            plan.spread(0, k)

    @pl.when(step == 0)
    def _():
        x = x_ref[...].astype(F32)
        scale = lax.rsqrt(jnp.mean(x * x, axis=-1, keepdims=True) + EPSILON)
        normed = (x * scale * gain_ref[...].astype(F32)).astype(BF16)
        normed_ref[...] = normed
        normed_t_ref[...] = normed.T

    projected = dot_nn(normed_ref[...], w_ref[...])
    turned = turn(
        projected[:, : QW + KW], cos_ref[...], left_ref[...], right_ref[...], 1.0
    ).astype(BF16)
    queries, keys = turned[:, :QW], turned[:, QW:]
    values = projected[:, QW + KW :].astype(BF16)
    proj_ref[...] = jnp.concatenate([turned, values], axis=1)
    seg_col, seg_row = seg_col_ref[...], seg_row_ref[...]
    for block in range(SEQ_LEN // QB):
        low, high = key_range(block)
        allowed = block_mask(seg_col, seg_row, block)
        outs = []
        for pair in range(2):
            q3 = heads_of(queries, pair, block)
            k1 = keys[low:high, HEAD * pair : HEAD * (pair + 1)]
            v1 = values[low:high, HEAD * pair : HEAD * (pair + 1)]
            scores = jnp.where(allowed, dot_nt(q3, k1) * HEAD**-0.5, MASKED)
            top = jnp.max(scores, axis=-1, keepdims=True)
            weights = jnp.exp(scores - top)
            total = jnp.sum(weights, axis=-1, keepdims=True)
            mixed = dot_nn(weights.astype(BF16), v1) * (1.0 / total)
            logsum = top + jnp.log(total)
            for h in range(GROUP):
                outs.append(mixed[h * QB : (h + 1) * QB, :])
                lse_ref[0, block * QB : (block + 1) * QB, pair * GROUP + h : pair * GROUP + h + 1] = (
                    logsum[h * QB : (h + 1) * QB, :]
                )
        mixed_ref[block * QB : (block + 1) * QB, :] = jnp.concatenate(outs, axis=1).astype(BF16)

    @pl.when(step == PAIRS - 1)
    def _():
        plan.team_to_mate(0)
        plan.mate_arrived(0)
        plan.finish()


def whole_spec(shape):
    return pl.BlockSpec(shape, lambda *_: (0,) * len(shape))


def attention_forward(x, gain_row, w_full, tables, seg_col, seg_row, out_part, groups, shards):
    tokens, width = x.shape
    parts, levels = gather_parts(groups, width // shards), shards // 2
    table = whole_spec((SEQ_LEN, 128))
    *kept, out_full = pl.pallas_call(
        functools.partial(attention_forward_kernel, parts, levels),
        grid=(PAIRS,),
        in_specs=[
            whole_spec((tokens, width)),
            whole_spec((1, width)),
            pl.BlockSpec((width, BLOCK), lambda j: (0, j)),
            table, table, table,
            whole_spec((SEQ_LEN, 1)),
            whole_spec((1, SEQ_LEN)),
            pl.BlockSpec(memory_space=pl.ANY),
        ],
        out_specs=[
            whole_spec((width, tokens)),
            pl.BlockSpec((tokens, BLOCK), lambda j: (0, j)),
            pl.BlockSpec((tokens, QW), lambda j: (0, j)),
            pl.BlockSpec((1, tokens, 8), lambda j: (j, 0, 0)),
            pl.BlockSpec(memory_space=pl.ANY),
        ],
        out_shape=[
            jax.ShapeDtypeStruct((width, tokens), BF16),
            jax.ShapeDtypeStruct((tokens, PAIRS * BLOCK), BF16),
            jax.ShapeDtypeStruct((tokens, HEADS * HEAD), BF16),
            jax.ShapeDtypeStruct((PAIRS, tokens, 8), F32),
            jax.ShapeDtypeStruct(out_part.shape, BF16),
        ],
        scratch_shapes=[pltpu.VMEM((tokens, width), BF16)] + gather_sems(levels, parts, 1),
        input_output_aliases={8: 4},
        compiler_params=pltpu.CompilerParams(
            vmem_limit_bytes=62 << 20, collective_id=4, has_side_effects=True
        ),
        cost_estimate=pl.CostEstimate(flops=10 * 10**9, bytes_accessed=20 << 20, transcendentals=4 << 20),
        name="attention_forward",
    )(x, gain_row, w_full, *tables, seg_col, seg_row, out_part)
    return *kept, out_full.reshape(width, -1)


def attention_backward_kernel(
    groups, levels, ag_ref, out_ref, proj_ref, mixed_ref, lse_ref, cos_ref, left_ref, right_ref,
    seg_col_ref, seg_row_ref, all_ref, dproj_ref, sum_ref, mixed_t, *rest,
):
    step = pl.program_id(0)
    plan = Reduce(groups, levels, ag_ref.shape[1], rest[:4], rest[4:])

    @pl.when(step == 0)
    def _():
        plan.greet(False)
        mixed_t[...] = all_ref[...].T
        plan.fill(mixed_t, ag_ref)

    @pl.when(step == 1)
    def _():
        plan.merge()

    @pl.when(step == 2)
    def _():
        plan.spread()

    grads = dot_nt(ag_ref[...], out_ref[...]).astype(BF16)
    product = grads.astype(F32) * mixed_ref[...].astype(F32)
    queries, keys, values = (
        proj_ref[:, :QW], proj_ref[:, QW : QW + KW], proj_ref[:, QW + KW :],
    )
    seg_col, seg_row = seg_col_ref[...], seg_row_ref[...]
    blocks = SEQ_LEN // QB
    dk = [[jnp.zeros((QB, HEAD), F32) for _ in range(blocks)] for _ in range(2)]
    dv = [[jnp.zeros((QB, HEAD), F32) for _ in range(blocks)] for _ in range(2)]
    dq_rows = []
    for block in range(blocks):
        low, high = key_range(block)
        allowed = block_mask(seg_col, seg_row, block)
        dqs = []
        for pair in range(2):
            q3, g3, o3 = (heads_of(v, pair, block) for v in (queries, grads, product))
            k1 = keys[low:high, HEAD * pair : HEAD * (pair + 1)]
            v1 = values[low:high, HEAD * pair : HEAD * (pair + 1)]
            logsum = jnp.concatenate(
                [
                    lse_ref[0, block * QB : (block + 1) * QB, pair * GROUP + h : pair * GROUP + h + 1]
                    for h in range(GROUP)
                ],
                axis=0,
            )
            scores = jnp.where(allowed, dot_nt(q3, k1) * HEAD**-0.5, MASKED)
            probs = jnp.exp(scores - logsum)
            inner = jnp.sum(o3, axis=-1, keepdims=True)
            score_grads = (probs * (dot_nt(g3, v1) - inner)).astype(BF16)
            dq = dot_nn(score_grads, k1)
            dk_part = dot_tn(score_grads, q3)
            dv_part = dot_tn(probs.astype(BF16), g3)
            for at in range(low // QB, high // QB):
                rows = slice(at * QB - low, (at + 1) * QB - low)
                dk[pair][at] += dk_part[rows]
                dv[pair][at] += dv_part[rows]
            dqs += [dq[h * QB : (h + 1) * QB, :] for h in range(GROUP)]
        dq_rows.append(jnp.concatenate(dqs, axis=1))
    dq_all = jnp.concatenate(dq_rows, axis=0)
    dk_all = jnp.concatenate([jnp.concatenate(d, axis=0) for d in dk], axis=1)
    dv_all = jnp.concatenate([jnp.concatenate(d, axis=0) for d in dv], axis=1)
    turned = jnp.concatenate([dq_all, dk_all], axis=1) * HEAD**-0.5
    back = turn(turned, cos_ref[...], left_ref[...], right_ref[...], -1.0)
    dproj_ref[...] = jnp.concatenate([back, dv_all], axis=1).astype(BF16)

    @pl.when(step == PAIRS - 1)
    def _():
        for k in range(levels):
            sum_ref[k] = plan.collect(k).astype(BF16)
        plan.finish()


def attention_backward(ag, out_full, proj, mixed, lse, tables, seg_col, seg_row, groups, shards):
    tokens, width = ag.shape
    levels, rows = shards // 2, width // shards
    chunk = chunk_of(width, groups)
    table = whole_spec((SEQ_LEN, 128))
    return pl.pallas_call(
        functools.partial(attention_backward_kernel, groups, levels),
        grid=(PAIRS,),
        in_specs=[
            whole_spec((tokens, width)),
            pl.BlockSpec((QW, width), lambda j: (j, 0)),
            pl.BlockSpec((tokens, BLOCK), lambda j: (0, j)),
            pl.BlockSpec((tokens, QW), lambda j: (0, j)),
            pl.BlockSpec((1, tokens, 8), lambda j: (j, 0, 0)),
            table, table, table,
            whole_spec((SEQ_LEN, 1)),
            whole_spec((1, SEQ_LEN)),
            whole_spec((tokens, mixed.shape[1])),
        ],
        out_specs=[
            pl.BlockSpec((tokens, BLOCK), lambda j: (0, j)),
            whole_spec((levels, rows, chunk)),
        ],
        out_shape=[
            jax.ShapeDtypeStruct((tokens, PAIRS * BLOCK), BF16),
            jax.ShapeDtypeStruct((levels, rows, chunk), BF16),
        ],
        scratch_shapes=[pltpu.VMEM((mixed.shape[1], tokens), BF16)]
        + reduce_buffers(groups, levels, rows, chunk)
        + reduce_sems(groups, levels),
        compiler_params=pltpu.CompilerParams(
            vmem_limit_bytes=62 << 20, collective_id=5, has_side_effects=True
        ),
        cost_estimate=pl.CostEstimate(flops=10 * 10**9, bytes_accessed=20 << 20, transcendentals=4 << 20),
        name="attention_backward",
    )(ag, out_full, proj, mixed, lse, *tables, seg_col, seg_row, mixed)


def middle_kernel(
    mixed_ref, out_ref, x_ref, gain_ref, router_ref, routes_ref,
    hidden_ref, ffn_ref, gates_ref, meta_ref,
):
    hidden = x_ref[...].astype(F32) + dot_nn(mixed_ref[...], out_ref[...])
    scale = lax.rsqrt(jnp.mean(hidden * hidden, axis=-1, keepdims=True) + EPSILON)
    hidden_ref[...] = hidden
    ffn_in = (hidden * scale * gain_ref[...].astype(F32)).astype(BF16)
    ffn_ref[...] = ffn_in
    logits = dot_nt(router_ref[...], ffn_in)
    experts, tokens = logits.shape
    index = lax.broadcasted_iota(jnp.int32, (experts, tokens), 0)
    flags = index == routes_ref[0:1, :]
    for k in range(1, TOP):
        flags = flags | (index == routes_ref[k : k + 1, :])
    chosen = jnp.where(flags, logits, MASKED)
    weights = jnp.where(flags, jnp.exp(chosen - jnp.max(chosen, axis=0, keepdims=True)), 0.0)
    gates = weights / jnp.sum(weights, axis=0, keepdims=True)
    gates_ref[...] = gates
    earlier = lax.broadcasted_iota(jnp.int32, (tokens, tokens), 0)
    later = lax.broadcasted_iota(jnp.int32, (tokens, tokens), 1)
    before = jnp.where(earlier < later, 1.0, 0.0).astype(BF16)
    ranks = dot_nn(jnp.where(flags, 1.0, 0.0).astype(BF16), before)
    slots = jnp.where(flags, ranks, -1.0)
    groups = meta_ref.shape[0]
    count = experts // groups
    meta_ref[...] = jnp.zeros(meta_ref.shape, F32)
    for e in range(experts):
        meta_ref[e // count, e % count : e % count + 1, :] = slots[e : e + 1]
        meta_ref[e // count, 8 + e % count : 9 + e % count, :] = gates[e : e + 1]


def middle(mixed, out_full, x, gain_row, router_rows, routes_rows, groups):
    tokens, width = x.shape
    experts = router_rows.shape[0]
    return pl.pallas_call(
        middle_kernel,
        out_shape=[
            jax.ShapeDtypeStruct((tokens, width), F32),
            jax.ShapeDtypeStruct((tokens, width), BF16),
            jax.ShapeDtypeStruct((experts, tokens), F32),
            jax.ShapeDtypeStruct((groups, 16, tokens), F32),
        ],
        compiler_params=pltpu.CompilerParams(vmem_limit_bytes=48 << 20),
        cost_estimate=pl.CostEstimate(flops=3 * 10**9, bytes_accessed=16 << 20, transcendentals=1 << 14),
        name="middle",
    )(mixed, out_full, x, gain_row, router_rows, routes_rows)


def flipped(index, mask):
    out, bit = index, 1
    while bit <= mask:
        if mask & bit:
            out = out + bit - 2 * bit * ((index // bit) % 2)
        bit *= 2
    return out


def send(source, target, send_sem, recv_sem, device):
    return pltpu.make_async_remote_copy(
        src_ref=source, dst_ref=target, send_sem=send_sem, recv_sem=recv_sem,
        device_id=device, device_id_type=pl.DeviceIdType.MESH,
    )


def greet(devices):
    barrier = pltpu.get_barrier_semaphore()
    for device in devices:
        pl.semaphore_signal(barrier, inc=1, device_id=device, device_id_type=pl.DeviceIdType.MESH)
    pl.semaphore_wait(barrier, len(devices))


class Gather:
    def __init__(self, parts, levels, blocks, sems):
        self.parts, self.levels, self.blocks = parts, levels, blocks
        self.near_send, self.near_recv, self.team_send, self.team_recv, self.core_send, self.core_recv = sems
        self.group, self.shard = lax.axis_index("expert"), lax.axis_index("shard")
        level, self.core = self.shard // 2, self.shard % 2
        self.part = self.group % parts
        self.other = self.shard + 1 - 2 * self.core
        self.far = [flipped(level, k) * 2 + self.core for k in range(levels)]
        self.far_other = [flipped(level, k) * 2 + 1 - self.core for k in range(levels)]
        self.team_part = [flipped(self.part, k) for k in range(parts)]
        self.team = [self.group - self.part + t for t in self.team_part]
        self.mate = (self.group, self.other)
        self.sends = []

    def greet(self, near=True):
        greet(
            [self.mate]
            + [(self.group, self.far[k]) for k in range(1, self.levels) if near]
            + [(self.team[t], self.shard) for t in range(1, self.parts)]
        )

    def push(self, make):
        make().start()
        self.sends.append(make)

    def arrived(self, piece, send_sem, recv_sem):
        send(piece, piece, send_sem, recv_sem, self.mate).wait_recv()

    def near(self, own, i):
        for k in range(1, self.levels):
            self.push(
                lambda k=k: send(
                    own.at[self.part], self.blocks[i].at[self.shard * self.parts + self.part],
                    self.near_send.at[i, k], self.near_recv.at[i, k], (self.group, self.far[k]),
                )
            )

    def near_arrived(self, i, k):
        piece = self.blocks[i].at[self.far[k] * self.parts + self.part]
        self.arrived(piece, self.near_send.at[i, k], self.near_recv.at[i, k])

    def spread(self, i, k):
        def piece():
            return self.blocks[i].at[self.far[k] * self.parts + self.part]

        for t in range(1, self.parts):
            self.push(
                lambda t=t: send(
                    piece(), piece(), self.team_send.at[i, k, t], self.team_recv.at[i, k, t],
                    (self.team[t], self.shard),
                )
            )
        self.push(
            lambda: send(
                piece(), piece(), self.core_send.at[i, k, 0], self.core_recv.at[i, k, 0], self.mate
            )
        )

    def own_to_mate(self, own, i):
        self.push(
            lambda: send(
                own(), self.blocks[i].at[pl.ds(self.shard * self.parts, self.parts)],
                self.core_send.at[i, 0, 0], self.core_recv.at[i, 0, 0], self.mate,
            )
        )

    def team_to_mate(self, i):
        for k in range(1, self.levels):
            for t in range(1, self.parts):

                def piece(k=k, t=t):
                    return self.blocks[i].at[self.far[k] * self.parts + self.team_part[t]]

                self.arrived(piece(), self.team_send.at[i, k, t], self.team_recv.at[i, k, t])
                self.push(
                    lambda piece=piece, k=k, t=t: send(
                        piece(), piece(), self.core_send.at[i, k, t], self.core_recv.at[i, k, t],
                        self.mate,
                    )
                )

    def mate_arrived(self, i):
        piece = self.blocks[i].at[pl.ds(self.other * self.parts, self.parts)]
        self.arrived(piece, self.core_send.at[i, 0, 0], self.core_recv.at[i, 0, 0])
        for k in range(1, self.levels):
            for t in range(self.parts):
                piece = self.blocks[i].at[self.far_other[k] * self.parts + self.team_part[t]]
                self.arrived(piece, self.core_send.at[i, k, t], self.core_recv.at[i, k, t])

    def finish(self):
        for make in self.sends:
            make().wait_send()


def gather_sems(levels, parts, count):
    dma = pltpu.SemaphoreType.DMA
    return [dma((count, levels))] * 2 + [dma((count, levels, parts))] * 4


def gather_parts(groups, rows):
    return next(p for p in (4, 2, 1) if groups % p == 0 and rows % (16 * p) == 0)


class Rows:
    def __init__(self, groups, own, outs, sems):
        self.own, self.outs = own, outs
        self.send_sem, self.recv_sem = sems
        group, self.shard = lax.axis_index("expert"), lax.axis_index("shard")
        self.team = [flipped(group, t) for t in range(groups)]
        self.near = range(1, 1 + len(outs))

    def copy(self, t):
        return send(
            self.own, self.outs[t - 1], self.send_sem.at[t], self.recv_sem.at[t],
            (self.team[t], self.shard),
        )

    def start(self):
        for t in self.near:
            self.copy(t).start()

    def finish(self):
        for t in self.near:
            self.copy(t).wait()


def gather_kernel(groups, parts, levels, *refs):
    ins, own_rows, outs, refs = refs[:2], refs[2], refs[3:5], refs[5:]
    count = 2 if groups == 4 else groups - 1
    others, refs = refs[:count], refs[count:]
    bounce, local_sem = refs[:2], refs[2]
    plan = Gather(parts, levels, outs, refs[3:9])
    rows = Rows(groups, own_rows, others, refs[9:11])
    greet(
        [plan.mate]
        + [(plan.group, plan.far[k]) for k in range(1, levels)]
        + [(rows.team[t], rows.shard) for t in range(1, groups)]
    )
    own = pl.ds(plan.shard * parts, parts)
    loads = [pltpu.make_async_copy(ins[i], bounce[i], local_sem.at[0, i]) for i in range(2)]
    stores = [pltpu.make_async_copy(bounce[i], outs[i].at[own], local_sem.at[1, i]) for i in range(2)]
    for copy in loads:
        copy.start()
    for i in range(2):
        plan.near(ins[i], i)
    rows.start()
    plan.own_to_mate(lambda: ins[0], 0)
    for load, store in zip(loads, stores):
        load.wait()
        store.start()
    for k in range(1, levels):
        plan.near_arrived(0, k)
        plan.spread(0, k)
    plan.team_to_mate(0)
    for k in range(1, levels):
        plan.near_arrived(1, k)
    plan.mate_arrived(0)
    plan.finish()
    rows.finish()
    for copy in stores:
        copy.wait()


def gather_weights(blocks, own_rows, groups, shards):
    rows = blocks[0].shape[0]
    parts = gather_parts(groups, rows)
    levels, count = shards // 2, 2 if groups == 4 else groups - 1
    blocks = [b.reshape(parts, rows // parts, b.shape[1]) for b in blocks]
    dma = pltpu.SemaphoreType.DMA
    return pl.pallas_call(
        functools.partial(gather_kernel, groups, parts, levels),
        in_specs=[pl.BlockSpec(memory_space=pl.ANY)] * 3,
        out_specs=[pl.BlockSpec(memory_space=pl.ANY)] * (2 + count),
        out_shape=[
            jax.ShapeDtypeStruct((shards * parts,) + b.shape[1:], b.dtype) for b in blocks
        ]
        + [jax.ShapeDtypeStruct(own_rows.shape, own_rows.dtype)] * count,
        scratch_shapes=[pltpu.VMEM(b.shape, b.dtype) for b in blocks]
        + [dma((2, 2))]
        + gather_sems(levels, parts, 2)
        + [dma((groups,)), dma((groups,))],
        compiler_params=pltpu.CompilerParams(collective_id=0, has_side_effects=True),
        name="gather_weights",
    )(*blocks, own_rows)


class Reduce:
    def __init__(self, groups, levels, cols, refs, sems):
        self.groups, self.levels, self.relay = groups, levels, groups == 4
        self.held, self.from_core, self.passing, self.from_group = refs
        self.core_send, self.core_recv, self.pass_send, self.pass_recv, self.group_send, self.group_recv = sems
        self.group, self.shard = lax.axis_index("expert"), lax.axis_index("shard")
        level, self.core = self.shard // 2, self.shard % 2
        self.mate = (self.group, self.shard + 1 - 2 * self.core)
        self.team = [flipped(self.group, t) for t in range(groups)]
        self.far = [flipped(level, k) for k in range(levels)]
        self.order = sorted(range(levels), key=lambda k: (k & -k or levels, k))
        self.near = [1, 2] if self.relay else list(range(1, groups))
        self.sends = []
        turns = ([3] if self.relay else []) + self.near + [0]
        self.even = self.held.shape[4] * groups == cols
        self.chunks = [self.team[t] if self.even else k for k, t in enumerate(turns)]

    def greet(self, climbs):
        greet(
            [self.mate]
            + [(self.group, self.far[k] * 2 + self.core) for k in range(1, self.levels) if climbs]
            + [(self.team[t], self.shard) for t in range(1, self.groups)]
        )

    def push(self, make):
        make().start()
        self.sends.append(make)

    def arrived(self, piece, send_sem, recv_sem):
        send(piece, piece, send_sem, recv_sem, self.mate).wait_recv()

    def fill(self, left, right):
        rows, chunk = self.held.shape[3:]
        tall = 768
        per = tall // rows
        even = self.even
        for k in self.chunks:
            low = k * chunk
            many = chunk if even else max(0, min(chunk, right.shape[1] - low))
            if many:
                at = pl.ds(pl.multiple_of(low, 128), many) if even else slice(low, low + many)

                @pl.loop(0, left.shape[0] // tall)
                def _(c):
                    part = pl.ds(pl.multiple_of(c * tall, tall), tall)
                    value = dot_nn(left[part, :], right[:, at]).astype(BF16)
                    for i in range(per):
                        s = c * per + i
                        self.held[k, s % 2, s // 2, :, :many] = value[i * rows : (i + 1) * rows]

            self.push(
                lambda k=k: send(
                    self.held.at[k, 1 - self.core], self.from_core.at[k],
                    self.core_send.at[k], self.core_recv.at[k], self.mate,
                )
            )

    def pass_copy(self, part, k):
        half = self.held.shape[3] // 2
        return send(
            self.held.at[self.team[3], self.core, self.far[k], pl.ds(part * half, half)],
            self.passing.at[part, k], self.pass_send.at[part, k], self.pass_recv.at[part, k],
            (self.team[1 + part], self.shard),
        )

    def group_copy(self, t, k):
        return send(
            self.held.at[self.team[t], self.core, self.far[k]], self.from_group.at[t, k],
            self.group_send.at[t, k], self.group_recv.at[t, k], (self.team[t], self.shard),
        )

    def merge(self):
        for n, k in enumerate(self.chunks):
            self.arrived(self.from_core.at[k], self.core_send.at[k], self.core_recv.at[k])

            @pl.loop(0, self.levels)
            def _(z):
                self.held[k, self.core, z] = (
                    self.held[k, self.core, z].astype(F32) + self.from_core[k, z].astype(F32)
                ).astype(BF16)

            if self.relay and n == 0:
                for j in self.order:
                    for part in range(2):
                        self.push(lambda part=part, j=j: self.pass_copy(part, j))
        if not self.relay:
            for j in self.order:
                for t in self.near:
                    self.push(lambda t=t, j=j: self.group_copy(t, j))

    def spread(self):
        if not self.relay:
            return
        half = self.held.shape[3] // 2
        for k in self.order:
            for part in range(2):
                self.arrived(
                    self.passing.at[part, k], self.pass_send.at[part, k], self.pass_recv.at[part, k]
                )
                at = pl.ds(part * half, half)
                piece = self.held.at[self.team[2 - part], self.core, self.far[k], at]
                piece[...] = (piece[...].astype(F32) + self.passing[part, k].astype(F32)).astype(BF16)
            for t in self.near:
                self.push(lambda t=t, k=k: self.group_copy(t, k))

    def collect(self, k):
        total = self.held[self.group, self.core, self.far[k]].astype(F32)
        for t in self.near:
            self.arrived(self.from_group.at[t, k], self.group_send.at[t, k], self.group_recv.at[t, k])
            total = total + self.from_group[t, k].astype(F32)
        return total

    def bits(self):
        return [bit for bit in (1, 2, 4, 8, 16) if bit < self.levels]

    def climb(self, summed, from_level, sems, bit, only=None):
        for k in range(self.levels) if only is None else [only]:
            if k & bit and not k & (bit - 1):
                self.push(
                    lambda k=k: send(
                        summed.at[k], from_level.at[k], sems[0].at[k], sems[1].at[k],
                        (self.group, self.far[bit] * 2 + self.core),
                    )
                )

    def climbed(self, summed, from_level, sems, bit):
        for k in range(self.levels):
            if k & bit and not k & (bit - 1):
                self.arrived(from_level.at[k], sems[0].at[k], sems[1].at[k])
                to = k - bit
                summed[to] = (summed[to].astype(F32) + from_level[k].astype(F32)).astype(BF16)

    def settle(self, summed, home, home_sems):
        home[self.group] = summed[0]
        for t in range(1, self.groups):
            self.push(
                lambda t=t: send(
                    home.at[self.group], home.at[self.group],
                    home_sems[0].at[t], home_sems[1].at[t], (self.team[t], self.shard),
                )
            )

    def landed(self, home, home_sems):
        for t in range(1, self.groups):
            self.arrived(home.at[self.team[t]], home_sems[0].at[t], home_sems[1].at[t])

    def finish(self):
        for make in self.sends:
            make().wait_send()


def chunk_of(total, groups):
    return 128 * (-(-total // (128 * groups)))


def reduce_buffers(groups, levels, rows, chunk):
    piece = (rows, chunk)
    passing = (2, levels, rows // 2, chunk) if groups == 4 else (1, 1, 16, 128)
    return [
        pltpu.VMEM((groups, 2, levels) + piece, BF16),
        pltpu.VMEM((groups, levels) + piece, BF16),
        pltpu.VMEM(passing, BF16),
        pltpu.VMEM((groups, levels) + piece, BF16),
    ]


def reduce_sems(groups, levels):
    dma = pltpu.SemaphoreType.DMA
    return [dma((groups,))] * 2 + [dma((2, levels))] * 2 + [dma((groups, levels))] * 2


class FewRows:
    def __init__(self, plan, refs, sems):
        self.plan = plan
        self.rows, self.from_core, self.from_group, self.pieces, self.from_level = refs
        self.core_send, self.core_recv, self.group_send, self.group_recv, self.level_send, self.level_recv = sems

    def start(self):
        plan = self.plan
        plan.push(
            lambda: send(self.rows, self.from_core, self.core_send, self.core_recv, plan.mate)
        )

    def over_groups(self):
        plan = self.plan
        plan.arrived(self.from_core, self.core_send, self.core_recv)
        total = self.rows[...].astype(F32) + self.from_core[...].astype(F32)
        self.from_group[plan.group] = total.astype(BF16)
        for t in range(1, plan.groups):
            plan.push(
                lambda t=t: send(
                    self.from_group.at[plan.group], self.from_group.at[plan.group],
                    self.group_send.at[t], self.group_recv.at[t], (plan.team[t], plan.shard),
                )
            )

    def over_levels(self):
        plan = self.plan
        for t in range(1, plan.groups):
            plan.arrived(self.from_group.at[plan.team[t]], self.group_send.at[t], self.group_recv.at[t])
        total = self.from_group[0].astype(F32)
        for g in range(1, plan.groups):
            total = total + self.from_group[g].astype(F32)
        wide = self.pieces.shape[2]
        for s in range(2 * plan.levels):
            self.pieces[s] = total[:, s * wide : (s + 1) * wide].astype(BF16)
        for k in range(1, plan.levels):
            plan.push(
                lambda k=k: send(
                    self.pieces.at[plan.far[k] * 2 + plan.core], self.from_level.at[k],
                    self.level_send.at[k], self.level_recv.at[k],
                    (plan.group, plan.far[k] * 2 + plan.core),
                )
            )

    def total(self):
        plan = self.plan
        total = self.pieces[plan.shard].astype(F32)
        for k in range(1, plan.levels):
            plan.arrived(self.from_level.at[k], self.level_send.at[k], self.level_recv.at[k])
            total = total + self.from_level[k].astype(F32)
        return total


def input_back(dproj_ref, w_ref, x_ref, gain_ref, held, inner, scale, gain_grad):
    width, step = x_ref.shape[1], 256
    x = x_ref[...].astype(F32)
    scale[...] = lax.rsqrt(jnp.mean(x * x, axis=-1, keepdims=True) + EPSILON)
    inner[...] = jnp.zeros(inner.shape, F32)

    @pl.loop(0, width // step)
    def _(c):
        at = pl.ds(pl.multiple_of(c * step, step), step)
        normed_grads = dot_nt(dproj_ref[...], w_ref[at, :])
        x = x_ref[:, at].astype(F32)
        weighted = normed_grads * gain_ref[:, at].astype(F32)
        inner[...] += jnp.sum(weighted * x, axis=-1, keepdims=True)
        gain_grad[:, at] = jnp.sum(normed_grads * x * scale[...], axis=0, keepdims=True)
        r = scale[...]
        held[:, at] += r * weighted

    r = scale[...]
    factor = r * r * r * (inner[...] * (1.0 / width))
    for low in range(0, width, step):
        cols = slice(low, low + step)
        held[:, cols] -= x_ref[:, cols].astype(F32) * factor


def reduce_kernel(groups, levels, *refs):
    normed_t, dproj_ref, gain_two_ref, router_ref, out_sum_ref, gain_ref = refs[:6]
    w_in, x_in, hidden_grads_in, *refs = refs[6:]
    count = 2 if groups == 4 else groups - 1
    out_sent, refs = refs[:count], refs[count:]
    out_ref, qkv_ref, misc_ref, input_grad_ref, *refs = refs
    out_came, refs = refs[:count], refs[count:]
    summed, from_level, home, out_summed, out_level, out_home = refs[:6]
    plan = Reduce(groups, levels, dproj_ref.shape[1], refs[6:10], refs[10:16])
    level_sems, home_sems, out_level_sems, out_home_sems = (refs[i : i + 2] for i in range(16, 24, 2))
    misc = FewRows(plan, refs[24:29], refs[29:35])
    w_buf, x_buf, held, inner, scale, gain_grad, load_sem, store_sem, row_send, row_recv = refs[35:]
    loads = [
        pltpu.make_async_copy(w_in.at[:, : dproj_ref.shape[1]], w_buf, load_sem.at[0]),
        pltpu.make_async_copy(x_in, x_buf, load_sem.at[1]),
        pltpu.make_async_copy(hidden_grads_in, held, load_sem.at[2]),
    ]
    for load in loads:
        load.start()
    first, *others = plan.bits()
    plan.greet(True)
    out_summed[...] = out_sum_ref[...]
    plan.climb(out_summed, out_level, out_level_sems, first)
    plan.fill(normed_t, dproj_ref)
    plan.merge()
    plan.spread()
    for load in loads:
        load.wait()
    input_back(dproj_ref, w_buf, x_buf, gain_ref, held, inner, scale, gain_grad)
    store = pltpu.make_async_copy(held, input_grad_ref, store_sem)
    store.start()
    experts = router_ref.shape[0]
    gains = jnp.concatenate(
        [gain_grad[...], gain_two_ref[...], jnp.zeros((6, gain_grad.shape[1]), F32)], axis=0
    )
    misc.rows[...] = jnp.zeros(misc.rows.shape, BF16)
    misc.rows[:8] = gains.astype(BF16)
    misc.rows[8 : 8 + experts] = router_ref[...].astype(BF16)
    misc.start()
    plan.climbed(out_summed, out_level, out_level_sems, first)
    for bit in others[:1]:
        plan.climb(out_summed, out_level, out_level_sems, bit)
    for k in plan.order:
        summed[k] = plan.collect(k).astype(BF16)
        plan.climb(summed, from_level, level_sems, first, k)
    row_copies = [
        send(
            out_sent[t - 1], out_came[t - 1], row_send.at[t], row_recv.at[t],
            (plan.team[t], plan.shard),
        )
        for t in range(1, count + 1)
    ]
    for copy in row_copies:
        copy.start()
    misc.over_groups()
    for n, bit in enumerate(others):
        plan.climbed(out_summed, out_level, out_level_sems, bit)
        for bit in others[n + 1 : n + 2]:
            plan.climb(out_summed, out_level, out_level_sems, bit)
    plan.settle(out_summed, out_home, out_home_sems)
    plan.climbed(summed, from_level, level_sems, first)
    for bit in others[:1]:
        plan.climb(summed, from_level, level_sems, bit)
    misc.over_levels()
    for n, bit in enumerate(others):
        plan.climbed(summed, from_level, level_sems, bit)
        for bit in others[n + 1 : n + 2]:
            plan.climb(summed, from_level, level_sems, bit)
    plan.settle(summed, home, home_sems)
    misc_ref[...] = misc.total()
    plan.landed(out_home, out_home_sems)
    out_ref[...] = out_home[...]
    plan.landed(home, home_sems)
    qkv_ref[...] = home[...]
    plan.finish()
    store.wait()
    for copy in row_copies:
        copy.wait()


def reduce_weights(normed_t, dproj, gain_two, router, out_sum, gain_row, w_full, x, hidden_grads, out_sent, groups, shards):
    tokens, width = x.shape
    levels, rows = shards // 2, width // shards
    total = dproj.shape[1]
    chunk, out_chunk = chunk_of(total, groups), out_sum.shape[2]
    dma = pltpu.SemaphoreType.DMA
    vmem, anywhere = (pl.BlockSpec(memory_space=m) for m in (pltpu.VMEM, pl.ANY))
    whole, out_whole = (groups, rows, chunk), (groups, rows, out_chunk)
    few = 16 * (-(-(8 + router.shape[0]) // 16))
    return pl.pallas_call(
        functools.partial(reduce_kernel, groups, levels),
        in_specs=[vmem] * 6 + [anywhere] * (3 + len(out_sent)),
        out_specs=[vmem] * 3 + [anywhere] * (1 + len(out_sent)),
        out_shape=[jax.ShapeDtypeStruct(s, BF16) for s in (out_whole, whole)]
        + [jax.ShapeDtypeStruct((few, rows), F32), jax.ShapeDtypeStruct((tokens, width), F32)]
        + [jax.ShapeDtypeStruct(o.shape, o.dtype) for o in out_sent],
        scratch_shapes=[
            pltpu.VMEM((levels, rows, chunk), BF16),
            pltpu.VMEM((levels, rows, chunk), BF16),
            pltpu.VMEM(whole, BF16),
            pltpu.VMEM((levels, rows, out_chunk), BF16),
            pltpu.VMEM((levels, rows, out_chunk), BF16),
            pltpu.VMEM(out_whole, BF16),
        ]
        + reduce_buffers(groups, levels, rows, chunk)
        + reduce_sems(groups, levels)
        + [dma((levels,))] * 2 + [dma((groups,))] * 2 + [dma((levels,))] * 2 + [dma((groups,))] * 2
        + [
            pltpu.VMEM((few, width), BF16),
            pltpu.VMEM((few, width), BF16),
            pltpu.VMEM((groups, few, width), BF16),
            pltpu.VMEM((shards, few, rows), BF16),
            pltpu.VMEM((levels, few, rows), BF16),
            dma, dma, dma((groups,)), dma((groups,)), dma((levels,)), dma((levels,)),
            pltpu.VMEM((width, total), BF16),
            pltpu.VMEM((tokens, width), BF16),
            pltpu.VMEM((tokens, width), F32),
            pltpu.VMEM((tokens, 1), F32),
            pltpu.VMEM((tokens, 1), F32),
            pltpu.VMEM((1, width), F32),
            dma((3,)), dma, dma((groups,)), dma((groups,)),
        ],
        compiler_params=pltpu.CompilerParams(
            collective_id=1, has_side_effects=True, vmem_limit_bytes=62 << 20
        ),
        cost_estimate=pl.CostEstimate(
            flops=2 * tokens * width * total, bytes_accessed=8 << 20, transcendentals=0
        ),
        name="reduce_weights",
    )(normed_t, dproj, gain_two, router, out_sum, gain_row, w_full, x, hidden_grads, *out_sent)


def expert_kernel(capacity, shards, groups, count, base, stage, *refs):
    refs = list(refs)
    take = lambda n: [refs.pop(0) for _ in range(n)]
    if stage == "first":
        x_own, meta_own = take(2)
        u_ins = take(3 if groups == 4 else groups)
    else:
        x_ref, u_ref, meta_ref, out_in, dx_in, gg_in = take(6)
    packed_ref = take(1)[0]
    if stage == "last":
        earlier_ref = take(1)[0]
    if stage == "first":
        x_all, u_all, meta_all, out_ref, dx_ref, gg_ref, dw_out = take(7)
    elif stage == "last":
        out_homes = take(3 if groups == 4 else groups)
        dx_home, gg_home, dw_out = take(3)
    else:
        out_ref, dx_ref, gg_ref, dw_out = take(4)
    xs, us, bs, inn, dw, dw_sem, we_all, wp_all, we_sem, wp_sem = take(10)
    if stage != "between":
        core_buf, core_send, core_recv, credit = take(4)
    if stage == "first":
        x_buf, u_buf, meta_buf = take(3)
        x_send, x_recv, meta_send, meta_recv, load_sem, u_sem, meta_sem, keep_sem, pass_sem = take(9)
    elif stage == "last":
        buf, passing, gg_buf = take(3)
        load_sem, pass_send, pass_recv, dx_send, dx_recv, gg_send, gg_recv, keep_sem = take(8)
    turn_at, expert = pl.program_id(0), pl.program_id(1)
    last_turn, last = groups - 1, count - 1
    group, shard = lax.axis_index("expert"), lax.axis_index("shard")
    team = [flipped(group, t) for t in range(groups)]
    core = shard % 2
    mate = (group, shard + 1 - 2 * core)
    width = xs.shape[2]
    tokens = x_buf.shape[0] if stage == "first" else x_ref.shape[1]
    tall, short = width // shards, FF // shards
    side = width - 2 * FF
    we_ref, wp_ref = we_all.at[expert], wp_all.at[expert]

    @pl.when((turn_at == 0) & (expert == 0))
    def _():
        for e in range(count):

            @pl.loop(0, shards)
            def _(s):
                a = pl.ds(pl.multiple_of(s * tall, 16), tall)
                b = pl.ds(pl.multiple_of(s * short, 16), short)
                low = pl.ds(pl.multiple_of(s * short, 16), short // 2)
                high = pl.ds(pl.multiple_of(s * short + short // 2, 16), short // 2)
                source = packed_ref.at[s, e]
                rest = pl.ds(tall + short, short // 2)
                for piece, target, sem in (
                    (source.at[:tall], we_all.at[e, a], we_sem),
                    (source.at[tall : tall + short], wp_all.at[e, b, : 2 * FF], wp_sem),
                    (source.at[rest, :side], wp_all.at[e, low, 2 * FF :], wp_sem),
                    (source.at[rest, side:], wp_all.at[e, high, 2 * FF :], wp_sem),
                ):
                    pltpu.make_async_copy(piece, target, sem.at[e]).start()

    def core_copy(source):
        return send(source.at[:, 1 - core], core_buf, core_send, core_recv, mate)

    def core_add(source):
        core_copy(source).wait()

        @pl.loop(0, shards // 2)
        def _(z):
            core_buf[z] = (dw[z, core].astype(F32) + core_buf[z].astype(F32)).astype(BF16)

    def store_half(at):
        return pltpu.make_async_copy(core_buf, dw_out.at[:, at], dw_sem)

    def core_free(at):
        store_half(at).wait()
        pl.semaphore_signal(credit, inc=1, device_id=mate, device_id_type=pl.DeviceIdType.MESH)

    def own_half():
        return pltpu.make_async_copy(earlier_ref.at[:, core], dw.at[:, core], keep_sem.at[1])

    before = 1 if stage == "last" else 0

    if stage == "first":
        relay = groups == 4
        near = [1, 2] if relay else list(range(1, groups))
        half = tokens // 2

        def x_copy(t):
            return send(x_own, x_all.at[t], x_send.at[t], x_recv.at[t], (team[t], shard))

        def passed(source, target, part, sems):
            at = pl.ds(part * half, half)
            return send(
                source.at[at], target.at[3, at], sems.at[0, part], sems.at[1, part],
                (team[2 - part], shard),
            )

        def x_pass(part):
            return passed(x_all.at[1 + part], x_all, part, pass_sem.at[0])

        def u_pass(part):
            return passed(u_ins[1 + part], u_all, part, pass_sem.at[1])

        def meta_copy(t):
            return send(
                meta_own.at[team[t]], meta_all.at[t], meta_send.at[t], meta_recv.at[t], (team[t], shard)
            )

        def u_load(t):
            source = u_all.at[t] if relay and t == 3 else u_ins[t]
            return pltpu.make_async_copy(source, u_buf.at[t % 2], u_sem.at[t % 2])

        def x_keep():
            return pltpu.make_async_copy(x_buf, x_all.at[0], keep_sem.at[0])

        def meta_keep():
            return pltpu.make_async_copy(meta_buf, meta_all.at[0], keep_sem.at[1])

        def u_keep(t):
            return pltpu.make_async_copy(u_buf.at[t % 2], u_all.at[t], keep_sem.at[2 + t])

        for t in range(groups):

            @pl.when((turn_at == t) & (expert == 0))
            def _():
                if t == 0:
                    u_load(0).start()
                    greet([mate] + [(team[k], shard) for k in range(1, groups)])
                    for k in range(1, groups):
                        meta_copy(k).start()
                    for k in near:
                        x_copy(k).start()
                    fetch_x, fetch_meta = x_own, meta_own.at[group]
                else:
                    if not relay:
                        x_copy(t).wait_recv()
                    elif t == 1:
                        for k in near:
                            x_copy(k).wait_recv()
                        for part in range(2):
                            x_pass(part).start()
                        for part in range(2):
                            u_pass(part).start()
                    elif t == 3:
                        for part in range(2):
                            x_pass(part).wait_recv()
                            u_pass(part).wait_recv()
                        u_load(3).start()
                    meta_copy(t).wait_recv()
                    u_keep(t - 1).wait()
                    if t == 1:
                        x_keep().wait()
                        meta_keep().wait()
                    fetch_x, fetch_meta = x_all.at[t], meta_all.at[t]
                load = pltpu.make_async_copy(fetch_x, x_buf, load_sem)
                load_meta = pltpu.make_async_copy(fetch_meta, meta_buf, meta_sem)
                load.start()
                load_meta.start()
                if t + 1 < groups and not (relay and t == 2):
                    u_load(t + 1).start()
                u_load(t).wait()
                load_meta.wait()
                load.wait()
                if not (relay and t == 3):
                    u_keep(t).start()
                if t == 0:
                    x_keep().start()
                    meta_keep().start()

        x_now, u_now, meta_now = x_buf, u_buf.at[turn_at % 2], meta_buf
    else:
        x_now, u_now, meta_now = x_ref.at[0], u_ref.at[0], meta_ref.at[0]

    if stage == "last":
        relay = groups == 4
        slots, half = buf.shape[1], tokens // 2
        halves = [pl.ds(0, half), pl.ds(half, half)]

        def kept(kind, i):
            return buf.at[kind, i % slots]

        def load(kind, i):
            source = dx_in if kind else out_in
            return pltpu.make_async_copy(
                source.at[last_turn - i], kept(kind, i), load_sem.at[kind, i % 2]
            )

        def store(i):
            return pltpu.make_async_copy(kept(0, i), out_homes[last_turn - i], keep_sem.at[2 + i])

        def pass_copy(kind, part):
            return send(
                kept(kind, 0).at[halves[part]], passing.at[kind, part],
                pass_send.at[kind, part], pass_recv.at[kind, part], (team[1 + part], shard),
            )

        def dx_copy(i):
            t = last_turn - i
            return send(kept(1, i), dx_home.at[t], dx_send.at[t], dx_recv.at[t], (team[t], shard))

        def dx_half(part):
            at = halves[part]
            return send(
                kept(1, 1).at[at], dx_home.at[2, at], dx_send.at[2 + part], dx_recv.at[2 + part],
                (team[2], shard),
            )

        def gg_copy(i):
            t = last_turn - i
            return send(gg_buf.at[i], gg_home.at[group], gg_send.at[t], gg_recv.at[t], (team[t], shard))

        def own_copies():
            return [
                pltpu.make_async_copy(kept(1, last_turn), dx_home.at[0], keep_sem.at[0]),
                pltpu.make_async_copy(gg_buf.at[last_turn], gg_home.at[group], keep_sem.at[1]),
            ]

        for i in range(groups):

            @pl.when((turn_at == i) & (expert == 0))
            def _():
                if i == 0:
                    for kind in range(2):
                        load(kind, 0).start()
                    greet([mate] + [(team[k], shard) for k in range(1, groups)])
                    core_copy(earlier_ref).start()
                    own_half().start()
                if i == 1:
                    own_half().wait()
                    core_add(earlier_ref)
                    store_half(0).start()
                if i == 2:
                    core_free(0)
                if i + 1 < groups:
                    if i + 1 >= slots:
                        dx_copy(i + 1 - slots).wait_send()
                        store(i + 1 - slots).wait()
                    for kind in range(2):
                        load(kind, i + 1).start()
                for kind in range(2):
                    load(kind, i).wait()

        at_now = turn_at % slots
        out_now, dx_now, gg_now = buf.at[0, at_now], buf.at[1, at_now], gg_buf.at[turn_at]
    else:
        out_now, dx_now, gg_now = out_ref.at[0], dx_ref.at[0], gg_ref.at[0]

    @pl.when(expert == 0)
    def _():
        if stage == "first":
            out_now[...] = jnp.zeros((tokens, width), BF16)
            dx_now[...] = jnp.zeros((tokens, width), BF16)
            gg_now[...] = jnp.zeros((8, tokens), F32)
        else:
            gg_now[...] = gg_in[0]
        if stage == "between":
            out_now[...] = out_in[0]
            dx_now[...] = dx_in[0]

    @pl.when(turn_at == 0)
    def _():
        pltpu.make_async_copy(we_ref, we_ref, we_sem.at[expert]).wait()
        pltpu.make_async_copy(wp_ref, wp_ref, wp_sem.at[expert]).wait()

    slot_row = meta_now[pl.ds(base + expert, 1), :]
    gate_row = meta_now[pl.ds(8 + base + expert, 1), :]
    index = lax.broadcasted_iota(jnp.int32, (capacity, tokens), 0).astype(F32)
    pick = jnp.where(index == slot_row, 1.0, 0.0)
    gate_col = jnp.sum(pick * gate_row, axis=1, keepdims=True)
    place = pick.astype(BF16)
    rows = pl.ds(pl.multiple_of(turn_at * capacity, capacity), capacity)
    x = dot_nn(place, x_now[...]).astype(BF16)
    xs[expert, rows, :] = x
    u_rows = dot_nn(place, u_now[...]).astype(BF16)
    us[expert, rows, :] = u_rows
    both_parts = dot_nn(x, we_ref[...])
    gate, up = both_parts[:, :FF], both_parts[:, FF:]
    back = dot_nt(u_rows, wp_ref[...])
    sig = 1.0 / (1.0 + jnp.exp(-gate))
    act = gate * sig
    inner = act * up
    inner_low = inner.astype(BF16)
    gate_grad = jnp.sum(inner * back, axis=1, keepdims=True)
    here = lax.broadcasted_iota(jnp.int32, (8, tokens), 0) == base + expert
    gg_now[...] = jnp.where(here, jnp.sum(pick * gate_grad, axis=0, keepdims=True), gg_now[...])
    inn[expert, rows, :] = (inner * gate_col).astype(BF16)
    inner_grads = back * gate_col
    bs[expert, rows, :FF] = (inner_grads * up * sig * (1.0 + gate * (1.0 - sig))).astype(BF16)
    bs[expert, rows, FF:] = (inner_grads * act).astype(BF16)
    both = bs[expert, rows, :]
    weighted_t = (pick * gate_row).astype(BF16).T
    place_t = place.T
    result = dot_nn(inner_low, wp_ref[...]).astype(BF16)
    out_now[...] = (out_now[...].astype(F32) + dot_nn(weighted_t, result)).astype(BF16)
    row_grads = dot_nt(both, we_ref[...]).astype(BF16)
    dx_now[...] = (dx_now[...].astype(F32) + dot_nn(place_t, row_grads)).astype(BF16)

    if stage == "last":

        def add_passed(kind):
            for part in range(2):
                pass_copy(kind, part).wait_recv()
                target = kept(kind, 1 + part).at[halves[part]]
                target[...] = (target[...].astype(F32) + passing[kind, part].astype(F32)).astype(BF16)

        for i in range(groups):

            @pl.when((turn_at == i) & (expert == last))
            def _():
                if i < last_turn:
                    gg_copy(i).start()
                else:
                    for copy in own_copies():
                        copy.start()
                if not relay:
                    store(i).start()
                    if i < last_turn:
                        dx_copy(i).start()
                elif i == 0:
                    for kind in (1, 0):
                        for part in range(2):
                            pass_copy(kind, part).start()
                elif i == 1:
                    dx_half(1).start()
                elif i == 2:
                    add_passed(1)
                    dx_copy(2).start()
                    dx_half(0).start()
                else:
                    add_passed(0)
                    for k in range(1, groups):
                        store(k).start()

    @pl.when(turn_at == last_turn)
    def _():
        if stage != "between" and count > 1:

            @pl.when(expert > 0)
            def _():
                core_add(dw)
                store_half(before + expert - 1).start()

        wide, half = 384, FF // 2

        @pl.loop(0, width // wide)
        def _(c):
            at = pl.ds(pl.multiple_of(c * wide, wide), wide)
            value = dot_tn(xs[expert, :, at], bs[expert]).astype(BF16)
            for i in range(wide // tall):
                s = c * (wide // tall) + i
                dw[s // 2, s % 2, :tall, :] = value[i * tall : (i + 1) * tall]

        @pl.loop(0, FF // half)
        def _(c):
            at = pl.ds(pl.multiple_of(c * half, half), half)
            value = dot_tn(inn[expert, :, at], us[expert]).astype(BF16)
            for i in range(half // short):
                s, low = c * (half // short) + i, i * short
                mid, high = low + short // 2, low + short
                dw[s // 2, s % 2, tall : tall + short, :] = value[low:high, : 2 * FF]
                dw[s // 2, s % 2, tall + short :, :side] = value[low:mid, 2 * FF :]
                dw[s // 2, s % 2, tall + short :, side:] = value[mid:high, 2 * FF :]

        if stage == "between":
            pltpu.make_async_copy(dw, dw_out, dw_sem).start()
        else:
            if count > 1:

                @pl.when(expert > 0)
                def _():
                    core_free(before + expert - 1)

            if before:
                pl.semaphore_wait(credit, 1)
            else:

                @pl.when(expert > 0)
                def _():
                    pl.semaphore_wait(credit, 1)

            core_copy(dw).start()

    @pl.when((turn_at == last_turn) & (expert == last))
    def _():
        if stage == "between":
            pltpu.make_async_copy(dw, dw_out, dw_sem).wait()
        else:
            core_add(dw)
            store_half(before + last).start()
            store_half(before + last).wait()
        if stage == "first":
            if not relay:
                u_keep(last_turn).wait()
            for t in range(1, groups):
                meta_copy(t).wait_send()
            for t in near:
                x_copy(t).wait_send()
            if relay:
                for part in range(2):
                    x_pass(part).wait_send()
                    u_pass(part).wait_send()
        if stage == "last":
            for i in range(groups - 1):
                t = last_turn - i
                gg_copy(i).wait_send()
                send(
                    gg_buf.at[i], gg_home.at[team[t]], gg_send.at[t], gg_recv.at[t], (team[t], shard)
                ).wait_recv()
            if relay:
                for part in range(2):
                    dx_half(part).wait()
                    for kind in range(2):
                        pass_copy(kind, part).wait_send()
                dx_copy(2).wait()
                for k in range(1, groups):
                    store(k).wait()
            else:
                for i in range(groups - 1):
                    if i + slots >= groups:
                        dx_copy(i).wait_send()
                    dx_copy(i).wait_recv()
                for i in range(groups - slots, groups):
                    store(i).wait()
            for copy in own_copies():
                copy.wait()


def expert_call(capacity, shards, groups, base, stage, data, packed_weights, *kept):
    count = packed_weights.shape[1]
    tokens, width = data[0].shape[-2:]
    total = groups * capacity
    anywhere = pl.BlockSpec(memory_space=pl.ANY)
    turned = (lambda i: i) if stage == "first" else (lambda i: groups - 1 - i)
    block = pl.BlockSpec((1, tokens, width), lambda i, e: (turned(i), 0, 0))
    small = pl.BlockSpec((1, 8, tokens), lambda i, e: (turned(i), 0, 0))
    dma = pltpu.SemaphoreType.DMA
    many = jax.ShapeDtypeStruct((groups, tokens, width), BF16)
    grads = jax.ShapeDtypeStruct((groups, 8, tokens), F32)
    piece = ((width + FF + FF // 2) // shards, 2 * FF)
    summed = 2 if stage == "between" else count + len(kept)
    weights = jax.ShapeDtypeStruct((shards // 2, summed) + piece, BF16)
    meta = jax.ShapeDtypeStruct((groups, 16, tokens), F32)
    scratch = [
        pltpu.VMEM((count, total, width), BF16),
        pltpu.VMEM((count, total, width), BF16),
        pltpu.VMEM((count, total, 2 * FF), BF16),
        pltpu.VMEM((count, total, FF), BF16),
        pltpu.VMEM((shards // 2, 2) + piece, BF16),
        dma,
        pltpu.VMEM((count, width, 2 * FF), BF16),
        pltpu.VMEM((count, FF, width), BF16),
        dma((count,)), dma((count,)),
    ]
    if stage != "between":
        scratch += [
            pltpu.VMEM((shards // 2,) + piece, BF16), dma, dma, pltpu.SemaphoreType.REGULAR,
        ]
    if stage == "first":
        in_specs = [anywhere] * len(data)
        out_specs = [anywhere] * 3 + [block, block, small, anywhere]
        out_shape = [many, many, meta, many, many, grads, weights]
        scratch += [
            pltpu.VMEM((tokens, width), BF16),
            pltpu.VMEM((2, tokens, width), BF16),
            pltpu.VMEM((16, tokens), F32),
            dma((groups,)), dma((groups,)), dma((groups,)), dma((groups,)),
            dma, dma((2,)), dma, dma((2 + groups,)), dma((2, 2, 2)),
        ]
    else:
        meta_block = pl.BlockSpec((1, 16, tokens), lambda i, e: (turned(i), 0, 0))
        in_specs = [block, block, meta_block, block, block, small]
        out_specs = [block, block, small, anywhere]
        if stage == "last":
            in_specs[3:5] = [anywhere] * 2
            sources = 3 if groups == 4 else groups
            out_specs = [anywhere] * (3 + sources)
            slots = groups if groups == 4 else 3
            passed = 2 if groups == 4 else 1
            scratch += [
                pltpu.VMEM((2, slots, tokens, width), BF16),
                pltpu.VMEM((passed, passed, tokens // 2, width), BF16),
                pltpu.VMEM((groups, 8, tokens), F32),
                dma((2, 2)), dma((2, 2)), dma((2, 2)),
                dma((groups,)), dma((groups,)), dma((groups,)), dma((groups,)), dma((2 + groups,)),
            ]
        out_shape = [many, many, grads, weights]
        if stage == "last":
            out_shape[:1] = [jax.ShapeDtypeStruct((tokens, width), BF16)] * sources
    remote = {"first": 2, "last": 3}
    return pl.pallas_call(
        functools.partial(expert_kernel, capacity, shards, groups, count, base, stage),
        grid=(groups, count),
        in_specs=in_specs + [anywhere] * (1 + len(kept)),
        out_specs=out_specs,
        out_shape=out_shape,
        scratch_shapes=scratch,
        compiler_params=pltpu.CompilerParams(
            vmem_limit_bytes=62 << 20,
            **({"collective_id": remote[stage], "has_side_effects": True} if stage in remote else {}),
        ),
        cost_estimate=pl.CostEstimate(
            flops=2 * count * total * width * (4 * tokens + 9 * FF),
            bytes_accessed=6 * groups * tokens * width * 2,
            transcendentals=count * total * FF,
        ),
        name="experts_" + stage,
    )(*data, packed_weights, *kept)


def norm_back(values, gain_row, grad_rows):
    scale_rows = lax.rsqrt(jnp.mean(values * values, axis=-1, keepdims=True) + EPSILON)
    weighted = gain_row * grad_rows
    inner_mean = jnp.mean(weighted * values, axis=-1, keepdims=True)
    input_part = (
        scale_rows * weighted - values * (scale_rows * scale_rows * scale_rows) * inner_mean
    )
    gain_part = jnp.sum(grad_rows * values * scale_rows, axis=0)
    return (input_part, gain_part)


def pack_kernel(
    cuts, expand_ref, project_ref, qkv_ref, gains_ref, router_ref, packed_ref, *refs
):
    *outs, misc = refs
    short = project_ref.shape[1]
    tall = expand_ref.shape[1]
    side = project_ref.shape[2] - 2 * FF
    for (low, high), out in zip(cuts, outs):
        for e in range(low, high):
            out[e - low, :tall] = expand_ref[e]
            out[e - low, tall : tall + short] = project_ref[e, :, : 2 * FF]
            out[e - low, tall + short :, :side] = project_ref[e, : short // 2, 2 * FF :]
            out[e - low, tall + short :, side:] = project_ref[e, short // 2 :, 2 * FF :]
    for j in range(PAIRS):
        at, to = HEADS * HEAD + j * KW, j * BLOCK + QW
        packed_ref[:, j * BLOCK : to] = qkv_ref[:, j * QW : (j + 1) * QW]
        packed_ref[:, to : to + KW] = qkv_ref[:, at : at + KW]
        at += KV_HEADS * HEAD
        packed_ref[:, to + KW : to + 2 * KW] = qkv_ref[:, at : at + KW]
    misc[...] = jnp.zeros(misc.shape, F32)
    misc[0:2] = gains_ref[...].astype(F32)
    misc[8 : 8 + router_ref.shape[0]] = router_ref[...].astype(F32)
    packed_ref[:, PAIRS * BLOCK :] = misc[...].T.astype(BF16)


def pack_weights(expand, project, qkv, gain_one, gain_two, router):
    cuts = bands(expand.shape[0])
    rows = expand.shape[1] + project.shape[1] + project.shape[1] // 2
    return pl.pallas_call(
        functools.partial(pack_kernel, cuts),
        out_shape=[jax.ShapeDtypeStruct((qkv.shape[0], PAIRS * BLOCK + MISC), BF16)]
        + [jax.ShapeDtypeStruct((high - low, rows, 2 * FF), BF16) for low, high in cuts],
        scratch_shapes=[pltpu.VMEM((MISC, qkv.shape[0]), F32)],
        compiler_params=pltpu.CompilerParams(vmem_limit_bytes=62 << 20),
        name="pack_weights",
    )(expand, project, qkv, jnp.stack([gain_one, gain_two]), router.T)


def hidden_back_kernel(
    dx_ref, gg_ref, gates_ref, router_ref, hidden_ref, gain_ref, up_ref, ffn_ref,
    grads_ref, low_ref, router_grad_ref, gain_grad_ref,
):
    gates, groups = gates_ref[...], gg_ref.shape[0]
    count = gates.shape[0] // groups
    gate_grads = jnp.concatenate([gg_ref[g, :count] for g in range(groups)], axis=0)
    mean = jnp.sum(gates * gate_grads, axis=0, keepdims=True)
    logit_grads = (gates * (gate_grads - mean)).astype(BF16)
    ffn_grads = dot_tn(logit_grads, router_ref[...])
    for g in range(dx_ref.shape[0]):
        ffn_grads = ffn_grads + dx_ref[g].astype(F32)
    hidden = hidden_ref[...]
    part, gain_part = norm_back(hidden, gain_ref[...].astype(F32), ffn_grads)
    hidden_grads = up_ref[...].astype(F32) + part
    grads_ref[...] = hidden_grads
    low_ref[...] = hidden_grads.astype(BF16)
    router_part = dot_nn(logit_grads, ffn_ref[...])

    @pl.when(pl.program_id(0) == 0)
    def _():
        router_grad_ref[...] = router_part
        gain_grad_ref[...] = gain_part[None]

    @pl.when(pl.program_id(0) > 0)
    def _():
        router_grad_ref[...] += router_part
        gain_grad_ref[...] += gain_part[None]


def hidden_back(sources, dx_home, gg_home, gates, router_rows, hidden, gain_row, out_grad, ffn_in):
    groups, tokens, width = dx_home.shape
    experts = gates.shape[0]
    step = 128
    rows = pl.BlockSpec((step, width), lambda i: (i, 0))
    return pl.pallas_call(
        hidden_back_kernel,
        grid=(tokens // step,),
        in_specs=[
            pl.BlockSpec((sources, step, width), lambda i: (0, i, 0)),
            pl.BlockSpec((groups, 8, step), lambda i: (0, 0, i)),
            pl.BlockSpec((experts, step), lambda i: (0, i)),
            whole_spec((experts, width)),
            rows,
            whole_spec((1, width)),
            rows,
            rows,
        ],
        out_specs=[rows, rows, whole_spec((experts, width)), whole_spec((1, width))],
        out_shape=[
            jax.ShapeDtypeStruct((tokens, width), F32),
            jax.ShapeDtypeStruct((tokens, width), BF16),
            jax.ShapeDtypeStruct((experts, width), F32),
            jax.ShapeDtypeStruct((1, width), F32),
        ],
        compiler_params=pltpu.CompilerParams(vmem_limit_bytes=62 << 20),
        cost_estimate=pl.CostEstimate(flops=10**8, bytes_accessed=20 << 20, transcendentals=0),
        name="hidden_back",
    )(dx_home, gg_home, gates, router_rows, hidden, gain_row, out_grad, ffn_in)


def unpack_experts(tall, short, held, expand_ref, project_ref):
    side = project_ref.shape[2] - 2 * FF
    for i in range(held.shape[0]):
        value = held[i].astype(F32)
        expand_ref[i] = value[:tall]
        project_ref[i, :, : 2 * FF] = value[tall : tall + short]
        project_ref[i, : short // 2, 2 * FF :] = value[tall + short :, :side]
        project_ref[i, short // 2 :, 2 * FF :] = value[tall + short :, side:]


def unpack_kernel(tall, short, counts, *refs):
    first_ref, last_ref, hidden_ref, *refs = refs
    others, refs = refs[: counts[2]], refs[counts[2] :]
    grad_in, *refs = refs
    out_ref, qkv_ref, few_ref, output_ref, grad_ref, expand_ref, project_ref = refs[:7]
    out_grad_ref, qkv_grad_ref, gain_one_ref, gain_two_ref, router_ref = refs[7:]
    i = pl.program_id(0)

    @pl.when(i < counts[0])
    def _():
        unpack_experts(tall, short, first_ref, expand_ref, project_ref)

    @pl.when(i >= counts[0])
    def _():
        unpack_experts(tall, short, last_ref, expand_ref, project_ref)

    @pl.when(i < 4)
    def _():
        total = hidden_ref[...]
        for other in others:
            total = total + other[...].astype(F32)
        output_ref[...] = total.astype(BF16)
        grad_ref[...] = grad_in[...]

    @pl.when(i == 4)
    def _():
        tile = 128
        chunk = out_ref.shape[2]
        for at in range(0, out_grad_ref.shape[1], tile):
            out_grad_ref[:, at : at + tile] = out_ref[
                at // chunk, :, at % chunk : at % chunk + tile
            ].astype(F32)
        chunk = qkv_ref.shape[2]
        for at in range(0, qkv_grad_ref.shape[1], tile):
            value = qkv_ref[at // chunk, :, at % chunk : at % chunk + tile].astype(F32)
            j, inside = divmod(at, BLOCK)
            if inside < QW:
                to = j * QW + inside
            elif inside < QW + KW:
                to = PAIRS * QW + j * KW + inside - QW
            else:
                to = PAIRS * (QW + KW) + j * KW + inside - QW - KW
            qkv_grad_ref[:, to : to + tile] = value
        gain_one_ref[...] = few_ref[0:1]
        gain_two_ref[...] = few_ref[1:2]
        router_ref[...] = few_ref[8 : 8 + router_ref.shape[0]]


def unpack_weights(shares, out_total, qkv_total, few, hidden, out_home, input_grad, tall, short, experts):
    tokens, width = hidden.shape
    rows = out_total.shape[1]
    first, last = shares
    counts = (first.shape[0], last.shape[0], len(out_home))
    count = counts[0] + counts[1]
    step = tokens // 4
    block = pl.BlockSpec((step, width), lambda i: (jnp.minimum(i, 3), 0))
    one = (1,) + first.shape[1:]
    return pl.pallas_call(
        functools.partial(unpack_kernel, tall, short, counts),
        grid=(count,),
        in_specs=[
            pl.BlockSpec(one, lambda i: (jnp.minimum(i, counts[0] - 1), 0, 0)),
            pl.BlockSpec(one, lambda i: (jnp.maximum(i - counts[0], 0), 0, 0)),
        ]
        + [block] * (2 + len(out_home))
        + [whole_spec(out_total.shape), whole_spec(qkv_total.shape), whole_spec(few.shape)],
        out_specs=[
            block,
            block,
            pl.BlockSpec((1, tall, 2 * FF), lambda i: (i, 0, 0)),
            pl.BlockSpec((1, short, width), lambda i: (i, 0, 0)),
            whole_spec((rows, HEADS * HEAD)),
            whole_spec((rows, PAIRS * BLOCK)),
            whole_spec((1, rows)),
            whole_spec((1, rows)),
            whole_spec((experts, rows)),
        ],
        out_shape=[
            jax.ShapeDtypeStruct(hidden.shape, BF16),
            jax.ShapeDtypeStruct(hidden.shape, F32),
            jax.ShapeDtypeStruct((count, tall, 2 * FF), F32),
            jax.ShapeDtypeStruct((count, short, width), F32),
            jax.ShapeDtypeStruct((rows, HEADS * HEAD), F32),
            jax.ShapeDtypeStruct((rows, PAIRS * BLOCK), F32),
            jax.ShapeDtypeStruct((1, rows), F32),
            jax.ShapeDtypeStruct((1, rows), F32),
            jax.ShapeDtypeStruct((experts, rows), F32),
        ],
        compiler_params=pltpu.CompilerParams(vmem_limit_bytes=62 << 20),
        cost_estimate=pl.CostEstimate(flops=10**7, bytes_accessed=24 << 20, transcendentals=0),
        name="unpack_weights",
    )(first, last, hidden, *out_home, input_grad, out_total, qkv_total, few)


def bands(count):
    return [(0, 2), (2, 3), (3, count)]


def local(
    inputs, attn_gain, qkv_weight, out_weight, ffn_gain, router_weight,
    expand_weight, project_weight, segment_ids, routes, out_grad,
):
    groups, shards = lax.axis_size("expert"), lax.axis_size("shard")
    tokens, width = inputs.shape
    experts = router_weight.shape[1]
    local_count = expand_weight.shape[0]
    capacity = 8 * ((5 * tokens * TOP + 32 * experts - 1) // (32 * experts))

    packed, *bands_packed = pack_weights(
        expand_weight, project_weight, qkv_weight, attn_gain, ffn_gain, router_weight
    )
    packed_full = [lax.all_gather(p, "shard", axis=0) for p in bands_packed]
    qkv_full, out_part, *u_others = gather_weights(
        [packed, out_weight], out_grad, groups, shards
    )
    qkv_full = qkv_full.reshape(width, -1)
    misc_rows = qkv_full[:, PAIRS * BLOCK :].T
    gain_one, gain_two = misc_rows[0:1], misc_rows[1:2]
    router_rows = misc_rows[8 : 8 + experts]
    tables = tuple(jnp.asarray(t) for t in rope_tables())
    seg_row = segment_ids.reshape(1, tokens)
    seg_col = segment_ids.reshape(tokens, 1)
    normed_t, proj, mixed, lse, out_full = attention_forward(
        inputs, gain_one, qkv_full, tables, seg_col, seg_row, out_part, groups, shards
    )
    hidden, ffn_in, gates, meta_own = middle(
        mixed, out_full, inputs, gain_two, router_rows, routes.T, groups
    )
    tall, short = expand_weight.shape[1], project_weight.shape[1]
    call = functools.partial(expert_call, capacity, shards, groups)

    cores = [[2 * z + core for z in range(shards // 2)] for core in range(2)]

    def share_out(dw):
        return lax.psum_scatter(
            dw, "shard", scatter_dimension=0, axis_index_groups=cores, tiled=True
        )[0]

    x_all, u_all, meta, out_acc, dx_acc, gg, dw = call(
        0, "first", (ffn_in, meta_own, out_grad, *u_others), packed_full[0]
    )
    shares = [share_out(dw)]
    out_acc, dx_acc, gg, dw = call(
        2, "between", (x_all, u_all, meta, out_acc, dx_acc, gg), packed_full[1]
    )
    *out_sent, dx_home, gg_home, dw = call(
        3, "last", (x_all, u_all, meta, out_acc, dx_acc, gg), packed_full[2], dw
    )
    shares.append(share_out(dw))
    sources = 3 if groups == 4 else groups
    hidden_grads, attended_grads, router_part, gain_two_grad = hidden_back(
        sources, dx_home, gg_home, gates, router_rows, hidden, gain_two, out_grad, ffn_in
    )
    dproj, out_sum = attention_backward(
        attended_grads, out_full, proj, mixed, lse, tables, seg_col, seg_row, groups, shards
    )
    out_total, qkv_total, few, input_grad, *out_came = reduce_weights(
        normed_t, dproj, gain_two_grad, router_part, out_sum, gain_one, qkv_full, inputs,
        hidden_grads, out_sent[1:], groups, shards,
    )
    output, input_grad, expand_grad, project_grad, out_weight_grad, qkv_grad, *gains = unpack_weights(
        shares, out_total, qkv_total, few, hidden, [out_sent[0], *out_came], input_grad, tall, short,
        experts,
    )
    return (
        output,
        input_grad,
        gains[0][0],
        qkv_grad,
        out_weight_grad,
        gains[1][0],
        gains[2].T,
        expand_grad,
        project_grad,
    )


def solution(mesh):
    rows = P(("expert", "shard"), None)
    return jax.shard_map(
        local,
        mesh=mesh,
        in_specs=(
            rows, P("shard"), P("shard", None), P("shard", None), P("shard"), P("shard", None),
            P("expert", "shard", None), P("expert", "shard", None), rows, rows, rows,
        ),
        out_specs=(
            rows, rows, P("shard"), P("shard", None), P("shard", None), P("shard"),
            P("shard", None), P("expert", "shard", None), P("expert", "shard", None),
        ),
        check_vma=False,
    )
```

```python
import functools

import jax
import jax.numpy as jnp
import numpy as np
from jax import lax
from jax.experimental import pallas as pl
from jax.experimental.pallas import tpu as pltpu
from jax.sharding import PartitionSpec as P

HEADS = 24
KV_HEADS = 8
HEAD = 64
FF = 512
TOP = 8
SEQ_LEN = 512
GROUP = HEADS // KV_HEADS
PAIRS = KV_HEADS // 2
QW = 2 * GROUP * HEAD
KW = 2 * HEAD
BLOCK = QW + 2 * KW
MISC = 128
QB = 128

EPSILON = 1e-06
ROPE_THETA = 10000.0
MASKED = -1e30
F32 = jnp.float32
BF16 = jnp.bfloat16


def dot_nn(a, b):
    return lax.dot_general(a, b, (((1,), (0,)), ((), ())), preferred_element_type=F32)


def dot_nt(a, b):
    return lax.dot_general(a, b, (((1,), (1,)), ((), ())), preferred_element_type=F32)


def dot_tn(a, b):
    return lax.dot_general(a, b, (((0,), (0,)), ((), ())), preferred_element_type=F32)


def rope_tables():
    frequency = (np.float32(ROPE_THETA) ** (-2.0 * np.arange(HEAD // 2) / HEAD)).astype(np.float32)
    angle = np.arange(SEQ_LEN, dtype=np.float32)[:, None] * frequency[None, :]
    cosine, sine = np.cos(angle).astype(np.float32), np.sin(angle).astype(np.float32)
    zero = np.zeros_like(sine)
    cos_table = np.concatenate([cosine] * 4, axis=1)
    left_table = np.concatenate([-sine, zero] * 2, axis=1)
    right_table = np.concatenate([zero, sine] * 2, axis=1)
    return cos_table, left_table, right_table


def turn(values, cos_table, left_table, right_table, sign):
    parts = []
    for c in range(values.shape[1] // 128):
        piece = values[:, 128 * c : 128 * (c + 1)]
        ahead = pltpu.roll(piece, 96, 1) * left_table
        behind = pltpu.roll(piece, 32, 1) * right_table
        parts.append(piece * cos_table + sign * (ahead + behind))
    return parts[0] if len(parts) == 1 else jnp.concatenate(parts, axis=1)


def key_range(block):
    return max(0, block - 2) * QB, (block + 1) * QB


def block_mask(seg_col, seg_row, block):
    low, high = key_range(block)
    rows = lax.broadcasted_iota(jnp.int32, (QB, high - low), 0) + block * QB
    cols = lax.broadcasted_iota(jnp.int32, (QB, high - low), 1) + low
    same = seg_col[block * QB : (block + 1) * QB, :] == seg_row[:, low:high]
    return jnp.concatenate([(rows >= cols) & same] * GROUP, axis=0)


def heads_of(values, pair, block):
    rows = values[block * QB : (block + 1) * QB, :]
    first = pair * GROUP
    return jnp.concatenate(
        [rows[:, HEAD * h : HEAD * (h + 1)] for h in range(first, first + GROUP)], axis=0
    )


def attention_forward_kernel(
    parts, levels, x_ref, gain_ref, w_ref, cos_ref, left_ref, right_ref, seg_col_ref, seg_row_ref,
    part_ref, normed_t_ref, proj_ref, mixed_ref, lse_ref, full_ref, normed_ref, *sems,
):
    step = pl.program_id(0)
    plan = Gather(parts, levels, [full_ref], sems)

    @pl.when(step == 0)
    def _():
        plan.greet(near=False)
        plan.own_to_mate(lambda: full_ref.at[pl.ds(plan.shard * parts, parts)], 0)
        for k in range(1, levels):
            plan.spread(0, k)

    @pl.when(step == 0)
    def _():
        x = x_ref[...].astype(F32)
        scale = lax.rsqrt(jnp.mean(x * x, axis=-1, keepdims=True) + EPSILON)
        normed = (x * scale * gain_ref[...].astype(F32)).astype(BF16)
        normed_ref[...] = normed
        normed_t_ref[...] = normed.T

    projected = dot_nn(normed_ref[...], w_ref[...])
    turned = turn(projected[:, : QW + KW], cos_ref[...], left_ref[...], right_ref[...], 1.0)
    queries = (turned[:, :QW] * HEAD**-0.5).astype(BF16)
    keys = turned[:, QW:].astype(BF16)
    values = projected[:, QW + KW :].astype(BF16)
    proj_ref[...] = jnp.concatenate([queries, keys, values], axis=1)
    seg_col, seg_row = seg_col_ref[...], seg_row_ref[...]
    for block in range(SEQ_LEN // QB):
        low, high = key_range(block)
        allowed = block_mask(seg_col, seg_row, block)
        outs = []
        for pair in range(2):
            q3 = heads_of(queries, pair, block)
            k1 = keys[low:high, HEAD * pair : HEAD * (pair + 1)]
            v1 = values[low:high, HEAD * pair : HEAD * (pair + 1)]
            scores = jnp.where(allowed, dot_nt(q3, k1), MASKED)
            top = jnp.max(scores, axis=-1, keepdims=True)
            weights = jnp.exp(scores - top)
            total = jnp.sum(weights, axis=-1, keepdims=True)
            mixed = dot_nn(weights.astype(BF16), v1) * (1.0 / total)
            logsum = top + jnp.log(total)
            for h in range(GROUP):
                outs.append(mixed[h * QB : (h + 1) * QB, :])
                lse_ref[0, block * QB : (block + 1) * QB, pair * GROUP + h : pair * GROUP + h + 1] = (
                    logsum[h * QB : (h + 1) * QB, :]
                )
        mixed_ref[block * QB : (block + 1) * QB, :] = jnp.concatenate(outs, axis=1).astype(BF16)

    @pl.when(step == PAIRS - 1)
    def _():
        plan.team_to_mate(0)
        plan.mate_arrived(0)
        plan.finish()


def whole_spec(shape):
    return pl.BlockSpec(shape, lambda *_: (0,) * len(shape))


def attention_forward(x, gain_row, w_full, tables, seg_col, seg_row, out_part, groups, shards):
    tokens, width = x.shape
    parts, levels = gather_parts(groups, width // shards), shards // 2
    table = whole_spec((SEQ_LEN, 128))
    *kept, out_full = pl.pallas_call(
        functools.partial(attention_forward_kernel, parts, levels),
        grid=(PAIRS,),
        in_specs=[
            whole_spec((tokens, width)),
            whole_spec((1, width)),
            pl.BlockSpec((width, BLOCK), lambda j: (0, j)),
            table, table, table,
            whole_spec((SEQ_LEN, 1)),
            whole_spec((1, SEQ_LEN)),
            pl.BlockSpec(memory_space=pl.ANY),
        ],
        out_specs=[
            whole_spec((width, tokens)),
            pl.BlockSpec((tokens, BLOCK), lambda j: (0, j)),
            pl.BlockSpec((tokens, QW), lambda j: (0, j)),
            pl.BlockSpec((1, tokens, 8), lambda j: (j, 0, 0)),
            pl.BlockSpec(memory_space=pl.ANY),
        ],
        out_shape=[
            jax.ShapeDtypeStruct((width, tokens), BF16),
            jax.ShapeDtypeStruct((tokens, PAIRS * BLOCK), BF16),
            jax.ShapeDtypeStruct((tokens, HEADS * HEAD), BF16),
            jax.ShapeDtypeStruct((PAIRS, tokens, 8), F32),
            jax.ShapeDtypeStruct(out_part.shape, BF16),
        ],
        scratch_shapes=[pltpu.VMEM((tokens, width), BF16)] + gather_sems(levels, parts, 1),
        input_output_aliases={8: 4},
        compiler_params=pltpu.CompilerParams(
            vmem_limit_bytes=62 << 20, collective_id=4, has_side_effects=True
        ),
        cost_estimate=pl.CostEstimate(flops=10 * 10**9, bytes_accessed=20 << 20, transcendentals=4 << 20),
        name="attention_forward",
    )(x, gain_row, w_full, *tables, seg_col, seg_row, out_part)
    return *kept, out_full.reshape(width, -1)


def attention_backward_kernel(
    groups, levels, ag_ref, out_ref, proj_ref, mixed_ref, lse_ref, cos_ref, left_ref, right_ref,
    seg_col_ref, seg_row_ref, all_ref, dproj_ref, sum_ref, mixed_t, *rest,
):
    step = pl.program_id(0)
    plan = Reduce(groups, levels, ag_ref.shape[1], rest[:4], rest[4:])

    @pl.when(step == 0)
    def _():
        plan.greet(False)
        mixed_t[...] = all_ref[...].T
        plan.fill(mixed_t, ag_ref)
        plan.merge()

    @pl.when(step == 1)
    def _():
        plan.spread()

    grads = dot_nt(ag_ref[...], out_ref[...]).astype(BF16)
    product = grads.astype(F32) * mixed_ref[...].astype(F32)
    queries, keys, values = (
        proj_ref[:, :QW], proj_ref[:, QW : QW + KW], proj_ref[:, QW + KW :],
    )
    seg_col, seg_row = seg_col_ref[...], seg_row_ref[...]
    blocks = SEQ_LEN // QB
    dk = [[jnp.zeros((QB, HEAD), F32) for _ in range(blocks)] for _ in range(2)]
    dv = [[jnp.zeros((QB, HEAD), F32) for _ in range(blocks)] for _ in range(2)]
    dq_rows = []
    for block in range(blocks):
        low, high = key_range(block)
        allowed = block_mask(seg_col, seg_row, block)
        dqs = []
        for pair in range(2):
            q3, g3, o3 = (heads_of(v, pair, block) for v in (queries, grads, product))
            k1 = keys[low:high, HEAD * pair : HEAD * (pair + 1)]
            v1 = values[low:high, HEAD * pair : HEAD * (pair + 1)]
            logsum = jnp.concatenate(
                [
                    lse_ref[0, block * QB : (block + 1) * QB, pair * GROUP + h : pair * GROUP + h + 1]
                    for h in range(GROUP)
                ],
                axis=0,
            )
            scores = jnp.where(allowed, dot_nt(q3, k1), MASKED)
            probs = jnp.exp(scores - logsum)
            inner = jnp.sum(o3, axis=-1, keepdims=True)
            score_grads = (probs * (dot_nt(g3, v1) - inner)).astype(BF16)
            dq = dot_nn(score_grads, k1)
            dk_part = dot_tn(score_grads, q3)
            dv_part = dot_tn(probs.astype(BF16), g3)
            for at in range(low // QB, high // QB):
                rows = slice(at * QB - low, (at + 1) * QB - low)
                dk[pair][at] += dk_part[rows]
                dv[pair][at] += dv_part[rows]
            dqs += [dq[h * QB : (h + 1) * QB, :] for h in range(GROUP)]
        dq_rows.append(jnp.concatenate(dqs, axis=1))
    dq_all = jnp.concatenate(dq_rows, axis=0)
    dk_all = jnp.concatenate([jnp.concatenate(d, axis=0) for d in dk], axis=1)
    dv_all = jnp.concatenate([jnp.concatenate(d, axis=0) for d in dv], axis=1)
    turned = jnp.concatenate([dq_all * HEAD**-0.5, dk_all], axis=1)
    back = turn(turned, cos_ref[...], left_ref[...], right_ref[...], -1.0)
    dproj_ref[...] = jnp.concatenate([back, dv_all], axis=1).astype(BF16)

    @pl.when(step == PAIRS - 1)
    def _():
        for k in range(levels):
            sum_ref[k] = plan.collect(k).astype(BF16)
        plan.finish()


def attention_backward(ag, out_full, proj, mixed, lse, tables, seg_col, seg_row, groups, shards):
    tokens, width = ag.shape
    levels, rows = shards // 2, width // shards
    chunk = chunk_of(width, groups)
    table = whole_spec((SEQ_LEN, 128))
    return pl.pallas_call(
        functools.partial(attention_backward_kernel, groups, levels),
        grid=(PAIRS,),
        in_specs=[
            whole_spec((tokens, width)),
            pl.BlockSpec((QW, width), lambda j: (j, 0)),
            pl.BlockSpec((tokens, BLOCK), lambda j: (0, j)),
            pl.BlockSpec((tokens, QW), lambda j: (0, j)),
            pl.BlockSpec((1, tokens, 8), lambda j: (j, 0, 0)),
            table, table, table,
            whole_spec((SEQ_LEN, 1)),
            whole_spec((1, SEQ_LEN)),
            whole_spec((tokens, mixed.shape[1])),
        ],
        out_specs=[
            pl.BlockSpec((tokens, BLOCK), lambda j: (0, j)),
            whole_spec((levels, rows, chunk)),
        ],
        out_shape=[
            jax.ShapeDtypeStruct((tokens, PAIRS * BLOCK), BF16),
            jax.ShapeDtypeStruct((levels, rows, chunk), BF16),
        ],
        scratch_shapes=[pltpu.VMEM((mixed.shape[1], tokens), BF16)]
        + reduce_buffers(groups, levels, rows, chunk)
        + reduce_sems(groups, levels),
        compiler_params=pltpu.CompilerParams(
            vmem_limit_bytes=62 << 20, collective_id=5, has_side_effects=True
        ),
        cost_estimate=pl.CostEstimate(flops=10 * 10**9, bytes_accessed=20 << 20, transcendentals=4 << 20),
        name="attention_backward",
    )(ag, out_full, proj, mixed, lse, *tables, seg_col, seg_row, mixed)


def middle_kernel(
    mixed_ref, out_ref, x_ref, gain_ref, router_ref, routes_ref,
    hidden_ref, ffn_ref, gates_ref, meta_ref,
):
    hidden = x_ref[...].astype(F32) + dot_nn(mixed_ref[...], out_ref[...])
    scale = lax.rsqrt(jnp.mean(hidden * hidden, axis=-1, keepdims=True) + EPSILON)
    hidden_ref[...] = hidden
    ffn_in = (hidden * scale * gain_ref[...].astype(F32)).astype(BF16)
    ffn_ref[...] = ffn_in
    logits = dot_nt(router_ref[...], ffn_in)
    experts, tokens = logits.shape
    index = lax.broadcasted_iota(jnp.int32, (experts, tokens), 0)
    flags = index == routes_ref[0:1, :]
    for k in range(1, TOP):
        flags = flags | (index == routes_ref[k : k + 1, :])
    chosen = jnp.where(flags, logits, MASKED)
    weights = jnp.where(flags, jnp.exp(chosen - jnp.max(chosen, axis=0, keepdims=True)), 0.0)
    gates = weights / jnp.sum(weights, axis=0, keepdims=True)
    gates_ref[...] = gates
    earlier = lax.broadcasted_iota(jnp.int32, (tokens, tokens), 0)
    later = lax.broadcasted_iota(jnp.int32, (tokens, tokens), 1)
    before = jnp.where(earlier < later, 1.0, 0.0).astype(BF16)
    ranks = dot_nn(jnp.where(flags, 1.0, 0.0).astype(BF16), before)
    slots = jnp.where(flags, ranks, -1.0)
    groups = meta_ref.shape[0]
    count = experts // groups
    meta_ref[...] = jnp.zeros(meta_ref.shape, F32)
    for e in range(experts):
        meta_ref[e // count, e % count : e % count + 1, :] = slots[e : e + 1]
        meta_ref[e // count, 8 + e % count : 9 + e % count, :] = gates[e : e + 1]


def middle(mixed, out_full, x, gain_row, router_rows, routes_rows, groups):
    tokens, width = x.shape
    experts = router_rows.shape[0]
    return pl.pallas_call(
        middle_kernel,
        out_shape=[
            jax.ShapeDtypeStruct((tokens, width), F32),
            jax.ShapeDtypeStruct((tokens, width), BF16),
            jax.ShapeDtypeStruct((experts, tokens), F32),
            jax.ShapeDtypeStruct((groups, 16, tokens), F32),
        ],
        compiler_params=pltpu.CompilerParams(vmem_limit_bytes=62 << 20),
        cost_estimate=pl.CostEstimate(flops=3 * 10**9, bytes_accessed=16 << 20, transcendentals=1 << 14),
        name="middle",
    )(mixed, out_full, x, gain_row, router_rows, routes_rows)


def flipped(index, mask):
    out, bit = index, 1
    while bit <= mask:
        if mask & bit:
            out = out + bit - 2 * bit * ((index // bit) % 2)
        bit *= 2
    return out


def send(source, target, send_sem, recv_sem, device):
    return pltpu.make_async_remote_copy(
        src_ref=source, dst_ref=target, send_sem=send_sem, recv_sem=recv_sem,
        device_id=device, device_id_type=pl.DeviceIdType.MESH,
    )


def greet(devices):
    barrier = pltpu.get_barrier_semaphore()
    for device in devices:
        pl.semaphore_signal(barrier, inc=1, device_id=device, device_id_type=pl.DeviceIdType.MESH)
    pl.semaphore_wait(barrier, len(devices))


class Gather:
    def __init__(self, parts, levels, blocks, sems):
        self.parts, self.levels, self.blocks = parts, levels, blocks
        self.near_send, self.near_recv, self.team_send, self.team_recv, self.core_send, self.core_recv = sems
        self.group, self.shard = lax.axis_index("expert"), lax.axis_index("shard")
        level, self.core = self.shard // 2, self.shard % 2
        self.part = self.group % parts
        self.other = self.shard + 1 - 2 * self.core
        self.far = [flipped(level, k) * 2 + self.core for k in range(levels)]
        self.far_other = [flipped(level, k) * 2 + 1 - self.core for k in range(levels)]
        self.team_part = [flipped(self.part, k) for k in range(parts)]
        self.team = [self.group - self.part + t for t in self.team_part]
        self.mate = (self.group, self.other)
        self.sends = []

    def greet(self, near=True):
        greet(
            [self.mate]
            + [(self.group, self.far[k]) for k in range(1, self.levels) if near]
            + [(self.team[t], self.shard) for t in range(1, self.parts)]
        )

    def push(self, make):
        make().start()
        self.sends.append(make)

    def arrived(self, piece, send_sem, recv_sem):
        send(piece, piece, send_sem, recv_sem, self.mate).wait_recv()

    def near(self, own, i):
        for k in range(1, self.levels):
            self.push(
                lambda k=k: send(
                    own.at[self.part], self.blocks[i].at[self.shard * self.parts + self.part],
                    self.near_send.at[i, k], self.near_recv.at[i, k], (self.group, self.far[k]),
                )
            )

    def near_arrived(self, i, k):
        piece = self.blocks[i].at[self.far[k] * self.parts + self.part]
        self.arrived(piece, self.near_send.at[i, k], self.near_recv.at[i, k])

    def spread(self, i, k):
        def piece():
            return self.blocks[i].at[self.far[k] * self.parts + self.part]

        for t in range(1, self.parts):
            self.push(
                lambda t=t: send(
                    piece(), piece(), self.team_send.at[i, k, t], self.team_recv.at[i, k, t],
                    (self.team[t], self.shard),
                )
            )
        self.push(
            lambda: send(
                piece(), piece(), self.core_send.at[i, k, 0], self.core_recv.at[i, k, 0], self.mate
            )
        )

    def own_to_mate(self, own, i):
        self.push(
            lambda: send(
                own(), self.blocks[i].at[pl.ds(self.shard * self.parts, self.parts)],
                self.core_send.at[i, 0, 0], self.core_recv.at[i, 0, 0], self.mate,
            )
        )

    def team_to_mate(self, i):
        for k in range(1, self.levels):
            for t in range(1, self.parts):

                def piece(k=k, t=t):
                    return self.blocks[i].at[self.far[k] * self.parts + self.team_part[t]]

                self.arrived(piece(), self.team_send.at[i, k, t], self.team_recv.at[i, k, t])
                self.push(
                    lambda piece=piece, k=k, t=t: send(
                        piece(), piece(), self.core_send.at[i, k, t], self.core_recv.at[i, k, t],
                        self.mate,
                    )
                )

    def mate_arrived(self, i):
        piece = self.blocks[i].at[pl.ds(self.other * self.parts, self.parts)]
        self.arrived(piece, self.core_send.at[i, 0, 0], self.core_recv.at[i, 0, 0])
        for k in range(1, self.levels):
            for t in range(self.parts):
                piece = self.blocks[i].at[self.far_other[k] * self.parts + self.team_part[t]]
                self.arrived(piece, self.core_send.at[i, k, t], self.core_recv.at[i, k, t])

    def finish(self):
        for make in self.sends:
            make().wait_send()


def gather_sems(levels, parts, count):
    dma = pltpu.SemaphoreType.DMA
    return [dma((count, levels))] * 2 + [dma((count, levels, parts))] * 4


def gather_parts(groups, rows):
    return next(p for p in (4, 2, 1) if groups % p == 0 and rows % (16 * p) == 0)


class Rows:
    def __init__(self, groups, own, outs, sems):
        self.own, self.outs = own, outs
        self.send_sem, self.recv_sem = sems
        group, self.shard = lax.axis_index("expert"), lax.axis_index("shard")
        self.team = [flipped(group, t) for t in range(groups)]
        self.near = range(1, 1 + len(outs))

    def copy(self, t):
        return send(
            self.own, self.outs[t - 1], self.send_sem.at[t], self.recv_sem.at[t],
            (self.team[t], self.shard),
        )

    def start(self):
        for t in self.near:
            self.copy(t).start()

    def finish(self):
        for t in self.near:
            self.copy(t).wait()


def gather_kernel(groups, parts, levels, *refs):
    ins, own_rows, outs, refs = refs[:2], refs[2], refs[3:5], refs[5:]
    count = 2 if groups == 4 else groups - 1
    others, refs = refs[:count], refs[count:]
    bounce, local_sem = refs[:2], refs[2]
    plan = Gather(parts, levels, outs, refs[3:9])
    rows = Rows(groups, own_rows, others, refs[9:11])
    greet(
        [plan.mate]
        + [(plan.group, plan.far[k]) for k in range(1, levels)]
        + [(rows.team[t], rows.shard) for t in range(1, groups)]
    )
    own = pl.ds(plan.shard * parts, parts)
    loads = [pltpu.make_async_copy(ins[i], bounce[i], local_sem.at[0, i]) for i in range(2)]
    stores = [pltpu.make_async_copy(bounce[i], outs[i].at[own], local_sem.at[1, i]) for i in range(2)]
    for copy in loads:
        copy.start()
    for i in range(2):
        plan.near(ins[i], i)
    rows.start()
    plan.own_to_mate(lambda: ins[0], 0)
    for load, store in zip(loads, stores):
        load.wait()
        store.start()
    for k in range(1, levels):
        plan.near_arrived(0, k)
        plan.spread(0, k)
    plan.team_to_mate(0)
    for k in range(1, levels):
        plan.near_arrived(1, k)
    plan.mate_arrived(0)
    plan.finish()
    rows.finish()
    for copy in stores:
        copy.wait()


def gather_weights(blocks, own_rows, groups, shards):
    rows = blocks[0].shape[0]
    parts = gather_parts(groups, rows)
    levels, count = shards // 2, 2 if groups == 4 else groups - 1
    blocks = [b.reshape(parts, rows // parts, b.shape[1]) for b in blocks]
    dma = pltpu.SemaphoreType.DMA
    return pl.pallas_call(
        functools.partial(gather_kernel, groups, parts, levels),
        in_specs=[pl.BlockSpec(memory_space=pl.ANY)] * 3,
        out_specs=[pl.BlockSpec(memory_space=pl.ANY)] * (2 + count),
        out_shape=[
            jax.ShapeDtypeStruct((shards * parts,) + b.shape[1:], b.dtype) for b in blocks
        ]
        + [jax.ShapeDtypeStruct(own_rows.shape, own_rows.dtype)] * count,
        scratch_shapes=[pltpu.VMEM(b.shape, b.dtype) for b in blocks]
        + [dma((2, 2))]
        + gather_sems(levels, parts, 2)
        + [dma((groups,)), dma((groups,))],
        compiler_params=pltpu.CompilerParams(
            collective_id=0, has_side_effects=True, vmem_limit_bytes=62 << 20
        ),
        name="gather_weights",
    )(*blocks, own_rows)


class Reduce:
    def __init__(self, groups, levels, cols, refs, sems):
        self.groups, self.levels, self.relay = groups, levels, groups == 4
        self.held, self.from_core, self.passing, self.from_group = refs
        self.core_send, self.core_recv, self.pass_send, self.pass_recv, self.group_send, self.group_recv = sems
        self.group, self.shard = lax.axis_index("expert"), lax.axis_index("shard")
        level, self.core = self.shard // 2, self.shard % 2
        self.mate = (self.group, self.shard + 1 - 2 * self.core)
        self.team = [flipped(self.group, t) for t in range(groups)]
        self.far = [flipped(level, k) for k in range(levels)]
        self.order = sorted(range(levels), key=lambda k: (k & -k or levels, k))
        self.near = [1, 2] if self.relay else list(range(1, groups))
        self.sends = []
        turns = ([3] if self.relay else []) + self.near + [0]
        self.even = self.held.shape[4] * groups == cols
        self.chunks = [self.team[t] if self.even else k for k, t in enumerate(turns)]

    def greet(self, climbs):
        greet(
            [self.mate]
            + [(self.group, self.far[k] * 2 + self.core) for k in range(1, self.levels) if climbs]
            + [(self.team[t], self.shard) for t in range(1, self.groups)]
        )

    def push(self, make):
        make().start()
        self.sends.append(make)

    def arrived(self, piece, send_sem, recv_sem):
        send(piece, piece, send_sem, recv_sem, self.mate).wait_recv()

    def fill(self, left, right):
        rows, chunk = self.held.shape[3:]
        tall = 768
        per = tall // rows
        even = self.even
        for k in self.chunks:
            low = k * chunk
            many = chunk if even else max(0, min(chunk, right.shape[1] - low))
            if many:
                at = pl.ds(pl.multiple_of(low, 128), many) if even else slice(low, low + many)

                @pl.loop(0, left.shape[0] // tall)
                def _(c):
                    part = pl.ds(pl.multiple_of(c * tall, tall), tall)
                    value = dot_nn(left[part, :], right[:, at]).astype(BF16)
                    for i in range(per):
                        s = c * per + i
                        self.held[k, s % 2, s // 2, :, :many] = value[i * rows : (i + 1) * rows]

            self.push(
                lambda k=k: send(
                    self.held.at[k, 1 - self.core], self.from_core.at[k],
                    self.core_send.at[k], self.core_recv.at[k], self.mate,
                )
            )

    def pass_copy(self, part, k):
        half = self.held.shape[3] // 2
        return send(
            self.held.at[self.team[3], self.core, self.far[k], pl.ds(part * half, half)],
            self.passing.at[part, k], self.pass_send.at[part, k], self.pass_recv.at[part, k],
            (self.team[1 + part], self.shard),
        )

    def group_copy(self, t, k):
        return send(
            self.held.at[self.team[t], self.core, self.far[k]], self.from_group.at[t, k],
            self.group_send.at[t, k], self.group_recv.at[t, k], (self.team[t], self.shard),
        )

    def merge(self):
        for n, k in enumerate(self.chunks):
            self.arrived(self.from_core.at[k], self.core_send.at[k], self.core_recv.at[k])

            @pl.loop(0, self.levels)
            def _(z):
                self.held[k, self.core, z] = (
                    self.held[k, self.core, z].astype(F32) + self.from_core[k, z].astype(F32)
                ).astype(BF16)

            if self.relay and n == 0:
                for j in self.order:
                    for part in range(2):
                        self.push(lambda part=part, j=j: self.pass_copy(part, j))
        if not self.relay:
            for j in self.order:
                for t in self.near:
                    self.push(lambda t=t, j=j: self.group_copy(t, j))

    def spread(self):
        if not self.relay:
            return
        half = self.held.shape[3] // 2
        for k in self.order:
            for part in range(2):
                self.arrived(
                    self.passing.at[part, k], self.pass_send.at[part, k], self.pass_recv.at[part, k]
                )
                at = pl.ds(part * half, half)
                piece = self.held.at[self.team[2 - part], self.core, self.far[k], at]
                piece[...] = (piece[...].astype(F32) + self.passing[part, k].astype(F32)).astype(BF16)
            for t in self.near:
                self.push(lambda t=t, k=k: self.group_copy(t, k))

    def collect(self, k):
        total = self.held[self.group, self.core, self.far[k]].astype(F32)
        for t in self.near:
            self.arrived(self.from_group.at[t, k], self.group_send.at[t, k], self.group_recv.at[t, k])
            total = total + self.from_group[t, k].astype(F32)
        return total

    def bits(self):
        return [bit for bit in (1, 2, 4, 8, 16) if bit < self.levels]

    def climb(self, summed, from_level, sems, bit, only=None):
        for k in range(self.levels) if only is None else [only]:
            if k & bit and not k & (bit - 1):
                self.push(
                    lambda k=k: send(
                        summed.at[k], from_level.at[k], sems[0].at[k], sems[1].at[k],
                        (self.group, self.far[bit] * 2 + self.core),
                    )
                )

    def climbed(self, summed, from_level, sems, bit):
        for k in range(self.levels):
            if k & bit and not k & (bit - 1):
                self.arrived(from_level.at[k], sems[0].at[k], sems[1].at[k])
                to = k - bit
                summed[to] = (summed[to].astype(F32) + from_level[k].astype(F32)).astype(BF16)

    def settle(self, summed, home, home_sems):
        home[self.group] = summed[0]
        for t in range(1, self.groups):
            self.push(
                lambda t=t: send(
                    home.at[self.group], home.at[self.group],
                    home_sems[0].at[t], home_sems[1].at[t], (self.team[t], self.shard),
                )
            )

    def landed(self, home, home_sems):
        for t in range(1, self.groups):
            self.arrived(home.at[self.team[t]], home_sems[0].at[t], home_sems[1].at[t])

    def finish(self):
        for make in self.sends:
            make().wait_send()


def chunk_of(total, groups):
    return 128 * (-(-total // (128 * groups)))


def reduce_buffers(groups, levels, rows, chunk):
    piece = (rows, chunk)
    passing = (2, levels, rows // 2, chunk) if groups == 4 else (1, 1, 16, 128)
    return [
        pltpu.VMEM((groups, 2, levels) + piece, BF16),
        pltpu.VMEM((groups, levels) + piece, BF16),
        pltpu.VMEM(passing, BF16),
        pltpu.VMEM((groups, levels) + piece, BF16),
    ]


def reduce_sems(groups, levels):
    dma = pltpu.SemaphoreType.DMA
    return [dma((groups,))] * 2 + [dma((2, levels))] * 2 + [dma((groups, levels))] * 2


class FewRows:
    def __init__(self, plan, refs, sems):
        self.plan = plan
        self.rows, self.from_core, self.from_group, self.pieces, self.from_level = refs
        self.core_send, self.core_recv, self.group_send, self.group_recv, self.level_send, self.level_recv = sems

    def start(self):
        plan = self.plan
        plan.push(
            lambda: send(self.rows, self.from_core, self.core_send, self.core_recv, plan.mate)
        )

    def over_groups(self):
        plan = self.plan
        plan.arrived(self.from_core, self.core_send, self.core_recv)
        total = self.rows[...].astype(F32) + self.from_core[...].astype(F32)
        self.from_group[plan.group] = total.astype(BF16)
        for t in range(1, plan.groups):
            plan.push(
                lambda t=t: send(
                    self.from_group.at[plan.group], self.from_group.at[plan.group],
                    self.group_send.at[t], self.group_recv.at[t], (plan.team[t], plan.shard),
                )
            )

    def over_levels(self):
        plan = self.plan
        for t in range(1, plan.groups):
            plan.arrived(self.from_group.at[plan.team[t]], self.group_send.at[t], self.group_recv.at[t])
        total = self.from_group[0].astype(F32)
        for g in range(1, plan.groups):
            total = total + self.from_group[g].astype(F32)
        wide = self.pieces.shape[2]
        for s in range(2 * plan.levels):
            self.pieces[s] = total[:, s * wide : (s + 1) * wide].astype(BF16)
        for k in range(1, plan.levels):
            plan.push(
                lambda k=k: send(
                    self.pieces.at[plan.far[k] * 2 + plan.core], self.from_level.at[k],
                    self.level_send.at[k], self.level_recv.at[k],
                    (plan.group, plan.far[k] * 2 + plan.core),
                )
            )

    def total(self):
        plan = self.plan
        total = self.pieces[plan.shard].astype(F32)
        for k in range(1, plan.levels):
            plan.arrived(self.from_level.at[k], self.level_send.at[k], self.level_recv.at[k])
            total = total + self.from_level[k].astype(F32)
        return total


def input_back(dproj_ref, w_ref, x_ref, gain_ref, held, inner, scale, gain_grad):
    width, step = x_ref.shape[1], 256
    x = x_ref[...].astype(F32)
    scale[...] = lax.rsqrt(jnp.mean(x * x, axis=-1, keepdims=True) + EPSILON)
    inner[...] = jnp.zeros(inner.shape, F32)

    @pl.loop(0, width // step)
    def _(c):
        at = pl.ds(pl.multiple_of(c * step, step), step)
        normed_grads = dot_nt(dproj_ref[...], w_ref[at, :])
        x = x_ref[:, at].astype(F32)
        weighted = normed_grads * gain_ref[:, at].astype(F32)
        inner[...] += jnp.sum(weighted * x, axis=-1, keepdims=True)
        gain_grad[:, at] = jnp.sum(normed_grads * x * scale[...], axis=0, keepdims=True)
        r = scale[...]
        held[:, at] += r * weighted

    r = scale[...]
    factor = r * r * r * (inner[...] * (1.0 / width))
    for low in range(0, width, step):
        cols = slice(low, low + step)
        held[:, cols] -= x_ref[:, cols].astype(F32) * factor


def reduce_kernel(groups, levels, *refs):
    normed_t, dproj_ref, gain_two_ref, router_ref, out_sum_ref, gain_ref = refs[:6]
    w_in, x_in, hidden_grads_in, *refs = refs[6:]
    count = 2 if groups == 4 else groups - 1
    out_sent, refs = refs[:count], refs[count:]
    out_ref, qkv_ref, misc_ref, input_grad_ref, *refs = refs
    out_came, refs = refs[:count], refs[count:]
    summed, from_level, home, out_summed, out_level, out_home = refs[:6]
    plan = Reduce(groups, levels, dproj_ref.shape[1], refs[6:10], refs[10:16])
    level_sems, home_sems, out_level_sems, out_home_sems = (refs[i : i + 2] for i in range(16, 24, 2))
    misc = FewRows(plan, refs[24:29], refs[29:35])
    w_buf, x_buf, held, inner, scale, gain_grad, load_sem, store_sem, row_send, row_recv = refs[35:]
    loads = [
        pltpu.make_async_copy(w_in.at[:, : dproj_ref.shape[1]], w_buf, load_sem.at[0]),
        pltpu.make_async_copy(x_in, x_buf, load_sem.at[1]),
        pltpu.make_async_copy(hidden_grads_in, held, load_sem.at[2]),
    ]
    for load in loads:
        load.start()
    first, *others = plan.bits()
    plan.greet(True)
    out_summed[...] = out_sum_ref[...]
    plan.climb(out_summed, out_level, out_level_sems, first)
    plan.fill(normed_t, dproj_ref)
    plan.merge()
    plan.spread()
    plan.climbed(out_summed, out_level, out_level_sems, first)
    for bit in others[:1]:
        plan.climb(out_summed, out_level, out_level_sems, bit)
    for k in plan.order:
        summed[k] = plan.collect(k).astype(BF16)
        plan.climb(summed, from_level, level_sems, first, k)
    row_copies = [
        send(
            out_sent[t - 1], out_came[t - 1], row_send.at[t], row_recv.at[t],
            (plan.team[t], plan.shard),
        )
        for t in range(1, count + 1)
    ]
    for copy in row_copies:
        copy.start()
    for load in loads:
        load.wait()
    input_back(dproj_ref, w_buf, x_buf, gain_ref, held, inner, scale, gain_grad)
    store = pltpu.make_async_copy(held, input_grad_ref, store_sem)
    store.start()
    experts = router_ref.shape[0]
    gains = jnp.concatenate(
        [gain_grad[...], gain_two_ref[...], jnp.zeros((6, gain_grad.shape[1]), F32)], axis=0
    )
    misc.rows[...] = jnp.zeros(misc.rows.shape, BF16)
    misc.rows[:8] = gains.astype(BF16)
    misc.rows[8 : 8 + experts] = router_ref[...].astype(BF16)
    misc.start()
    misc.over_groups()
    for n, bit in enumerate(others):
        plan.climbed(out_summed, out_level, out_level_sems, bit)
        for bit in others[n + 1 : n + 2]:
            plan.climb(out_summed, out_level, out_level_sems, bit)
    plan.settle(out_summed, out_home, out_home_sems)
    plan.climbed(summed, from_level, level_sems, first)
    for bit in others[:1]:
        plan.climb(summed, from_level, level_sems, bit)
    misc.over_levels()
    for n, bit in enumerate(others):
        plan.climbed(summed, from_level, level_sems, bit)
        for bit in others[n + 1 : n + 2]:
            plan.climb(summed, from_level, level_sems, bit)
    plan.settle(summed, home, home_sems)
    misc_ref[...] = misc.total()
    plan.landed(out_home, out_home_sems)
    out_ref[...] = out_home[...]
    plan.landed(home, home_sems)
    qkv_ref[...] = home[...]
    plan.finish()
    store.wait()
    for copy in row_copies:
        copy.wait()


def reduce_weights(normed_t, dproj, gain_two, router, out_sum, gain_row, w_full, x, hidden_grads, out_sent, groups, shards):
    tokens, width = x.shape
    levels, rows = shards // 2, width // shards
    total = dproj.shape[1]
    chunk, out_chunk = chunk_of(total, groups), out_sum.shape[2]
    dma = pltpu.SemaphoreType.DMA
    vmem, anywhere = (pl.BlockSpec(memory_space=m) for m in (pltpu.VMEM, pl.ANY))
    whole, out_whole = (groups, rows, chunk), (groups, rows, out_chunk)
    few = 16 * (-(-(8 + router.shape[0]) // 16))
    return pl.pallas_call(
        functools.partial(reduce_kernel, groups, levels),
        in_specs=[vmem] * 6 + [anywhere] * (3 + len(out_sent)),
        out_specs=[vmem] * 3 + [anywhere] * (1 + len(out_sent)),
        out_shape=[jax.ShapeDtypeStruct(s, BF16) for s in (out_whole, whole)]
        + [jax.ShapeDtypeStruct((few, rows), F32), jax.ShapeDtypeStruct((tokens, width), F32)]
        + [jax.ShapeDtypeStruct(o.shape, o.dtype) for o in out_sent],
        scratch_shapes=[
            pltpu.VMEM((levels, rows, chunk), BF16),
            pltpu.VMEM((levels, rows, chunk), BF16),
            pltpu.VMEM(whole, BF16),
            pltpu.VMEM((levels, rows, out_chunk), BF16),
            pltpu.VMEM((levels, rows, out_chunk), BF16),
            pltpu.VMEM(out_whole, BF16),
        ]
        + reduce_buffers(groups, levels, rows, chunk)
        + reduce_sems(groups, levels)
        + [dma((levels,))] * 2 + [dma((groups,))] * 2 + [dma((levels,))] * 2 + [dma((groups,))] * 2
        + [
            pltpu.VMEM((few, width), BF16),
            pltpu.VMEM((few, width), BF16),
            pltpu.VMEM((groups, few, width), BF16),
            pltpu.VMEM((shards, few, rows), BF16),
            pltpu.VMEM((levels, few, rows), BF16),
            dma, dma, dma((groups,)), dma((groups,)), dma((levels,)), dma((levels,)),
            pltpu.VMEM((width, total), BF16),
            pltpu.VMEM((tokens, width), BF16),
            pltpu.VMEM((tokens, width), F32),
            pltpu.VMEM((tokens, 1), F32),
            pltpu.VMEM((tokens, 1), F32),
            pltpu.VMEM((1, width), F32),
            dma((3,)), dma, dma((groups,)), dma((groups,)),
        ],
        compiler_params=pltpu.CompilerParams(
            collective_id=1, has_side_effects=True, vmem_limit_bytes=62 << 20
        ),
        cost_estimate=pl.CostEstimate(
            flops=2 * tokens * width * total, bytes_accessed=8 << 20, transcendentals=0
        ),
        name="reduce_weights",
    )(normed_t, dproj, gain_two, router, out_sum, gain_row, w_full, x, hidden_grads, *out_sent)


def expert_kernel(capacity, shards, groups, count, base, stage, *refs):
    refs = list(refs)
    take = lambda n: [refs.pop(0) for _ in range(n)]
    if stage == "first":
        x_own, meta_own = take(2)
        u_ins = take(3 if groups == 4 else groups)
    else:
        x_ref, u_ref, meta_ref, out_in, dx_in, gg_in = take(6)
    packed_ref = take(1)[0]
    if stage == "last":
        earlier_ref = take(1)[0]
    if stage == "first":
        x_all, u_all, meta_all, out_ref, dx_ref, gg_ref, dw_out = take(7)
    elif stage == "last":
        out_homes = take(3 if groups == 4 else groups)
        dx_home, gg_home, dw_out = take(3)
    else:
        out_ref, dx_ref, gg_ref, dw_out = take(4)
    xs, us, bs, inn, dw, dw_sem, we_all, wp_all, we_sem, wp_sem = take(10)
    if stage != "between":
        core_buf, core_send, core_recv, credit = take(4)
    if stage == "first":
        x_buf, u_buf, meta_buf = take(3)
        x_send, x_recv, meta_send, meta_recv, load_sem, u_sem, meta_sem, keep_sem, pass_sem = take(9)
    elif stage == "last":
        buf, passing, gg_buf = take(3)
        load_sem, pass_send, pass_recv, dx_send, dx_recv, gg_send, gg_recv, keep_sem = take(8)
    turn_at, expert = pl.program_id(0), pl.program_id(1)
    last_turn, last = groups - 1, count - 1
    group, shard = lax.axis_index("expert"), lax.axis_index("shard")
    team = [flipped(group, t) for t in range(groups)]
    core = shard % 2
    mate = (group, shard + 1 - 2 * core)
    width = xs.shape[2]
    tokens = x_buf.shape[0] if stage == "first" else x_ref.shape[1]
    tall, short = width // shards, FF // shards
    side = width - 2 * FF
    we_ref, wp_ref = we_all.at[expert], wp_all.at[expert]

    @pl.when((turn_at == 0) & (expert == 0))
    def _():
        for e in range(count):

            @pl.loop(0, shards)
            def _(s):
                a = pl.ds(pl.multiple_of(s * tall, 16), tall)
                b = pl.ds(pl.multiple_of(s * short, 16), short)
                low = pl.ds(pl.multiple_of(s * short, 16), short // 2)
                high = pl.ds(pl.multiple_of(s * short + short // 2, 16), short // 2)
                source = packed_ref.at[s, e]
                rest = pl.ds(tall + short, short // 2)
                for piece, target, sem in (
                    (source.at[:tall], we_all.at[e, a], we_sem),
                    (source.at[tall : tall + short], wp_all.at[e, b, : 2 * FF], wp_sem),
                    (source.at[rest, :side], wp_all.at[e, low, 2 * FF :], wp_sem),
                    (source.at[rest, side:], wp_all.at[e, high, 2 * FF :], wp_sem),
                ):
                    pltpu.make_async_copy(piece, target, sem.at[e]).start()

    def core_copy(source):
        return send(source.at[:, 1 - core], core_buf, core_send, core_recv, mate)

    def core_add(source):
        core_copy(source).wait()

        @pl.loop(0, shards // 2)
        def _(z):
            core_buf[z] = (dw[z, core].astype(F32) + core_buf[z].astype(F32)).astype(BF16)

    def store_half(at):
        return pltpu.make_async_copy(core_buf, dw_out.at[:, at], dw_sem)

    def core_free(at):
        store_half(at).wait()
        pl.semaphore_signal(credit, inc=1, device_id=mate, device_id_type=pl.DeviceIdType.MESH)

    def own_half():
        return pltpu.make_async_copy(earlier_ref.at[:, core], dw.at[:, core], keep_sem.at[1])

    before = 1 if stage == "last" else 0

    if stage == "first":
        relay = groups == 4
        near = [1, 2] if relay else list(range(1, groups))
        half = tokens // 2

        def x_copy(t):
            return send(x_own, x_all.at[t], x_send.at[t], x_recv.at[t], (team[t], shard))

        def passed(source, target, part, sems):
            at = pl.ds(part * half, half)
            return send(
                source.at[at], target.at[3, at], sems.at[0, part], sems.at[1, part],
                (team[2 - part], shard),
            )

        def x_pass(part):
            return passed(x_all.at[1 + part], x_all, part, pass_sem.at[0])

        def u_pass(part):
            return passed(u_ins[1 + part], u_all, part, pass_sem.at[1])

        def meta_copy(t):
            return send(
                meta_own.at[team[t]], meta_all.at[t], meta_send.at[t], meta_recv.at[t], (team[t], shard)
            )

        def u_load(t):
            source = u_all.at[t] if relay and t == 3 else u_ins[t]
            return pltpu.make_async_copy(source, u_buf.at[t % 2], u_sem.at[t % 2])

        def x_keep():
            return pltpu.make_async_copy(x_buf, x_all.at[0], keep_sem.at[0])

        def meta_keep():
            return pltpu.make_async_copy(meta_buf, meta_all.at[0], keep_sem.at[1])

        def u_keep(t):
            return pltpu.make_async_copy(u_buf.at[t % 2], u_all.at[t], keep_sem.at[2 + t])

        for t in range(groups):

            @pl.when((turn_at == t) & (expert == 0))
            def _():
                if t == 0:
                    u_load(0).start()
                    greet([mate] + [(team[k], shard) for k in range(1, groups)])
                    for k in range(1, groups):
                        meta_copy(k).start()
                    for k in near:
                        x_copy(k).start()
                    fetch_x, fetch_meta = x_own, meta_own.at[group]
                else:
                    if not relay:
                        x_copy(t).wait_recv()
                    elif t == 1:
                        for k in near:
                            x_copy(k).wait_recv()
                        for part in range(2):
                            x_pass(part).start()
                        for part in range(2):
                            u_pass(part).start()
                    elif t == 3:
                        for part in range(2):
                            x_pass(part).wait_recv()
                            u_pass(part).wait_recv()
                        u_load(3).start()
                    meta_copy(t).wait_recv()
                    u_keep(t - 1).wait()
                    if t == 1:
                        x_keep().wait()
                        meta_keep().wait()
                    fetch_x, fetch_meta = x_all.at[t], meta_all.at[t]
                load = pltpu.make_async_copy(fetch_x, x_buf, load_sem)
                load_meta = pltpu.make_async_copy(fetch_meta, meta_buf, meta_sem)
                load.start()
                load_meta.start()
                if t + 1 < groups and not (relay and t == 2):
                    u_load(t + 1).start()
                u_load(t).wait()
                load_meta.wait()
                load.wait()
                if not (relay and t == 3):
                    u_keep(t).start()
                if t == 0:
                    x_keep().start()
                    meta_keep().start()

        x_now, u_now, meta_now = x_buf, u_buf.at[turn_at % 2], meta_buf
    else:
        x_now, u_now, meta_now = x_ref.at[0], u_ref.at[0], meta_ref.at[0]

    if stage == "last":
        relay = groups == 4
        slots, half = buf.shape[1], tokens // 2
        halves = [pl.ds(0, half), pl.ds(half, half)]

        def kept(kind, i):
            return buf.at[kind, i % slots]

        def load(kind, i):
            source = dx_in if kind else out_in
            return pltpu.make_async_copy(
                source.at[last_turn - i], kept(kind, i), load_sem.at[kind, i % 2]
            )

        def store(i):
            return pltpu.make_async_copy(kept(0, i), out_homes[last_turn - i], keep_sem.at[2 + i])

        def pass_copy(kind, part):
            return send(
                kept(kind, 0).at[halves[part]], passing.at[kind, part],
                pass_send.at[kind, part], pass_recv.at[kind, part], (team[1 + part], shard),
            )

        def dx_copy(i):
            t = last_turn - i
            return send(kept(1, i), dx_home.at[t], dx_send.at[t], dx_recv.at[t], (team[t], shard))

        def dx_half(part):
            at = halves[part]
            return send(
                kept(1, 1).at[at], dx_home.at[2, at], dx_send.at[2 + part], dx_recv.at[2 + part],
                (team[2], shard),
            )

        def gg_copy(i):
            t = last_turn - i
            return send(gg_buf.at[i], gg_home.at[group], gg_send.at[t], gg_recv.at[t], (team[t], shard))

        def own_copies():
            return [
                pltpu.make_async_copy(kept(1, last_turn), dx_home.at[0], keep_sem.at[0]),
                pltpu.make_async_copy(gg_buf.at[last_turn], gg_home.at[group], keep_sem.at[1]),
            ]

        for i in range(groups):

            @pl.when((turn_at == i) & (expert == 0))
            def _():
                if i == 0:
                    for kind in range(2):
                        load(kind, 0).start()
                    greet([mate] + [(team[k], shard) for k in range(1, groups)])
                    core_copy(earlier_ref).start()
                    own_half().start()
                if i == 1:
                    own_half().wait()
                    core_add(earlier_ref)
                    store_half(0).start()
                if i == 2:
                    core_free(0)
                if i + 1 < groups:
                    if i + 1 >= slots:
                        dx_copy(i + 1 - slots).wait_send()
                        store(i + 1 - slots).wait()
                    for kind in range(2):
                        load(kind, i + 1).start()
                for kind in range(2):
                    load(kind, i).wait()

        at_now = turn_at % slots
        out_now, dx_now, gg_now = buf.at[0, at_now], buf.at[1, at_now], gg_buf.at[turn_at]
    else:
        out_now, dx_now, gg_now = out_ref.at[0], dx_ref.at[0], gg_ref.at[0]

    @pl.when(expert == 0)
    def _():
        if stage == "first":
            out_now[...] = jnp.zeros((tokens, width), BF16)
            dx_now[...] = jnp.zeros((tokens, width), BF16)
            gg_now[...] = jnp.zeros((8, tokens), F32)
        else:
            gg_now[...] = gg_in[0]
        if stage == "between":
            out_now[...] = out_in[0]
            dx_now[...] = dx_in[0]

    @pl.when(turn_at == 0)
    def _():
        pltpu.make_async_copy(we_ref, we_ref, we_sem.at[expert]).wait()
        pltpu.make_async_copy(wp_ref, wp_ref, wp_sem.at[expert]).wait()

    slot_row = meta_now[pl.ds(base + expert, 1), :]
    gate_row = meta_now[pl.ds(8 + base + expert, 1), :]
    index = lax.broadcasted_iota(jnp.int32, (capacity, tokens), 0).astype(F32)
    pick = jnp.where(index == slot_row, 1.0, 0.0)
    gate_col = jnp.sum(pick * gate_row, axis=1, keepdims=True)
    place = pick.astype(BF16)
    rows = pl.ds(pl.multiple_of(turn_at * capacity, capacity), capacity)
    x = dot_nn(place, x_now[...]).astype(BF16)
    xs[expert, rows, :] = x
    u_rows = dot_nn(place, u_now[...]).astype(BF16)
    us[expert, rows, :] = u_rows
    both_parts = dot_nn(x, we_ref[...])
    gate, up = both_parts[:, :FF], both_parts[:, FF:]
    back = dot_nt(u_rows, wp_ref[...])
    sig = 1.0 / (1.0 + jnp.exp(-gate))
    act = gate * sig
    inner = act * up
    inner_low = inner.astype(BF16)
    gate_grad = jnp.sum(inner * back, axis=1, keepdims=True)
    here = lax.broadcasted_iota(jnp.int32, (8, tokens), 0) == base + expert
    gg_now[...] = jnp.where(here, jnp.sum(pick * gate_grad, axis=0, keepdims=True), gg_now[...])
    inn[expert, rows, :] = (inner * gate_col).astype(BF16)
    inner_grads = back * gate_col
    bs[expert, rows, :FF] = (inner_grads * up * sig * (1.0 + gate * (1.0 - sig))).astype(BF16)
    bs[expert, rows, FF:] = (inner_grads * act).astype(BF16)
    both = bs[expert, rows, :]
    weighted_t = (pick * gate_row).astype(BF16).T
    place_t = place.T
    result = dot_nn(inner_low, wp_ref[...]).astype(BF16)
    out_now[...] = (out_now[...].astype(F32) + dot_nn(weighted_t, result)).astype(BF16)
    row_grads = dot_nt(both, we_ref[...]).astype(BF16)
    dx_now[...] = (dx_now[...].astype(F32) + dot_nn(place_t, row_grads)).astype(BF16)

    if stage == "last":

        def add_passed(kind):
            for part in range(2):
                pass_copy(kind, part).wait_recv()
                target = kept(kind, 1 + part).at[halves[part]]
                target[...] = (target[...].astype(F32) + passing[kind, part].astype(F32)).astype(BF16)

        for i in range(groups):

            @pl.when((turn_at == i) & (expert == last))
            def _():
                if i < last_turn:
                    gg_copy(i).start()
                else:
                    for copy in own_copies():
                        copy.start()
                if not relay:
                    store(i).start()
                    if i < last_turn:
                        dx_copy(i).start()
                elif i == 0:
                    for kind in (1, 0):
                        for part in range(2):
                            pass_copy(kind, part).start()
                elif i == 1:
                    dx_half(1).start()
                elif i == 2:
                    add_passed(1)
                    dx_copy(2).start()
                    dx_half(0).start()
                else:
                    add_passed(0)
                    for k in range(1, groups):
                        store(k).start()

    @pl.when(turn_at == last_turn)
    def _():
        if stage != "between" and count > 1:

            @pl.when(expert > 0)
            def _():
                core_add(dw)
                store_half(before + expert - 1).start()

        wide, half = 384, FF // 2

        @pl.loop(0, width // wide)
        def _(c):
            at = pl.ds(pl.multiple_of(c * wide, wide), wide)
            value = dot_tn(xs[expert, :, at], bs[expert]).astype(BF16)
            for i in range(wide // tall):
                s = c * (wide // tall) + i
                dw[s // 2, s % 2, :tall, :] = value[i * tall : (i + 1) * tall]

        @pl.loop(0, FF // half)
        def _(c):
            at = pl.ds(pl.multiple_of(c * half, half), half)
            value = dot_tn(inn[expert, :, at], us[expert]).astype(BF16)
            for i in range(half // short):
                s, low = c * (half // short) + i, i * short
                mid, high = low + short // 2, low + short
                dw[s // 2, s % 2, tall : tall + short, :] = value[low:high, : 2 * FF]
                dw[s // 2, s % 2, tall + short :, :side] = value[low:mid, 2 * FF :]
                dw[s // 2, s % 2, tall + short :, side:] = value[mid:high, 2 * FF :]

        if stage == "between":
            pltpu.make_async_copy(dw, dw_out, dw_sem).start()
        else:
            if count > 1:

                @pl.when(expert > 0)
                def _():
                    core_free(before + expert - 1)

            if before:
                pl.semaphore_wait(credit, 1)
            else:

                @pl.when(expert > 0)
                def _():
                    pl.semaphore_wait(credit, 1)

            core_copy(dw).start()

    @pl.when((turn_at == last_turn) & (expert == last))
    def _():
        if stage == "between":
            pltpu.make_async_copy(dw, dw_out, dw_sem).wait()
        else:
            core_add(dw)
            store_half(before + last).start()
            store_half(before + last).wait()
        if stage == "first":
            if not relay:
                u_keep(last_turn).wait()
            for t in range(1, groups):
                meta_copy(t).wait_send()
            for t in near:
                x_copy(t).wait_send()
            if relay:
                for part in range(2):
                    x_pass(part).wait_send()
                    u_pass(part).wait_send()
        if stage == "last":
            for i in range(groups - 1):
                t = last_turn - i
                gg_copy(i).wait_send()
                send(
                    gg_buf.at[i], gg_home.at[team[t]], gg_send.at[t], gg_recv.at[t], (team[t], shard)
                ).wait_recv()
            if relay:
                for part in range(2):
                    dx_half(part).wait()
                    for kind in range(2):
                        pass_copy(kind, part).wait_send()
                dx_copy(2).wait()
                for k in range(1, groups):
                    store(k).wait()
            else:
                for i in range(groups - 1):
                    if i + slots >= groups:
                        dx_copy(i).wait_send()
                    dx_copy(i).wait_recv()
                for i in range(groups - slots, groups):
                    store(i).wait()
            for copy in own_copies():
                copy.wait()


def expert_call(capacity, shards, groups, base, stage, data, packed_weights, *kept):
    count = packed_weights.shape[1]
    tokens, width = data[0].shape[-2:]
    total = groups * capacity
    anywhere = pl.BlockSpec(memory_space=pl.ANY)
    turned = (lambda i: i) if stage == "first" else (lambda i: groups - 1 - i)
    block = pl.BlockSpec((1, tokens, width), lambda i, e: (turned(i), 0, 0))
    small = pl.BlockSpec((1, 8, tokens), lambda i, e: (turned(i), 0, 0))
    dma = pltpu.SemaphoreType.DMA
    many = jax.ShapeDtypeStruct((groups, tokens, width), BF16)
    grads = jax.ShapeDtypeStruct((groups, 8, tokens), F32)
    piece = ((width + FF + FF // 2) // shards, 2 * FF)
    summed = 2 if stage == "between" else count + len(kept)
    weights = jax.ShapeDtypeStruct((shards // 2, summed) + piece, BF16)
    meta = jax.ShapeDtypeStruct((groups, 16, tokens), F32)
    scratch = [
        pltpu.VMEM((count, total, width), BF16),
        pltpu.VMEM((count, total, width), BF16),
        pltpu.VMEM((count, total, 2 * FF), BF16),
        pltpu.VMEM((count, total, FF), BF16),
        pltpu.VMEM((shards // 2, 2) + piece, BF16),
        dma,
        pltpu.VMEM((count, width, 2 * FF), BF16),
        pltpu.VMEM((count, FF, width), BF16),
        dma((count,)), dma((count,)),
    ]
    if stage != "between":
        scratch += [
            pltpu.VMEM((shards // 2,) + piece, BF16), dma, dma, pltpu.SemaphoreType.REGULAR,
        ]
    if stage == "first":
        in_specs = [anywhere] * len(data)
        out_specs = [anywhere] * 3 + [block, block, small, anywhere]
        out_shape = [many, many, meta, many, many, grads, weights]
        scratch += [
            pltpu.VMEM((tokens, width), BF16),
            pltpu.VMEM((2, tokens, width), BF16),
            pltpu.VMEM((16, tokens), F32),
            dma((groups,)), dma((groups,)), dma((groups,)), dma((groups,)),
            dma, dma((2,)), dma, dma((2 + groups,)), dma((2, 2, 2)),
        ]
    else:
        meta_block = pl.BlockSpec((1, 16, tokens), lambda i, e: (turned(i), 0, 0))
        in_specs = [block, block, meta_block, block, block, small]
        out_specs = [block, block, small, anywhere]
        if stage == "last":
            in_specs[3:5] = [anywhere] * 2
            sources = 3 if groups == 4 else groups
            out_specs = [anywhere] * (3 + sources)
            slots = groups if groups == 4 else 3
            passed = 2 if groups == 4 else 1
            scratch += [
                pltpu.VMEM((2, slots, tokens, width), BF16),
                pltpu.VMEM((passed, passed, tokens // 2, width), BF16),
                pltpu.VMEM((groups, 8, tokens), F32),
                dma((2, 2)), dma((2, 2)), dma((2, 2)),
                dma((groups,)), dma((groups,)), dma((groups,)), dma((groups,)), dma((2 + groups,)),
            ]
        out_shape = [many, many, grads, weights]
        if stage == "last":
            out_shape[:1] = [jax.ShapeDtypeStruct((tokens, width), BF16)] * sources
    remote = {"first": 2, "last": 3}
    return pl.pallas_call(
        functools.partial(expert_kernel, capacity, shards, groups, count, base, stage),
        grid=(groups, count),
        in_specs=in_specs + [anywhere] * (1 + len(kept)),
        out_specs=out_specs,
        out_shape=out_shape,
        scratch_shapes=scratch,
        compiler_params=pltpu.CompilerParams(
            vmem_limit_bytes=62 << 20,
            **({"collective_id": remote[stage], "has_side_effects": True} if stage in remote else {}),
        ),
        cost_estimate=pl.CostEstimate(
            flops=2 * count * total * width * (4 * tokens + 9 * FF),
            bytes_accessed=6 * groups * tokens * width * 2,
            transcendentals=count * total * FF,
        ),
        name="experts_" + stage,
    )(*data, packed_weights, *kept)


def norm_back(values, gain_row, grad_rows):
    scale_rows = lax.rsqrt(jnp.mean(values * values, axis=-1, keepdims=True) + EPSILON)
    weighted = gain_row * grad_rows
    inner_mean = jnp.mean(weighted * values, axis=-1, keepdims=True)
    input_part = (
        scale_rows * weighted - values * (scale_rows * scale_rows * scale_rows) * inner_mean
    )
    gain_part = jnp.sum(grad_rows * values * scale_rows, axis=0)
    return (input_part, gain_part)


def pack_kernel(
    cuts, expand_ref, project_ref, qkv_ref, gain_one_ref, gain_two_ref, router_ref, packed_ref, *refs
):
    *outs, misc = refs
    short = project_ref.shape[1]
    tall = expand_ref.shape[1]
    side = project_ref.shape[2] - 2 * FF
    for (low, high), out in zip(cuts, outs):
        for e in range(low, high):
            out[e - low, :tall] = expand_ref[e]
            out[e - low, tall : tall + short] = project_ref[e, :, : 2 * FF]
            out[e - low, tall + short :, :side] = project_ref[e, : short // 2, 2 * FF :]
            out[e - low, tall + short :, side:] = project_ref[e, short // 2 :, 2 * FF :]
    for j in range(PAIRS):
        at, to = HEADS * HEAD + j * KW, j * BLOCK + QW
        packed_ref[:, j * BLOCK : to] = qkv_ref[:, j * QW : (j + 1) * QW]
        packed_ref[:, to : to + KW] = qkv_ref[:, at : at + KW]
        at += KV_HEADS * HEAD
        packed_ref[:, to + KW : to + 2 * KW] = qkv_ref[:, at : at + KW]
    misc[...] = jnp.zeros(misc.shape, F32)
    misc[0:1] = gain_one_ref[...].astype(F32)[None]
    misc[1:2] = gain_two_ref[...].astype(F32)[None]
    misc[8 : 8 + router_ref.shape[0]] = router_ref[...].astype(F32)
    packed_ref[:, PAIRS * BLOCK :] = misc[...].T.astype(BF16)


def pack_weights(expand, project, qkv, gain_one, gain_two, router):
    cuts = bands(expand.shape[0])
    rows = expand.shape[1] + project.shape[1] + project.shape[1] // 2
    return pl.pallas_call(
        functools.partial(pack_kernel, cuts),
        out_shape=[jax.ShapeDtypeStruct((qkv.shape[0], PAIRS * BLOCK + MISC), BF16)]
        + [jax.ShapeDtypeStruct((high - low, rows, 2 * FF), BF16) for low, high in cuts],
        scratch_shapes=[pltpu.VMEM((MISC, qkv.shape[0]), F32)],
        compiler_params=pltpu.CompilerParams(vmem_limit_bytes=62 << 20),
        name="pack_weights",
    )(expand, project, qkv, gain_one, gain_two, router.T)


def hidden_back_kernel(
    dx_ref, gg_ref, gates_ref, router_ref, hidden_ref, gain_ref, up_ref, ffn_ref,
    grads_ref, low_ref, router_grad_ref, gain_grad_ref,
):
    gates, groups = gates_ref[...], gg_ref.shape[0]
    count = gates.shape[0] // groups
    gate_grads = jnp.concatenate([gg_ref[g, :count] for g in range(groups)], axis=0)
    mean = jnp.sum(gates * gate_grads, axis=0, keepdims=True)
    logit_grads = (gates * (gate_grads - mean)).astype(BF16)
    ffn_grads = dot_tn(logit_grads, router_ref[...])
    for g in range(dx_ref.shape[0]):
        ffn_grads = ffn_grads + dx_ref[g].astype(F32)
    hidden = hidden_ref[...]
    part, gain_part = norm_back(hidden, gain_ref[...].astype(F32), ffn_grads)
    hidden_grads = up_ref[...].astype(F32) + part
    grads_ref[...] = hidden_grads
    low_ref[...] = hidden_grads.astype(BF16)
    router_part = dot_nn(logit_grads, ffn_ref[...])

    @pl.when(pl.program_id(0) == 0)
    def _():
        router_grad_ref[...] = router_part
        gain_grad_ref[...] = gain_part[None]

    @pl.when(pl.program_id(0) > 0)
    def _():
        router_grad_ref[...] += router_part
        gain_grad_ref[...] += gain_part[None]


def hidden_back(sources, dx_home, gg_home, gates, router_rows, hidden, gain_row, out_grad, ffn_in):
    groups, tokens, width = dx_home.shape
    experts = gates.shape[0]
    step = 128
    rows = pl.BlockSpec((step, width), lambda i: (i, 0))
    return pl.pallas_call(
        hidden_back_kernel,
        grid=(tokens // step,),
        in_specs=[
            pl.BlockSpec((sources, step, width), lambda i: (0, i, 0)),
            pl.BlockSpec((groups, 8, step), lambda i: (0, 0, i)),
            pl.BlockSpec((experts, step), lambda i: (0, i)),
            whole_spec((experts, width)),
            rows,
            whole_spec((1, width)),
            rows,
            rows,
        ],
        out_specs=[rows, rows, whole_spec((experts, width)), whole_spec((1, width))],
        out_shape=[
            jax.ShapeDtypeStruct((tokens, width), F32),
            jax.ShapeDtypeStruct((tokens, width), BF16),
            jax.ShapeDtypeStruct((experts, width), F32),
            jax.ShapeDtypeStruct((1, width), F32),
        ],
        compiler_params=pltpu.CompilerParams(vmem_limit_bytes=62 << 20),
        cost_estimate=pl.CostEstimate(flops=10**8, bytes_accessed=20 << 20, transcendentals=0),
        name="hidden_back",
    )(dx_home, gg_home, gates, router_rows, hidden, gain_row, out_grad, ffn_in)


def unpack_experts(tall, short, held, expand_ref, project_ref):
    side = project_ref.shape[2] - 2 * FF
    for i in range(held.shape[0]):
        value = held[i].astype(F32)
        expand_ref[i] = value[:tall]
        project_ref[i, :, : 2 * FF] = value[tall : tall + short]
        project_ref[i, : short // 2, 2 * FF :] = value[tall + short :, :side]
        project_ref[i, short // 2 :, 2 * FF :] = value[tall + short :, side:]


def unpack_kernel(tall, short, counts, *refs):
    first_ref, last_ref, hidden_ref, *refs = refs
    others, refs = refs[: counts[2]], refs[counts[2] :]
    grad_in, *refs = refs
    out_ref, qkv_ref, few_ref, output_ref, grad_ref, expand_ref, project_ref = refs[:7]
    out_grad_ref, qkv_grad_ref, gain_one_ref, gain_two_ref, router_ref = refs[7:]
    i = pl.program_id(0)

    @pl.when(i < counts[0])
    def _():
        unpack_experts(tall, short, first_ref, expand_ref, project_ref)

    @pl.when(i >= counts[0])
    def _():
        unpack_experts(tall, short, last_ref, expand_ref, project_ref)

    @pl.when(i < 4)
    def _():
        total = hidden_ref[...]
        for other in others:
            total = total + other[...].astype(F32)
        output_ref[...] = total.astype(BF16)
        grad_ref[...] = grad_in[...]

        tile = 128
        chunk = out_ref.shape[2]
        for at in range(0, out_grad_ref.shape[1], tile):
            out_grad_ref[:, at : at + tile] = out_ref[
                at // chunk, :, at % chunk : at % chunk + tile
            ].astype(F32)
        chunk = qkv_ref.shape[2]
        for at in range(0, qkv_grad_ref.shape[1], tile):
            value = qkv_ref[at // chunk, :, at % chunk : at % chunk + tile].astype(F32)
            j, inside = divmod(at, BLOCK)
            if inside < QW:
                to = j * QW + inside
            elif inside < QW + KW:
                to = PAIRS * QW + j * KW + inside - QW
            else:
                to = PAIRS * (QW + KW) + j * KW + inside - QW - KW
            qkv_grad_ref[:, to : to + tile] = value

    @pl.when(i == 4)
    def _():
        gain_one_ref[...] = few_ref[0:1]
        gain_two_ref[...] = few_ref[1:2]
        router_ref[...] = few_ref[8 : 8 + router_ref.shape[0]]


def unpack_weights(shares, out_total, qkv_total, few, hidden, out_home, input_grad, tall, short, experts):
    tokens, width = hidden.shape
    rows = out_total.shape[1]
    first, last = shares
    counts = (first.shape[0], last.shape[0], len(out_home))
    count = counts[0] + counts[1]
    step = tokens // 4
    block = pl.BlockSpec((step, width), lambda i: (jnp.minimum(i, 3), 0))
    splits = 4 if rows % 64 == 0 else 2
    short_rows = rows // splits
    one = (1,) + first.shape[1:]
    return pl.pallas_call(
        functools.partial(unpack_kernel, tall, short, counts),
        grid=(count,),
        in_specs=[
            pl.BlockSpec(one, lambda i: (jnp.minimum(i, counts[0] - 1), 0, 0)),
            pl.BlockSpec(one, lambda i: (jnp.maximum(i - counts[0], 0), 0, 0)),
        ]
        + [block] * (2 + len(out_home))
        + [
            pl.BlockSpec(
                (t.shape[0], short_rows, t.shape[2]), lambda i: (0, jnp.minimum(i, splits - 1), 0)
            )
            for t in (out_total, qkv_total)
        ]
        + [whole_spec(few.shape)],
        out_specs=[
            block,
            block,
            pl.BlockSpec((1, tall, 2 * FF), lambda i: (i, 0, 0)),
            pl.BlockSpec((1, short, width), lambda i: (i, 0, 0)),
            pl.BlockSpec((short_rows, HEADS * HEAD), lambda i: (jnp.minimum(i, splits - 1), 0)),
            pl.BlockSpec((short_rows, PAIRS * BLOCK), lambda i: (jnp.minimum(i, splits - 1), 0)),
            whole_spec((1, rows)),
            whole_spec((1, rows)),
            whole_spec((experts, rows)),
        ],
        out_shape=[
            jax.ShapeDtypeStruct(hidden.shape, BF16),
            jax.ShapeDtypeStruct(hidden.shape, F32),
            jax.ShapeDtypeStruct((count, tall, 2 * FF), F32),
            jax.ShapeDtypeStruct((count, short, width), F32),
            jax.ShapeDtypeStruct((rows, HEADS * HEAD), F32),
            jax.ShapeDtypeStruct((rows, PAIRS * BLOCK), F32),
            jax.ShapeDtypeStruct((1, rows), F32),
            jax.ShapeDtypeStruct((1, rows), F32),
            jax.ShapeDtypeStruct((experts, rows), F32),
        ],
        compiler_params=pltpu.CompilerParams(vmem_limit_bytes=62 << 20),
        cost_estimate=pl.CostEstimate(flops=10**7, bytes_accessed=24 << 20, transcendentals=0),
        name="unpack_weights",
    )(first, last, hidden, *out_home, input_grad, out_total, qkv_total, few)


def bands(count):
    return [(0, 2), (2, 3), (3, count)]


def local(
    inputs, attn_gain, qkv_weight, out_weight, ffn_gain, router_weight,
    expand_weight, project_weight, segment_ids, routes, out_grad,
):
    groups, shards = lax.axis_size("expert"), lax.axis_size("shard")
    tokens, width = inputs.shape
    experts = router_weight.shape[1]
    local_count = expand_weight.shape[0]
    capacity = 8 * ((5 * tokens * TOP + 32 * experts - 1) // (32 * experts))

    packed, *bands_packed = pack_weights(
        expand_weight, project_weight, qkv_weight, attn_gain, ffn_gain, router_weight
    )
    packed_full = [lax.all_gather(p, "shard", axis=0) for p in bands_packed]
    qkv_full, out_part, *u_others = gather_weights(
        [packed, out_weight], out_grad, groups, shards
    )
    qkv_full = qkv_full.reshape(width, -1)
    misc_rows = qkv_full[:, PAIRS * BLOCK :].T
    gain_one, gain_two = misc_rows[0:1], misc_rows[1:2]
    router_rows = misc_rows[8 : 8 + experts]
    tables = tuple(jnp.asarray(t) for t in rope_tables())
    seg_row = segment_ids.reshape(1, tokens)
    seg_col = segment_ids.reshape(tokens, 1)
    normed_t, proj, mixed, lse, out_full = attention_forward(
        inputs, gain_one, qkv_full, tables, seg_col, seg_row, out_part, groups, shards
    )
    hidden, ffn_in, gates, meta_own = middle(
        mixed, out_full, inputs, gain_two, router_rows, routes.T, groups
    )
    tall, short = expand_weight.shape[1], project_weight.shape[1]
    call = functools.partial(expert_call, capacity, shards, groups)

    cores = [[2 * z + core for z in range(shards // 2)] for core in range(2)]

    def share_out(dw):
        return lax.psum_scatter(
            dw, "shard", scatter_dimension=0, axis_index_groups=cores, tiled=True
        )[0]

    x_all, u_all, meta, out_acc, dx_acc, gg, dw = call(
        0, "first", (ffn_in, meta_own, out_grad, *u_others), packed_full[0]
    )
    shares = [share_out(dw)]
    out_acc, dx_acc, gg, dw = call(
        2, "between", (x_all, u_all, meta, out_acc, dx_acc, gg), packed_full[1]
    )
    *out_sent, dx_home, gg_home, dw = call(
        3, "last", (x_all, u_all, meta, out_acc, dx_acc, gg), packed_full[2], dw
    )
    shares.append(share_out(dw))
    sources = 3 if groups == 4 else groups
    hidden_grads, attended_grads, router_part, gain_two_grad = hidden_back(
        sources, dx_home, gg_home, gates, router_rows, hidden, gain_two, out_grad, ffn_in
    )
    dproj, out_sum = attention_backward(
        attended_grads, out_full, proj, mixed, lse, tables, seg_col, seg_row, groups, shards
    )
    out_total, qkv_total, few, input_grad, *out_came = reduce_weights(
        normed_t, dproj, gain_two_grad, router_part, out_sum, gain_one, qkv_full, inputs,
        hidden_grads, out_sent[1:], groups, shards,
    )
    output, input_grad, expand_grad, project_grad, out_weight_grad, qkv_grad, *gains = unpack_weights(
        shares, out_total, qkv_total, few, hidden, [out_sent[0], *out_came], input_grad, tall, short,
        experts,
    )
    return (
        output,
        input_grad,
        gains[0][0],
        qkv_grad,
        out_weight_grad,
        gains[1][0],
        gains[2].T,
        expand_grad,
        project_grad,
    )


def solution(mesh):
    rows = P(("expert", "shard"), None)
    return jax.shard_map(
        local,
        mesh=mesh,
        in_specs=(
            rows, P("shard"), P("shard", None), P("shard", None), P("shard"), P("shard", None),
            P("expert", "shard", None), P("expert", "shard", None), rows, rows, rows,
        ),
        out_specs=(
            rows, rows, P("shard"), P("shard", None), P("shard", None), P("shard"),
            P("shard", None), P("expert", "shard", None), P("expert", "shard", None),
        ),
        check_vma=False,
    )
```

```python
import functools

import jax
import jax.numpy as jnp
import numpy as np
from jax import lax
from jax.experimental import pallas as pl
from jax.experimental.pallas import tpu as pltpu
from jax.sharding import PartitionSpec as P

HEADS = 24
KV_HEADS = 8
HEAD = 64
FF = 512
TOP = 8
SEQ_LEN = 512
GROUP = HEADS // KV_HEADS
PAIRS = KV_HEADS // 2
QW = 2 * GROUP * HEAD
KW = 2 * HEAD
BLOCK = QW + 2 * KW
MISC = 128
QB = 128

EPSILON = 1e-06
ROPE_THETA = 10000.0
MASKED = -1e30
F32 = jnp.float32
BF16 = jnp.bfloat16


def dot_nn(a, b):
    return lax.dot_general(a, b, (((1,), (0,)), ((), ())), preferred_element_type=F32)


def dot_nt(a, b):
    return lax.dot_general(a, b, (((1,), (1,)), ((), ())), preferred_element_type=F32)


def dot_tn(a, b):
    return lax.dot_general(a, b, (((0,), (0,)), ((), ())), preferred_element_type=F32)


def rope_tables():
    frequency = (np.float32(ROPE_THETA) ** (-2.0 * np.arange(HEAD // 2) / HEAD)).astype(np.float32)
    angle = np.arange(SEQ_LEN, dtype=np.float32)[:, None] * frequency[None, :]
    cosine, sine = np.cos(angle).astype(np.float32), np.sin(angle).astype(np.float32)
    zero = np.zeros_like(sine)
    cos_table = np.concatenate([cosine] * 4, axis=1)
    left_table = np.concatenate([-sine, zero] * 2, axis=1)
    right_table = np.concatenate([zero, sine] * 2, axis=1)
    return cos_table, left_table, right_table


def turn(values, cos_table, left_table, right_table, sign):
    parts = []
    for c in range(values.shape[1] // 128):
        piece = values[:, 128 * c : 128 * (c + 1)]
        ahead = pltpu.roll(piece, 96, 1) * left_table
        behind = pltpu.roll(piece, 32, 1) * right_table
        parts.append(piece * cos_table + sign * (ahead + behind))
    return parts[0] if len(parts) == 1 else jnp.concatenate(parts, axis=1)


def key_range(block):
    return max(0, block - 2) * QB, (block + 1) * QB


def block_mask(seg_col, seg_row, block):
    low, high = key_range(block)
    rows = lax.broadcasted_iota(jnp.int32, (QB, high - low), 0) + block * QB
    cols = lax.broadcasted_iota(jnp.int32, (QB, high - low), 1) + low
    same = seg_col[block * QB : (block + 1) * QB, :] == seg_row[:, low:high]
    return jnp.concatenate([(rows >= cols) & same] * GROUP, axis=0)


def heads_of(values, pair, block):
    rows = values[block * QB : (block + 1) * QB, :]
    first = pair * GROUP
    return jnp.concatenate(
        [rows[:, HEAD * h : HEAD * (h + 1)] for h in range(first, first + GROUP)], axis=0
    )


def attention_forward_kernel(
    parts, levels, x_ref, gain_ref, w_ref, cos_ref, left_ref, right_ref, seg_col_ref, seg_row_ref,
    part_ref, normed_t_ref, proj_ref, mixed_ref, lse_ref, full_ref, normed_ref, *sems,
):
    step = pl.program_id(0)
    plan = Gather(parts, levels, [full_ref], sems)

    @pl.when(step == 0)
    def _():
        plan.greet(near=False)
        plan.own_to_mate(lambda: full_ref.at[pl.ds(plan.shard * parts, parts)], 0)
        for k in range(1, levels):
            plan.spread(0, k)

    @pl.when(step == 0)
    def _():
        x = x_ref[...].astype(F32)
        scale = lax.rsqrt(jnp.mean(x * x, axis=-1, keepdims=True) + EPSILON)
        normed = (x * scale * gain_ref[...].astype(F32)).astype(BF16)
        normed_ref[...] = normed
        normed_t_ref[...] = normed.T

    projected = dot_nn(normed_ref[...], w_ref[...])
    turned = turn(projected[:, : QW + KW], cos_ref[...], left_ref[...], right_ref[...], 1.0)
    queries = (turned[:, :QW] * HEAD**-0.5).astype(BF16)
    keys = turned[:, QW:].astype(BF16)
    values = projected[:, QW + KW :].astype(BF16)
    proj_ref[...] = jnp.concatenate([queries, keys, values], axis=1)
    seg_col, seg_row = seg_col_ref[...], seg_row_ref[...]
    for block in range(SEQ_LEN // QB):
        low, high = key_range(block)
        allowed = block_mask(seg_col, seg_row, block)
        outs = []
        for pair in range(2):
            q3 = heads_of(queries, pair, block)
            k1 = keys[low:high, HEAD * pair : HEAD * (pair + 1)]
            v1 = values[low:high, HEAD * pair : HEAD * (pair + 1)]
            scores = jnp.where(allowed, dot_nt(q3, k1), MASKED)
            top = jnp.max(scores, axis=-1, keepdims=True)
            weights = jnp.exp(scores - top)
            total = jnp.sum(weights, axis=-1, keepdims=True)
            mixed = dot_nn(weights.astype(BF16), v1) * (1.0 / total)
            logsum = top + jnp.log(total)
            for h in range(GROUP):
                outs.append(mixed[h * QB : (h + 1) * QB, :])
                lse_ref[0, block * QB : (block + 1) * QB, pair * GROUP + h : pair * GROUP + h + 1] = (
                    logsum[h * QB : (h + 1) * QB, :]
                )
        mixed_ref[block * QB : (block + 1) * QB, :] = jnp.concatenate(outs, axis=1).astype(BF16)

    @pl.when(step == PAIRS - 1)
    def _():
        plan.team_to_mate(0)
        plan.mate_arrived(0)
        plan.finish()


def whole_spec(shape):
    return pl.BlockSpec(shape, lambda *_: (0,) * len(shape))


def attention_forward(x, gain_row, w_full, tables, seg_col, seg_row, out_part, groups, shards):
    tokens, width = x.shape
    parts, levels = gather_parts(groups, width // shards), shards // 2
    table = whole_spec((SEQ_LEN, 128))
    *kept, out_full = pl.pallas_call(
        functools.partial(attention_forward_kernel, parts, levels),
        grid=(PAIRS,),
        in_specs=[
            whole_spec((tokens, width)),
            whole_spec((1, width)),
            pl.BlockSpec((width, BLOCK), lambda j: (0, j)),
            table, table, table,
            whole_spec((SEQ_LEN, 1)),
            whole_spec((1, SEQ_LEN)),
            pl.BlockSpec(memory_space=pl.ANY),
        ],
        out_specs=[
            whole_spec((width, tokens)),
            pl.BlockSpec((tokens, BLOCK), lambda j: (0, j)),
            pl.BlockSpec((tokens, QW), lambda j: (0, j)),
            pl.BlockSpec((1, tokens, 8), lambda j: (j, 0, 0)),
            pl.BlockSpec(memory_space=pl.ANY),
        ],
        out_shape=[
            jax.ShapeDtypeStruct((width, tokens), BF16),
            jax.ShapeDtypeStruct((tokens, PAIRS * BLOCK), BF16),
            jax.ShapeDtypeStruct((tokens, HEADS * HEAD), BF16),
            jax.ShapeDtypeStruct((PAIRS, tokens, 8), F32),
            jax.ShapeDtypeStruct(out_part.shape, BF16),
        ],
        scratch_shapes=[pltpu.VMEM((tokens, width), BF16)] + gather_sems(levels, parts, 1),
        input_output_aliases={8: 4},
        compiler_params=pltpu.CompilerParams(
            vmem_limit_bytes=62 << 20, collective_id=4, has_side_effects=True
        ),
        cost_estimate=pl.CostEstimate(flops=10 * 10**9, bytes_accessed=20 << 20, transcendentals=4 << 20),
        name="attention_forward",
    )(x, gain_row, w_full, *tables, seg_col, seg_row, out_part)
    return *kept, out_full.reshape(width, -1)


def attention_backward_kernel(
    groups, levels, ag_ref, out_ref, proj_ref, mixed_ref, lse_ref, cos_ref, left_ref, right_ref,
    seg_col_ref, seg_row_ref, all_ref, dproj_ref, sum_ref, mixed_t, *rest,
):
    step = pl.program_id(0)
    plan = Reduce(groups, levels, ag_ref.shape[1], rest[:4], rest[4:])

    @pl.when(step == 0)
    def _():
        plan.greet(False)
        mixed_t[...] = all_ref[...].T
        plan.fill(mixed_t, ag_ref)
        plan.merge()

    @pl.when(step == 1)
    def _():
        plan.spread()

    grads = dot_nt(ag_ref[...], out_ref[...]).astype(BF16)
    product = grads.astype(F32) * mixed_ref[...].astype(F32)
    queries, keys, values = (
        proj_ref[:, :QW], proj_ref[:, QW : QW + KW], proj_ref[:, QW + KW :],
    )
    seg_col, seg_row = seg_col_ref[...], seg_row_ref[...]
    blocks = SEQ_LEN // QB
    dk = [[jnp.zeros((QB, HEAD), F32) for _ in range(blocks)] for _ in range(2)]
    dv = [[jnp.zeros((QB, HEAD), F32) for _ in range(blocks)] for _ in range(2)]
    dq_rows = []
    for block in range(blocks):
        low, high = key_range(block)
        allowed = block_mask(seg_col, seg_row, block)
        dqs = []
        for pair in range(2):
            q3, g3, o3 = (heads_of(v, pair, block) for v in (queries, grads, product))
            k1 = keys[low:high, HEAD * pair : HEAD * (pair + 1)]
            v1 = values[low:high, HEAD * pair : HEAD * (pair + 1)]
            logsum = jnp.concatenate(
                [
                    lse_ref[0, block * QB : (block + 1) * QB, pair * GROUP + h : pair * GROUP + h + 1]
                    for h in range(GROUP)
                ],
                axis=0,
            )
            scores = jnp.where(allowed, dot_nt(q3, k1), MASKED)
            probs = jnp.exp(scores - logsum)
            inner = jnp.sum(o3, axis=-1, keepdims=True)
            score_grads = (probs * (dot_nt(g3, v1) - inner)).astype(BF16)
            dq = dot_nn(score_grads, k1)
            dk_part = dot_tn(score_grads, q3)
            dv_part = dot_tn(probs.astype(BF16), g3)
            for at in range(low // QB, high // QB):
                rows = slice(at * QB - low, (at + 1) * QB - low)
                dk[pair][at] += dk_part[rows]
                dv[pair][at] += dv_part[rows]
            dqs += [dq[h * QB : (h + 1) * QB, :] for h in range(GROUP)]
        dq_rows.append(jnp.concatenate(dqs, axis=1))
    dq_all = jnp.concatenate(dq_rows, axis=0)
    dk_all = jnp.concatenate([jnp.concatenate(d, axis=0) for d in dk], axis=1)
    dv_all = jnp.concatenate([jnp.concatenate(d, axis=0) for d in dv], axis=1)
    turned = jnp.concatenate([dq_all * HEAD**-0.5, dk_all], axis=1)
    back = turn(turned, cos_ref[...], left_ref[...], right_ref[...], -1.0)
    dproj_ref[...] = jnp.concatenate([back, dv_all], axis=1).astype(BF16)

    @pl.when(step == PAIRS - 1)
    def _():
        for k in range(levels):
            sum_ref[k] = plan.collect(k).astype(BF16)
        plan.finish()


def attention_backward(ag, out_full, proj, mixed, lse, tables, seg_col, seg_row, groups, shards):
    tokens, width = ag.shape
    levels, rows = shards // 2, width // shards
    chunk = chunk_of(width, groups)
    table = whole_spec((SEQ_LEN, 128))
    return pl.pallas_call(
        functools.partial(attention_backward_kernel, groups, levels),
        grid=(PAIRS,),
        in_specs=[
            whole_spec((tokens, width)),
            pl.BlockSpec((QW, width), lambda j: (j, 0)),
            pl.BlockSpec((tokens, BLOCK), lambda j: (0, j)),
            pl.BlockSpec((tokens, QW), lambda j: (0, j)),
            pl.BlockSpec((1, tokens, 8), lambda j: (j, 0, 0)),
            table, table, table,
            whole_spec((SEQ_LEN, 1)),
            whole_spec((1, SEQ_LEN)),
            whole_spec((tokens, mixed.shape[1])),
        ],
        out_specs=[
            pl.BlockSpec((tokens, BLOCK), lambda j: (0, j)),
            whole_spec((levels, rows, chunk)),
        ],
        out_shape=[
            jax.ShapeDtypeStruct((tokens, PAIRS * BLOCK), BF16),
            jax.ShapeDtypeStruct((levels, rows, chunk), BF16),
        ],
        scratch_shapes=[pltpu.VMEM((mixed.shape[1], tokens), BF16)]
        + reduce_buffers(groups, levels, rows, chunk)
        + reduce_sems(groups, levels),
        compiler_params=pltpu.CompilerParams(
            vmem_limit_bytes=62 << 20, collective_id=5, has_side_effects=True
        ),
        cost_estimate=pl.CostEstimate(flops=10 * 10**9, bytes_accessed=20 << 20, transcendentals=4 << 20),
        name="attention_backward",
    )(ag, out_full, proj, mixed, lse, *tables, seg_col, seg_row, mixed)


def middle_kernel(
    mixed_ref, out_ref, x_ref, gain_ref, router_ref, routes_ref,
    hidden_ref, ffn_ref, gates_ref, meta_ref,
):
    hidden = x_ref[...].astype(F32) + dot_nn(mixed_ref[...], out_ref[...])
    scale = lax.rsqrt(jnp.mean(hidden * hidden, axis=-1, keepdims=True) + EPSILON)
    hidden_ref[...] = hidden
    ffn_in = (hidden * scale * gain_ref[...].astype(F32)).astype(BF16)
    ffn_ref[...] = ffn_in
    logits = dot_nt(router_ref[...], ffn_in)
    experts, tokens = logits.shape
    index = lax.broadcasted_iota(jnp.int32, (experts, tokens), 0)
    flags = index == routes_ref[0:1, :]
    for k in range(1, TOP):
        flags = flags | (index == routes_ref[k : k + 1, :])
    chosen = jnp.where(flags, logits, MASKED)
    weights = jnp.where(flags, jnp.exp(chosen - jnp.max(chosen, axis=0, keepdims=True)), 0.0)
    gates = weights / jnp.sum(weights, axis=0, keepdims=True)
    gates_ref[...] = gates
    earlier = lax.broadcasted_iota(jnp.int32, (tokens, tokens), 0)
    later = lax.broadcasted_iota(jnp.int32, (tokens, tokens), 1)
    before = jnp.where(earlier < later, 1.0, 0.0).astype(BF16)
    ranks = dot_nn(jnp.where(flags, 1.0, 0.0).astype(BF16), before)
    slots = jnp.where(flags, ranks, -1.0)
    groups = meta_ref.shape[0]
    count = experts // groups
    meta_ref[...] = jnp.zeros(meta_ref.shape, F32)
    for e in range(experts):
        meta_ref[e // count, e % count : e % count + 1, :] = slots[e : e + 1]
        meta_ref[e // count, 8 + e % count : 9 + e % count, :] = gates[e : e + 1]


def middle(mixed, out_full, x, gain_row, router_rows, routes_rows, groups):
    tokens, width = x.shape
    experts = router_rows.shape[0]
    return pl.pallas_call(
        middle_kernel,
        out_shape=[
            jax.ShapeDtypeStruct((tokens, width), F32),
            jax.ShapeDtypeStruct((tokens, width), BF16),
            jax.ShapeDtypeStruct((experts, tokens), F32),
            jax.ShapeDtypeStruct((groups, 16, tokens), F32),
        ],
        compiler_params=pltpu.CompilerParams(vmem_limit_bytes=62 << 20),
        cost_estimate=pl.CostEstimate(flops=3 * 10**9, bytes_accessed=16 << 20, transcendentals=1 << 14),
        name="middle",
    )(mixed, out_full, x, gain_row, router_rows, routes_rows)


def flipped(index, mask):
    out, bit = index, 1
    while bit <= mask:
        if mask & bit:
            out = out + bit - 2 * bit * ((index // bit) % 2)
        bit *= 2
    return out


def send(source, target, send_sem, recv_sem, device):
    return pltpu.make_async_remote_copy(
        src_ref=source, dst_ref=target, send_sem=send_sem, recv_sem=recv_sem,
        device_id=device, device_id_type=pl.DeviceIdType.MESH,
    )


def greet(devices):
    barrier = pltpu.get_barrier_semaphore()
    for device in devices:
        pl.semaphore_signal(barrier, inc=1, device_id=device, device_id_type=pl.DeviceIdType.MESH)
    pl.semaphore_wait(barrier, len(devices))


class Gather:
    def __init__(self, parts, levels, blocks, sems):
        self.parts, self.levels, self.blocks = parts, levels, blocks
        self.near_send, self.near_recv, self.team_send, self.team_recv, self.core_send, self.core_recv = sems
        self.group, self.shard = lax.axis_index("expert"), lax.axis_index("shard")
        level, self.core = self.shard // 2, self.shard % 2
        self.part = self.group % parts
        self.other = self.shard + 1 - 2 * self.core
        self.far = [flipped(level, k) * 2 + self.core for k in range(levels)]
        self.far_other = [flipped(level, k) * 2 + 1 - self.core for k in range(levels)]
        self.team_part = [flipped(self.part, k) for k in range(parts)]
        self.team = [self.group - self.part + t for t in self.team_part]
        self.mate = (self.group, self.other)
        self.sends = []

    def greet(self, near=True):
        greet(
            [self.mate]
            + [(self.group, self.far[k]) for k in range(1, self.levels) if near]
            + [(self.team[t], self.shard) for t in range(1, self.parts)]
        )

    def push(self, make):
        make().start()
        self.sends.append(make)

    def arrived(self, piece, send_sem, recv_sem):
        send(piece, piece, send_sem, recv_sem, self.mate).wait_recv()

    def near(self, own, i):
        for k in range(1, self.levels):
            self.push(
                lambda k=k: send(
                    own.at[self.part], self.blocks[i].at[self.shard * self.parts + self.part],
                    self.near_send.at[i, k], self.near_recv.at[i, k], (self.group, self.far[k]),
                )
            )

    def near_arrived(self, i, k):
        piece = self.blocks[i].at[self.far[k] * self.parts + self.part]
        self.arrived(piece, self.near_send.at[i, k], self.near_recv.at[i, k])

    def spread(self, i, k):
        def piece():
            return self.blocks[i].at[self.far[k] * self.parts + self.part]

        for t in range(1, self.parts):
            self.push(
                lambda t=t: send(
                    piece(), piece(), self.team_send.at[i, k, t], self.team_recv.at[i, k, t],
                    (self.team[t], self.shard),
                )
            )
        self.push(
            lambda: send(
                piece(), piece(), self.core_send.at[i, k, 0], self.core_recv.at[i, k, 0], self.mate
            )
        )

    def own_to_mate(self, own, i):
        self.push(
            lambda: send(
                own(), self.blocks[i].at[pl.ds(self.shard * self.parts, self.parts)],
                self.core_send.at[i, 0, 0], self.core_recv.at[i, 0, 0], self.mate,
            )
        )

    def team_to_mate(self, i):
        for k in range(1, self.levels):
            for t in range(1, self.parts):

                def piece(k=k, t=t):
                    return self.blocks[i].at[self.far[k] * self.parts + self.team_part[t]]

                self.arrived(piece(), self.team_send.at[i, k, t], self.team_recv.at[i, k, t])
                self.push(
                    lambda piece=piece, k=k, t=t: send(
                        piece(), piece(), self.core_send.at[i, k, t], self.core_recv.at[i, k, t],
                        self.mate,
                    )
                )

    def mate_arrived(self, i):
        piece = self.blocks[i].at[pl.ds(self.other * self.parts, self.parts)]
        self.arrived(piece, self.core_send.at[i, 0, 0], self.core_recv.at[i, 0, 0])
        for k in range(1, self.levels):
            for t in range(self.parts):
                piece = self.blocks[i].at[self.far_other[k] * self.parts + self.team_part[t]]
                self.arrived(piece, self.core_send.at[i, k, t], self.core_recv.at[i, k, t])

    def finish(self):
        for make in self.sends:
            make().wait_send()


def gather_sems(levels, parts, count):
    dma = pltpu.SemaphoreType.DMA
    return [dma((count, levels))] * 2 + [dma((count, levels, parts))] * 4


def gather_parts(groups, rows):
    return next(p for p in (4, 2, 1) if groups % p == 0 and rows % (16 * p) == 0)


class Rows:
    def __init__(self, groups, own, outs, sems):
        self.own, self.outs = own, outs
        self.send_sem, self.recv_sem = sems
        group, self.shard = lax.axis_index("expert"), lax.axis_index("shard")
        self.team = [flipped(group, t) for t in range(groups)]
        self.near = range(1, 1 + len(outs))

    def copy(self, t):
        return send(
            self.own, self.outs[t - 1], self.send_sem.at[t], self.recv_sem.at[t],
            (self.team[t], self.shard),
        )

    def start(self):
        for t in self.near:
            self.copy(t).start()

    def finish(self):
        for t in self.near:
            self.copy(t).wait()


def gather_kernel(groups, parts, levels, *refs):
    ins, own_rows, outs, refs = refs[:2], refs[2], refs[3:5], refs[5:]
    count = 2 if groups == 4 else groups - 1
    others, refs = refs[:count], refs[count:]
    bounce, local_sem = refs[:2], refs[2]
    plan = Gather(parts, levels, outs, refs[3:9])
    rows = Rows(groups, own_rows, others, refs[9:11])
    greet(
        [plan.mate]
        + [(plan.group, plan.far[k]) for k in range(1, levels)]
        + [(rows.team[t], rows.shard) for t in range(1, groups)]
    )
    own = pl.ds(plan.shard * parts, parts)
    loads = [pltpu.make_async_copy(ins[i], bounce[i], local_sem.at[0, i]) for i in range(2)]
    stores = [pltpu.make_async_copy(bounce[i], outs[i].at[own], local_sem.at[1, i]) for i in range(2)]
    for copy in loads:
        copy.start()
    for i in range(2):
        plan.near(ins[i], i)
    rows.start()
    plan.own_to_mate(lambda: ins[0], 0)
    for load, store in zip(loads, stores):
        load.wait()
        store.start()
    for k in range(1, levels):
        plan.near_arrived(0, k)
        plan.spread(0, k)
    plan.team_to_mate(0)
    for k in range(1, levels):
        plan.near_arrived(1, k)
    plan.mate_arrived(0)
    plan.finish()
    rows.finish()
    for copy in stores:
        copy.wait()


def gather_weights(blocks, own_rows, groups, shards):
    rows = blocks[0].shape[0]
    parts = gather_parts(groups, rows)
    levels, count = shards // 2, 2 if groups == 4 else groups - 1
    blocks = [b.reshape(parts, rows // parts, b.shape[1]) for b in blocks]
    dma = pltpu.SemaphoreType.DMA
    return pl.pallas_call(
        functools.partial(gather_kernel, groups, parts, levels),
        in_specs=[pl.BlockSpec(memory_space=pl.ANY)] * 3,
        out_specs=[pl.BlockSpec(memory_space=pl.ANY)] * (2 + count),
        out_shape=[
            jax.ShapeDtypeStruct((shards * parts,) + b.shape[1:], b.dtype) for b in blocks
        ]
        + [jax.ShapeDtypeStruct(own_rows.shape, own_rows.dtype)] * count,
        scratch_shapes=[pltpu.VMEM(b.shape, b.dtype) for b in blocks]
        + [dma((2, 2))]
        + gather_sems(levels, parts, 2)
        + [dma((groups,)), dma((groups,))],
        compiler_params=pltpu.CompilerParams(
            collective_id=0, has_side_effects=True, vmem_limit_bytes=62 << 20
        ),
        name="gather_weights",
    )(*blocks, own_rows)


class Reduce:
    def __init__(self, groups, levels, cols, refs, sems):
        self.groups, self.levels, self.relay = groups, levels, groups == 4
        self.held, self.from_core, self.passing, self.from_group = refs
        self.core_send, self.core_recv, self.pass_send, self.pass_recv, self.group_send, self.group_recv = sems
        self.group, self.shard = lax.axis_index("expert"), lax.axis_index("shard")
        level, self.core = self.shard // 2, self.shard % 2
        self.mate = (self.group, self.shard + 1 - 2 * self.core)
        self.team = [flipped(self.group, t) for t in range(groups)]
        self.far = [flipped(level, k) for k in range(levels)]
        self.order = sorted(range(levels), key=lambda k: (k & -k or levels, k))
        self.near = [1, 2] if self.relay else list(range(1, groups))
        self.sends = []
        turns = ([3] if self.relay else []) + self.near + [0]
        self.even = self.held.shape[4] * groups == cols
        self.chunks = [self.team[t] if self.even else k for k, t in enumerate(turns)]

    def greet(self, climbs):
        greet(
            [self.mate]
            + [(self.group, self.far[k] * 2 + self.core) for k in range(1, self.levels) if climbs]
            + [(self.team[t], self.shard) for t in range(1, self.groups)]
        )

    def push(self, make):
        make().start()
        self.sends.append(make)

    def arrived(self, piece, send_sem, recv_sem):
        send(piece, piece, send_sem, recv_sem, self.mate).wait_recv()

    def fill(self, left, right):
        rows, chunk = self.held.shape[3:]
        tall = 768
        per = tall // rows
        even = self.even
        for k in self.chunks:
            low = k * chunk
            many = chunk if even else max(0, min(chunk, right.shape[1] - low))
            if many:
                at = pl.ds(pl.multiple_of(low, 128), many) if even else slice(low, low + many)

                @pl.loop(0, left.shape[0] // tall)
                def _(c):
                    part = pl.ds(pl.multiple_of(c * tall, tall), tall)
                    value = dot_nn(left[part, :], right[:, at]).astype(BF16)
                    for i in range(per):
                        s = c * per + i
                        self.held[k, s % 2, s // 2, :, :many] = value[i * rows : (i + 1) * rows]

            self.push(
                lambda k=k: send(
                    self.held.at[k, 1 - self.core], self.from_core.at[k],
                    self.core_send.at[k], self.core_recv.at[k], self.mate,
                )
            )

    def pass_copy(self, part, k):
        half = self.held.shape[3] // 2
        return send(
            self.held.at[self.team[3], self.core, self.far[k], pl.ds(part * half, half)],
            self.passing.at[part, k], self.pass_send.at[part, k], self.pass_recv.at[part, k],
            (self.team[1 + part], self.shard),
        )

    def group_copy(self, t, k):
        return send(
            self.held.at[self.team[t], self.core, self.far[k]], self.from_group.at[t, k],
            self.group_send.at[t, k], self.group_recv.at[t, k], (self.team[t], self.shard),
        )

    def merge(self):
        for n, k in enumerate(self.chunks):
            self.arrived(self.from_core.at[k], self.core_send.at[k], self.core_recv.at[k])

            @pl.loop(0, self.levels)
            def _(z):
                self.held[k, self.core, z] = (
                    self.held[k, self.core, z].astype(F32) + self.from_core[k, z].astype(F32)
                ).astype(BF16)

            if self.relay and n == 0:
                for j in self.order:
                    for part in range(2):
                        self.push(lambda part=part, j=j: self.pass_copy(part, j))
        if not self.relay:
            for j in self.order:
                for t in self.near:
                    self.push(lambda t=t, j=j: self.group_copy(t, j))

    def spread(self):
        if not self.relay:
            return
        half = self.held.shape[3] // 2
        for k in self.order:
            for part in range(2):
                self.arrived(
                    self.passing.at[part, k], self.pass_send.at[part, k], self.pass_recv.at[part, k]
                )
                at = pl.ds(part * half, half)
                piece = self.held.at[self.team[2 - part], self.core, self.far[k], at]
                piece[...] = (piece[...].astype(F32) + self.passing[part, k].astype(F32)).astype(BF16)
            for t in self.near:
                self.push(lambda t=t, k=k: self.group_copy(t, k))

    def collect(self, k):
        total = self.held[self.group, self.core, self.far[k]].astype(F32)
        for t in self.near:
            self.arrived(self.from_group.at[t, k], self.group_send.at[t, k], self.group_recv.at[t, k])
            total = total + self.from_group[t, k].astype(F32)
        return total

    def bits(self):
        return [bit for bit in (1, 2, 4, 8, 16) if bit < self.levels]

    def climb(self, summed, from_level, sems, bit, only=None):
        for k in range(self.levels) if only is None else [only]:
            if k & bit and not k & (bit - 1):
                self.push(
                    lambda k=k: send(
                        summed.at[k], from_level.at[k], sems[0].at[k], sems[1].at[k],
                        (self.group, self.far[bit] * 2 + self.core),
                    )
                )

    def climbed(self, summed, from_level, sems, bit):
        for k in range(self.levels):
            if k & bit and not k & (bit - 1):
                self.arrived(from_level.at[k], sems[0].at[k], sems[1].at[k])
                to = k - bit
                summed[to] = (summed[to].astype(F32) + from_level[k].astype(F32)).astype(BF16)

    def settle(self, summed, home, home_sems):
        home[self.group] = summed[0]
        for t in range(1, self.groups):
            self.push(
                lambda t=t: send(
                    home.at[self.group], home.at[self.group],
                    home_sems[0].at[t], home_sems[1].at[t], (self.team[t], self.shard),
                )
            )

    def landed(self, home, home_sems):
        for t in range(1, self.groups):
            self.arrived(home.at[self.team[t]], home_sems[0].at[t], home_sems[1].at[t])

    def finish(self):
        for make in self.sends:
            make().wait_send()


def chunk_of(total, groups):
    return 128 * (-(-total // (128 * groups)))


def reduce_buffers(groups, levels, rows, chunk):
    piece = (rows, chunk)
    passing = (2, levels, rows // 2, chunk) if groups == 4 else (1, 1, 16, 128)
    return [
        pltpu.VMEM((groups, 2, levels) + piece, BF16),
        pltpu.VMEM((groups, levels) + piece, BF16),
        pltpu.VMEM(passing, BF16),
        pltpu.VMEM((groups, levels) + piece, BF16),
    ]


def reduce_sems(groups, levels):
    dma = pltpu.SemaphoreType.DMA
    return [dma((groups,))] * 2 + [dma((2, levels))] * 2 + [dma((groups, levels))] * 2


class FewRows:
    def __init__(self, plan, refs, sems):
        self.plan = plan
        self.rows, self.from_core, self.from_group, self.pieces, self.from_level = refs
        self.core_send, self.core_recv, self.group_send, self.group_recv, self.level_send, self.level_recv = sems

    def start(self):
        plan = self.plan
        plan.push(
            lambda: send(self.rows, self.from_core, self.core_send, self.core_recv, plan.mate)
        )

    def over_groups(self):
        plan = self.plan
        plan.arrived(self.from_core, self.core_send, self.core_recv)
        total = self.rows[...].astype(F32) + self.from_core[...].astype(F32)
        self.from_group[plan.group] = total.astype(BF16)
        for t in range(1, plan.groups):
            plan.push(
                lambda t=t: send(
                    self.from_group.at[plan.group], self.from_group.at[plan.group],
                    self.group_send.at[t], self.group_recv.at[t], (plan.team[t], plan.shard),
                )
            )

    def over_levels(self):
        plan = self.plan
        for t in range(1, plan.groups):
            plan.arrived(self.from_group.at[plan.team[t]], self.group_send.at[t], self.group_recv.at[t])
        total = self.from_group[0].astype(F32)
        for g in range(1, plan.groups):
            total = total + self.from_group[g].astype(F32)
        wide = self.pieces.shape[2]
        for s in range(2 * plan.levels):
            self.pieces[s] = total[:, s * wide : (s + 1) * wide].astype(BF16)
        for k in range(1, plan.levels):
            plan.push(
                lambda k=k: send(
                    self.pieces.at[plan.far[k] * 2 + plan.core], self.from_level.at[k],
                    self.level_send.at[k], self.level_recv.at[k],
                    (plan.group, plan.far[k] * 2 + plan.core),
                )
            )

    def total(self):
        plan = self.plan
        total = self.pieces[plan.shard].astype(F32)
        for k in range(1, plan.levels):
            plan.arrived(self.from_level.at[k], self.level_send.at[k], self.level_recv.at[k])
            total = total + self.from_level[k].astype(F32)
        return total


def input_back(dproj_ref, w_ref, x_ref, gain_ref, held, inner, scale, gain_grad):
    width, step = x_ref.shape[1], 256
    x = x_ref[...].astype(F32)
    scale[...] = lax.rsqrt(jnp.mean(x * x, axis=-1, keepdims=True) + EPSILON)
    inner[...] = jnp.zeros(inner.shape, F32)

    @pl.loop(0, width // step)
    def _(c):
        at = pl.ds(pl.multiple_of(c * step, step), step)
        normed_grads = dot_nt(dproj_ref[...], w_ref[at, :])
        x = x_ref[:, at].astype(F32)
        weighted = normed_grads * gain_ref[:, at].astype(F32)
        inner[...] += jnp.sum(weighted * x, axis=-1, keepdims=True)
        gain_grad[:, at] = jnp.sum(normed_grads * x * scale[...], axis=0, keepdims=True)
        r = scale[...]
        held[:, at] += r * weighted

    r = scale[...]
    factor = r * r * r * (inner[...] * (1.0 / width))
    for low in range(0, width, step):
        cols = slice(low, low + step)
        held[:, cols] -= x_ref[:, cols].astype(F32) * factor


def reduce_kernel(groups, levels, *refs):
    normed_t, dproj_ref, gain_two_ref, router_ref, out_sum_ref, gain_ref = refs[:6]
    w_in, x_in, hidden_grads_in, *refs = refs[6:]
    count = 2 if groups == 4 else groups - 1
    out_sent, refs = refs[:count], refs[count:]
    out_ref, qkv_ref, misc_ref, input_grad_ref, *refs = refs
    out_came, refs = refs[:count], refs[count:]
    summed, from_level, home, out_summed, out_level, out_home = refs[:6]
    plan = Reduce(groups, levels, dproj_ref.shape[1], refs[6:10], refs[10:16])
    level_sems, home_sems, out_level_sems, out_home_sems = (refs[i : i + 2] for i in range(16, 24, 2))
    misc = FewRows(plan, refs[24:29], refs[29:35])
    w_buf, x_buf, held, inner, scale, gain_grad, load_sem, store_sem, row_send, row_recv = refs[35:]
    loads = [
        pltpu.make_async_copy(w_in.at[:, : dproj_ref.shape[1]], w_buf, load_sem.at[0]),
        pltpu.make_async_copy(x_in, x_buf, load_sem.at[1]),
        pltpu.make_async_copy(hidden_grads_in, held, load_sem.at[2]),
    ]
    for load in loads:
        load.start()
    first, *others = plan.bits()
    plan.greet(True)
    out_summed[...] = out_sum_ref[...]
    plan.climb(out_summed, out_level, out_level_sems, first)
    plan.fill(normed_t, dproj_ref)
    plan.merge()
    plan.spread()
    plan.climbed(out_summed, out_level, out_level_sems, first)
    for bit in others[:1]:
        plan.climb(out_summed, out_level, out_level_sems, bit)
    for k in plan.order:
        summed[k] = plan.collect(k).astype(BF16)
        plan.climb(summed, from_level, level_sems, first, k)
    row_copies = [
        send(
            out_sent[t - 1], out_came[t - 1], row_send.at[t], row_recv.at[t],
            (plan.team[t], plan.shard),
        )
        for t in range(1, count + 1)
    ]
    for copy in row_copies:
        copy.start()
    for load in loads:
        load.wait()
    input_back(dproj_ref, w_buf, x_buf, gain_ref, held, inner, scale, gain_grad)
    store = pltpu.make_async_copy(held, input_grad_ref, store_sem)
    store.start()
    experts = router_ref.shape[0]
    gains = jnp.concatenate(
        [gain_grad[...], gain_two_ref[...], jnp.zeros((6, gain_grad.shape[1]), F32)], axis=0
    )
    misc.rows[...] = jnp.zeros(misc.rows.shape, BF16)
    misc.rows[:8] = gains.astype(BF16)
    misc.rows[8 : 8 + experts] = router_ref[...].astype(BF16)
    misc.start()
    misc.over_groups()
    for n, bit in enumerate(others):
        plan.climbed(out_summed, out_level, out_level_sems, bit)
        for bit in others[n + 1 : n + 2]:
            plan.climb(out_summed, out_level, out_level_sems, bit)
    plan.settle(out_summed, out_home, out_home_sems)
    plan.climbed(summed, from_level, level_sems, first)
    for bit in others[:1]:
        plan.climb(summed, from_level, level_sems, bit)
    misc.over_levels()
    for n, bit in enumerate(others):
        plan.climbed(summed, from_level, level_sems, bit)
        for bit in others[n + 1 : n + 2]:
            plan.climb(summed, from_level, level_sems, bit)
    plan.settle(summed, home, home_sems)
    misc_ref[...] = misc.total()
    plan.landed(out_home, out_home_sems)
    out_ref[...] = out_home[...]
    plan.landed(home, home_sems)
    qkv_ref[...] = home[...]
    plan.finish()
    store.wait()
    for copy in row_copies:
        copy.wait()


def reduce_weights(normed_t, dproj, gain_two, router, out_sum, gain_row, w_full, x, hidden_grads, out_sent, groups, shards):
    tokens, width = x.shape
    levels, rows = shards // 2, width // shards
    total = dproj.shape[1]
    chunk, out_chunk = chunk_of(total, groups), out_sum.shape[2]
    dma = pltpu.SemaphoreType.DMA
    vmem, anywhere = (pl.BlockSpec(memory_space=m) for m in (pltpu.VMEM, pl.ANY))
    whole, out_whole = (groups, rows, chunk), (groups, rows, out_chunk)
    few = 16 * (-(-(8 + router.shape[0]) // 16))
    return pl.pallas_call(
        functools.partial(reduce_kernel, groups, levels),
        in_specs=[vmem] * 6 + [anywhere] * (3 + len(out_sent)),
        out_specs=[vmem] * 3 + [anywhere] * (1 + len(out_sent)),
        out_shape=[jax.ShapeDtypeStruct(s, BF16) for s in (out_whole, whole)]
        + [jax.ShapeDtypeStruct((few, rows), F32), jax.ShapeDtypeStruct((tokens, width), F32)]
        + [jax.ShapeDtypeStruct(o.shape, o.dtype) for o in out_sent],
        scratch_shapes=[
            pltpu.VMEM((levels, rows, chunk), BF16),
            pltpu.VMEM((levels, rows, chunk), BF16),
            pltpu.VMEM(whole, BF16),
            pltpu.VMEM((levels, rows, out_chunk), BF16),
            pltpu.VMEM((levels, rows, out_chunk), BF16),
            pltpu.VMEM(out_whole, BF16),
        ]
        + reduce_buffers(groups, levels, rows, chunk)
        + reduce_sems(groups, levels)
        + [dma((levels,))] * 2 + [dma((groups,))] * 2 + [dma((levels,))] * 2 + [dma((groups,))] * 2
        + [
            pltpu.VMEM((few, width), BF16),
            pltpu.VMEM((few, width), BF16),
            pltpu.VMEM((groups, few, width), BF16),
            pltpu.VMEM((shards, few, rows), BF16),
            pltpu.VMEM((levels, few, rows), BF16),
            dma, dma, dma((groups,)), dma((groups,)), dma((levels,)), dma((levels,)),
            pltpu.VMEM((width, total), BF16),
            pltpu.VMEM((tokens, width), BF16),
            pltpu.VMEM((tokens, width), F32),
            pltpu.VMEM((tokens, 1), F32),
            pltpu.VMEM((tokens, 1), F32),
            pltpu.VMEM((1, width), F32),
            dma((3,)), dma, dma((groups,)), dma((groups,)),
        ],
        compiler_params=pltpu.CompilerParams(
            collective_id=1, has_side_effects=True, vmem_limit_bytes=62 << 20
        ),
        cost_estimate=pl.CostEstimate(
            flops=2 * tokens * width * total, bytes_accessed=8 << 20, transcendentals=0
        ),
        name="reduce_weights",
    )(normed_t, dproj, gain_two, router, out_sum, gain_row, w_full, x, hidden_grads, *out_sent)


def expert_kernel(capacity, shards, groups, count, base, stage, *refs):
    refs = list(refs)
    take = lambda n: [refs.pop(0) for _ in range(n)]
    if stage == "first":
        x_own, meta_own = take(2)
        u_ins = take(3 if groups == 4 else groups)
    else:
        x_ref, u_ref, meta_ref, out_in, dx_in, gg_in = take(6)
    packed_ref = take(1)[0]
    if stage == "last":
        earlier_ref = take(1)[0]
    if stage == "first":
        x_all, u_all, meta_all, out_ref, dx_ref, gg_ref, dw_out = take(7)
    elif stage == "last":
        out_homes = take(3 if groups == 4 else groups)
        dx_home, gg_home, dw_out = take(3)
    else:
        out_ref, dx_ref, gg_ref, dw_out = take(4)
    xs, us, bs, inn, dw, dw_sem, we_all, wp_all, we_sem, wp_sem = take(10)
    if stage != "between":
        core_buf, core_send, core_recv, credit = take(4)
    if stage == "first":
        x_buf, u_buf, meta_buf = take(3)
        x_send, x_recv, meta_send, meta_recv, load_sem, u_sem, meta_sem, keep_sem, pass_sem = take(9)
    elif stage == "last":
        buf, passing, gg_buf = take(3)
        load_sem, pass_send, pass_recv, dx_send, dx_recv, gg_send, gg_recv, keep_sem = take(8)
    turn_at, expert = pl.program_id(0), pl.program_id(1)
    last_turn, last = groups - 1, count - 1
    group, shard = lax.axis_index("expert"), lax.axis_index("shard")
    team = [flipped(group, t) for t in range(groups)]
    core = shard % 2
    mate = (group, shard + 1 - 2 * core)
    width = xs.shape[2]
    tokens = x_buf.shape[0] if stage == "first" else x_ref.shape[1]
    tall, short = width // shards, FF // shards
    side = width - 2 * FF
    we_ref, wp_ref = we_all.at[expert], wp_all.at[expert]

    @pl.when((turn_at == 0) & (expert == 0))
    def _():
        for e in range(count):

            @pl.loop(0, shards)
            def _(s):
                a = pl.ds(pl.multiple_of(s * tall, 16), tall)
                b = pl.ds(pl.multiple_of(s * short, 16), short)
                low = pl.ds(pl.multiple_of(s * short, 16), short // 2)
                high = pl.ds(pl.multiple_of(s * short + short // 2, 16), short // 2)
                source = packed_ref.at[s, e]
                rest = pl.ds(tall + short, short // 2)
                for piece, target, sem in (
                    (source.at[:tall], we_all.at[e, a], we_sem),
                    (source.at[tall : tall + short], wp_all.at[e, b, : 2 * FF], wp_sem),
                    (source.at[rest, :side], wp_all.at[e, low, 2 * FF :], wp_sem),
                    (source.at[rest, side:], wp_all.at[e, high, 2 * FF :], wp_sem),
                ):
                    pltpu.make_async_copy(piece, target, sem.at[e]).start()

    def core_copy(source):
        return send(source.at[:, 1 - core], core_buf, core_send, core_recv, mate)

    def core_add(source):
        core_copy(source).wait()

        @pl.loop(0, shards // 2)
        def _(z):
            core_buf[z] = (dw[z, core].astype(F32) + core_buf[z].astype(F32)).astype(BF16)

    def store_half(at):
        return pltpu.make_async_copy(core_buf, dw_out.at[:, at], dw_sem)

    def core_free(at):
        store_half(at).wait()
        pl.semaphore_signal(credit, inc=1, device_id=mate, device_id_type=pl.DeviceIdType.MESH)

    def own_half():
        return pltpu.make_async_copy(earlier_ref.at[:, core], dw.at[:, core], keep_sem.at[1])

    before = 1 if stage == "last" else 0

    if stage == "first":
        relay = groups == 4
        near = [1, 2] if relay else list(range(1, groups))
        half = tokens // 2

        def x_copy(t):
            return send(x_own, x_all.at[t], x_send.at[t], x_recv.at[t], (team[t], shard))

        def passed(source, target, part, sems):
            at = pl.ds(part * half, half)
            return send(
                source.at[at], target.at[3, at], sems.at[0, part], sems.at[1, part],
                (team[2 - part], shard),
            )

        def x_pass(part):
            return passed(x_all.at[1 + part], x_all, part, pass_sem.at[0])

        def u_pass(part):
            return passed(u_ins[1 + part], u_all, part, pass_sem.at[1])

        def meta_copy(t):
            return send(
                meta_own.at[team[t]], meta_all.at[t], meta_send.at[t], meta_recv.at[t], (team[t], shard)
            )

        def u_load(t):
            source = u_all.at[t] if relay and t == 3 else u_ins[t]
            return pltpu.make_async_copy(source, u_buf.at[t % 2], u_sem.at[t % 2])

        def x_keep():
            return pltpu.make_async_copy(x_buf, x_all.at[0], keep_sem.at[0])

        def meta_keep():
            return pltpu.make_async_copy(meta_buf, meta_all.at[0], keep_sem.at[1])

        def u_keep(t):
            return pltpu.make_async_copy(u_buf.at[t % 2], u_all.at[t], keep_sem.at[2 + t])

        for t in range(groups):

            @pl.when((turn_at == t) & (expert == 0))
            def _():
                if t == 0:
                    u_load(0).start()
                    greet([mate] + [(team[k], shard) for k in range(1, groups)])
                    for k in range(1, groups):
                        meta_copy(k).start()
                    for k in near:
                        x_copy(k).start()
                    fetch_x, fetch_meta = x_own, meta_own.at[group]
                else:
                    if not relay:
                        x_copy(t).wait_recv()
                    elif t == 1:
                        for k in near:
                            x_copy(k).wait_recv()
                        for part in range(2):
                            x_pass(part).start()
                        for part in range(2):
                            u_pass(part).start()
                    elif t == 3:
                        for part in range(2):
                            x_pass(part).wait_recv()
                            u_pass(part).wait_recv()
                        u_load(3).start()
                    meta_copy(t).wait_recv()
                    u_keep(t - 1).wait()
                    if t == 1:
                        x_keep().wait()
                        meta_keep().wait()
                    fetch_x, fetch_meta = x_all.at[t], meta_all.at[t]
                load = pltpu.make_async_copy(fetch_x, x_buf, load_sem)
                load_meta = pltpu.make_async_copy(fetch_meta, meta_buf, meta_sem)
                load.start()
                load_meta.start()
                if t + 1 < groups and not (relay and t == 2):
                    u_load(t + 1).start()
                u_load(t).wait()
                load_meta.wait()
                load.wait()
                if not (relay and t == 3):
                    u_keep(t).start()
                if t == 0:
                    x_keep().start()
                    meta_keep().start()

        x_now, u_now, meta_now = x_buf, u_buf.at[turn_at % 2], meta_buf
    else:
        x_now, u_now, meta_now = x_ref.at[0], u_ref.at[0], meta_ref.at[0]

    if stage == "last":
        relay = groups == 4
        slots, half = buf.shape[1], tokens // 2
        halves = [pl.ds(0, half), pl.ds(half, half)]

        def kept(kind, i):
            return buf.at[kind, i % slots]

        def load(kind, i):
            source = dx_in if kind else out_in
            return pltpu.make_async_copy(
                source.at[last_turn - i], kept(kind, i), load_sem.at[kind, i % 2]
            )

        def store(i):
            return pltpu.make_async_copy(kept(0, i), out_homes[last_turn - i], keep_sem.at[2 + i])

        def pass_copy(kind, part):
            return send(
                kept(kind, 0).at[halves[part]], passing.at[kind, part],
                pass_send.at[kind, part], pass_recv.at[kind, part], (team[1 + part], shard),
            )

        def dx_copy(i):
            t = last_turn - i
            return send(kept(1, i), dx_home.at[t], dx_send.at[t], dx_recv.at[t], (team[t], shard))

        def dx_half(part):
            at = halves[part]
            return send(
                kept(1, 1).at[at], dx_home.at[2, at], dx_send.at[2 + part], dx_recv.at[2 + part],
                (team[2], shard),
            )

        def gg_copy(i):
            t = last_turn - i
            return send(gg_buf.at[i], gg_home.at[group], gg_send.at[t], gg_recv.at[t], (team[t], shard))

        def own_copies():
            return [
                pltpu.make_async_copy(kept(1, last_turn), dx_home.at[0], keep_sem.at[0]),
                pltpu.make_async_copy(gg_buf.at[last_turn], gg_home.at[group], keep_sem.at[1]),
            ]

        for i in range(groups):

            @pl.when((turn_at == i) & (expert == 0))
            def _():
                if i == 0:
                    for kind in range(2):
                        load(kind, 0).start()
                    greet([mate] + [(team[k], shard) for k in range(1, groups)])
                    core_copy(earlier_ref).start()
                    own_half().start()
                if i == 1:
                    own_half().wait()
                    core_add(earlier_ref)
                    store_half(0).start()
                if i == 2:
                    core_free(0)
                if i + 1 < groups:
                    if i + 1 >= slots:
                        dx_copy(i + 1 - slots).wait_send()
                        store(i + 1 - slots).wait()
                    for kind in range(2):
                        load(kind, i + 1).start()
                for kind in range(2):
                    load(kind, i).wait()

        at_now = turn_at % slots
        out_now, dx_now, gg_now = buf.at[0, at_now], buf.at[1, at_now], gg_buf.at[turn_at]
    else:
        out_now, dx_now, gg_now = out_ref.at[0], dx_ref.at[0], gg_ref.at[0]

    @pl.when(expert == 0)
    def _():
        if stage == "first":
            out_now[...] = jnp.zeros((tokens, width), BF16)
            dx_now[...] = jnp.zeros((tokens, width), BF16)
            gg_now[...] = jnp.zeros((8, tokens), F32)
        else:
            gg_now[...] = gg_in[0]
        if stage == "between":
            out_now[...] = out_in[0]
            dx_now[...] = dx_in[0]

    @pl.when(turn_at == 0)
    def _():
        pltpu.make_async_copy(we_ref, we_ref, we_sem.at[expert]).wait()
        pltpu.make_async_copy(wp_ref, wp_ref, wp_sem.at[expert]).wait()

    slot_row = meta_now[pl.ds(base + expert, 1), :]
    gate_row = meta_now[pl.ds(8 + base + expert, 1), :]
    index = lax.broadcasted_iota(jnp.int32, (capacity, tokens), 0).astype(F32)
    pick = jnp.where(index == slot_row, 1.0, 0.0)
    gate_col = jnp.sum(pick * gate_row, axis=1, keepdims=True)
    place = pick.astype(BF16)
    rows = pl.ds(pl.multiple_of(turn_at * capacity, capacity), capacity)
    x = dot_nn(place, x_now[...]).astype(BF16)
    xs[expert, rows, :] = x
    u_rows = dot_nn(place, u_now[...]).astype(BF16)
    us[expert, rows, :] = u_rows
    both_parts = dot_nn(x, we_ref[...])
    gate, up = both_parts[:, :FF], both_parts[:, FF:]
    back = dot_nt(u_rows, wp_ref[...])
    sig = 1.0 / (1.0 + jnp.exp(-gate))
    act = gate * sig
    inner = act * up
    inner_low = inner.astype(BF16)
    gate_grad = jnp.sum(inner * back, axis=1, keepdims=True)
    here = lax.broadcasted_iota(jnp.int32, (8, tokens), 0) == base + expert
    gg_now[...] = jnp.where(here, jnp.sum(pick * gate_grad, axis=0, keepdims=True), gg_now[...])
    inn[expert, rows, :] = (inner * gate_col).astype(BF16)
    inner_grads = back * gate_col
    bs[expert, rows, :FF] = (inner_grads * up * sig * (1.0 + gate * (1.0 - sig))).astype(BF16)
    bs[expert, rows, FF:] = (inner_grads * act).astype(BF16)
    both = bs[expert, rows, :]
    weighted_t = (pick * gate_row).astype(BF16).T
    place_t = place.T
    result = dot_nn(inner_low, wp_ref[...]).astype(BF16)
    out_now[...] = (out_now[...].astype(F32) + dot_nn(weighted_t, result)).astype(BF16)
    row_grads = dot_nt(both, we_ref[...]).astype(BF16)
    dx_now[...] = (dx_now[...].astype(F32) + dot_nn(place_t, row_grads)).astype(BF16)

    if stage == "last":

        def add_passed(kind):
            for part in range(2):
                pass_copy(kind, part).wait_recv()
                target = kept(kind, 1 + part).at[halves[part]]
                target[...] = (target[...].astype(F32) + passing[kind, part].astype(F32)).astype(BF16)

        for i in range(groups):

            @pl.when((turn_at == i) & (expert == last))
            def _():
                if i < last_turn:
                    gg_copy(i).start()
                else:
                    for copy in own_copies():
                        copy.start()
                if not relay:
                    store(i).start()
                    if i < last_turn:
                        dx_copy(i).start()
                elif i == 0:
                    for kind in (1, 0):
                        for part in range(2):
                            pass_copy(kind, part).start()
                elif i == 1:
                    dx_half(1).start()
                elif i == 2:
                    add_passed(1)
                    dx_copy(2).start()
                    dx_half(0).start()
                else:
                    add_passed(0)
                    for k in range(1, groups):
                        store(k).start()

    @pl.when(turn_at == last_turn)
    def _():
        if stage != "between" and count > 1:

            @pl.when(expert > 0)
            def _():
                core_add(dw)
                store_half(before + expert - 1).start()

        wide, half = 384, FF // 2

        @pl.loop(0, width // wide)
        def _(c):
            at = pl.ds(pl.multiple_of(c * wide, wide), wide)
            value = dot_tn(xs[expert, :, at], bs[expert]).astype(BF16)
            for i in range(wide // tall):
                s = c * (wide // tall) + i
                dw[s // 2, s % 2, :tall, :] = value[i * tall : (i + 1) * tall]

        @pl.loop(0, FF // half)
        def _(c):
            at = pl.ds(pl.multiple_of(c * half, half), half)
            value = dot_tn(inn[expert, :, at], us[expert]).astype(BF16)
            for i in range(half // short):
                s, low = c * (half // short) + i, i * short
                mid, high = low + short // 2, low + short
                dw[s // 2, s % 2, tall : tall + short, :] = value[low:high, : 2 * FF]
                dw[s // 2, s % 2, tall + short :, :side] = value[low:mid, 2 * FF :]
                dw[s // 2, s % 2, tall + short :, side:] = value[mid:high, 2 * FF :]

        if stage == "between":
            pltpu.make_async_copy(dw, dw_out, dw_sem).start()
        else:
            if count > 1:

                @pl.when(expert > 0)
                def _():
                    core_free(before + expert - 1)

            if before:
                pl.semaphore_wait(credit, 1)
            else:

                @pl.when(expert > 0)
                def _():
                    pl.semaphore_wait(credit, 1)

            core_copy(dw).start()

    @pl.when((turn_at == last_turn) & (expert == last))
    def _():
        if stage == "between":
            pltpu.make_async_copy(dw, dw_out, dw_sem).wait()
        else:
            core_add(dw)
            store_half(before + last).start()
            store_half(before + last).wait()
        if stage == "first":
            if not relay:
                u_keep(last_turn).wait()
            for t in range(1, groups):
                meta_copy(t).wait_send()
            for t in near:
                x_copy(t).wait_send()
            if relay:
                for part in range(2):
                    x_pass(part).wait_send()
                    u_pass(part).wait_send()
        if stage == "last":
            for i in range(groups - 1):
                t = last_turn - i
                gg_copy(i).wait_send()
                send(
                    gg_buf.at[i], gg_home.at[team[t]], gg_send.at[t], gg_recv.at[t], (team[t], shard)
                ).wait_recv()
            if relay:
                for part in range(2):
                    dx_half(part).wait()
                    for kind in range(2):
                        pass_copy(kind, part).wait_send()
                dx_copy(2).wait()
                for k in range(1, groups):
                    store(k).wait()
            else:
                for i in range(groups - 1):
                    if i + slots >= groups:
                        dx_copy(i).wait_send()
                    dx_copy(i).wait_recv()
                for i in range(groups - slots, groups):
                    store(i).wait()
            for copy in own_copies():
                copy.wait()


def expert_call(capacity, shards, groups, base, stage, data, packed_weights, *kept):
    count = packed_weights.shape[1]
    tokens, width = data[0].shape[-2:]
    total = groups * capacity
    anywhere = pl.BlockSpec(memory_space=pl.ANY)
    turned = (lambda i: i) if stage == "first" else (lambda i: groups - 1 - i)
    block = pl.BlockSpec((1, tokens, width), lambda i, e: (turned(i), 0, 0))
    small = pl.BlockSpec((1, 8, tokens), lambda i, e: (turned(i), 0, 0))
    dma = pltpu.SemaphoreType.DMA
    many = jax.ShapeDtypeStruct((groups, tokens, width), BF16)
    grads = jax.ShapeDtypeStruct((groups, 8, tokens), F32)
    piece = ((width + FF + FF // 2) // shards, 2 * FF)
    summed = 2 if stage == "between" else count + len(kept)
    weights = jax.ShapeDtypeStruct((shards // 2, summed) + piece, BF16)
    meta = jax.ShapeDtypeStruct((groups, 16, tokens), F32)
    scratch = [
        pltpu.VMEM((count, total, width), BF16),
        pltpu.VMEM((count, total, width), BF16),
        pltpu.VMEM((count, total, 2 * FF), BF16),
        pltpu.VMEM((count, total, FF), BF16),
        pltpu.VMEM((shards // 2, 2) + piece, BF16),
        dma,
        pltpu.VMEM((count, width, 2 * FF), BF16),
        pltpu.VMEM((count, FF, width), BF16),
        dma((count,)), dma((count,)),
    ]
    if stage != "between":
        scratch += [
            pltpu.VMEM((shards // 2,) + piece, BF16), dma, dma, pltpu.SemaphoreType.REGULAR,
        ]
    if stage == "first":
        in_specs = [anywhere] * len(data)
        out_specs = [anywhere] * 3 + [block, block, small, anywhere]
        out_shape = [many, many, meta, many, many, grads, weights]
        scratch += [
            pltpu.VMEM((tokens, width), BF16),
            pltpu.VMEM((2, tokens, width), BF16),
            pltpu.VMEM((16, tokens), F32),
            dma((groups,)), dma((groups,)), dma((groups,)), dma((groups,)),
            dma, dma((2,)), dma, dma((2 + groups,)), dma((2, 2, 2)),
        ]
    else:
        meta_block = pl.BlockSpec((1, 16, tokens), lambda i, e: (turned(i), 0, 0))
        in_specs = [block, block, meta_block, block, block, small]
        out_specs = [block, block, small, anywhere]
        if stage == "last":
            in_specs[3:5] = [anywhere] * 2
            sources = 3 if groups == 4 else groups
            out_specs = [anywhere] * (3 + sources)
            slots = groups if groups == 4 else 3
            passed = 2 if groups == 4 else 1
            scratch += [
                pltpu.VMEM((2, slots, tokens, width), BF16),
                pltpu.VMEM((passed, passed, tokens // 2, width), BF16),
                pltpu.VMEM((groups, 8, tokens), F32),
                dma((2, 2)), dma((2, 2)), dma((2, 2)),
                dma((groups,)), dma((groups,)), dma((groups,)), dma((groups,)), dma((2 + groups,)),
            ]
        out_shape = [many, many, grads, weights]
        if stage == "last":
            out_shape[:1] = [jax.ShapeDtypeStruct((tokens, width), BF16)] * sources
    remote = {"first": 2, "last": 3}
    return pl.pallas_call(
        functools.partial(expert_kernel, capacity, shards, groups, count, base, stage),
        grid=(groups, count),
        in_specs=in_specs + [anywhere] * (1 + len(kept)),
        out_specs=out_specs,
        out_shape=out_shape,
        scratch_shapes=scratch,
        compiler_params=pltpu.CompilerParams(
            vmem_limit_bytes=62 << 20,
            **({"collective_id": remote[stage], "has_side_effects": True} if stage in remote else {}),
        ),
        cost_estimate=pl.CostEstimate(
            flops=2 * count * total * width * (4 * tokens + 9 * FF),
            bytes_accessed=6 * groups * tokens * width * 2,
            transcendentals=count * total * FF,
        ),
        name="experts_" + stage,
    )(*data, packed_weights, *kept)


def norm_back(values, gain_row, grad_rows):
    scale_rows = lax.rsqrt(jnp.mean(values * values, axis=-1, keepdims=True) + EPSILON)
    weighted = gain_row * grad_rows
    inner_mean = jnp.mean(weighted * values, axis=-1, keepdims=True)
    input_part = (
        scale_rows * weighted - values * (scale_rows * scale_rows * scale_rows) * inner_mean
    )
    gain_part = jnp.sum(grad_rows * values * scale_rows, axis=0)
    return (input_part, gain_part)


def pack_kernel(
    cuts, expand_ref, project_ref, qkv_ref, gain_one_ref, gain_two_ref, router_ref, packed_ref, *refs
):
    *outs, misc = refs
    short = project_ref.shape[1]
    tall = expand_ref.shape[1]
    side = project_ref.shape[2] - 2 * FF
    for (low, high), out in zip(cuts, outs):
        for e in range(low, high):
            out[e - low, :tall] = expand_ref[e]
            out[e - low, tall : tall + short] = project_ref[e, :, : 2 * FF]
            out[e - low, tall + short :, :side] = project_ref[e, : short // 2, 2 * FF :]
            out[e - low, tall + short :, side:] = project_ref[e, short // 2 :, 2 * FF :]
    for j in range(PAIRS):
        at, to = HEADS * HEAD + j * KW, j * BLOCK + QW
        packed_ref[:, j * BLOCK : to] = qkv_ref[:, j * QW : (j + 1) * QW]
        packed_ref[:, to : to + KW] = qkv_ref[:, at : at + KW]
        at += KV_HEADS * HEAD
        packed_ref[:, to + KW : to + 2 * KW] = qkv_ref[:, at : at + KW]
    misc[...] = jnp.zeros(misc.shape, F32)
    misc[0:1] = gain_one_ref[...].astype(F32)[None]
    misc[1:2] = gain_two_ref[...].astype(F32)[None]
    misc[8 : 8 + router_ref.shape[0]] = router_ref[...].astype(F32)
    packed_ref[:, PAIRS * BLOCK :] = misc[...].T.astype(BF16)


def pack_weights(expand, project, qkv, gain_one, gain_two, router):
    cuts = bands(expand.shape[0])
    rows = expand.shape[1] + project.shape[1] + project.shape[1] // 2
    return pl.pallas_call(
        functools.partial(pack_kernel, cuts),
        out_shape=[jax.ShapeDtypeStruct((qkv.shape[0], PAIRS * BLOCK + MISC), BF16)]
        + [jax.ShapeDtypeStruct((high - low, rows, 2 * FF), BF16) for low, high in cuts],
        scratch_shapes=[pltpu.VMEM((MISC, qkv.shape[0]), F32)],
        compiler_params=pltpu.CompilerParams(vmem_limit_bytes=62 << 20),
        name="pack_weights",
    )(expand, project, qkv, gain_one, gain_two, router.T)


def hidden_back_kernel(
    dx_ref, gg_ref, gates_ref, router_ref, hidden_ref, gain_ref, up_ref, ffn_ref,
    grads_ref, low_ref, router_grad_ref, gain_grad_ref,
):
    gates, groups = gates_ref[...], gg_ref.shape[0]
    count = gates.shape[0] // groups
    gate_grads = jnp.concatenate([gg_ref[g, :count] for g in range(groups)], axis=0)
    mean = jnp.sum(gates * gate_grads, axis=0, keepdims=True)
    logit_grads = (gates * (gate_grads - mean)).astype(BF16)
    ffn_grads = dot_tn(logit_grads, router_ref[...])
    for g in range(dx_ref.shape[0]):
        ffn_grads = ffn_grads + dx_ref[g].astype(F32)
    hidden = hidden_ref[...]
    part, gain_part = norm_back(hidden, gain_ref[...].astype(F32), ffn_grads)
    hidden_grads = up_ref[...].astype(F32) + part
    grads_ref[...] = hidden_grads
    low_ref[...] = hidden_grads.astype(BF16)
    router_part = dot_nn(logit_grads, ffn_ref[...])

    @pl.when(pl.program_id(0) == 0)
    def _():
        router_grad_ref[...] = router_part
        gain_grad_ref[...] = gain_part[None]

    @pl.when(pl.program_id(0) > 0)
    def _():
        router_grad_ref[...] += router_part
        gain_grad_ref[...] += gain_part[None]


def hidden_back(sources, dx_home, gg_home, gates, router_rows, hidden, gain_row, out_grad, ffn_in):
    groups, tokens, width = dx_home.shape
    experts = gates.shape[0]
    step = 256
    rows = pl.BlockSpec((step, width), lambda i: (i, 0))
    return pl.pallas_call(
        hidden_back_kernel,
        grid=(tokens // step,),
        in_specs=[
            pl.BlockSpec((sources, step, width), lambda i: (0, i, 0)),
            pl.BlockSpec((groups, 8, step), lambda i: (0, 0, i)),
            pl.BlockSpec((experts, step), lambda i: (0, i)),
            whole_spec((experts, width)),
            rows,
            whole_spec((1, width)),
            rows,
            rows,
        ],
        out_specs=[rows, rows, whole_spec((experts, width)), whole_spec((1, width))],
        out_shape=[
            jax.ShapeDtypeStruct((tokens, width), F32),
            jax.ShapeDtypeStruct((tokens, width), BF16),
            jax.ShapeDtypeStruct((experts, width), F32),
            jax.ShapeDtypeStruct((1, width), F32),
        ],
        compiler_params=pltpu.CompilerParams(vmem_limit_bytes=62 << 20),
        cost_estimate=pl.CostEstimate(flops=10**8, bytes_accessed=20 << 20, transcendentals=0),
        name="hidden_back",
    )(dx_home, gg_home, gates, router_rows, hidden, gain_row, out_grad, ffn_in)


def unpack_experts(tall, short, held, expand_ref, project_ref):
    side = project_ref.shape[2] - 2 * FF
    for i in range(held.shape[0]):
        value = held[i].astype(F32)
        expand_ref[i] = value[:tall]
        project_ref[i, :, : 2 * FF] = value[tall : tall + short]
        project_ref[i, : short // 2, 2 * FF :] = value[tall + short :, :side]
        project_ref[i, short // 2 :, 2 * FF :] = value[tall + short :, side:]


def unpack_kernel(tall, short, counts, *refs):
    first_ref, last_ref, hidden_ref, *refs = refs
    others, refs = refs[: counts[2]], refs[counts[2] :]
    grad_in, *refs = refs
    out_ref, qkv_ref, few_ref, output_ref, grad_ref, expand_ref, project_ref = refs[:7]
    out_grad_ref, qkv_grad_ref, gain_one_ref, gain_two_ref, router_ref = refs[7:]
    i = pl.program_id(0)

    @pl.when(i < counts[0])
    def _():
        unpack_experts(tall, short, first_ref, expand_ref, project_ref)

    @pl.when(i >= counts[0])
    def _():
        unpack_experts(tall, short, last_ref, expand_ref, project_ref)

    @pl.when(i < 4)
    def _():
        total = hidden_ref[...]
        for other in others:
            total = total + other[...].astype(F32)
        output_ref[...] = total.astype(BF16)
        grad_ref[...] = grad_in[...]

        tile = 128
        chunk = out_ref.shape[2]
        for at in range(0, out_grad_ref.shape[1], tile):
            out_grad_ref[:, at : at + tile] = out_ref[
                at // chunk, :, at % chunk : at % chunk + tile
            ].astype(F32)
        chunk = qkv_ref.shape[2]
        for at in range(0, qkv_grad_ref.shape[1], tile):
            value = qkv_ref[at // chunk, :, at % chunk : at % chunk + tile].astype(F32)
            j, inside = divmod(at, BLOCK)
            if inside < QW:
                to = j * QW + inside
            elif inside < QW + KW:
                to = PAIRS * QW + j * KW + inside - QW
            else:
                to = PAIRS * (QW + KW) + j * KW + inside - QW - KW
            qkv_grad_ref[:, to : to + tile] = value

    @pl.when(i == 4)
    def _():
        gain_one_ref[...] = few_ref[0:1]
        gain_two_ref[...] = few_ref[1:2]
        router_ref[...] = few_ref[8 : 8 + router_ref.shape[0]]


def unpack_weights(shares, out_total, qkv_total, few, hidden, out_home, input_grad, tall, short, experts):
    tokens, width = hidden.shape
    rows = out_total.shape[1]
    first, last = shares
    counts = (first.shape[0], last.shape[0], len(out_home))
    count = counts[0] + counts[1]
    step = tokens // 4
    block = pl.BlockSpec((step, width), lambda i: (jnp.minimum(i, 3), 0))
    splits = 4 if rows % 64 == 0 else 2
    short_rows = rows // splits
    one = (1,) + first.shape[1:]
    return pl.pallas_call(
        functools.partial(unpack_kernel, tall, short, counts),
        grid=(count,),
        in_specs=[
            pl.BlockSpec(one, lambda i: (jnp.minimum(i, counts[0] - 1), 0, 0)),
            pl.BlockSpec(one, lambda i: (jnp.maximum(i - counts[0], 0), 0, 0)),
        ]
        + [block] * (2 + len(out_home))
        + [
            pl.BlockSpec(
                (t.shape[0], short_rows, t.shape[2]), lambda i: (0, jnp.minimum(i, splits - 1), 0)
            )
            for t in (out_total, qkv_total)
        ]
        + [whole_spec(few.shape)],
        out_specs=[
            block,
            block,
            pl.BlockSpec((1, tall, 2 * FF), lambda i: (i, 0, 0)),
            pl.BlockSpec((1, short, width), lambda i: (i, 0, 0)),
            pl.BlockSpec((short_rows, HEADS * HEAD), lambda i: (jnp.minimum(i, splits - 1), 0)),
            pl.BlockSpec((short_rows, PAIRS * BLOCK), lambda i: (jnp.minimum(i, splits - 1), 0)),
            whole_spec((1, rows)),
            whole_spec((1, rows)),
            whole_spec((experts, rows)),
        ],
        out_shape=[
            jax.ShapeDtypeStruct(hidden.shape, BF16),
            jax.ShapeDtypeStruct(hidden.shape, F32),
            jax.ShapeDtypeStruct((count, tall, 2 * FF), F32),
            jax.ShapeDtypeStruct((count, short, width), F32),
            jax.ShapeDtypeStruct((rows, HEADS * HEAD), F32),
            jax.ShapeDtypeStruct((rows, PAIRS * BLOCK), F32),
            jax.ShapeDtypeStruct((1, rows), F32),
            jax.ShapeDtypeStruct((1, rows), F32),
            jax.ShapeDtypeStruct((experts, rows), F32),
        ],
        compiler_params=pltpu.CompilerParams(vmem_limit_bytes=62 << 20),
        cost_estimate=pl.CostEstimate(flops=10**7, bytes_accessed=24 << 20, transcendentals=0),
        name="unpack_weights",
    )(first, last, hidden, *out_home, input_grad, out_total, qkv_total, few)


def bands(count):
    return [(0, 2), (2, 3), (3, count)]


def local(
    inputs, attn_gain, qkv_weight, out_weight, ffn_gain, router_weight,
    expand_weight, project_weight, segment_ids, routes, out_grad,
):
    groups, shards = lax.axis_size("expert"), lax.axis_size("shard")
    tokens, width = inputs.shape
    experts = router_weight.shape[1]
    local_count = expand_weight.shape[0]
    capacity = 8 * ((5 * tokens * TOP + 32 * experts - 1) // (32 * experts))

    packed, *bands_packed = pack_weights(
        expand_weight, project_weight, qkv_weight, attn_gain, ffn_gain, router_weight
    )
    packed_full = [lax.all_gather(p, "shard", axis=0) for p in bands_packed]
    qkv_full, out_part, *u_others = gather_weights(
        [packed, out_weight], out_grad, groups, shards
    )
    qkv_full = qkv_full.reshape(width, -1)
    misc_rows = qkv_full[:, PAIRS * BLOCK :].T
    gain_one, gain_two = misc_rows[0:1], misc_rows[1:2]
    router_rows = misc_rows[8 : 8 + experts]
    tables = tuple(jnp.asarray(t) for t in rope_tables())
    seg_row = segment_ids.reshape(1, tokens)
    seg_col = segment_ids.reshape(tokens, 1)
    normed_t, proj, mixed, lse, out_full = attention_forward(
        inputs, gain_one, qkv_full, tables, seg_col, seg_row, out_part, groups, shards
    )
    hidden, ffn_in, gates, meta_own = middle(
        mixed, out_full, inputs, gain_two, router_rows, routes.T, groups
    )
    tall, short = expand_weight.shape[1], project_weight.shape[1]
    call = functools.partial(expert_call, capacity, shards, groups)

    cores = [[2 * z + core for z in range(shards // 2)] for core in range(2)]

    def share_out(dw):
        return lax.psum_scatter(
            dw, "shard", scatter_dimension=0, axis_index_groups=cores, tiled=True
        )[0]

    x_all, u_all, meta, out_acc, dx_acc, gg, dw = call(
        0, "first", (ffn_in, meta_own, out_grad, *u_others), packed_full[0]
    )
    shares = [share_out(dw)]
    out_acc, dx_acc, gg, dw = call(
        2, "between", (x_all, u_all, meta, out_acc, dx_acc, gg), packed_full[1]
    )
    *out_sent, dx_home, gg_home, dw = call(
        3, "last", (x_all, u_all, meta, out_acc, dx_acc, gg), packed_full[2], dw
    )
    shares.append(share_out(dw))
    sources = 3 if groups == 4 else groups
    hidden_grads, attended_grads, router_part, gain_two_grad = hidden_back(
        sources, dx_home, gg_home, gates, router_rows, hidden, gain_two, out_grad, ffn_in
    )
    dproj, out_sum = attention_backward(
        attended_grads, out_full, proj, mixed, lse, tables, seg_col, seg_row, groups, shards
    )
    out_total, qkv_total, few, input_grad, *out_came = reduce_weights(
        normed_t, dproj, gain_two_grad, router_part, out_sum, gain_one, qkv_full, inputs,
        hidden_grads, out_sent[1:], groups, shards,
    )
    output, input_grad, expand_grad, project_grad, out_weight_grad, qkv_grad, *gains = unpack_weights(
        shares, out_total, qkv_total, few, hidden, [out_sent[0], *out_came], input_grad, tall, short,
        experts,
    )
    return (
        output,
        input_grad,
        gains[0][0],
        qkv_grad,
        out_weight_grad,
        gains[1][0],
        gains[2].T,
        expand_grad,
        project_grad,
    )


def solution(mesh):
    rows = P(("expert", "shard"), None)
    return jax.shard_map(
        local,
        mesh=mesh,
        in_specs=(
            rows, P("shard"), P("shard", None), P("shard", None), P("shard"), P("shard", None),
            P("expert", "shard", None), P("expert", "shard", None), rows, rows, rows,
        ),
        out_specs=(
            rows, rows, P("shard"), P("shard", None), P("shard", None), P("shard"),
            P("shard", None), P("expert", "shard", None), P("expert", "shard", None),
        ),
        check_vma=False,
    )
```
